32 devices in a mesh: row: 4 (over x, core), col: 8 (over z, y).
Axes of the slice: x: 2, y: 2, z: 4, core: 2. Of those that a mesh axis runs over, the one named last changes fastest.
Arguments:
- imu: bfloat16 [16384, 128], P(('row', 'col')), may hold values from -30 to 30
- camera: bfloat16 [8, 2048, 128], P('col', 'row'), may hold values from -30 to 30
- imu_mass: float32 [16384], P('row'), may hold values from 0.3 to 3
- cam_mass: float32 [16384], P('col'), may hold values from 0.3 to 3
Outputs:
- grad_imu: float32 [16384, 128], P(('row', 'col'))
- grad_camera: float32 [8, 2048, 128], P('col', 'row')
The draws below stay inside these ranges and needn't reach their ends.
All inputs are finite; a program needn't handle non-finite values.
Results may differ from the reference program's by a relative error of at most 0.0028.
Values may be sent and summed in bfloat16 or wider, within the bound.
No kernel may reach another device: no remote copies, remote signals or barrier semaphores. Data moves between devices by JAX's collectives and lax.ppermute only.
A program may use at most 128 MiB of HBM per device.

```python
import math
import jax
import jax.numpy as jnp
from jax import lax

D = 128
ITERS = 3
COL_DEV = 2048
IMU_TOTAL = 16384
CAM_TOTAL = 16384
CAM_BLOCKS = 8


def embeddings(key):
    imu = jax.random.normal(jax.random.fold_in(key, 101), (IMU_TOTAL, D), jnp.float32)
    cams = jax.random.normal(jax.random.fold_in(key, 102), (CAM_TOTAL, D), jnp.float32)
    return (jnp.clip(imu, -30.0, 30.0), jnp.clip(cams, -30.0, 30.0))


def draw_imu(key, part):
    imu, cams = embeddings(key)
    return imu.astype(jnp.bfloat16)


def draw_camera(key, part):
    imu, cams = embeddings(key)
    return cams.reshape(CAM_BLOCKS, COL_DEV, D).astype(jnp.bfloat16)


def steps_of(own_key, dims, shards, least, top_value):
    loudness, own = 1.0, jax.random.fold_in(own_key, 6)
    for position, blocks in shards:
        heights = jnp.exp(jax.random.uniform(jax.random.fold_in(own, position), (blocks,), jnp.float32, least / len(shards), top_value / len(shards)))
        loudness = loudness * jnp.repeat(heights, dims[position] // blocks).reshape([-1 if axis == position else 1 for axis in range(len(dims))])
    return loudness


def setup_inputs(seed: int = 0) -> dict:
    splits = jax.random.split(jax.random.key(seed), 5)
    return {
        "imu": draw_imu(jax.random.fold_in(splits[4], 71), 0),
        "camera": draw_camera(jax.random.fold_in(splits[4], 71), 0),
        "imu_mass": jnp.clip(jnp.exp(math.log(3.0) - 2.3025851 * jax.random.uniform(splits[2], (IMU_TOTAL,), jnp.float32) ** steps_of(splits[2], (IMU_TOTAL,), ((0, 4),), -0.2, 0.2)), 0.3, 3.0),
        "cam_mass": jnp.clip(jnp.exp(math.log(3.0) - 2.3025851 * jax.random.uniform(splits[3], (CAM_TOTAL,), jnp.float32) ** steps_of(splits[3], (CAM_TOTAL,), ((0, 8),), -0.2, 0.2)), 0.3, 3.0),
    }


def cost_block(rows, cols):
    rows_sq = jnp.sum(jnp.square(rows.astype(jnp.float32)), axis=1)
    cols_sq = jnp.sum(jnp.square(cols.astype(jnp.float32)), axis=1)
    cross = jnp.dot(rows, cols.T, preferred_element_type=jnp.float32)
    return rows_sq[:, None] + cols_sq[None, :] - 2.0 * cross


def reference(imu, camera, imu_mass, cam_mass):
    epsilon = D / 20.0
    cams = camera.reshape(CAM_TOTAL, D)
    block = math.gcd(IMU_TOTAL, 512)
    count = IMU_TOTAL // block
    imu_blocks = imu.reshape(count, block, D)
    log_a = jnp.log(imu_mass)
    log_b = jnp.log(cam_mass)

    def row_lse(g):
        def single(x_blk):
            scores = (g[None, :] - cost_block(x_blk, cams)) / epsilon
            peak = jnp.max(scores, axis=1)
            return peak + jnp.log(jnp.sum(jnp.exp(scores - peak[:, None]), axis=1))
        return lax.map(single, imu_blocks).reshape(IMU_TOTAL)

    def col_lse(f):
        f_blocks = f.reshape(count, block)

        def advance(carry, item):
            peak, total = carry
            x_blk, f_blk = item
            scores = (f_blk[:, None] - cost_block(x_blk, cams)) / epsilon
            new_peak = jnp.maximum(peak, jnp.max(scores, axis=0))
            total = total * jnp.exp(peak - new_peak) + jnp.sum(jnp.exp(scores - new_peak[None, :]), axis=0)
            return (new_peak, total), None

        start = (jnp.full((CAM_TOTAL,), -1e30, jnp.float32), jnp.zeros((CAM_TOTAL,), jnp.float32))
        (peak, total), unused = lax.scan(advance, start, (imu_blocks, f_blocks))
        return peak + jnp.log(total)

    g = jnp.zeros((CAM_TOTAL,), jnp.float32)
    f = jnp.zeros((IMU_TOTAL,), jnp.float32)
    for step in range(ITERS):
        f = epsilon * log_a - epsilon * row_lse(g)
        g = epsilon * log_b - epsilon * col_lse(f)

    def final(carry, item):
        col_total, pulled_cam = carry
        x_blk, f_blk = item
        plan = jnp.exp((f_blk[:, None] + g[None, :] - cost_block(x_blk, cams)) / epsilon).astype(jnp.bfloat16)
        row_total = jnp.sum(plan.astype(jnp.float32), axis=1)
        pulled = jnp.dot(plan, cams, preferred_element_type=jnp.float32)
        grad_rows = 2.0 * (row_total[:, None] * x_blk.astype(jnp.float32) - pulled)
        col_total = col_total + jnp.sum(plan.astype(jnp.float32), axis=0)
        pulled_cam = pulled_cam + jnp.dot(plan.T, x_blk, preferred_element_type=jnp.float32)
        return (col_total, pulled_cam), grad_rows

    start = (jnp.zeros((CAM_TOTAL,), jnp.float32), jnp.zeros((CAM_TOTAL, D), jnp.float32))
    (col_total, pulled_cam), grad_rows = lax.scan(final, start, (imu_blocks, f.reshape(count, block)))
    grad_imu = grad_rows.reshape(IMU_TOTAL, D)
    grad_cam = 2.0 * (col_total[:, None] * cams.astype(jnp.float32) - pulled_cam)
    return grad_imu, grad_cam.reshape(CAM_BLOCKS, COL_DEV, D)
```

```python
import functools
import math

import jax
import jax.numpy as jnp
from jax import lax
from jax.experimental import pallas as pl
from jax.experimental.pallas import tpu as pltpu
from jax.sharding import PartitionSpec as P

D = 128
ITERS = 3
EPSILON = D / 20.0
LOG2E = math.log2(math.e)
CROSS = 2.0 * LOG2E / EPSILON
NT = (((1,), (1,)), ((), ()))
VMEM = pl.BlockSpec(memory_space=pltpu.VMEM)


def spread(s_ref, sb_ref):
    chunks = s_ref.shape[0]
    turned = jnp.transpose(s_ref[...])
    for k in range(chunks):
        sb_ref[k * 128:(k + 1) * 128, :] = jnp.broadcast_to(turned[:, k:k + 1], (128, 128))


def first_kernel(chunk, width, a_ref, b_ref, s_ref, o_ref, sb_ref):
    depth, lanes = a_ref.shape[0], b_ref.shape[0]
    tiles = width // 128
    spread(s_ref, sb_ref)

    def column(n, _):
        start = pl.multiple_of(n * width, width)
        b = b_ref[pl.ds(start, width), :]

        def step(m, carry):
            peak, total = carry
            at = pl.multiple_of(m * chunk, chunk)
            d = lax.dot_general(a_ref[pl.ds(at, chunk), :], b, NT, preferred_element_type=jnp.float32)
            s = sb_ref[pl.ds(at, chunk), :]
            peaks, totals = [], []
            for q in range(tiles):
                t = (d[:, q * 128:(q + 1) * 128] * CROSS + s).reshape(chunk // 8, 8, 128)
                old = peak[:, q * 128:(q + 1) * 128]
                new = jnp.maximum(old, jnp.max(t, axis=0))
                part = jnp.sum(jnp.exp2(t - new[None]), axis=0)
                peaks.append(new)
                totals.append(total[:, q * 128:(q + 1) * 128] * jnp.exp2(old - new) + part)
            return jnp.concatenate(peaks, axis=1), jnp.concatenate(totals, axis=1)

        init = (jnp.full((8, width), -1e30, jnp.float32), jnp.zeros((8, width), jnp.float32))
        peak, total = lax.fori_loop(0, depth // chunk, step, init, unroll=True)
        top = jnp.max(peak, axis=0, keepdims=True)
        whole = jnp.sum(total * jnp.exp2(peak - top), axis=0, keepdims=True)
        o_ref[:, pl.ds(start, width)] = top + jnp.log2(whole)
        return 0

    lax.fori_loop(0, lanes // width, column, 0)


def sum_kernel(chunk, width, a_ref, b_ref, s_ref, l_ref, o_ref, sb_ref):
    depth, lanes = a_ref.shape[0], b_ref.shape[0]
    tiles = width // 128
    spread(s_ref, sb_ref)

    def column(n, _):
        start = pl.multiple_of(n * width, width)
        b = b_ref[pl.ds(start, width), :]
        l = l_ref[:, pl.ds(start, width)]
        total = [jnp.zeros((8, 128), jnp.float32) for q in range(tiles)]
        for m in range(depth // chunk):
            d = lax.dot_general(a_ref[m * chunk:(m + 1) * chunk, :], b, NT, preferred_element_type=jnp.float32)
            s = sb_ref[m * chunk:(m + 1) * chunk, :]
            for q in range(tiles):
                t = d[:, q * 128:(q + 1) * 128] * CROSS + s + l[:, q * 128:(q + 1) * 128]
                total[q] = total[q] + jnp.sum(jnp.exp2(t).reshape(chunk // 8, 8, 128), axis=0)
        o_ref[:, pl.ds(start, width)] = jnp.sum(jnp.concatenate(total, axis=1), axis=0, keepdims=True)
        return 0

    lax.fori_loop(0, lanes // width, column, 0)


def pass_cost(a, b):
    size = a.shape[0] * b.shape[0]
    return pl.CostEstimate(flops=2 * size * D, bytes_accessed=2 * (a.size + b.size), transcendentals=size)


def first_pass(a, b, s, chunk=512, width=256):
    depth, lanes = a.shape[0], b.shape[0]
    out = pl.pallas_call(
        functools.partial(first_kernel, chunk, width),
        out_shape=jax.ShapeDtypeStruct((1, lanes), jnp.float32),
        in_specs=[VMEM] * 3,
        out_specs=VMEM,
        scratch_shapes=[pltpu.VMEM((depth, 128), jnp.float32)],
        compiler_params=pltpu.CompilerParams(vmem_limit_bytes=32 << 20),
        cost_estimate=pass_cost(a, b),
        name="first_pass",
    )(a, b, s.reshape(depth // 128, 128))
    return out.reshape(lanes)


def sum_pass(a, b, s, l, chunk=512, width=256):
    depth, lanes = a.shape[0], b.shape[0]
    out = pl.pallas_call(
        functools.partial(sum_kernel, chunk, width),
        out_shape=jax.ShapeDtypeStruct((1, lanes), jnp.float32),
        in_specs=[VMEM] * 4,
        out_specs=VMEM,
        scratch_shapes=[pltpu.VMEM((depth, 128), jnp.float32)],
        compiler_params=pltpu.CompilerParams(vmem_limit_bytes=32 << 20),
        cost_estimate=pass_cost(a, b),
        name="sum_pass",
    )(a, b, s.reshape(depth // 128, 128), l.reshape(1, lanes))
    return out.reshape(lanes)


def final_kernel(chunk, x_ref, xt_ref, y_ref, u_ref, v_ref, gi_ref, gc_ref, ub_ref, acc_ref):
    rows, cols = x_ref.shape[0], y_ref.shape[0]
    spread(u_ref, ub_ref)
    acc_ref[...] = jnp.zeros_like(acc_ref)
    y = y_ref[...]
    v = v_ref[...]
    y_one = jnp.concatenate([y, jnp.ones((cols, 128), jnp.bfloat16)], axis=1)

    def block(k, _):
        at = pl.multiple_of(k * chunk, chunk)
        x = x_ref[pl.ds(at, chunk), :]
        d = lax.dot_general(x, y, NT, preferred_element_type=jnp.float32)
        u = ub_ref[pl.ds(at, chunk), :]
        parts = []
        for q in range(cols // 128):
            t = d[:, q * 128:(q + 1) * 128] * CROSS + u + v[:, q * 128:(q + 1) * 128]
            parts.append(jnp.exp2(t).astype(jnp.bfloat16))
        plan = jnp.concatenate(parts, axis=1)
        pulled = jnp.dot(plan, y_one, preferred_element_type=jnp.float32)
        gi_ref[pl.ds(at, chunk), :] = 2.0 * (pulled[:, 128:] * x.astype(jnp.float32) - pulled[:, :128])
        acc_ref[...] += jnp.dot(xt_ref[:, pl.ds(at, chunk)], plan, preferred_element_type=jnp.float32)
        return 0

    lax.fori_loop(0, rows // chunk, block, 0)
    yf = y.astype(jnp.float32)
    for q in range(cols // 128):
        pulled = jnp.transpose(acc_ref[0:128, q * 128:(q + 1) * 128])
        count = jnp.transpose(jnp.broadcast_to(acc_ref[128:129, q * 128:(q + 1) * 128], (128, 128)))
        gc_ref[q * 128:(q + 1) * 128, :] = 2.0 * (count * yf[q * 128:(q + 1) * 128, :] - pulled)


def final_pass(x, y, u, v, chunk=256):
    rows, cols = x.shape[0], y.shape[0]
    size = rows * cols
    xt = jnp.concatenate([x.T, jnp.ones((16, rows), jnp.bfloat16)], axis=0)
    return pl.pallas_call(
        functools.partial(final_kernel, chunk),
        out_shape=(
            jax.ShapeDtypeStruct((rows, D), jnp.float32),
            jax.ShapeDtypeStruct((cols, D), jnp.float32),
        ),
        in_specs=[VMEM] * 5,
        out_specs=(VMEM, VMEM),
        scratch_shapes=[
            pltpu.VMEM((rows, 128), jnp.float32),
            pltpu.VMEM((144, cols), jnp.float32),
        ],
        compiler_params=pltpu.CompilerParams(vmem_limit_bytes=48 << 20),
        cost_estimate=pl.CostEstimate(flops=6 * size * D, bytes_accessed=4 * D * (rows + cols), transcendentals=size),
        name="final_pass",
    )(x, xt, y, u.reshape(rows // 128, 128), v.reshape(1, cols))


def shifted(value, axis, count, shift):
    return lax.ppermute(value, axis, [(i, (i + shift) % count) for i in range(count)])


def everyone(value, axis, count):
    return [value] + [shifted(value, axis, count, s) for s in range(1, count)]


def gathered(value, axis, count):
    parts = everyone(value, axis, count)
    me = lax.axis_index(axis)
    size = value.shape[0]
    out = jnp.zeros((count * size,) + value.shape[1:], value.dtype)
    for s, part in enumerate(parts):
        place = lax.rem(me + count - s, count) * size
        out = lax.dynamic_update_slice_in_dim(out, part, place, 0)
    return out


def lse2(parts):
    top = functools.reduce(jnp.maximum, parts)
    return top + jnp.log2(sum(jnp.exp2(part - top) for part in parts))


def doubled(value, axis, count):
    step = 1
    while step < count:
        value = value + lax.ppermute(value, axis, [(i, i ^ step) for i in range(count)])
        step *= 2
    return value


def scattered(value, axis, count):
    me = lax.axis_index(axis)
    size = value.shape[0] // count

    def share(owner):
        return lax.dynamic_slice_in_dim(value, owner * size, size, 0)

    total = share(me)
    for s in range(1, count):
        part = share(lax.rem(me + s, count)).astype(jnp.bfloat16)
        total = total + shifted(part, axis, count, s).astype(jnp.float32)
    return total


def local(imu, camera, imu_mass, cam_mass):
    nrow, ncol = lax.axis_size("row"), lax.axis_size("col")
    y = gathered(camera[0], "row", nrow)
    x = gathered(imu, "col", ncol)
    log_a = jnp.log2(imu_mass)
    log_b = jnp.log2(cam_mass)
    v = jnp.sum(jnp.square(y.astype(jnp.float32)), axis=1) * (-LOG2E / EPSILON)
    u = log_a - lse2(everyone(first_pass(y, x, v), "col", ncol))
    v = log_b - lse2(everyone(first_pass(x, y, u), "row", nrow))
    u = u + log_a - jnp.log2(doubled(sum_pass(y, x, v, u), "col", ncol))
    v = v + log_b - jnp.log2(doubled(sum_pass(x, y, u, v), "row", nrow))
    u = u + log_a - jnp.log2(jnp.sum(lax.all_gather(sum_pass(y, x, v, u, 2048), "col"), axis=0))
    v = v + log_b - jnp.log2(jnp.sum(lax.all_gather(sum_pass(x, y, u, v, 1024, 512), "row"), axis=0))
    grad_imu, grad_cam = final_pass(x, y, u, v)
    return scattered(grad_imu, "col", ncol), scattered(grad_cam, "row", nrow)[None]


def solution(mesh):
    in_specs = (P(("row", "col"), None), P("col", "row", None), P("row"), P("col"))
    out_specs = (P(("row", "col"), None), P("col", "row", None))
    return jax.shard_map(local, mesh=mesh, in_specs=in_specs, out_specs=out_specs, check_vma=False)
```

```python
import functools
import math

import jax
import jax.numpy as jnp
from jax import lax
from jax.experimental import pallas as pl
from jax.experimental.pallas import tpu as pltpu
from jax.sharding import PartitionSpec as P

D = 128
ITERS = 3
EPSILON = D / 20.0
LOG2E = math.log2(math.e)
CROSS = 2.0 * LOG2E / EPSILON
NT = (((1,), (1,)), ((), ()))
VMEM = pl.BlockSpec(memory_space=pltpu.VMEM)


def spread(s_ref, sb_ref):
    chunks = s_ref.shape[0]
    turned = jnp.transpose(s_ref[...])
    for k in range(chunks):
        sb_ref[k * 128:(k + 1) * 128, :] = jnp.broadcast_to(turned[:, k:k + 1], (128, 128))


def norms(a_ref, sb_ref, chunk):
    def block(k, _):
        at = pl.multiple_of(k * chunk, chunk)
        a = a_ref[pl.ds(at, chunk), :].astype(jnp.float32)
        total = jnp.sum(a * a, axis=1, keepdims=True) * (-LOG2E / EPSILON)
        sb_ref[pl.ds(at, chunk), :] = jnp.broadcast_to(total, (chunk, 128))
        return 0

    lax.fori_loop(0, a_ref.shape[0] // chunk, block, 0)


def first_kernel(chunk, width, from_norms, a_ref, b_ref, s_ref, mass_ref, o_ref, sb_ref):
    depth, lanes = a_ref.shape[0], b_ref.shape[0]
    tiles = width // 128
    if from_norms:
        norms(a_ref, sb_ref, chunk)
    else:
        spread(s_ref, sb_ref)
    o_ref[:, lanes:] = jnp.log2(mass_ref[...])

    def column(n, _):
        start = pl.multiple_of(n * width, width)
        b = b_ref[pl.ds(start, width), :]

        def step(m, carry):
            peak, total = carry
            at = pl.multiple_of(m * chunk, chunk)
            d = lax.dot_general(a_ref[pl.ds(at, chunk), :], b, NT, preferred_element_type=jnp.float32)
            s = sb_ref[pl.ds(at, chunk), :]
            peaks, totals = [], []
            for q in range(tiles):
                t = (d[:, q * 128:(q + 1) * 128] * CROSS + s).reshape(chunk // 8, 8, 128)
                old = peak[:, q * 128:(q + 1) * 128]
                new = jnp.maximum(old, jnp.max(t, axis=0))
                part = jnp.sum(jnp.exp2(t - new[None]), axis=0)
                peaks.append(new)
                totals.append(total[:, q * 128:(q + 1) * 128] * jnp.exp2(old - new) + part)
            return jnp.concatenate(peaks, axis=1), jnp.concatenate(totals, axis=1)

        init = (jnp.full((8, width), -1e30, jnp.float32), jnp.zeros((8, width), jnp.float32))
        peak, total = lax.fori_loop(0, depth // chunk, step, init, unroll=True)
        top = jnp.max(peak, axis=0, keepdims=True)
        whole = jnp.sum(total * jnp.exp2(peak - top), axis=0, keepdims=True)
        o_ref[:, pl.ds(start, width)] = top + jnp.log2(whole)
        return 0

    lax.fori_loop(0, lanes // width, column, 0)


def sum_kernel(chunk, width, a_ref, b_ref, s_ref, l_ref, o_ref, sb_ref):
    depth, lanes = a_ref.shape[0], b_ref.shape[0]
    tiles = width // 128
    spread(s_ref, sb_ref)

    def column(n, _):
        start = pl.multiple_of(n * width, width)
        b = b_ref[pl.ds(start, width), :]
        l = l_ref[:, pl.ds(start, width)]
        total = [jnp.zeros((8, 128), jnp.float32) for q in range(tiles)]
        for m in range(depth // chunk):
            d = lax.dot_general(a_ref[m * chunk:(m + 1) * chunk, :], b, NT, preferred_element_type=jnp.float32)
            s = sb_ref[m * chunk:(m + 1) * chunk, :]
            for q in range(tiles):
                t = d[:, q * 128:(q + 1) * 128] * CROSS + s + l[:, q * 128:(q + 1) * 128]
                total[q] = total[q] + jnp.sum(jnp.exp2(t).reshape(chunk // 8, 8, 128), axis=0)
        o_ref[:, pl.ds(start, width)] = jnp.sum(jnp.concatenate(total, axis=1), axis=0, keepdims=True)
        return 0

    lax.fori_loop(0, lanes // width, column, 0)


def pass_cost(a, b):
    size = a.shape[0] * b.shape[0]
    return pl.CostEstimate(flops=2 * size * D, bytes_accessed=2 * (a.size + b.size), transcendentals=size)


def first_pass(a, b, s, mass, chunk=512, width=256):
    depth, lanes, extra = a.shape[0], b.shape[0], mass.shape[0]
    from_norms = s is None
    s = jnp.zeros((8, 128), jnp.float32) if from_norms else s.reshape(depth // 128, 128)
    out = pl.pallas_call(
        functools.partial(first_kernel, chunk, width, from_norms),
        out_shape=jax.ShapeDtypeStruct((1, lanes + extra), jnp.float32),
        in_specs=[VMEM] * 4,
        out_specs=VMEM,
        scratch_shapes=[pltpu.VMEM((depth, 128), jnp.float32)],
        compiler_params=pltpu.CompilerParams(vmem_limit_bytes=32 << 20),
        cost_estimate=pass_cost(a, b),
        name="first_pass",
    )(a, b, s, mass.reshape(1, extra))
    return out.reshape(lanes + extra)


def sum_pass(a, b, s, l, chunk=512, width=256):
    depth, lanes = a.shape[0], b.shape[0]
    out = pl.pallas_call(
        functools.partial(sum_kernel, chunk, width),
        out_shape=jax.ShapeDtypeStruct((1, lanes), jnp.float32),
        in_specs=[VMEM] * 4,
        out_specs=VMEM,
        scratch_shapes=[pltpu.VMEM((depth, 128), jnp.float32)],
        compiler_params=pltpu.CompilerParams(vmem_limit_bytes=32 << 20),
        cost_estimate=pass_cost(a, b),
        name="sum_pass",
    )(a, b, s.reshape(depth // 128, 128), l.reshape(1, lanes))
    return out.reshape(lanes)


def final_kernel(chunk, own_x, own_y, x_ref, y_ref, u_ref, v_ref, gi_ref, gis_ref, gc_ref, gcs_ref, ub_ref, acc_ref):
    rows, cols = x_ref.shape[0], y_ref.shape[0]
    spread(u_ref, ub_ref)
    acc_ref[...] = jnp.zeros_like(acc_ref)
    y_one = jnp.concatenate([y_ref[...], jnp.ones((cols, 128), jnp.bfloat16)], axis=1)

    def block(at):
        x = x_ref[pl.ds(at, chunk), :]
        d = lax.dot_general(x, y_ref[...], NT, preferred_element_type=jnp.float32)
        u = ub_ref[pl.ds(at, chunk), :]
        parts = []
        for q in range(cols // 128):
            t = d[:, q * 128:(q + 1) * 128] * CROSS + u + v_ref[:, q * 128:(q + 1) * 128]
            parts.append(jnp.exp2(t).astype(jnp.bfloat16))
        plan = jnp.concatenate(parts, axis=1)
        pulled = jnp.dot(plan, y_one, preferred_element_type=jnp.float32)
        xf = x.astype(jnp.float32)
        xt = jnp.concatenate([jnp.transpose(xf).astype(jnp.bfloat16), jnp.ones((16, chunk), jnp.bfloat16)], axis=0)
        acc_ref[...] += jnp.dot(xt, plan, preferred_element_type=jnp.float32)
        return 2.0 * (pulled[:, 128:] * xf - pulled[:, :128])

    def own_block(k, _):
        at = pl.multiple_of(k * chunk, chunk)
        gi_ref[pl.ds(at, chunk), :] = block(at)
        return 0

    def sent_block(k, _):
        at = pl.multiple_of(k * chunk, chunk)
        gis_ref[pl.ds(pl.multiple_of(at - own_x, chunk), chunk), :] = block(at).astype(jnp.bfloat16)
        return 0

    lax.fori_loop(0, own_x // chunk, own_block, 0)
    lax.fori_loop(own_x // chunk, rows // chunk, sent_block, 0)
    for q in range(cols // 128):
        at = q * 128
        pulled = jnp.transpose(acc_ref[0:128, at:at + 128])
        count = jnp.transpose(jnp.broadcast_to(acc_ref[128:129, at:at + 128], (128, 128)))
        grad = 2.0 * (count * y_ref[at:at + 128, :].astype(jnp.float32) - pulled)
        if at < own_y:
            gc_ref[at:at + 128, :] = grad
        else:
            gcs_ref[at - own_y:at - own_y + 128, :] = grad


def final_pass(x, y, u, v, own_x, own_y, chunk=256):
    rows, cols = x.shape[0], y.shape[0]
    size = rows * cols
    return pl.pallas_call(
        functools.partial(final_kernel, chunk, own_x, own_y),
        out_shape=(
            jax.ShapeDtypeStruct((own_x, D), jnp.float32),
            jax.ShapeDtypeStruct((rows - own_x, D), jnp.bfloat16),
            jax.ShapeDtypeStruct((own_y, D), jnp.float32),
            jax.ShapeDtypeStruct((cols - own_y, D), jnp.float32),
        ),
        in_specs=[VMEM] * 4,
        out_specs=(VMEM,) * 4,
        scratch_shapes=[
            pltpu.VMEM((rows, 128), jnp.float32),
            pltpu.VMEM((144, cols), jnp.float32),
        ],
        compiler_params=pltpu.CompilerParams(vmem_limit_bytes=48 << 20),
        cost_estimate=pl.CostEstimate(flops=6 * size * D, bytes_accessed=4 * D * (rows + cols), transcendentals=size),
        name="final_pass",
    )(x, y, u.reshape(rows // 128, 128), v.reshape(1, cols))


class Groups:
    def __init__(self, nrow, ncol):
        self.count = nrow * ncol
        self.across = [(a << 1) * ncol + b for a in range(nrow // 2) for b in range(2)]
        self.along = [z << 1 for z in range(ncol // 2)]
        self.core = ncol

    def swap(self, value, mask):
        if mask == 0:
            return value
        return lax.ppermute(value, ("row", "col"), [(i, i ^ mask) for i in range(self.count)])


def reordered(value, shift, parts):
    if shift == 0:
        return value
    blocks = value.reshape(parts, -1)
    return jnp.concatenate([blocks[s ^ shift] for s in range(parts)])


def lse2(parts):
    top = functools.reduce(jnp.maximum, parts)
    return top + jnp.log2(sum(jnp.exp2(part - top) for part in parts))


def local(imu, camera, imu_mass, cam_mass):
    nrow, ncol = lax.axis_size("row"), lax.axis_size("col")
    row, col = lax.axis_index("row"), lax.axis_index("col")
    groups = Groups(nrow, ncol)
    swap, across, along, core = groups.swap, groups.across, groups.along, groups.core
    na, nz = len(across), len(along)
    share_x, share_y = imu.shape[0], camera.shape[1]

    x = jnp.concatenate([swap(imu, mask) for mask in across])
    near = [swap(camera[0], mask) for mask in along]
    y = jnp.concatenate(near + [swap(part, core) for part in near])

    def pair(mass, place, share):
        return jnp.concatenate([lax.dynamic_slice_in_dim(mass, (place ^ k) * share, share, 0) for k in range(2)])

    def row_exchange(local_value):
        return [reordered(swap(local_value, mask), s, na) for s, mask in enumerate(across)]

    def halves(value):
        return jnp.concatenate([value[value.shape[0] // 2:], value[:value.shape[0] // 2]])

    sent = first_pass(y, x, None, pair(imu_mass, col, share_x))
    got = [swap(sent, mask) for mask in across]
    size = na * share_x
    log_a = jnp.concatenate([got[2 * a][size:] for a in range(na // 2)])
    u = log_a - lse2([reordered(got[s][:size], s, na) for s in range(na)])

    sent = first_pass(x, y, u, pair(cam_mass, row, share_y))
    size = 2 * nz * share_y
    lse, mass = sent[:size], sent[size:]
    lse = lse2([lse, halves(swap(lse, core))])
    sent = jnp.concatenate([lse, mass])
    got = [swap(sent, mask) for mask in along]

    def turned(value, z):
        half = value.shape[0] // 2
        return jnp.concatenate([reordered(value[:half], z, nz), reordered(value[half:], z, nz)])

    masses = [part[size:].reshape(2, share_y) for part in got]
    log_b = jnp.concatenate([part[0] for part in masses] + [part[1] for part in masses])
    v = log_b - lse2([turned(got[z][:size], z) for z in range(nz)])

    for step in range(1, ITERS):
        total = sum(row_exchange(sum_pass(y, x, v, u, 1024, 512)))
        u = u + log_a - jnp.log2(total)
        part = sum_pass(x, y, u, v, 1024, 512)
        part = part + halves(swap(part, core))
        v = v + log_b - jnp.log2(sum(turned(swap(part, mask), z) for z, mask in enumerate(along)))

    gi, gi_send, gc, gc_send = final_pass(x, y, u, v, share_x, nz * share_y)
    gc = gc + swap(gc_send, core)
    for s in range(1, na):
        gi = gi + swap(gi_send[(s - 1) * share_x:s * share_x], across[s]).astype(jnp.float32)
    grad_cam = gc[:share_y]
    for z in range(1, nz):
        part = gc[z * share_y:(z + 1) * share_y].astype(jnp.bfloat16)
        grad_cam = grad_cam + swap(part, along[z]).astype(jnp.float32)
    return gi, grad_cam[None]


def solution(mesh):
    in_specs = (P(("row", "col"), None), P("col", "row", None), P("row"), P("col"))
    out_specs = (P(("row", "col"), None), P("col", "row", None))
    return jax.shard_map(local, mesh=mesh, in_specs=in_specs, out_specs=out_specs, check_vma=False)
```

```python
import functools
import math

import jax
import jax.numpy as jnp
from jax import lax
from jax.experimental import pallas as pl
from jax.experimental.pallas import tpu as pltpu
from jax.sharding import PartitionSpec as P

D = 128
ITERS = 3
EPSILON = D / 20.0
LOG2E = math.log2(math.e)
CROSS = 2.0 * LOG2E / EPSILON
NT = (((1,), (1,)), ((), ()))
VMEM = pl.BlockSpec(memory_space=pltpu.VMEM)


def spread(s_ref, sb_ref):
    chunks = s_ref.shape[0]
    turned = jnp.transpose(s_ref[...])
    for k in range(chunks):
        sb_ref[k * 128:(k + 1) * 128, :] = jnp.broadcast_to(turned[:, k:k + 1], (128, 128))


def norms(a_ref, sb_ref, chunk):
    def block(k, _):
        at = pl.multiple_of(k * chunk, chunk)
        a = a_ref[pl.ds(at, chunk), :].astype(jnp.float32)
        total = jnp.sum(a * a, axis=1, keepdims=True) * (-LOG2E / EPSILON)
        sb_ref[pl.ds(at, chunk), :] = jnp.broadcast_to(total, (chunk, 128))
        return 0

    lax.fori_loop(0, a_ref.shape[0] // chunk, block, 0)


def scores(d, s, l, q):
    return d * CROSS + s + l[:, q * 128:(q + 1) * 128]


def fold(t):
    return jnp.sum(t.reshape(t.shape[0] // 8, 8, 128), axis=0)


def pipelined(chunk, width, a_ref, b_ref, sb_ref, d_ref, head, tile, finish):
    depth, lanes = a_ref.shape[0], b_ref.shape[0]
    steps, last = depth // chunk, lanes // width - 1
    tiles = width // 128

    def product(n, m):
        b = b_ref[pl.ds(pl.multiple_of(n * width, width), width), :]
        a = a_ref[m * chunk:(m + 1) * chunk, :]
        d_ref[m % 2] = lax.dot_general(a, b, NT, preferred_element_type=jnp.float32)

    product(0, 0)

    def column(n, _):
        start = pl.multiple_of(n * width, width)
        state = head(start)
        for m in range(steps):
            if m + 1 < steps:
                product(n, m + 1)
            else:
                product(jnp.minimum(n + 1, last), 0)
            s = sb_ref[m * chunk:(m + 1) * chunk, :]
            state = tile(m, lambda q: d_ref[m % 2, :, q * 128:(q + 1) * 128], s, state)
        finish(start, state)
        return 0

    lax.fori_loop(0, last + 1, column, 0)


def running_max(chunk, width, a_ref, b_ref, sb_ref, o_ref):
    depth, lanes = a_ref.shape[0], b_ref.shape[0]

    def column(n, _):
        start = pl.multiple_of(n * width, width)
        b = b_ref[pl.ds(start, width), :]

        def step(m, carry):
            peak, total = carry
            at = pl.multiple_of(m * chunk, chunk)
            d = lax.dot_general(a_ref[pl.ds(at, chunk), :], b, NT, preferred_element_type=jnp.float32)
            s = sb_ref[pl.ds(at, chunk), :]
            peaks, totals = [], []
            for q in range(width // 128):
                t = d[:, q * 128:(q + 1) * 128] * CROSS + s
                old = peak[:, q * 128:(q + 1) * 128]
                new = jnp.maximum(old, jnp.max(t, axis=0, keepdims=True))
                part = jnp.sum(jnp.exp2(t - new), axis=0, keepdims=True)
                peaks.append(new)
                totals.append(total[:, q * 128:(q + 1) * 128] * jnp.exp2(old - new) + part)
            return jnp.concatenate(peaks, axis=1), jnp.concatenate(totals, axis=1)

        init = (jnp.full((1, width), -1e30, jnp.float32), jnp.zeros((1, width), jnp.float32))
        peak, total = lax.fori_loop(0, depth // chunk, step, init)
        o_ref[:, pl.ds(start, width)] = peak + jnp.log2(total)
        return 0

    lax.fori_loop(0, lanes // width, column, 0)


def first_kernel(chunk, width, from_norms, a_ref, b_ref, s_ref, mass_ref, o_ref, sb_ref, d_ref, top_ref):
    lanes = b_ref.shape[0]
    tiles = width // 128
    if from_norms:
        norms(a_ref, sb_ref, chunk)
    else:
        spread(s_ref, sb_ref)
    o_ref[:, lanes:] = jnp.log2(mass_ref[...])
    top_ref[...] = jnp.zeros_like(top_ref)

    def tile(m, piece, s, state):
        if m == 0:
            state = []
            for q in range(tiles):
                t = piece(q) * CROSS + s
                peak = jnp.max(t, axis=0, keepdims=True)
                state.append((peak, fold(jnp.exp2(t - peak))))
            return state
        return [(peak, total + fold(jnp.exp2(piece(q) * CROSS + s - peak))) for q, (peak, total) in enumerate(state)]

    def finish(start, state):
        for q, (peak, total) in enumerate(state):
            top_ref[...] = jnp.maximum(top_ref[...], total)
            whole = jnp.sum(total, axis=0, keepdims=True)
            o_ref[:, pl.ds(pl.multiple_of(start + q * 128, 128), 128)] = peak + jnp.log2(whole)

    pipelined(chunk, width, a_ref, b_ref, sb_ref, d_ref, lambda start: None, tile, finish)

    @pl.when(jnp.logical_not(jnp.max(top_ref[...]) < 2.0 ** 100))
    def _():
        running_max(min(chunk, 256), min(width, 256), a_ref, b_ref, sb_ref, o_ref)


def sum_kernel(chunk, width, a_ref, b_ref, s_ref, l_ref, o_ref, sb_ref, d_ref):
    tiles = width // 128
    spread(s_ref, sb_ref)

    def head(start):
        return l_ref[:, pl.ds(start, width)], [jnp.zeros((8, 128), jnp.float32)] * tiles

    def tile(m, piece, s, state):
        l, total = state
        return l, [total[q] + fold(jnp.exp2(scores(piece(q), s, l, q))) for q in range(tiles)]

    def finish(start, state):
        o_ref[:, pl.ds(start, width)] = jnp.sum(jnp.concatenate(state[1], axis=1), axis=0, keepdims=True)

    pipelined(chunk, width, a_ref, b_ref, sb_ref, d_ref, head, tile, finish)


def pass_cost(a, b):
    size = a.shape[0] * b.shape[0]
    return pl.CostEstimate(flops=2 * size * D, bytes_accessed=2 * (a.size + b.size), transcendentals=size)


def first_pass(a, b, s, mass, chunk=512, width=512):
    depth, lanes, extra = a.shape[0], b.shape[0], mass.shape[0]
    from_norms = s is None
    s = jnp.zeros((8, 128), jnp.float32) if from_norms else s.reshape(depth // 128, 128)
    out = pl.pallas_call(
        functools.partial(first_kernel, chunk, width, from_norms),
        out_shape=jax.ShapeDtypeStruct((1, lanes + extra), jnp.float32),
        in_specs=[VMEM] * 4,
        out_specs=VMEM,
        scratch_shapes=[
            pltpu.VMEM((depth, 128), jnp.float32),
            pltpu.VMEM((2, chunk, width), jnp.float32),
            pltpu.VMEM((8, 128), jnp.float32),
        ],
        compiler_params=pltpu.CompilerParams(vmem_limit_bytes=32 << 20),
        cost_estimate=pass_cost(a, b),
        name="first_pass",
    )(a, b, s, mass.reshape(1, extra))
    return out.reshape(lanes + extra)


def sum_pass(a, b, s, l, chunk=512, width=256):
    depth, lanes = a.shape[0], b.shape[0]
    out = pl.pallas_call(
        functools.partial(sum_kernel, chunk, width),
        out_shape=jax.ShapeDtypeStruct((1, lanes), jnp.float32),
        in_specs=[VMEM] * 4,
        out_specs=VMEM,
        scratch_shapes=[
            pltpu.VMEM((depth, 128), jnp.float32),
            pltpu.VMEM((2, chunk, width), jnp.float32),
        ],
        compiler_params=pltpu.CompilerParams(vmem_limit_bytes=32 << 20),
        cost_estimate=pass_cost(a, b),
        name="sum_pass",
    )(a, b, s.reshape(depth // 128, 128), l.reshape(1, lanes))
    return out.reshape(lanes)


def final_kernel(chunk, width, own_x, own_y, x_ref, y_ref, u_ref, v_ref, gi_ref, gis_ref, gc_ref, gcs_ref,
                 ub_ref, d_ref, p_ref, y1_ref, xt_ref, acc_ref, pull_ref):
    rows, cols = x_ref.shape[0], y_ref.shape[0]
    steps, last = cols // width, rows // chunk - 1
    spread(u_ref, ub_ref)
    acc_ref[...] = jnp.zeros_like(acc_ref)
    y1_ref[:, :128] = y_ref[...]
    y1_ref[:, 128:] = jnp.ones((cols, 128), jnp.bfloat16)
    for k in range(rows // 128):
        at = k * 128
        xt_ref[:128, at:at + 128] = jnp.transpose(x_ref[at:at + 128, :].astype(jnp.float32)).astype(jnp.bfloat16)
    xt_ref[128:, :] = jnp.ones((16, rows), jnp.bfloat16)

    def product(k, j):
        x = x_ref[pl.ds(pl.multiple_of(k * chunk, chunk), chunk), :]
        y = y_ref[j * width:(j + 1) * width, :]
        d_ref[j % 2] = lax.dot_general(x, y, NT, preferred_element_type=jnp.float32)

    def plan(at, j):
        u = ub_ref[pl.ds(at, chunk), :]
        for q in range(width // 128):
            t = scores(d_ref[j % 2, :, q * 128:(q + 1) * 128], u, v_ref[:, j * width:(j + 1) * width], q)
            p_ref[j % 2, :, q * 128:(q + 1) * 128] = jnp.exp2(t).astype(jnp.bfloat16)

    def pull(at, j):
        p = p_ref[j % 2]
        part = jnp.dot(p, y1_ref[j * width:(j + 1) * width, :], preferred_element_type=jnp.float32)
        pull_ref[...] = part if j == 0 else pull_ref[...] + part
        xt = xt_ref[:, pl.ds(at, chunk)]
        acc_ref[:, j * width:(j + 1) * width] += jnp.dot(xt, p, preferred_element_type=jnp.float32)

    def block(k):
        at = pl.multiple_of(k * chunk, chunk)
        for j in range(steps):
            if j + 1 < steps:
                product(k, j + 1)
            else:
                product(jnp.minimum(k + 1, last), 0)
            if j > 0:
                pull(at, j - 1)
            plan(at, j)
        pull(at, steps - 1)
        x = x_ref[pl.ds(at, chunk), :].astype(jnp.float32)
        return at, 2.0 * (pull_ref[:, 128:] * x - pull_ref[:, :128])

    def own_block(k, _):
        at, grad = block(k)
        gi_ref[pl.ds(at, chunk), :] = grad
        return 0

    def sent_block(k, _):
        at, grad = block(k)
        gis_ref[pl.ds(pl.multiple_of(at - own_x, chunk), chunk), :] = grad.astype(jnp.bfloat16)
        return 0

    product(0, 0)
    lax.fori_loop(0, own_x // chunk, own_block, 0)
    lax.fori_loop(own_x // chunk, rows // chunk, sent_block, 0)
    for q in range(cols // 128):
        at = q * 128
        pulled = jnp.transpose(acc_ref[0:128, at:at + 128])
        count = jnp.transpose(jnp.broadcast_to(acc_ref[128:129, at:at + 128], (128, 128)))
        grad = 2.0 * (count * y_ref[at:at + 128, :].astype(jnp.float32) - pulled)
        if at < own_y:
            gc_ref[at:at + 128, :] = grad
        else:
            gcs_ref[at - own_y:at - own_y + 128, :] = grad


def final_pass(x, y, u, v, own_x, own_y, width=1024):
    rows, cols = x.shape[0], y.shape[0]
    chunk = math.gcd(own_x, 512)
    size = rows * cols
    return pl.pallas_call(
        functools.partial(final_kernel, chunk, width, own_x, own_y),
        out_shape=(
            jax.ShapeDtypeStruct((own_x, D), jnp.float32),
            jax.ShapeDtypeStruct((rows - own_x, D), jnp.bfloat16),
            jax.ShapeDtypeStruct((own_y, D), jnp.float32),
            jax.ShapeDtypeStruct((cols - own_y, D), jnp.float32),
        ),
        in_specs=[VMEM] * 4,
        out_specs=(VMEM,) * 4,
        scratch_shapes=[
            pltpu.VMEM((rows, 128), jnp.float32),
            pltpu.VMEM((2, chunk, width), jnp.float32),
            pltpu.VMEM((2, chunk, width), jnp.bfloat16),
            pltpu.VMEM((cols, 256), jnp.bfloat16),
            pltpu.VMEM((144, rows), jnp.bfloat16),
            pltpu.VMEM((144, cols), jnp.float32),
            pltpu.VMEM((chunk, 256), jnp.float32),
        ],
        compiler_params=pltpu.CompilerParams(vmem_limit_bytes=48 << 20),
        cost_estimate=pl.CostEstimate(flops=6 * size * D, bytes_accessed=4 * D * (rows + cols), transcendentals=size),
        name="final_pass",
    )(x, y, u.reshape(rows // 128, 128), v.reshape(1, cols))


class Groups:
    def __init__(self, nrow, ncol):
        self.count = nrow * ncol
        self.across = [(a << 1) * ncol + b for a in range(nrow // 2) for b in range(2)]
        self.along = [z << 1 for z in range(ncol // 2)]
        self.core = ncol

    def swap(self, value, mask):
        if mask == 0:
            return value
        return lax.ppermute(value, ("row", "col"), [(i, i ^ mask) for i in range(self.count)])


def reordered(value, shift, parts):
    if shift == 0:
        return value
    blocks = value.reshape(parts, -1)
    return jnp.concatenate([blocks[s ^ shift] for s in range(parts)])


def lse2(parts):
    top = functools.reduce(jnp.maximum, parts)
    return top + jnp.log2(sum(jnp.exp2(part - top) for part in parts))


def local(imu, camera, imu_mass, cam_mass):
    nrow, ncol = lax.axis_size("row"), lax.axis_size("col")
    row, col = lax.axis_index("row"), lax.axis_index("col")
    groups = Groups(nrow, ncol)
    swap, across, along, core = groups.swap, groups.across, groups.along, groups.core
    na, nz = len(across), len(along)
    share_x, share_y = imu.shape[0], camera.shape[1]

    x = jnp.concatenate([swap(imu, mask) for mask in across])
    near = [swap(camera[0], mask) for mask in along]
    y = jnp.concatenate(near + [swap(part, core) for part in near])

    def pair(mass, place, share):
        return jnp.concatenate([lax.dynamic_slice_in_dim(mass, (place ^ k) * share, share, 0) for k in range(2)])

    def row_exchange(local_value):
        return [reordered(swap(local_value, mask), s, na) for s, mask in enumerate(across)]

    def halves(value):
        return jnp.concatenate([value[value.shape[0] // 2:], value[:value.shape[0] // 2]])

    sent = first_pass(y, x, None, pair(imu_mass, col, share_x))
    got = [swap(sent, mask) for mask in across]
    size = na * share_x
    log_a = jnp.concatenate([got[2 * a][size:] for a in range(na // 2)])
    u = log_a - lse2([reordered(got[s][:size], s, na) for s in range(na)])

    sent = first_pass(x, y, u, pair(cam_mass, row, share_y))
    size = 2 * nz * share_y
    lse, mass = sent[:size], sent[size:]
    lse = lse2([lse, halves(swap(lse, core))])
    sent = jnp.concatenate([lse, mass])
    got = [swap(sent, mask) for mask in along]

    def turned(value, z):
        half = value.shape[0] // 2
        return jnp.concatenate([reordered(value[:half], z, nz), reordered(value[half:], z, nz)])

    masses = [part[size:].reshape(2, share_y) for part in got]
    log_b = jnp.concatenate([part[0] for part in masses] + [part[1] for part in masses])
    v = log_b - lse2([turned(got[z][:size], z) for z in range(nz)])

    for step in range(1, ITERS):
        chunk = 512 if step == 1 else 256
        total = sum(row_exchange(sum_pass(y, x, v, u, chunk, 512)))
        u = u + log_a - jnp.log2(total)
        part = sum_pass(x, y, u, v, chunk, 512)
        part = part + halves(swap(part, core))
        v = v + log_b - jnp.log2(sum(turned(swap(part, mask), z) for z, mask in enumerate(along)))

    gi, gi_send, gc, gc_send = final_pass(x, y, u, v, share_x, nz * share_y)
    gc = gc + swap(gc_send, core)
    for s in range(1, na):
        gi = gi + swap(gi_send[(s - 1) * share_x:s * share_x], across[s]).astype(jnp.float32)
    grad_cam = gc[:share_y]
    for z in range(1, nz):
        part = gc[z * share_y:(z + 1) * share_y].astype(jnp.bfloat16)
        grad_cam = grad_cam + swap(part, along[z]).astype(jnp.float32)
    return gi, grad_cam[None]


def solution(mesh):
    in_specs = (P(("row", "col"), None), P("col", "row", None), P("row"), P("col"))
    out_specs = (P(("row", "col"), None), P("col", "row", None))
    return jax.shard_map(local, mesh=mesh, in_specs=in_specs, out_specs=out_specs, check_vma=False)
```

```python
import functools
import math

import jax
import jax.numpy as jnp
from jax import lax
from jax.experimental import pallas as pl
from jax.experimental.pallas import tpu as pltpu
from jax.sharding import PartitionSpec as P

D = 128
ITERS = 3
EPSILON = D / 20.0
LOG2E = math.log2(math.e)
CROSS = 2.0 * LOG2E / EPSILON
NT = (((1,), (1,)), ((), ()))
VMEM = pl.BlockSpec(memory_space=pltpu.VMEM)


def spread(s_ref, sb_ref):
    chunks = s_ref.shape[0]
    turned = jnp.transpose(s_ref[...])
    for k in range(chunks):
        sb_ref[k * 128:(k + 1) * 128, :] = jnp.broadcast_to(turned[:, k:k + 1], (128, 128))


def norms(a_ref, sb_ref, chunk):
    def block(k, _):
        at = pl.multiple_of(k * chunk, chunk)
        a = a_ref[pl.ds(at, chunk), :].astype(jnp.float32)
        total = jnp.sum(a * a, axis=1, keepdims=True) * (-LOG2E / EPSILON)
        sb_ref[pl.ds(at, chunk), :] = jnp.broadcast_to(total, (chunk, 128))
        return 0

    lax.fori_loop(0, a_ref.shape[0] // chunk, block, 0)


def fold(t):
    return jnp.sum(t.reshape(t.shape[0] // 8, 8, 128), axis=0)


def pipelined(chunk, width, a_ref, b_ref, sb_ref, d_ref, head, tile, finish):
    depth, lanes = a_ref.shape[0], b_ref.shape[0]
    steps, last = depth // chunk, lanes // width - 1
    tiles = width // 128

    def product(n, m):
        b = b_ref[pl.ds(pl.multiple_of(n * width, width), width), :]
        a = a_ref[m * chunk:(m + 1) * chunk, :]
        d_ref[m % 2] = lax.dot_general(a, b, NT, preferred_element_type=jnp.float32)

    product(0, 0)

    def column(n, _):
        start = pl.multiple_of(n * width, width)
        state = head(start)
        for m in range(steps):
            if m + 1 < steps:
                product(n, m + 1)
            else:
                product(jnp.minimum(n + 1, last), 0)
            s = sb_ref[m * chunk:(m + 1) * chunk, :]
            state = tile(m, lambda q: d_ref[m % 2, :, q * 128:(q + 1) * 128], s, state)
        finish(start, state)
        return 0

    lax.fori_loop(0, last + 1, column, 0)


def running_max(chunk, width, a_ref, b_ref, sb_ref, o_ref, e_ref, shift_ref):
    depth, lanes = a_ref.shape[0], b_ref.shape[0]

    def column(n, _):
        start = pl.multiple_of(n * width, width)
        b = b_ref[pl.ds(start, width), :]

        def exponents(m):
            at = pl.multiple_of(m * chunk, chunk)
            d = lax.dot_general(a_ref[pl.ds(at, chunk), :], b, NT, preferred_element_type=jnp.float32)
            s = sb_ref[pl.ds(at, chunk), :]
            return at, [d[:, q * 128:(q + 1) * 128] * CROSS + s for q in range(width // 128)]

        def step(m, carry):
            peak, total = carry
            peaks, totals = [], []
            for q, t in enumerate(exponents(m)[1]):
                old = peak[:, q * 128:(q + 1) * 128]
                new = jnp.maximum(old, jnp.max(t, axis=0, keepdims=True))
                part = jnp.sum(jnp.exp2(t - new), axis=0, keepdims=True)
                peaks.append(new)
                totals.append(total[:, q * 128:(q + 1) * 128] * jnp.exp2(old - new) + part)
            return jnp.concatenate(peaks, axis=1), jnp.concatenate(totals, axis=1)

        def store(m, _):
            at, ts = exponents(m)
            for q, t in enumerate(ts):
                place = pl.ds(pl.multiple_of(start + q * 128, 128), 128)
                e_ref[pl.ds(at, chunk), place] = jnp.exp2(t - shift_ref[:, place]).astype(jnp.bfloat16)
            return 0

        init = (jnp.full((1, width), -1e30, jnp.float32), jnp.zeros((1, width), jnp.float32))
        peak, total = lax.fori_loop(0, depth // chunk, step, init)
        o_ref[:, pl.ds(start, width)] = peak + jnp.log2(total)
        if e_ref is not None:
            shift_ref[:, pl.ds(start, width)] = peak
            lax.fori_loop(0, depth // chunk, store, 0)
        return 0

    lax.fori_loop(0, lanes // width, column, 0)


def first_kernel(chunk, width, is_row, a_ref, b_ref, s_ref, mass_ref, o_ref, *rest):
    e_ref, shift_ref = (None, None) if is_row else rest[:2]
    sb_ref, d_ref, top_ref = rest[-3:]
    lanes = b_ref.shape[0]
    tiles = width // 128
    if is_row:
        norms(a_ref, sb_ref, chunk)
    else:
        spread(s_ref, sb_ref)
    o_ref[:, lanes:] = mass_ref[...]
    top_ref[...] = jnp.zeros_like(top_ref)

    def exponential(m, start, q, t):
        e = jnp.exp2(t)
        if e_ref is not None:
            place = pl.ds(pl.multiple_of(start + q * 128, 128), 128)
            e_ref[m * chunk:(m + 1) * chunk, place] = e.astype(jnp.bfloat16)
        return fold(e)

    def tile(m, piece, s, state):
        start, sums = state
        if m == 0:
            sums = []
            for q in range(tiles):
                t = piece(q) * CROSS + s
                peak = jnp.max(t, axis=0, keepdims=True)
                sums.append((peak, exponential(m, start, q, t - peak)))
            return start, sums
        return start, [
            (peak, total + exponential(m, start, q, piece(q) * CROSS + s - peak))
            for q, (peak, total) in enumerate(sums)
        ]

    def finish(start, state):
        for q, (peak, total) in enumerate(state[1]):
            top_ref[...] = jnp.maximum(top_ref[...], total)
            whole = jnp.sum(total, axis=0, keepdims=True)
            place = pl.ds(pl.multiple_of(start + q * 128, 128), 128)
            o_ref[:, place] = peak + jnp.log2(whole)
            if e_ref is not None:
                shift_ref[:, place] = peak

    pipelined(chunk, width, a_ref, b_ref, sb_ref, d_ref, lambda start: (start, None), tile, finish)

    @pl.when(jnp.logical_not(jnp.max(top_ref[...]) < 2.0 ** 60))
    def _():
        running_max(min(chunk, 256), min(width, 256), a_ref, b_ref, sb_ref, o_ref, e_ref, shift_ref)


def split3(value):
    high = value.astype(jnp.bfloat16)
    rest = value - high.astype(jnp.float32)
    mid = rest.astype(jnp.bfloat16)
    return high, mid, (rest - mid.astype(jnp.float32)).astype(jnp.bfloat16)


def stacked(w_ref):
    high, mid, low = [part.astype(jnp.float32) for part in split3(w_ref[...])]
    shape = (16, w_ref.shape[1])
    place = lax.broadcasted_iota(jnp.int32, shape, 0)
    parts = jnp.where(place == 0, high, jnp.where(place == 1, mid, jnp.where(place == 2, low, 0.0)))
    return parts.astype(jnp.bfloat16)


def row_kernel(width, e_ref, w_ref, o_ref, w16_ref):
    w16_ref[...] = stacked(w_ref)

    def block(k, _):
        at = pl.multiple_of(k * width, width)
        got = lax.dot_general(w16_ref[...], e_ref[pl.ds(at, width), :], NT, preferred_element_type=jnp.float32)
        o_ref[:, pl.ds(at, width)] = jnp.sum(got, axis=0, keepdims=True)
        return 0

    lax.fori_loop(0, e_ref.shape[0] // width, block, 0)


def row_turned_kernel(width, e_ref, w_ref, o_ref, w16_ref):
    w16_ref[...] = stacked(w_ref)

    def block(k, _):
        at = pl.multiple_of(k * width, width)
        got = lax.dot_general(e_ref[pl.ds(at, width), :], w16_ref[...], NT, preferred_element_type=jnp.float32)
        o_ref[:, pl.ds(at, width)] = jnp.sum(jnp.transpose(got), axis=0, keepdims=True)
        return 0

    lax.fori_loop(0, e_ref.shape[0] // width, block, 0)


def col_kernel(width, e_ref, w_ref, o_ref, w16_ref):
    w16_ref[...] = stacked(w_ref)

    def block(k, _):
        at = pl.multiple_of(k * width, width)
        got = jnp.dot(w16_ref[...], e_ref[:, pl.ds(at, width)], preferred_element_type=jnp.float32)
        o_ref[:, pl.ds(at, width)] = jnp.sum(got, axis=0, keepdims=True)
        return 0

    lax.fori_loop(0, e_ref.shape[1] // width, block, 0)


def weighted(kernel, e, w, lanes, width=512):
    out = pl.pallas_call(
        functools.partial(kernel, width),
        out_shape=jax.ShapeDtypeStruct((1, lanes), jnp.float32),
        in_specs=[VMEM] * 2,
        out_specs=VMEM,
        scratch_shapes=[pltpu.VMEM((16, w.shape[0]), jnp.bfloat16)],
        compiler_params=pltpu.CompilerParams(vmem_limit_bytes=16 << 20),
        cost_estimate=pl.CostEstimate(flops=2 * e.size, bytes_accessed=2 * e.size, transcendentals=0),
        name="weighted_sum",
    )(e, w.reshape(1, w.shape[0]))
    return out.reshape(lanes)


def pass_cost(a, b):
    size = a.shape[0] * b.shape[0]
    return pl.CostEstimate(flops=2 * size * D, bytes_accessed=2 * (a.size + b.size), transcendentals=size)


def first_pass(a, b, s, mass, chunk=512, width=512):
    depth, lanes, extra = a.shape[0], b.shape[0], mass.shape[0]
    is_row = s is None
    s = jnp.zeros((8, 128), jnp.float32) if is_row else s.reshape(depth // 128, 128)
    out_shape = [jax.ShapeDtypeStruct((1, lanes + extra), jnp.float32)]
    if not is_row:
        out_shape += [jax.ShapeDtypeStruct((depth, lanes), jnp.bfloat16), jax.ShapeDtypeStruct((1, lanes), jnp.float32)]
    out = pl.pallas_call(
        functools.partial(first_kernel, chunk, width, is_row),
        out_shape=out_shape,
        in_specs=[VMEM] * 4,
        out_specs=[VMEM] * len(out_shape),
        scratch_shapes=[
            pltpu.VMEM((depth, 128), jnp.float32),
            pltpu.VMEM((2, chunk, width), jnp.float32),
            pltpu.VMEM((8, 128), jnp.float32),
        ],
        compiler_params=pltpu.CompilerParams(vmem_limit_bytes=16 << 20),
        cost_estimate=pass_cost(a, b),
        name="first_pass",
    )(a, b, s, mass.reshape(1, extra))
    sent = out[0].reshape(lanes + extra)
    return sent if is_row else (sent, out[1], out[2].reshape(lanes))


def final_kernel(chunk, width, own_x, own_y, x_ref, y_ref, e_ref, alpha_ref, arow_ref, beta_ref, brow_ref,
                 gi_ref, gis_ref, gc_ref, gcs_ref, ab_ref, bb_ref, yb_ref, xa_ref, b16_ref, sums_ref, rb_ref, acc_ref):
    rows, cols = x_ref.shape[0], y_ref.shape[0]
    spread(alpha_ref, ab_ref)
    spread(beta_ref, bb_ref)
    b16_ref[...] = stacked(brow_ref)

    def high_low(value):
        high = value.astype(jnp.bfloat16)
        return high, (value - high.astype(jnp.float32)).astype(jnp.bfloat16)

    for k in range(cols // 512):
        at = k * 512
        yb_ref[at:at + 512, :128], yb_ref[at:at + 512, 128:] = high_low(
            y_ref[at:at + 512, :].astype(jnp.float32) * bb_ref[at:at + 512, :])
    for k in range(rows // 128):
        at = k * 128
        xa = jnp.transpose(x_ref[at:at + 128, :].astype(jnp.float32)) * arow_ref[:, at:at + 128]
        xa_ref[:128, at:at + 128], xa_ref[128:256, at:at + 128] = high_low(xa)
    xa_ref[256:, :] = stacked(arow_ref)

    for k in range(rows // 512):
        got = lax.dot_general(b16_ref[...], e_ref[k * 512:(k + 1) * 512, :], NT, preferred_element_type=jnp.float32)
        got = jnp.sum(got, axis=0, keepdims=True)
        for q in range(4):
            sums_ref[k * 4 + q:k * 4 + q + 1, :] = got[:, q * 128:(q + 1) * 128]
    spread(sums_ref, rb_ref)

    def block(at):
        pulled = jnp.dot(e_ref[pl.ds(at, chunk), :], yb_ref[...], preferred_element_type=jnp.float32)
        scale = 2.0 * ab_ref[pl.ds(at, chunk), :]
        x = x_ref[pl.ds(at, chunk), :].astype(jnp.float32)
        return scale * (rb_ref[pl.ds(at, chunk), :] * x - (pulled[:, :128] + pulled[:, 128:]))

    def own_block(k, _):
        at = pl.multiple_of(k * chunk, chunk)
        gi_ref[pl.ds(at, chunk), :] = block(at)
        return 0

    def sent_block(k, _):
        at = pl.multiple_of(k * chunk, chunk)
        gis_ref[pl.ds(pl.multiple_of(at - own_x, chunk), chunk), :] = block(at).astype(jnp.bfloat16)
        return 0

    lax.fori_loop(0, own_x // chunk, own_block, 0)
    lax.fori_loop(own_x // chunk, rows // chunk, sent_block, 0)

    for k in range(cols // width):
        got = jnp.dot(xa_ref[...], e_ref[:, k * width:(k + 1) * width], preferred_element_type=jnp.float32)
        acc_ref[:, k * width:(k + 1) * width] = got[:128] + got[128:256]
        count = jnp.sum(got[256:], axis=0, keepdims=True)
        for q in range(width // 128):
            at = k * width + q * 128
            whole = jnp.transpose(jnp.broadcast_to(count[:, q * 128:(q + 1) * 128], (128, 128)))
            pulled = jnp.transpose(acc_ref[:, at:at + 128])
            grad = 2.0 * bb_ref[at:at + 128, :] * (whole * y_ref[at:at + 128, :].astype(jnp.float32) - pulled)
            if at < own_y:
                gc_ref[at:at + 128, :] = grad
            else:
                gcs_ref[at - own_y:at - own_y + 128, :] = grad


def final_pass(x, y, e, alpha, beta, own_x, own_y, width=512):
    rows, cols = x.shape[0], y.shape[0]
    size = rows * cols
    chunk = math.gcd(own_x, 512)
    return pl.pallas_call(
        functools.partial(final_kernel, chunk, width, own_x, own_y),
        out_shape=(
            jax.ShapeDtypeStruct((own_x, D), jnp.float32),
            jax.ShapeDtypeStruct((rows - own_x, D), jnp.bfloat16),
            jax.ShapeDtypeStruct((own_y, D), jnp.float32),
            jax.ShapeDtypeStruct((cols - own_y, D), jnp.float32),
        ),
        in_specs=[VMEM] * 7,
        out_specs=(VMEM,) * 4,
        scratch_shapes=[
            pltpu.VMEM((rows, 128), jnp.float32),
            pltpu.VMEM((cols, 128), jnp.float32),
            pltpu.VMEM((cols, 256), jnp.bfloat16),
            pltpu.VMEM((272, rows), jnp.bfloat16),
            pltpu.VMEM((16, cols), jnp.bfloat16),
            pltpu.VMEM((rows // 128, 128), jnp.float32),
            pltpu.VMEM((rows, 128), jnp.float32),
            pltpu.VMEM((128, cols), jnp.float32),
        ],
        compiler_params=pltpu.CompilerParams(vmem_limit_bytes=28 << 20),
        cost_estimate=pl.CostEstimate(flops=8 * size * D, bytes_accessed=2 * size, transcendentals=0),
        name="final_pass",
    )(x, y, e, alpha.reshape(rows // 128, 128), alpha.reshape(1, rows), beta.reshape(cols // 128, 128),
      beta.reshape(1, cols))


class Groups:
    def __init__(self, nrow, ncol):
        self.count = nrow * ncol
        self.across = [(a << 1) * ncol + b for a in range(nrow // 2) for b in range(2)]
        self.along = [z << 1 for z in range(ncol // 2)]
        self.core = ncol

    def swap(self, value, mask):
        if mask == 0:
            return value
        return lax.ppermute(value, ("row", "col"), [(i, i ^ mask) for i in range(self.count)])


def reordered(value, shift, parts):
    if shift == 0:
        return value
    blocks = value.reshape(parts, -1)
    return jnp.concatenate([blocks[s ^ shift] for s in range(parts)])


def lse2(parts):
    top = functools.reduce(jnp.maximum, parts)
    return top + jnp.log2(sum(jnp.exp2(part - top) for part in parts))


def local(imu, camera, imu_mass, cam_mass):
    nrow, ncol = lax.axis_size("row"), lax.axis_size("col")
    row, col = lax.axis_index("row"), lax.axis_index("col")
    groups = Groups(nrow, ncol)
    swap, across, along, core = groups.swap, groups.across, groups.along, groups.core
    na, nz = len(across), len(along)
    share_x, share_y = imu.shape[0], camera.shape[1]

    x = jnp.concatenate([swap(imu, mask) for mask in across])
    near = [swap(camera[0], mask) for mask in along]
    y = jnp.concatenate(near + [swap(part, core) for part in near])

    def pair(mass, place, share):
        return jnp.concatenate([lax.dynamic_slice_in_dim(mass, (place ^ k) * share, share, 0) for k in range(2)])

    def row_exchange(local_value):
        return [reordered(swap(local_value, mask), s, na) for s, mask in enumerate(across)]

    def halves(value):
        return jnp.concatenate([value[value.shape[0] // 2:], value[:value.shape[0] // 2]])

    sent = first_pass(y, x, None, pair(imu_mass, col, share_x))
    got = [swap(sent, mask) for mask in across]
    size = na * share_x
    mass_a = jnp.concatenate([got[2 * a][size:] for a in range(na // 2)])
    u = jnp.log2(mass_a) - lse2([reordered(got[s][:size], s, na) for s in range(na)])

    sent, e, shift = first_pass(x, y, u, pair(cam_mass, row, share_y))
    size = 2 * nz * share_y
    lse, mass = sent[:size], sent[size:]
    lse = lse2([lse, halves(swap(lse, core))])
    sent = jnp.concatenate([lse, mass])
    got = [swap(sent, mask) for mask in along]

    def turned(value, z):
        half = value.shape[0] // 2
        return jnp.concatenate([reordered(value[:half], z, nz), reordered(value[half:], z, nz)])

    masses = [part[size:].reshape(2, share_y) for part in got]
    mass_b = jnp.concatenate([part[0] for part in masses] + [part[1] for part in masses])
    v = jnp.log2(mass_b) - lse2([turned(got[z][:size], z) for z in range(nz)])

    first_beta = beta = jnp.exp2(v + shift)
    for step in range(1, ITERS):
        kernel = row_kernel if step == 1 else row_turned_kernel
        alpha = mass_a / sum(row_exchange(weighted(kernel, e, beta, x.shape[0])))
        part = first_beta * weighted(col_kernel, e, alpha, y.shape[0])
        part = part + halves(swap(part, core))
        beta = first_beta * (mass_b / sum(turned(swap(part, mask), z) for z, mask in enumerate(along)))

    gi, gi_send, gc, gc_send = final_pass(x, y, e, alpha, beta, share_x, nz * share_y)
    gc = gc + swap(gc_send, core)
    for s in range(1, na):
        gi = gi + swap(gi_send[(s - 1) * share_x:s * share_x], across[s]).astype(jnp.float32)
    grad_cam = gc[:share_y]
    for z in range(1, nz):
        part = gc[z * share_y:(z + 1) * share_y].astype(jnp.bfloat16)
        grad_cam = grad_cam + swap(part, along[z]).astype(jnp.float32)
    return gi, grad_cam[None]


def solution(mesh):
    in_specs = (P(("row", "col"), None), P("col", "row", None), P("row"), P("col"))
    out_specs = (P(("row", "col"), None), P("col", "row", None))
    return jax.shard_map(local, mesh=mesh, in_specs=in_specs, out_specs=out_specs, check_vma=False)
```

```python
import functools
import math

import jax
import jax.numpy as jnp
from jax import lax
from jax.experimental import pallas as pl
from jax.experimental.pallas import tpu as pltpu
from jax.sharding import PartitionSpec as P

D = 128
ITERS = 3
EPSILON = D / 20.0
LOG2E = math.log2(math.e)
CROSS = 2.0 * LOG2E / EPSILON
NT = (((1,), (1,)), ((), ()))
VMEM = pl.BlockSpec(memory_space=pltpu.VMEM)
GROUP = 32


def spread(s_ref, sb_ref):
    chunks = s_ref.shape[0]
    turned = jnp.transpose(s_ref[...])
    for k in range(chunks):
        sb_ref[k * 128:(k + 1) * 128, :] = jnp.broadcast_to(turned[:, k:k + 1], (128, 128))


def norms(a_ref, sb_ref, chunk):
    def block(k, _):
        at = pl.multiple_of(k * chunk, chunk)
        a = a_ref[pl.ds(at, chunk), :].astype(jnp.float32)
        total = jnp.sum(a * a, axis=1, keepdims=True) * (-LOG2E / EPSILON)
        sb_ref[pl.ds(at, chunk), :] = jnp.broadcast_to(total, (chunk, 128))
        return 0

    lax.fori_loop(0, a_ref.shape[0] // chunk, block, 0)


def pipelined(chunk, width, a_ref, b_ref, d_ref, head, tile, finish):
    depth, lanes = a_ref.shape[0], b_ref.shape[0]
    steps, last = depth // chunk, lanes // width - 1

    def product(n, m):
        b = b_ref[pl.ds(pl.multiple_of(n * width, width), width), :]
        a = a_ref[m * chunk:(m + 1) * chunk, :]
        d_ref[m % 2] = lax.dot_general(a, b, NT, preferred_element_type=jnp.float32)

    product(0, 0)

    def column(n, _):
        start = pl.multiple_of(n * width, width)
        state = head(start)
        for m in range(steps):
            if m + 1 < steps:
                product(n, m + 1)
            else:
                product(jnp.minimum(n + 1, last), 0)
            state = tile(m, start, state)
        finish(start, state)
        return 0

    lax.fori_loop(0, last + 1, column, 0)


def running_max(chunk, width, a_ref, b_ref, sb_ref, o_ref, e_ref, shift_ref):
    depth, lanes = a_ref.shape[0], b_ref.shape[0]

    def column(n, _):
        start = pl.multiple_of(n * width, width)
        b = b_ref[pl.ds(start, width), :]

        def exponents(m):
            at = pl.multiple_of(m * chunk, chunk)
            d = lax.dot_general(a_ref[pl.ds(at, chunk), :], b, NT, preferred_element_type=jnp.float32)
            s = sb_ref[pl.ds(at, chunk), :]
            return at, [d[:, q * 128:(q + 1) * 128] * CROSS + s for q in range(width // 128)]

        def step(m, carry):
            peak, total = carry
            peaks, totals = [], []
            for q, t in enumerate(exponents(m)[1]):
                old = peak[:, q * 128:(q + 1) * 128]
                new = jnp.maximum(old, jnp.max(t, axis=0, keepdims=True))
                part = jnp.sum(jnp.exp2(t - new), axis=0, keepdims=True)
                peaks.append(new)
                totals.append(total[:, q * 128:(q + 1) * 128] * jnp.exp2(old - new) + part)
            return jnp.concatenate(peaks, axis=1), jnp.concatenate(totals, axis=1)

        def store(m, _):
            at, ts = exponents(m)
            for q, t in enumerate(ts):
                place = pl.ds(pl.multiple_of(start + q * 128, 128), 128)
                e_ref[pl.ds(at, chunk), place] = jnp.exp2(t - shift_ref[:, place]).astype(jnp.bfloat16)
            return 0

        init = (jnp.full((1, width), -1e30, jnp.float32), jnp.zeros((1, width), jnp.float32))
        peak, total = lax.fori_loop(0, depth // chunk, step, init)
        o_ref[:, pl.ds(start, width)] = peak + jnp.log2(total)
        if e_ref is not None:
            shift_ref[:, pl.ds(start, width)] = peak
            lax.fori_loop(0, depth // chunk, store, 0)
        return 0

    lax.fori_loop(0, lanes // width, column, 0)


def first_kernel(chunk, width, is_row, a_ref, b_ref, s_ref, mass_ref, o_ref, *rest):
    e_ref, shift_ref = (None, None) if is_row else rest[:2]
    sb_ref, d_ref, top_ref = rest[-3:]
    lanes = b_ref.shape[0]
    tiles = width // 128
    if is_row:
        norms(a_ref, sb_ref, chunk)
    else:
        spread(s_ref, sb_ref)
    o_ref[:, lanes:] = mass_ref[...]
    top_ref[...] = jnp.zeros_like(top_ref)

    def lanes_of(start, q):
        return pl.ds(pl.multiple_of(start + q * 128, 128), 128)

    def tile(m, start, state):
        def exponents(g, q):
            at = g * GROUP
            s = sb_ref[m * chunk + at:m * chunk + at + GROUP, :]
            return d_ref[m % 2, at:at + GROUP, q * 128:(q + 1) * 128] * CROSS + s

        if m == 0:
            tops = [exponents(0, q) for q in range(tiles)]
            for g in range(1, 128 // GROUP):
                tops = [jnp.maximum(top, exponents(g, q)) for q, top in enumerate(tops)]
            state = [(jnp.max(top, axis=0, keepdims=True), jnp.zeros((GROUP, 128), jnp.float32)) for top in tops]
        for g in range(chunk // GROUP):
            for q, (peak, total) in enumerate(state):
                e = jnp.exp2(exponents(g, q) - peak)
                if e_ref is not None:
                    at = m * chunk + g * GROUP
                    e_ref[at:at + GROUP, lanes_of(start, q)] = e.astype(jnp.bfloat16)
                state[q] = peak, total + e
        return state

    def finish(start, state):
        for q, (peak, total) in enumerate(state):
            top_ref[...] = jnp.maximum(top_ref[...], total)
            o_ref[:, lanes_of(start, q)] = peak + jnp.log2(jnp.sum(total, axis=0, keepdims=True))
            if e_ref is not None:
                shift_ref[:, lanes_of(start, q)] = peak

    pipelined(chunk, width, a_ref, b_ref, d_ref, lambda start: None, tile, finish)

    @pl.when(jnp.logical_not(jnp.max(top_ref[...]) < 2.0 ** 60))
    def _():
        running_max(min(chunk, 256), min(width, 256), a_ref, b_ref, sb_ref, o_ref, e_ref, shift_ref)


def split3(value):
    high = value.astype(jnp.bfloat16)
    rest = value - high.astype(jnp.float32)
    mid = rest.astype(jnp.bfloat16)
    return high, mid, (rest - mid.astype(jnp.float32)).astype(jnp.bfloat16)


def stacked(w_ref):
    high, mid, low = [part.astype(jnp.float32) for part in split3(w_ref[...])]
    shape = (16, w_ref.shape[1])
    place = lax.broadcasted_iota(jnp.int32, shape, 0)
    parts = jnp.where(place == 0, high, jnp.where(place == 1, mid, jnp.where(place == 2, low, 0.0)))
    return parts.astype(jnp.bfloat16)


def row_kernel(width, e_ref, w_ref, o_ref, w16_ref):
    w16_ref[...] = stacked(w_ref)

    def block(k, _):
        at = pl.multiple_of(k * width, width)
        got = lax.dot_general(w16_ref[...], e_ref[pl.ds(at, width), :], NT, preferred_element_type=jnp.float32)
        o_ref[:, pl.ds(at, width)] = jnp.sum(got, axis=0, keepdims=True)
        return 0

    lax.fori_loop(0, e_ref.shape[0] // width, block, 0)


def col_kernel(width, e_ref, w_ref, o_ref, w16_ref):
    w16_ref[...] = stacked(w_ref)

    def block(k, _):
        at = pl.multiple_of(k * width, width)
        got = jnp.dot(w16_ref[...], e_ref[:, pl.ds(at, width)], preferred_element_type=jnp.float32)
        o_ref[:, pl.ds(at, width)] = jnp.sum(got, axis=0, keepdims=True)
        return 0

    lax.fori_loop(0, e_ref.shape[1] // width, block, 0)


def weighted(kernel, e, w, lanes, width=512):
    out = pl.pallas_call(
        functools.partial(kernel, width),
        out_shape=jax.ShapeDtypeStruct((1, lanes), jnp.float32),
        in_specs=[VMEM] * 2,
        out_specs=VMEM,
        scratch_shapes=[pltpu.VMEM((16, w.shape[0]), jnp.bfloat16)],
        compiler_params=pltpu.CompilerParams(vmem_limit_bytes=16 << 20),
        cost_estimate=pl.CostEstimate(flops=2 * e.size, bytes_accessed=2 * e.size, transcendentals=0),
        name="weighted_sum",
    )(e, w.reshape(1, w.shape[0]))
    return out.reshape(lanes)


def pass_cost(a, b):
    size = a.shape[0] * b.shape[0]
    return pl.CostEstimate(flops=2 * size * D, bytes_accessed=2 * (a.size + b.size), transcendentals=size)


def first_pass(a, b, s, mass, chunk=512, width=512):
    depth, lanes, extra = a.shape[0], b.shape[0], mass.shape[0]
    is_row = s is None
    s = jnp.zeros((8, 128), jnp.float32) if is_row else s.reshape(depth // 128, 128)
    out_shape = [jax.ShapeDtypeStruct((1, lanes + extra), jnp.float32)]
    if not is_row:
        out_shape += [jax.ShapeDtypeStruct((depth, lanes), jnp.bfloat16), jax.ShapeDtypeStruct((1, lanes), jnp.float32)]
    out = pl.pallas_call(
        functools.partial(first_kernel, chunk, width, is_row),
        out_shape=out_shape,
        in_specs=[VMEM] * 4,
        out_specs=[VMEM] * len(out_shape),
        scratch_shapes=[
            pltpu.VMEM((depth, 128), jnp.float32),
            pltpu.VMEM((2, chunk, width), jnp.float32),
            pltpu.VMEM((GROUP, 128), jnp.float32),
        ],
        compiler_params=pltpu.CompilerParams(vmem_limit_bytes=16 << 20),
        cost_estimate=pass_cost(a, b),
        name="first_pass",
    )(a, b, s, mass.reshape(1, extra))
    sent = out[0].reshape(lanes + extra)
    return sent if is_row else (sent, out[1], out[2].reshape(lanes))


def high_low(value):
    high = value.astype(jnp.bfloat16)
    return high, (value - high.astype(jnp.float32)).astype(jnp.bfloat16)


def column_grad_kernel(width, own, xt_ref, y_ref, e_ref, alpha_ref, beta_ref, gc_ref, gcs_ref,
                       bb_ref, cb_ref, xa_ref, sums_ref, acc_ref):
    rows, cols = xt_ref.shape[1], y_ref.shape[0]
    spread(beta_ref, bb_ref)
    place = lax.broadcasted_iota(jnp.int32, (128, 512), 0)
    for k in range(rows // 512):
        at = k * 512
        alpha = alpha_ref[:, at:at + 512]
        high, low = high_low(xt_ref[:, at:at + 512].astype(jnp.float32) * alpha)
        first, second = high_low(alpha)
        low = jnp.where(place == 126, first.astype(jnp.float32), low.astype(jnp.float32))
        low = jnp.where(place == 127, second.astype(jnp.float32), low)
        xa_ref[:128, at:at + 512] = high
        xa_ref[128:, at:at + 512] = low.astype(jnp.bfloat16)

    lower = lax.broadcasted_iota(jnp.int32, (128, width), 0) < 126
    for k in range(cols // width):
        at = k * width
        got = jnp.dot(xa_ref[...], e_ref[:, at:at + width], preferred_element_type=jnp.float32)
        acc_ref[:, at:at + width] = got[:128] + jnp.where(lower, got[128:], 0.0)
        count = got[254:255] + got[255:256]
        for q in range(width // 128):
            sums_ref[at // 128 + q:at // 128 + q + 1, :] = count[:, q * 128:(q + 1) * 128]
    spread(sums_ref, cb_ref)
    for k in range(cols // 128):
        at = k * 128
        pulled = jnp.transpose(acc_ref[:, at:at + 128])
        whole = cb_ref[at:at + 128, :] * y_ref[at:at + 128, :].astype(jnp.float32)
        grad = 2.0 * bb_ref[at:at + 128, :] * (whole - pulled)
        if at < own:
            gc_ref[at:at + 128, :] = grad
        else:
            gcs_ref[at - own:at - own + 128, :] = grad.astype(jnp.bfloat16)


def column_grad(xt, y, e, alpha, beta, own, width=512):
    rows, cols = xt.shape[1], y.shape[0]
    return pl.pallas_call(
        functools.partial(column_grad_kernel, width, own),
        out_shape=(
            jax.ShapeDtypeStruct((own, D), jnp.float32),
            jax.ShapeDtypeStruct((cols - own, D), jnp.bfloat16),
        ),
        in_specs=[VMEM] * 5,
        out_specs=(VMEM,) * 2,
        scratch_shapes=[
            pltpu.VMEM((cols, 128), jnp.float32),
            pltpu.VMEM((cols, 128), jnp.float32),
            pltpu.VMEM((256, rows), jnp.bfloat16),
            pltpu.VMEM((cols // 128, 128), jnp.float32),
            pltpu.VMEM((128, cols), jnp.float32),
        ],
        compiler_params=pltpu.CompilerParams(vmem_limit_bytes=16 << 20),
        cost_estimate=pl.CostEstimate(flops=4 * e.size * D, bytes_accessed=2 * e.size, transcendentals=0),
        name="column_grad",
    )(xt, y, e, alpha.reshape(1, rows), beta.reshape(cols // 128, 128))


def row_grad_kernel(chunk, own, x_ref, y_ref, e_ref, alpha_ref, beta_ref, gi_ref, gis_ref, ab_ref, bb_ref, yb_ref):
    rows, cols = x_ref.shape[0], y_ref.shape[0]
    spread(alpha_ref, ab_ref)
    spread(beta_ref, bb_ref)
    place = lax.broadcasted_iota(jnp.int32, (256, 128), 1)
    for k in range(cols // 256):
        at = k * 256
        beta = bb_ref[at:at + 256, :]
        high, low = high_low(y_ref[at:at + 256, :].astype(jnp.float32) * beta)
        first, second = high_low(beta)
        low = jnp.where(place == 126, first.astype(jnp.float32), low.astype(jnp.float32))
        low = jnp.where(place == 127, second.astype(jnp.float32), low)
        yb_ref[at:at + 256, :128] = high
        yb_ref[at:at + 256, 128:] = low.astype(jnp.bfloat16)

    lower = lax.broadcasted_iota(jnp.int32, (chunk, 128), 1) < 126

    def block(at):
        got = jnp.dot(e_ref[pl.ds(at, chunk), :], yb_ref[...], preferred_element_type=jnp.float32)
        total = got[:, 254:255] + got[:, 255:256]
        pulled = got[:, :128] + jnp.where(lower, got[:, 128:], 0.0)
        x = x_ref[pl.ds(at, chunk), :].astype(jnp.float32)
        return 2.0 * ab_ref[pl.ds(at, chunk), :] * (total * x - pulled)

    def own_block(k, _):
        at = pl.multiple_of(k * chunk, chunk)
        gi_ref[pl.ds(at, chunk), :] = block(at)
        return 0

    def sent_block(k, _):
        at = pl.multiple_of(k * chunk, chunk)
        gis_ref[pl.ds(pl.multiple_of(at - own, chunk), chunk), :] = block(at).astype(jnp.bfloat16)
        return 0

    lax.fori_loop(own // chunk, rows // chunk, sent_block, 0)
    lax.fori_loop(0, own // chunk, own_block, 0)


def row_grad(x, y, e, alpha, beta, own):
    rows, cols = x.shape[0], y.shape[0]
    return pl.pallas_call(
        functools.partial(row_grad_kernel, math.gcd(own, 512), own),
        out_shape=(
            jax.ShapeDtypeStruct((own, D), jnp.float32),
            jax.ShapeDtypeStruct((rows - own, D), jnp.bfloat16),
        ),
        in_specs=[VMEM] * 5,
        out_specs=(VMEM,) * 2,
        scratch_shapes=[
            pltpu.VMEM((rows, 128), jnp.float32),
            pltpu.VMEM((cols, 128), jnp.float32),
            pltpu.VMEM((cols, 256), jnp.bfloat16),
        ],
        compiler_params=pltpu.CompilerParams(vmem_limit_bytes=16 << 20),
        cost_estimate=pl.CostEstimate(flops=4 * e.size * D, bytes_accessed=2 * e.size, transcendentals=0),
        name="row_grad",
    )(x, y, e, alpha.reshape(rows // 128, 128), beta.reshape(cols // 128, 128))


class Groups:
    def __init__(self, nrow, ncol):
        self.count = nrow * ncol
        self.across = [(a << 1) * ncol + b for a in range(nrow // 2) for b in range(2)]
        self.along = [z << 1 for z in range(ncol // 2)]
        self.core = ncol

    def swap(self, value, mask):
        if mask == 0:
            return value
        return lax.ppermute(value, ("row", "col"), [(i, i ^ mask) for i in range(self.count)])


def reordered(value, shift, parts):
    if shift == 0:
        return value
    blocks = value.reshape(parts, -1)
    return jnp.concatenate([blocks[s ^ shift] for s in range(parts)])


def lse2(parts):
    top = functools.reduce(jnp.maximum, parts)
    return top + jnp.log2(sum(jnp.exp2(part - top) for part in parts))


def local(imu, camera, imu_mass, cam_mass):
    nrow, ncol = lax.axis_size("row"), lax.axis_size("col")
    row, col = lax.axis_index("row"), lax.axis_index("col")
    groups = Groups(nrow, ncol)
    swap, across, along, core = groups.swap, groups.across, groups.along, groups.core
    na, nz = len(across), len(along)
    share_x, share_y = imu.shape[0], camera.shape[1]

    x = jnp.concatenate([swap(imu, mask) for mask in across])
    near = [swap(camera[0], mask) for mask in along]
    y = jnp.concatenate(near + [swap(part, core) for part in near])

    def pair(mass, place, share):
        return jnp.concatenate([lax.dynamic_slice_in_dim(mass, (place ^ k) * share, share, 0) for k in range(2)])

    def row_exchange(local_value):
        return [reordered(swap(local_value, mask), s, na) for s, mask in enumerate(across)]

    def halves(value):
        return jnp.concatenate([value[value.shape[0] // 2:], value[:value.shape[0] // 2]])

    sent = first_pass(y, x, None, pair(imu_mass, col, share_x))
    got = [swap(sent, mask) for mask in across]
    size = na * share_x
    mass_a = jnp.concatenate([got[2 * a][size:] for a in range(na // 2)])
    u = jnp.log2(mass_a) - lse2([reordered(got[s][:size], s, na) for s in range(na)])

    sent, e, shift = first_pass(x, y, u, pair(cam_mass, row, share_y))
    size = 2 * nz * share_y
    lse, mass = sent[:size], sent[size:]
    lse = lse2([lse, halves(swap(lse, core))])
    sent = jnp.concatenate([lse, mass])
    got = [swap(sent, mask) for mask in along]

    def turned(value, z):
        half = value.shape[0] // 2
        return jnp.concatenate([reordered(value[:half], z, nz), reordered(value[half:], z, nz)])

    masses = [part[size:].reshape(2, share_y) for part in got]
    mass_b = jnp.concatenate([part[0] for part in masses] + [part[1] for part in masses])
    v = jnp.log2(mass_b) - lse2([turned(got[z][:size], z) for z in range(nz)])

    first_beta = beta = jnp.exp2(v + shift)
    for step in range(1, ITERS):
        alpha = mass_a / sum(row_exchange(weighted(row_kernel, e, beta, x.shape[0])))
        part = first_beta * weighted(col_kernel, e, alpha, y.shape[0])
        part = part + halves(swap(part, core))
        beta = first_beta * (mass_b / sum(turned(swap(part, mask), z) for z, mask in enumerate(along)))

    gc, gc_send = column_grad(x.T, y, e, alpha, beta, nz * share_y)
    gc = gc + swap(gc_send, core).astype(jnp.float32)
    gi, gi_send = row_grad(x, y, e, alpha, beta, share_x)
    for s in range(1, na):
        gi = gi + swap(gi_send[(s - 1) * share_x:s * share_x], across[s]).astype(jnp.float32)
    grad_cam = gc[:share_y]
    for z in range(1, nz):
        part = gc[z * share_y:(z + 1) * share_y].astype(jnp.bfloat16)
        grad_cam = grad_cam + swap(part, along[z]).astype(jnp.float32)
    return gi, grad_cam[None]


def solution(mesh):
    in_specs = (P(("row", "col"), None), P("col", "row", None), P("row"), P("col"))
    out_specs = (P(("row", "col"), None), P("col", "row", None))
    return jax.shard_map(local, mesh=mesh, in_specs=in_specs, out_specs=out_specs, check_vma=False)
```

```python
import functools
import math

import jax
import jax.numpy as jnp
from jax import lax
from jax.experimental import pallas as pl
from jax.experimental.pallas import tpu as pltpu
from jax.sharding import PartitionSpec as P

D = 128
ITERS = 3
EPSILON = D / 20.0
LOG2E = math.log2(math.e)
CROSS = 2.0 * LOG2E / EPSILON
NT = (((1,), (1,)), ((), ()))
VMEM = pl.BlockSpec(memory_space=pltpu.VMEM)
GROUP = 32
ROOM = 8 << 20


def spread(s_ref, sb_ref):
    chunks = s_ref.shape[0]
    turned = jnp.transpose(s_ref[...])
    for k in range(chunks):
        sb_ref[k * 128:(k + 1) * 128, :] = jnp.broadcast_to(turned[:, k:k + 1], (128, 128))


def pipelined(places, chunk, width, a_ref, b_ref, d_ref, tile, finish):
    last = b_ref.shape[0] // width - 1

    def product(n, m):
        b = b_ref[pl.ds(pl.multiple_of(n * width, width), width), :]
        a = a_ref[places[m]:places[m] + chunk, :]
        d_ref[m % 2] = lax.dot_general(a, b, NT, preferred_element_type=jnp.float32)

    product(0, 0)

    def column(n, _):
        start = pl.multiple_of(n * width, width)
        state = None
        for m in range(len(places)):
            if m + 1 < len(places):
                product(n, m + 1)
            else:
                product(jnp.minimum(n + 1, last), 0)
            state = tile(m, start, state)
        finish(start, state)
        return 0

    lax.fori_loop(0, last + 1, column, 0)


def running_max(places, chunk, width, a_ref, b_ref, sb_ref, o_ref, e_ref, shift_ref):
    def column(n, _):
        start = pl.multiple_of(n * width, width)
        b = b_ref[pl.ds(start, width), :]

        def exponents(at):
            d = lax.dot_general(a_ref[at:at + chunk, :], b, NT, preferred_element_type=jnp.float32)
            s = sb_ref[at:at + chunk, :]
            return [d[:, q * 128:(q + 1) * 128] * CROSS + s for q in range(width // 128)]

        peak, total = jnp.full((1, width), -1e30, jnp.float32), jnp.zeros((1, width), jnp.float32)
        for at in places:
            peaks, totals = [], []
            for q, t in enumerate(exponents(at)):
                old = peak[:, q * 128:(q + 1) * 128]
                new = jnp.maximum(old, jnp.max(t, axis=0, keepdims=True))
                part = jnp.sum(jnp.exp2(t - new), axis=0, keepdims=True)
                peaks.append(new)
                totals.append(total[:, q * 128:(q + 1) * 128] * jnp.exp2(old - new) + part)
            peak, total = jnp.concatenate(peaks, axis=1), jnp.concatenate(totals, axis=1)
        o_ref[:, pl.ds(start, width)] = peak + jnp.log2(total)
        if e_ref is not None:
            shift_ref[:, pl.ds(start, width)] = peak
            for at in places:
                for q, t in enumerate(exponents(at)):
                    place = pl.ds(pl.multiple_of(start + q * 128, 128), 128)
                    e_ref[at:at + chunk, place] = jnp.exp2(t - shift_ref[:, place]).astype(jnp.bfloat16)
        return 0

    lax.fori_loop(0, b_ref.shape[0] // width, column, 0)


def lse_pass(places, chunk, width, a_ref, b_ref, sb_ref, d_ref, top_ref, o_ref, e_ref=None, shift_ref=None):
    tiles = width // 128
    top_ref[...] = jnp.zeros_like(top_ref)

    def lanes_of(start, q):
        return pl.ds(pl.multiple_of(start + q * 128, 128), 128)

    def tile(m, start, state):
        def exponents(g, q):
            at = g * GROUP
            s = sb_ref[places[m] + at:places[m] + at + GROUP, :]
            return d_ref[m % 2, at:at + GROUP, q * 128:(q + 1) * 128] * CROSS + s

        if m == 0:
            tops = [exponents(0, q) for q in range(tiles)]
            for g in range(1, 128 // GROUP):
                tops = [jnp.maximum(top, exponents(g, q)) for q, top in enumerate(tops)]
            state = [(jnp.max(top, axis=0, keepdims=True), jnp.zeros((GROUP, 128), jnp.float32)) for top in tops]
        for g in range(chunk // GROUP):
            for q, (peak, total) in enumerate(state):
                e = jnp.exp2(exponents(g, q) - peak)
                if e_ref is not None:
                    at = places[m] + g * GROUP
                    e_ref[at:at + GROUP, lanes_of(start, q)] = e.astype(jnp.bfloat16)
                state[q] = peak, total + e
        return state

    def finish(start, state):
        for q, (peak, total) in enumerate(state):
            top_ref[...] = jnp.maximum(top_ref[...], total)
            o_ref[:, lanes_of(start, q)] = peak + jnp.log2(jnp.sum(total, axis=0, keepdims=True))
            if e_ref is not None:
                shift_ref[:, lanes_of(start, q)] = peak

    pipelined(places, chunk, width, a_ref, b_ref, d_ref, tile, finish)

    @pl.when(jnp.logical_not(jnp.max(top_ref[...]) < 2.0 ** 60))
    def _():
        running_max(places, chunk, min(width, 256), a_ref, b_ref, sb_ref, o_ref, e_ref, shift_ref)


def put_pair(o_ref, at, mass_ref, axis):
    share = mass_ref.shape[1]
    place = lax.axis_index(axis)
    for k in range(2):
        o_ref[:, at + k * share:at + (k + 1) * share] = mass_ref[pl.ds(place ^ k, 1), :]


def row_lse_kernel(width, early, nx, ny, *refs):
    xs, ys, refs = refs[:nx], refs[nx:nx + ny], refs[nx + ny:]
    share = ys[0].shape[0]
    if early:
        x_ref, xt_ref, o_ref, y_ref, sb_ref, d_ref, top_ref = refs
        part = xs[0].shape[0]
        for k, shard in enumerate(xs):
            x_ref[k * part:(k + 1) * part, :] = shard[...]
        for k in range(x_ref.shape[0] // 128):
            at = k * 128
            turned = jnp.transpose(x_ref[at:at + 128, :].astype(jnp.float32))
            xt_ref[:, at:at + 128] = turned.astype(jnp.bfloat16)
        places = [k * share for k in range(ny)]
    else:
        x_ref, first_ref, mass_ref, y_ref, o_ref, sb_ref, d_ref, top_ref, sum_ref = refs
        places = [k * share for k in range(ny) if k % (ny // 2)]
    for k, shard in enumerate(ys):
        y_ref[k * share:(k + 1) * share, :] = shard[...]
    for at in places:
        y = y_ref[at:at + share, :].astype(jnp.float32)
        total = jnp.sum(y * y, axis=1, keepdims=True) * (-LOG2E / EPSILON)
        sb_ref[at:at + share, :] = jnp.broadcast_to(total, (share, 128))
    if early:
        lse_pass(places, share, width, y_ref, x_ref, sb_ref, d_ref, top_ref, o_ref)
    else:
        lse_pass(places, share, width, y_ref, x_ref, sb_ref, d_ref, top_ref, sum_ref)
        rows = x_ref.shape[0]
        one, two = first_ref[...], sum_ref[...]
        top = jnp.maximum(one, two)
        o_ref[:, :rows] = top + jnp.log2(jnp.exp2(one - top) + jnp.exp2(two - top))
        put_pair(o_ref, rows, mass_ref, "col")


def column_lse_kernel(width, chunk, x_ref, y_ref, u_ref, mass_ref, o_ref, e_ref, shift_ref,
                      sb_ref, d_ref, top_ref, room_ref):
    spread(u_ref, sb_ref)
    put_pair(o_ref, y_ref.shape[0], mass_ref, "row")
    places = list(range(0, x_ref.shape[0], chunk))
    lse_pass(places, chunk, width, x_ref, y_ref, sb_ref, d_ref, top_ref, o_ref, e_ref, shift_ref)


def split3(value):
    high = value.astype(jnp.bfloat16)
    rest = value - high.astype(jnp.float32)
    mid = rest.astype(jnp.bfloat16)
    return high, mid, (rest - mid.astype(jnp.float32)).astype(jnp.bfloat16)


def stacked(w_ref):
    high, mid, low = [part.astype(jnp.float32) for part in split3(w_ref[...])]
    shape = (16, w_ref.shape[1])
    place = lax.broadcasted_iota(jnp.int32, shape, 0)
    parts = jnp.where(place == 0, high, jnp.where(place == 1, mid, jnp.where(place == 2, low, 0.0)))
    return parts.astype(jnp.bfloat16)


def row_kernel(width, e_ref, w_ref, o_ref, w16_ref):
    w16_ref[...] = stacked(w_ref)

    def block(k, _):
        at = pl.multiple_of(k * width, width)
        got = lax.dot_general(w16_ref[...], e_ref[pl.ds(at, width), :], NT, preferred_element_type=jnp.float32)
        o_ref[:, pl.ds(at, width)] = jnp.sum(got, axis=0, keepdims=True)
        return 0

    lax.fori_loop(0, e_ref.shape[0] // width, block, 0)


def col_kernel(width, e_ref, w_ref, o_ref, w16_ref):
    w16_ref[...] = stacked(w_ref)

    def block(k, _):
        at = pl.multiple_of(k * width, width)
        got = jnp.dot(w16_ref[...], e_ref[:, pl.ds(at, width)], preferred_element_type=jnp.float32)
        o_ref[:, pl.ds(at, width)] = jnp.sum(got, axis=0, keepdims=True)
        return 0

    lax.fori_loop(0, e_ref.shape[1] // width, block, 0)


def weighted(kernel, e, w, lanes, width=512):
    out = pl.pallas_call(
        functools.partial(kernel, width),
        out_shape=jax.ShapeDtypeStruct((1, lanes), jnp.float32),
        in_specs=[VMEM] * 2,
        out_specs=VMEM,
        scratch_shapes=[pltpu.VMEM((16, w.shape[0]), jnp.bfloat16)],
        compiler_params=pltpu.CompilerParams(vmem_limit_bytes=16 << 20),
        cost_estimate=pl.CostEstimate(flops=2 * e.size, bytes_accessed=2 * e.size, transcendentals=0),
        name="weighted_sum",
    )(e, w.reshape(1, w.shape[0]))
    return out.reshape(lanes)


def pass_cost(depth, lanes):
    return pl.CostEstimate(flops=2 * depth * lanes * D, bytes_accessed=2 * D * (depth + lanes), transcendentals=depth * lanes)


def shape(*dims, dtype=jnp.float32):
    return jax.ShapeDtypeStruct(dims, dtype)


def lse_scratch(depth, chunk, width):
    return [
        pltpu.VMEM((depth, 128), jnp.float32),
        pltpu.VMEM((2, chunk, width), jnp.float32),
        pltpu.VMEM((GROUP, 128), jnp.float32),
    ]


def row_lse_early(xs, ys, width=512):
    rows, share = len(xs) * xs[0].shape[0], ys[0].shape[0]
    depth = len(ys) * share
    return pl.pallas_call(
        functools.partial(row_lse_kernel, width, True, len(xs), len(ys)),
        out_shape=(shape(rows, D, dtype=jnp.bfloat16), shape(D, rows, dtype=jnp.bfloat16), shape(1, rows)),
        in_specs=[VMEM] * (len(xs) + len(ys)),
        out_specs=(VMEM,) * 3,
        scratch_shapes=[pltpu.VMEM((depth, D), jnp.bfloat16)] + lse_scratch(depth, share, width),
        compiler_params=pltpu.CompilerParams(vmem_limit_bytes=16 << 20),
        cost_estimate=pass_cost(depth, rows),
        name="row_lse_early",
    )(*xs, *ys)


def row_lse_late(x, ys, first, mass, width=512):
    rows, share = x.shape[0], ys[0].shape[0]
    depth = len(ys) * share
    tail = mass.shape[0] // lax.axis_size("col")
    return pl.pallas_call(
        functools.partial(row_lse_kernel, width, False, 0, len(ys)),
        out_shape=(shape(depth, D, dtype=jnp.bfloat16), shape(1, rows + 2 * tail)),
        in_specs=[VMEM] * (len(ys) + 3),
        out_specs=(VMEM,) * 2,
        scratch_shapes=lse_scratch(depth, share, width) + [pltpu.VMEM((1, rows), jnp.float32)],
        compiler_params=pltpu.CompilerParams(vmem_limit_bytes=16 << 20),
        cost_estimate=pass_cost(depth - 2 * share, rows),
        name="row_lse_late",
    )(*ys, x, first, mass.reshape(-1, tail))


def column_lse(x, y, u, mass, width=512, chunk=512):
    rows, cols = x.shape[0], y.shape[0]
    tail = mass.shape[0] // lax.axis_size("row")
    return pl.pallas_call(
        functools.partial(column_lse_kernel, width, chunk),
        out_shape=(shape(1, cols + 2 * tail), shape(rows, cols, dtype=jnp.bfloat16), shape(1, cols)),
        in_specs=[VMEM] * 4,
        out_specs=(VMEM,) * 3,
        scratch_shapes=lse_scratch(rows, chunk, width) + [pltpu.VMEM((ROOM // 512, 128), jnp.float32)],
        compiler_params=pltpu.CompilerParams(vmem_limit_bytes=24 << 20),
        cost_estimate=pass_cost(rows, cols),
        name="column_lse",
    )(x, y, u.reshape(rows // 128, 128), mass.reshape(-1, tail))


def high_low(value):
    high = value.astype(jnp.bfloat16)
    return high, (value - high.astype(jnp.float32)).astype(jnp.bfloat16)


def column_grad_kernel(width, own, xt_ref, y_ref, e_ref, alpha_ref, beta_ref, gc_ref, gcs_ref,
                       bb_ref, cb_ref, xa_ref, sums_ref, acc_ref):
    rows, cols = xt_ref.shape[1], y_ref.shape[0]
    spread(beta_ref, bb_ref)
    place = lax.broadcasted_iota(jnp.int32, (128, 512), 0)
    for k in range(rows // 512):
        at = k * 512
        alpha = alpha_ref[:, at:at + 512]
        high, low = high_low(xt_ref[:, at:at + 512].astype(jnp.float32) * alpha)
        first, second = high_low(alpha)
        low = jnp.where(place == 126, first.astype(jnp.float32), low.astype(jnp.float32))
        low = jnp.where(place == 127, second.astype(jnp.float32), low)
        xa_ref[:128, at:at + 512] = high
        xa_ref[128:, at:at + 512] = low.astype(jnp.bfloat16)

    lower = lax.broadcasted_iota(jnp.int32, (128, width), 0) < 126
    for k in range(cols // width):
        at = k * width
        got = jnp.dot(xa_ref[...], e_ref[:, at:at + width], preferred_element_type=jnp.float32)
        acc_ref[:, at:at + width] = got[:128] + jnp.where(lower, got[128:], 0.0)
        count = got[254:255] + got[255:256]
        for q in range(width // 128):
            sums_ref[at // 128 + q:at // 128 + q + 1, :] = count[:, q * 128:(q + 1) * 128]
    spread(sums_ref, cb_ref)
    for k in range(cols // 128):
        at = k * 128
        pulled = jnp.transpose(acc_ref[:, at:at + 128])
        whole = cb_ref[at:at + 128, :] * y_ref[at:at + 128, :].astype(jnp.float32)
        grad = 2.0 * bb_ref[at:at + 128, :] * (whole - pulled)
        if at < own:
            gc_ref[at:at + 128, :] = grad
        else:
            gcs_ref[at - own:at - own + 128, :] = grad.astype(jnp.bfloat16)


def column_grad(xt, y, e, alpha, beta, own, width=512):
    rows, cols = xt.shape[1], y.shape[0]
    return pl.pallas_call(
        functools.partial(column_grad_kernel, width, own),
        out_shape=(
            jax.ShapeDtypeStruct((own, D), jnp.float32),
            jax.ShapeDtypeStruct((cols - own, D), jnp.bfloat16),
        ),
        in_specs=[VMEM] * 5,
        out_specs=(VMEM,) * 2,
        scratch_shapes=[
            pltpu.VMEM((cols, 128), jnp.float32),
            pltpu.VMEM((cols, 128), jnp.float32),
            pltpu.VMEM((256, rows), jnp.bfloat16),
            pltpu.VMEM((cols // 128, 128), jnp.float32),
            pltpu.VMEM((128, cols), jnp.float32),
        ],
        compiler_params=pltpu.CompilerParams(vmem_limit_bytes=16 << 20),
        cost_estimate=pl.CostEstimate(flops=4 * e.size * D, bytes_accessed=2 * e.size, transcendentals=0),
        name="column_grad",
    )(xt, y, e, alpha.reshape(1, rows), beta.reshape(cols // 128, 128))


def row_block(at, chunk, x_ref, e_ref, yb_ref, scale):
    got = jnp.dot(e_ref[pl.ds(at, chunk), :], yb_ref[...], preferred_element_type=jnp.float32)
    lower = lax.broadcasted_iota(jnp.int32, (chunk, 128), 1) < 126
    total = got[:, 254:255] + got[:, 255:256]
    pulled = got[:, :128] + jnp.where(lower, got[:, 128:], 0.0)
    x = x_ref[pl.ds(at, chunk), :].astype(jnp.float32)
    return 2.0 * scale * (total * x - pulled)


def own_rows_kernel(x_ref, y_ref, e_ref, alpha_ref, beta_ref, gi_ref, yb_ref, ab_ref, bb_ref):
    own, cols = gi_ref.shape[0], y_ref.shape[0]
    spread(alpha_ref, ab_ref)
    spread(beta_ref, bb_ref)
    place = lax.broadcasted_iota(jnp.int32, (256, 128), 1)
    for k in range(cols // 256):
        at = k * 256
        beta = bb_ref[at:at + 256, :]
        high, low = high_low(y_ref[at:at + 256, :].astype(jnp.float32) * beta)
        first, second = high_low(beta)
        low = jnp.where(place == 126, first.astype(jnp.float32), low.astype(jnp.float32))
        low = jnp.where(place == 127, second.astype(jnp.float32), low)
        yb_ref[at:at + 256, :128] = high
        yb_ref[at:at + 256, 128:] = low.astype(jnp.bfloat16)
    gi_ref[...] = row_block(0, own, x_ref, e_ref, yb_ref, ab_ref[:own, :])


def sent_rows_kernel(chunk, own, x_ref, yb_ref, e_ref, alpha_ref, gis_ref, ab_ref):
    spread(alpha_ref, ab_ref)

    def block(k, _):
        at = pl.multiple_of(k * chunk, chunk)
        grad = row_block(at, chunk, x_ref, e_ref, yb_ref, ab_ref[pl.ds(at, chunk), :])
        gis_ref[pl.ds(pl.multiple_of(at - own, chunk), chunk), :] = grad.astype(jnp.bfloat16)
        return 0

    lax.fori_loop(own // chunk, x_ref.shape[0] // chunk, block, 0)


def own_rows(x, y, e, alpha, beta, own):
    rows, cols = x.shape[0], y.shape[0]
    return pl.pallas_call(
        own_rows_kernel,
        out_shape=(shape(own, D), shape(cols, 256, dtype=jnp.bfloat16)),
        in_specs=[VMEM] * 5,
        out_specs=(VMEM,) * 2,
        scratch_shapes=[pltpu.VMEM((rows, 128), jnp.float32), pltpu.VMEM((cols, 128), jnp.float32)],
        compiler_params=pltpu.CompilerParams(vmem_limit_bytes=16 << 20),
        cost_estimate=pl.CostEstimate(flops=4 * own * cols * D, bytes_accessed=2 * own * cols, transcendentals=0),
        name="own_rows",
    )(x, y, e, alpha.reshape(rows // 128, 128), beta.reshape(cols // 128, 128))


def sent_rows(x, yb, e, alpha, own):
    rows, cols = x.shape[0], yb.shape[0]
    rest = rows - own
    return pl.pallas_call(
        functools.partial(sent_rows_kernel, math.gcd(own, 512), own),
        out_shape=shape(rest, D, dtype=jnp.bfloat16),
        in_specs=[VMEM] * 4,
        out_specs=VMEM,
        scratch_shapes=[pltpu.VMEM((rows, 128), jnp.float32)],
        compiler_params=pltpu.CompilerParams(vmem_limit_bytes=16 << 20),
        cost_estimate=pl.CostEstimate(flops=4 * rest * cols * D, bytes_accessed=2 * rest * cols, transcendentals=0),
        name="sent_rows",
    )(x, yb, e, alpha.reshape(rows // 128, 128))


class Groups:
    def __init__(self, nrow, ncol):
        self.count = nrow * ncol
        self.across = [(a << 1) * ncol + b for a in range(nrow // 2) for b in range(2)]
        self.along = [z << 1 for z in range(ncol // 2)]
        self.core = ncol

    def swap(self, value, mask):
        if mask == 0:
            return value
        return lax.ppermute(value, ("row", "col"), [(i, i ^ mask) for i in range(self.count)])


def reordered(value, shift, parts):
    if shift == 0:
        return value
    blocks = value.reshape(parts, -1)
    return jnp.concatenate([blocks[s ^ shift] for s in range(parts)])


def lse2(parts):
    top = functools.reduce(jnp.maximum, parts)
    return top + jnp.log2(sum(jnp.exp2(part - top) for part in parts))


def local(imu, camera, imu_mass, cam_mass):
    nrow, ncol = lax.axis_size("row"), lax.axis_size("col")
    groups = Groups(nrow, ncol)
    swap, across, along, core = groups.swap, groups.across, groups.along, groups.core
    na, nz = len(across), len(along)
    share_x, share_y = imu.shape[0], camera.shape[1]

    mine = camera[0]
    xs = [swap(imu, mask) for mask in across]
    near = [swap(mine, mask) for mask in along]
    far = [swap(part, core) for part in near]

    def row_exchange(local_value):
        return [reordered(swap(local_value, mask), s, na) for s, mask in enumerate(across)]

    def halves(value):
        return jnp.concatenate([value[value.shape[0] // 2:], value[:value.shape[0] // 2]])

    x, xt, first = row_lse_early(xs, [near[0], far[0]])
    y, sent = row_lse_late(x, near + far, first, imu_mass)
    sent = sent.reshape(-1)
    got = [swap(sent, mask) for mask in across]
    size = na * share_x
    mass_a = jnp.concatenate([got[2 * a][size:] for a in range(na // 2)])
    u = jnp.log2(mass_a) - lse2([reordered(got[s][:size], s, na) for s in range(na)])

    sent, e, shift = column_lse(x, y, u, cam_mass)
    sent, shift = sent.reshape(-1), shift.reshape(-1)
    size = 2 * nz * share_y
    lse, mass = sent[:size], sent[size:]
    lse = lse2([lse, halves(swap(lse, core))])
    sent = jnp.concatenate([lse, mass])
    got = [swap(sent, mask) for mask in along]

    def turned(value, z):
        half = value.shape[0] // 2
        return jnp.concatenate([reordered(value[:half], z, nz), reordered(value[half:], z, nz)])

    masses = [part[size:].reshape(2, share_y) for part in got]
    mass_b = jnp.concatenate([part[0] for part in masses] + [part[1] for part in masses])
    v = jnp.log2(mass_b) - lse2([turned(got[z][:size], z) for z in range(nz)])

    first_beta = beta = jnp.exp2(v + shift)
    for step in range(1, ITERS):
        alpha = mass_a / sum(row_exchange(weighted(row_kernel, e, beta, x.shape[0])))
        part = first_beta * weighted(col_kernel, e, alpha, y.shape[0])
        part = part + halves(swap(part, core))
        beta = first_beta * (mass_b / sum(turned(swap(part, mask), z) for z, mask in enumerate(along)))

    gc, gc_send = column_grad(xt, y, e, alpha, beta, nz * share_y)
    gi, yb = own_rows(x, y, e, alpha, beta, share_x)
    gc = gc + swap(gc_send, core).astype(jnp.float32)
    gc, yb = lax.optimization_barrier((gc, yb))
    grad_cam = gc[:share_y]
    for z in range(1, nz):
        part = gc[z * share_y:(z + 1) * share_y].astype(jnp.bfloat16)
        grad_cam = grad_cam + swap(part, along[z]).astype(jnp.float32)
    gi_send = sent_rows(x, yb, e, alpha, share_x)
    for s in range(1, na):
        gi = gi + swap(gi_send[(s - 1) * share_x:s * share_x], across[s]).astype(jnp.float32)
    return gi, grad_cam[None]


def solution(mesh):
    in_specs = (P(("row", "col"), None), P("col", "row", None), P("row"), P("col"))
    out_specs = (P(("row", "col"), None), P("col", "row", None))
    return jax.shard_map(local, mesh=mesh, in_specs=in_specs, out_specs=out_specs, check_vma=False)
```

```python
import functools
import math

import jax
import jax.numpy as jnp
from jax import lax
from jax.experimental import pallas as pl
from jax.experimental.pallas import tpu as pltpu
from jax.sharding import PartitionSpec as P

D = 128
ITERS = 3
EPSILON = D / 20.0
LOG2E = math.log2(math.e)
CROSS = 2.0 * LOG2E / EPSILON
NT = (((1,), (1,)), ((), ()))
VMEM = pl.BlockSpec(memory_space=pltpu.VMEM)
GROUP = 32


def spread(value, s_ref, sb_ref):
    chunks = value.shape[1] // 128
    for k in range(chunks):
        s_ref[k:k + 1, :] = value[:, k * 128:(k + 1) * 128]
    turned = jnp.transpose(s_ref[...])
    for k in range(chunks):
        sb_ref[k * 128:(k + 1) * 128, :] = jnp.broadcast_to(turned[:, k:k + 1], (128, 128))


def ordered(refs, size, parts):
    share = size // parts
    return [
        jnp.concatenate([ref[:, (k ^ s) * share:((k ^ s) + 1) * share] for k in range(parts)], axis=1)
        for s, ref in enumerate(refs)
    ]


def lse2(parts):
    top = functools.reduce(jnp.maximum, parts)
    return top + jnp.log2(sum(jnp.exp2(part - top) for part in parts))


def pipelined(places, chunk, width, a_ref, b_ref, d_ref, tile, finish):
    last = b_ref.shape[0] // width - 1

    def product(n, m):
        b = b_ref[pl.ds(pl.multiple_of(n * width, width), width), :]
        a = a_ref[places[m]:places[m] + chunk, :]
        d_ref[m % 2] = lax.dot_general(a, b, NT, preferred_element_type=jnp.float32)

    product(0, 0)

    def column(n, _):
        start = pl.multiple_of(n * width, width)
        state = None
        for m in range(len(places)):
            if m + 1 < len(places):
                product(n, m + 1)
            else:
                product(jnp.minimum(n + 1, last), 0)
            state = tile(m, start, state)
        finish(start, state)
        return 0

    lax.fori_loop(0, last + 1, column, 0)


def running_max(places, chunk, width, a_ref, b_ref, sb_ref, o_ref, e_ref, shift_ref):
    def column(n, _):
        start = pl.multiple_of(n * width, width)
        b = b_ref[pl.ds(start, width), :]

        def exponents(at):
            d = lax.dot_general(a_ref[at:at + chunk, :], b, NT, preferred_element_type=jnp.float32)
            s = sb_ref[at:at + chunk, :]
            return [d[:, q * 128:(q + 1) * 128] * CROSS + s for q in range(width // 128)]

        peak, total = jnp.full((1, width), -1e30, jnp.float32), jnp.zeros((1, width), jnp.float32)
        for at in places:
            peaks, totals = [], []
            for q, t in enumerate(exponents(at)):
                old = peak[:, q * 128:(q + 1) * 128]
                new = jnp.maximum(old, jnp.max(t, axis=0, keepdims=True))
                part = jnp.sum(jnp.exp2(t - new), axis=0, keepdims=True)
                peaks.append(new)
                totals.append(total[:, q * 128:(q + 1) * 128] * jnp.exp2(old - new) + part)
            peak, total = jnp.concatenate(peaks, axis=1), jnp.concatenate(totals, axis=1)
        o_ref[:, pl.ds(start, width)] = peak + jnp.log2(total)
        if e_ref is not None:
            shift_ref[:, pl.ds(start, width)] = peak
            for at in places:
                for q, t in enumerate(exponents(at)):
                    place = pl.ds(pl.multiple_of(start + q * 128, 128), 128)
                    e_ref[at:at + chunk, place] = jnp.exp2(t - shift_ref[:, place]).astype(jnp.bfloat16)
        return 0

    lax.fori_loop(0, b_ref.shape[0] // width, column, 0)


def lse_pass(places, chunk, width, a_ref, b_ref, sb_ref, d_ref, top_ref, o_ref, e_ref=None, shift_ref=None):
    tiles = width // 128
    top_ref[...] = jnp.zeros_like(top_ref)

    def lanes_of(start, q):
        return pl.ds(pl.multiple_of(start + q * 128, 128), 128)

    def tile(m, start, state):
        def exponents(g, q):
            at = g * GROUP
            s = sb_ref[places[m] + at:places[m] + at + GROUP, :]
            return d_ref[m % 2, at:at + GROUP, q * 128:(q + 1) * 128] * CROSS + s

        if m == 0:
            tops = [exponents(0, q) for q in range(tiles)]
            for g in range(1, 128 // GROUP):
                tops = [jnp.maximum(top, exponents(g, q)) for q, top in enumerate(tops)]
            state = [(jnp.max(top, axis=0, keepdims=True), jnp.zeros((GROUP, 128), jnp.float32)) for top in tops]
        for g in range(chunk // GROUP):
            for q, (peak, total) in enumerate(state):
                e = jnp.exp2(exponents(g, q) - peak)
                if e_ref is not None:
                    at = places[m] + g * GROUP
                    e_ref[at:at + GROUP, lanes_of(start, q)] = e.astype(jnp.bfloat16)
                state[q] = peak, total + e
        return state

    def finish(start, state):
        for q, (peak, total) in enumerate(state):
            top_ref[...] = jnp.maximum(top_ref[...], total)
            o_ref[:, lanes_of(start, q)] = peak + jnp.log2(jnp.sum(total, axis=0, keepdims=True))
            if e_ref is not None:
                shift_ref[:, lanes_of(start, q)] = peak

    pipelined(places, chunk, width, a_ref, b_ref, d_ref, tile, finish)

    @pl.when(jnp.logical_not(jnp.max(top_ref[...]) < 2.0 ** 60))
    def _():
        running_max(places, chunk, min(width, 256), a_ref, b_ref, sb_ref, o_ref, e_ref, shift_ref)


def put_pair(o_ref, at, share, mass_ref, axis):
    place = lax.axis_index(axis)
    for k in range(2):
        start = pl.multiple_of((place ^ k) * share, share)
        o_ref[:, at + k * share:at + (k + 1) * share] = mass_ref[:, pl.ds(start, share)]


def row_lse_kernel(width, early, nx, ny, *refs):
    xs, ys, refs = refs[:nx], refs[nx:nx + ny], refs[nx + ny:]
    share = ys[0].shape[0]
    if early:
        x_ref, xt_ref, o_ref, y_ref, sb_ref, d_ref, top_ref = refs
        part = xs[0].shape[0]
        for k, shard in enumerate(xs):
            x_ref[k * part:(k + 1) * part, :] = shard[...]
        for k in range(x_ref.shape[0] // 128):
            at = k * 128
            turned = jnp.transpose(x_ref[at:at + 128, :].astype(jnp.float32))
            xt_ref[:, at:at + 128] = turned.astype(jnp.bfloat16)
        places = [k * share for k in range(ny)]
    else:
        x_ref, first_ref, mass_ref, y_ref, o_ref, sb_ref, d_ref, top_ref, sum_ref = refs
        places = [k * share for k in range(ny) if k % (ny // 2)]
    for k, shard in enumerate(ys):
        y_ref[k * share:(k + 1) * share, :] = shard[...]
    for at in places:
        y = y_ref[at:at + share, :].astype(jnp.float32)
        total = jnp.sum(y * y, axis=1, keepdims=True) * (-LOG2E / EPSILON)
        sb_ref[at:at + share, :] = jnp.broadcast_to(total, (share, 128))
    if early:
        lse_pass(places, share, width, y_ref, x_ref, sb_ref, d_ref, top_ref, o_ref)
    else:
        lse_pass(places, share, width, y_ref, x_ref, sb_ref, d_ref, top_ref, sum_ref)
        rows = x_ref.shape[0]
        one, two = first_ref[...], sum_ref[...]
        top = jnp.maximum(one, two)
        o_ref[:, :rows] = top + jnp.log2(jnp.exp2(one - top) + jnp.exp2(two - top))
        put_pair(o_ref, rows, (o_ref.shape[1] - rows) // 2, mass_ref, "col")


def column_lse_kernel(width, chunk, na, x_ref, y_ref, mass_ref, *refs):
    got, (o_ref, e_ref, shift_ref, a_ref, s_ref, sb_ref, d_ref, top_ref) = refs[:na], refs[na:]
    rows, cols = x_ref.shape[0], y_ref.shape[0]
    share = rows // na
    for k in range(na):
        at = rows + (k % 2) * share
        a_ref[:, k * share:(k + 1) * share] = got[k - k % 2][:, at:at + share]
    u = jnp.log2(a_ref[...]) - lse2(ordered(got, rows, na))
    spread(u, s_ref, sb_ref)
    put_pair(o_ref, cols, (o_ref.shape[1] - cols) // 2, mass_ref, "row")
    places = list(range(0, rows, chunk))
    lse_pass(places, chunk, width, x_ref, y_ref, sb_ref, d_ref, top_ref, o_ref, e_ref, shift_ref)


def pair_kernel(cols, combine, one_ref, two_ref, o_ref):
    half = cols // 2
    two = jnp.concatenate([two_ref[:, half:cols], two_ref[:, :half]], axis=1)
    o_ref[:, :cols] = combine([one_ref[:, :cols], two])
    if o_ref.shape[1] > cols:
        o_ref[:, cols:] = one_ref[:, cols:]


def split3(value):
    high = value.astype(jnp.bfloat16)
    rest = value - high.astype(jnp.float32)
    mid = rest.astype(jnp.bfloat16)
    return high, mid, (rest - mid.astype(jnp.float32)).astype(jnp.bfloat16)


def stacked(value):
    high, mid, low = [part.astype(jnp.float32) for part in split3(value)]
    dims = (16, value.shape[1])
    place = lax.broadcasted_iota(jnp.int32, dims, 0)
    parts = jnp.where(place == 0, high, jnp.where(place == 1, mid, jnp.where(place == 2, low, 0.0)))
    return parts.astype(jnp.bfloat16)


def row_sums(width, e_ref, w16_ref, o_ref):
    def block(k, _):
        at = pl.multiple_of(k * width, width)
        got = lax.dot_general(w16_ref[...], e_ref[pl.ds(at, width), :], NT, preferred_element_type=jnp.float32)
        o_ref[:, pl.ds(at, width)] = jnp.sum(got, axis=0, keepdims=True)
        return 0

    lax.fori_loop(0, e_ref.shape[0] // width, block, 0)


def first_row_kernel(width, nz, e_ref, shift_ref, *refs):
    got, (o_ref, beta_ref, b_ref, w16_ref) = refs[:nz], refs[nz:]
    cols = e_ref.shape[1]
    share = cols // (2 * nz)
    for k in range(2 * nz):
        at = cols + (k // nz) * share
        b_ref[:, k * share:(k + 1) * share] = got[k % nz][:, at:at + share]
    beta_ref[...] = jnp.exp2(jnp.log2(b_ref[...]) - lse2(ordered(got, cols, 2 * nz)) + shift_ref[...])
    w16_ref[...] = stacked(beta_ref[...])
    row_sums(width, e_ref, w16_ref, o_ref)


def new_beta(first_ref, b_ref, got):
    return first_ref[...] * (b_ref[...] / sum(ordered(got, b_ref.shape[1], 2 * len(got))))


def row_kernel(width, nz, e_ref, first_ref, b_ref, *refs):
    got, (o_ref, w16_ref) = refs[:nz], refs[nz:]
    w16_ref[...] = stacked(new_beta(first_ref, b_ref, got))
    row_sums(width, e_ref, w16_ref, o_ref)


def column_kernel(width, na, e_ref, a_ref, first_ref, *refs):
    got, (o_ref, alpha_ref, w16_ref) = refs[:na], refs[na:]
    alpha_ref[...] = a_ref[...] / sum(ordered(got, a_ref.shape[1], na))
    w16_ref[...] = stacked(alpha_ref[...])

    def block(k, _):
        at = pl.multiple_of(k * width, width)
        got = jnp.dot(w16_ref[...], e_ref[:, pl.ds(at, width)], preferred_element_type=jnp.float32)
        o_ref[:, pl.ds(at, width)] = first_ref[:, pl.ds(at, width)] * jnp.sum(got, axis=0, keepdims=True)
        return 0

    lax.fori_loop(0, e_ref.shape[1] // width, block, 0)


def weighted(kernel, outs, e, rows, got, width=512):
    size = e.shape[0] if kernel is column_kernel else e.shape[1]
    return pl.pallas_call(
        functools.partial(kernel, width, len(got)),
        out_shape=[shape(1, n) for n in outs],
        in_specs=[VMEM] * (1 + len(rows) + len(got)),
        out_specs=[VMEM] * len(outs),
        scratch_shapes=[pltpu.VMEM((16, size), jnp.bfloat16)],
        compiler_params=pltpu.CompilerParams(vmem_limit_bytes=16 << 20),
        cost_estimate=pl.CostEstimate(flops=2 * e.size, bytes_accessed=2 * e.size, transcendentals=0),
        name="weighted_sum",
    )(e, *rows, *[part.reshape(1, -1) for part in got])


def pass_cost(depth, lanes):
    return pl.CostEstimate(flops=2 * depth * lanes * D, bytes_accessed=2 * D * (depth + lanes), transcendentals=depth * lanes)


def shape(*dims, dtype=jnp.float32):
    return jax.ShapeDtypeStruct(dims, dtype)


def lse_scratch(depth, chunk, width):
    return [
        pltpu.VMEM((depth, 128), jnp.float32),
        pltpu.VMEM((2, chunk, width), jnp.float32),
        pltpu.VMEM((GROUP, 128), jnp.float32),
    ]


def row_lse_early(xs, ys, width=512):
    rows, share = len(xs) * xs[0].shape[0], ys[0].shape[0]
    depth = len(ys) * share
    return pl.pallas_call(
        functools.partial(row_lse_kernel, width, True, len(xs), len(ys)),
        out_shape=(shape(rows, D, dtype=jnp.bfloat16), shape(D, rows, dtype=jnp.bfloat16), shape(1, rows)),
        in_specs=[VMEM] * (len(xs) + len(ys)),
        out_specs=(VMEM,) * 3,
        scratch_shapes=[pltpu.VMEM((depth, D), jnp.bfloat16)] + lse_scratch(depth, share, width),
        compiler_params=pltpu.CompilerParams(vmem_limit_bytes=16 << 20),
        cost_estimate=pass_cost(depth, rows),
        name="row_lse_early",
    )(*xs, *ys)


def row_lse_late(x, ys, first, mass, width=512):
    rows, share = x.shape[0], ys[0].shape[0]
    depth = len(ys) * share
    tail = mass.shape[0] // lax.axis_size("col")
    return pl.pallas_call(
        functools.partial(row_lse_kernel, width, False, 0, len(ys)),
        out_shape=(shape(depth, D, dtype=jnp.bfloat16), shape(1, rows + 2 * tail)),
        in_specs=[VMEM] * (len(ys) + 3),
        out_specs=(VMEM,) * 2,
        scratch_shapes=lse_scratch(depth, share, width) + [pltpu.VMEM((1, rows), jnp.float32)],
        compiler_params=pltpu.CompilerParams(vmem_limit_bytes=16 << 20),
        cost_estimate=pass_cost(depth - 2 * share, rows),
        name="row_lse_late",
    )(*ys, x, first, mass.reshape(1, -1))


def column_lse(x, y, mass, got, width=512, chunk=512):
    rows, cols = x.shape[0], y.shape[0]
    tail = mass.shape[0] // lax.axis_size("row")
    return pl.pallas_call(
        functools.partial(column_lse_kernel, width, chunk, len(got)),
        out_shape=(shape(1, cols + 2 * tail), shape(rows, cols, dtype=jnp.bfloat16), shape(1, cols), shape(1, rows)),
        in_specs=[VMEM] * (3 + len(got)),
        out_specs=(VMEM,) * 4,
        scratch_shapes=[pltpu.VMEM((rows // 128, 128), jnp.float32)] + lse_scratch(rows, chunk, width),
        compiler_params=pltpu.CompilerParams(vmem_limit_bytes=16 << 20),
        cost_estimate=pass_cost(rows, cols),
        name="column_lse",
    )(x, y, mass.reshape(1, -1), *[part.reshape(1, -1) for part in got])


def pair_of(combine, one, two, cols):
    size = one.shape[-1]
    return pl.pallas_call(
        functools.partial(pair_kernel, cols, combine),
        out_shape=shape(1, size),
        in_specs=[VMEM] * 2,
        out_specs=VMEM,
        compiler_params=pltpu.CompilerParams(vmem_limit_bytes=16 << 20),
        name="pair",
    )(one.reshape(1, size), two.reshape(1, size))


def high_low(value):
    high = value.astype(jnp.bfloat16)
    return high, (value - high.astype(jnp.float32)).astype(jnp.bfloat16)


def column_grad_kernel(width, own, nz, xt_ref, y_ref, e_ref, alpha_ref, first_ref, b_ref, *refs):
    got, (gc_ref, gcs_ref, beta_ref, bb_ref, cb_ref, xa_ref, s_ref, count_ref, acc_ref) = refs[:nz], refs[nz:]
    rows, cols = xt_ref.shape[1], y_ref.shape[0]
    beta_ref[...] = new_beta(first_ref, b_ref, got)
    spread(beta_ref[...], s_ref, bb_ref)
    place = lax.broadcasted_iota(jnp.int32, (128, 512), 0)
    for k in range(rows // 512):
        at = k * 512
        alpha = alpha_ref[:, at:at + 512]
        high, low = high_low(xt_ref[:, at:at + 512].astype(jnp.float32) * alpha)
        first, second = high_low(alpha)
        low = jnp.where(place == 126, first.astype(jnp.float32), low.astype(jnp.float32))
        low = jnp.where(place == 127, second.astype(jnp.float32), low)
        xa_ref[:128, at:at + 512] = high
        xa_ref[128:, at:at + 512] = low.astype(jnp.bfloat16)

    lower = lax.broadcasted_iota(jnp.int32, (128, width), 0) < 126
    for k in range(cols // width):
        at = k * width
        got = jnp.dot(xa_ref[...], e_ref[:, at:at + width], preferred_element_type=jnp.float32)
        acc_ref[:, at:at + width] = got[:128] + jnp.where(lower, got[128:], 0.0)
        count_ref[:, at:at + width] = got[254:255] + got[255:256]
    spread(count_ref[...], s_ref, cb_ref)
    for k in range(cols // 128):
        at = k * 128
        pulled = jnp.transpose(acc_ref[:, at:at + 128])
        whole = cb_ref[at:at + 128, :] * y_ref[at:at + 128, :].astype(jnp.float32)
        grad = 2.0 * bb_ref[at:at + 128, :] * (whole - pulled)
        if at < own:
            gc_ref[at:at + 128, :] = grad
        else:
            gcs_ref[at - own:at - own + 128, :] = grad.astype(jnp.bfloat16)


def column_grad(xt, y, e, alpha, first, mass, got, own, width=512):
    rows, cols = xt.shape[1], y.shape[0]
    return pl.pallas_call(
        functools.partial(column_grad_kernel, width, own, len(got)),
        out_shape=(shape(own, D), shape(cols - own, D, dtype=jnp.bfloat16), shape(1, cols)),
        in_specs=[VMEM] * (6 + len(got)),
        out_specs=(VMEM,) * 3,
        scratch_shapes=[
            pltpu.VMEM((cols, 128), jnp.float32),
            pltpu.VMEM((cols, 128), jnp.float32),
            pltpu.VMEM((256, rows), jnp.bfloat16),
            pltpu.VMEM((cols // 128, 128), jnp.float32),
            pltpu.VMEM((1, cols), jnp.float32),
            pltpu.VMEM((128, cols), jnp.float32),
        ],
        compiler_params=pltpu.CompilerParams(vmem_limit_bytes=16 << 20),
        cost_estimate=pl.CostEstimate(flops=4 * e.size * D, bytes_accessed=2 * e.size, transcendentals=0),
        name="column_grad",
    )(xt, y, e, alpha, first, mass, *[part.reshape(1, -1) for part in got])


def row_block(at, chunk, x_ref, e_ref, yb_ref, scale):
    got = jnp.dot(e_ref[pl.ds(at, chunk), :], yb_ref[...], preferred_element_type=jnp.float32)
    lower = lax.broadcasted_iota(jnp.int32, (chunk, 128), 1) < 126
    total = got[:, 254:255] + got[:, 255:256]
    pulled = got[:, :128] + jnp.where(lower, got[:, 128:], 0.0)
    x = x_ref[pl.ds(at, chunk), :].astype(jnp.float32)
    return 2.0 * scale * (total * x - pulled)


def own_rows_kernel(x_ref, y_ref, e_ref, alpha_ref, beta_ref, gi_ref, yb_ref, sa_ref, ab_ref, sb_ref, bb_ref):
    own, cols = gi_ref.shape[0], y_ref.shape[0]
    spread(alpha_ref[:, :own], sa_ref, ab_ref)
    spread(beta_ref[...], sb_ref, bb_ref)
    place = lax.broadcasted_iota(jnp.int32, (256, 128), 1)
    for k in range(cols // 256):
        at = k * 256
        beta = bb_ref[at:at + 256, :]
        high, low = high_low(y_ref[at:at + 256, :].astype(jnp.float32) * beta)
        first, second = high_low(beta)
        low = jnp.where(place == 126, first.astype(jnp.float32), low.astype(jnp.float32))
        low = jnp.where(place == 127, second.astype(jnp.float32), low)
        yb_ref[at:at + 256, :128] = high
        yb_ref[at:at + 256, 128:] = low.astype(jnp.bfloat16)
    gi_ref[...] = row_block(0, own, x_ref, e_ref, yb_ref, ab_ref[...])


def sent_rows_kernel(chunk, own, x_ref, yb_ref, e_ref, alpha_ref, *refs):
    outs, (sa_ref, ab_ref) = refs[:-2], refs[-2:]
    spread(alpha_ref[...], sa_ref, ab_ref)
    for k, out_ref in enumerate(outs):
        for part in range(own // chunk):
            at = (k + 1) * own + part * chunk
            grad = row_block(at, chunk, x_ref, e_ref, yb_ref, ab_ref[at:at + chunk, :])
            out_ref[part * chunk:(part + 1) * chunk, :] = grad.astype(jnp.bfloat16)


def own_rows(x, y, e, alpha, beta, own):
    rows, cols = x.shape[0], y.shape[0]
    return pl.pallas_call(
        own_rows_kernel,
        out_shape=(shape(own, D), shape(cols, 256, dtype=jnp.bfloat16)),
        in_specs=[VMEM] * 5,
        out_specs=(VMEM,) * 2,
        scratch_shapes=[
            pltpu.VMEM((own // 128, 128), jnp.float32),
            pltpu.VMEM((own, 128), jnp.float32),
            pltpu.VMEM((cols // 128, 128), jnp.float32),
            pltpu.VMEM((cols, 128), jnp.float32),
        ],
        compiler_params=pltpu.CompilerParams(vmem_limit_bytes=16 << 20),
        cost_estimate=pl.CostEstimate(flops=4 * own * cols * D, bytes_accessed=2 * own * cols, transcendentals=0),
        name="own_rows",
    )(x, y, e, alpha, beta)


def sent_rows(x, yb, e, alpha, own):
    rows, cols = x.shape[0], yb.shape[0]
    rest = rows - own
    return pl.pallas_call(
        functools.partial(sent_rows_kernel, math.gcd(own, 512), own),
        out_shape=[shape(own, D, dtype=jnp.bfloat16)] * (rest // own),
        in_specs=[VMEM] * 4,
        out_specs=[VMEM] * (rest // own),
        scratch_shapes=[pltpu.VMEM((rows // 128, 128), jnp.float32), pltpu.VMEM((rows, 128), jnp.float32)],
        compiler_params=pltpu.CompilerParams(vmem_limit_bytes=16 << 20),
        cost_estimate=pl.CostEstimate(flops=4 * rest * cols * D, bytes_accessed=2 * rest * cols, transcendentals=0),
        name="sent_rows",
    )(x, yb, e, alpha)


def shares_kernel(gc_ref, other_ref, own_ref, *outs):
    share = own_ref.shape[0]
    for k in range(len(outs) + 1):
        at = k * share
        total = gc_ref[at:at + share, :] + other_ref[at:at + share, :].astype(jnp.float32)
        if k == 0:
            own_ref[...] = total
        else:
            outs[k - 1][...] = total.astype(jnp.bfloat16)


def shares(gc, other, count):
    share = gc.shape[0] // count
    return pl.pallas_call(
        shares_kernel,
        out_shape=[shape(share, D)] + [shape(share, D, dtype=jnp.bfloat16)] * (count - 1),
        in_specs=[VMEM] * 2,
        out_specs=[VMEM] * count,
        compiler_params=pltpu.CompilerParams(vmem_limit_bytes=16 << 20),
        name="shares",
    )(gc, other)


class Groups:
    def __init__(self, nrow, ncol):
        self.count = nrow * ncol
        self.across = [(a << 1) * ncol + b for a in range(nrow // 2) for b in range(2)]
        self.along = [z << 1 for z in range(ncol // 2)]
        self.core = ncol

    def swap(self, value, mask):
        if mask == 0:
            return value
        return lax.ppermute(value, ("row", "col"), [(i, i ^ mask) for i in range(self.count)])


def local(imu, camera, imu_mass, cam_mass):
    nrow, ncol = lax.axis_size("row"), lax.axis_size("col")
    groups = Groups(nrow, ncol)
    swap, across, along, core = groups.swap, groups.across, groups.along, groups.core
    na, nz = len(across), len(along)
    share_x, share_y = imu.shape[0], camera.shape[1]
    rows, cols = na * share_x, 2 * nz * share_y

    def from_rows(value):
        return [swap(value, mask) for mask in across]

    def from_columns(value):
        return [swap(value, mask) for mask in along]

    near, far = [camera[0]], [swap(camera[0], core)]
    for z in range(1, nz):
        near.append(swap(near[z & (z - 1)], along[z & -z]))
    xs = from_rows(imu)

    x, xt, first = row_lse_early(xs, [near[0], far[0]])
    rest = lax.optimization_barrier((first, *near[1:]))
    far += [swap(part, core) for part in rest[1:]]
    y, sent = row_lse_late(x, [near[0], *rest[1:], *far], rest[0], imu_mass)
    got = from_rows(sent.reshape(-1))

    sent, e, shift, mass_a = column_lse(x, y, cam_mass, got)
    sent = pair_of(lse2, sent, swap(sent.reshape(-1), core), cols)
    got = from_columns(sent.reshape(-1))

    sums, first_beta, mass_b = weighted(first_row_kernel, [rows, cols, cols], e, [shift], got)
    for step in range(1, ITERS):
        if step > 1:
            sums, = weighted(row_kernel, [rows], e, [first_beta, mass_b], got)
        part, alpha = weighted(column_kernel, [cols, rows], e, [mass_a, first_beta], from_rows(sums.reshape(-1)))
        part = pair_of(sum, part, swap(part.reshape(-1), core), cols)
        got = from_columns(part.reshape(-1))

    gc, gc_send, beta = column_grad(xt, y, e, alpha, first_beta, mass_b, got, nz * share_y)
    gi, yb = own_rows(x, y, e, alpha, beta, share_x)
    (grad_cam, *parts), yb = lax.optimization_barrier((shares(gc, swap(gc_send, core), nz), yb))
    parts = [swap(part, along[z + 1]) for z, part in enumerate(parts)]
    sent = sent_rows(x, yb, e, alpha, share_x)
    sent, parts[0] = lax.optimization_barrier((sent, parts[0]))
    for s, part in enumerate(sent):
        gi = gi + swap(part, across[s + 1]).astype(jnp.float32)
    for part in parts:
        grad_cam = grad_cam + part.astype(jnp.float32)
    return gi, grad_cam[None]


def solution(mesh):
    in_specs = (P(("row", "col"), None), P("col", "row", None), P("row"), P("col"))
    out_specs = (P(("row", "col"), None), P("col", "row", None))
    return jax.shard_map(local, mesh=mesh, in_specs=in_specs, out_specs=out_specs, check_vma=False)
```

```python
import functools
import math

import jax
import jax.numpy as jnp
from jax import lax
from jax.experimental import pallas as pl
from jax.experimental.pallas import tpu as pltpu
from jax.sharding import PartitionSpec as P

D = 128
ITERS = 3
EPSILON = D / 20.0
LOG2E = math.log2(math.e)
CROSS = 2.0 * LOG2E / EPSILON
NT = (((1,), (1,)), ((), ()))
VMEM = pl.BlockSpec(memory_space=pltpu.VMEM)
HBM = pl.BlockSpec(memory_space=pltpu.HBM)
GROUP = 32


def spread(value, s_ref, sb_ref):
    chunks = value.shape[1] // 128
    for k in range(chunks):
        s_ref[k:k + 1, :] = value[:, k * 128:(k + 1) * 128]
    turned = jnp.transpose(s_ref[...])
    for k in range(chunks):
        sb_ref[k * 128:(k + 1) * 128, :] = jnp.broadcast_to(turned[:, k:k + 1], (128, 128))


def ordered(values, shifts, parts):
    share = values[0].shape[1] // parts
    return [
        jnp.concatenate([value[:, (k ^ s) * share:((k ^ s) + 1) * share] for k in range(parts)], axis=1)
        for value, s in zip(values, shifts)
    ]


def lse2(parts):
    top = functools.reduce(jnp.maximum, parts)
    return top + jnp.log2(sum(jnp.exp2(part - top) for part in parts))


def pipelined(places, chunk, width, a_ref, b_ref, d_ref, tile, finish):
    last = b_ref.shape[0] // width - 1

    def product(n, m):
        b = b_ref[pl.ds(pl.multiple_of(n * width, width), width), :]
        a = a_ref[places[m]:places[m] + chunk, :]
        d_ref[m % 2] = lax.dot_general(a, b, NT, preferred_element_type=jnp.float32)

    product(0, 0)

    def column(n, _):
        start = pl.multiple_of(n * width, width)
        state = None
        for m in range(len(places)):
            if m + 1 < len(places):
                product(n, m + 1)
            else:
                product(jnp.minimum(n + 1, last), 0)
            state = tile(m, start, state)
        finish(start, state)
        return 0

    lax.fori_loop(0, last + 1, column, 0)


def running_max(places, chunk, width, a_ref, b_ref, sb_ref, o_ref, e_ref, shift_ref):
    def column(n, _):
        start = pl.multiple_of(n * width, width)
        b = b_ref[pl.ds(start, width), :]

        def exponents(at):
            d = lax.dot_general(a_ref[at:at + chunk, :], b, NT, preferred_element_type=jnp.float32)
            s = sb_ref[at:at + chunk, :]
            return [d[:, q * 128:(q + 1) * 128] * CROSS + s for q in range(width // 128)]

        peak, total = jnp.full((1, width), -1e30, jnp.float32), jnp.zeros((1, width), jnp.float32)
        for at in places:
            peaks, totals = [], []
            for q, t in enumerate(exponents(at)):
                old = peak[:, q * 128:(q + 1) * 128]
                new = jnp.maximum(old, jnp.max(t, axis=0, keepdims=True))
                part = jnp.sum(jnp.exp2(t - new), axis=0, keepdims=True)
                peaks.append(new)
                totals.append(total[:, q * 128:(q + 1) * 128] * jnp.exp2(old - new) + part)
            peak, total = jnp.concatenate(peaks, axis=1), jnp.concatenate(totals, axis=1)
        o_ref[:, pl.ds(start, width)] = peak + jnp.log2(total)
        if e_ref is not None:
            shift_ref[:, pl.ds(start, width)] = peak
            for at in places:
                for q, t in enumerate(exponents(at)):
                    place = pl.ds(pl.multiple_of(start + q * 128, 128), 128)
                    e_ref[at:at + chunk, place] = jnp.exp2(t - shift_ref[:, place]).astype(jnp.bfloat16)
        return 0

    lax.fori_loop(0, b_ref.shape[0] // width, column, 0)


def lse_pass(places, chunk, width, a_ref, b_ref, sb_ref, d_ref, top_ref, o_ref, e_ref=None, shift_ref=None):
    tiles = width // 128
    top_ref[...] = jnp.zeros_like(top_ref)

    def lanes_of(start, q):
        return pl.ds(pl.multiple_of(start + q * 128, 128), 128)

    def tile(m, start, state):
        def exponents(g, q):
            at = g * GROUP
            s = sb_ref[places[m] + at:places[m] + at + GROUP, :]
            return d_ref[m % 2, at:at + GROUP, q * 128:(q + 1) * 128] * CROSS + s

        if m == 0:
            tops = [exponents(0, q) for q in range(tiles)]
            for g in range(1, 128 // GROUP):
                tops = [jnp.maximum(top, exponents(g, q)) for q, top in enumerate(tops)]
            state = [(jnp.max(top, axis=0, keepdims=True), jnp.zeros((GROUP, 128), jnp.float32)) for top in tops]
        for g in range(chunk // GROUP):
            for q, (peak, total) in enumerate(state):
                e = jnp.exp2(exponents(g, q) - peak)
                if e_ref is not None:
                    at = places[m] + g * GROUP
                    e_ref[at:at + GROUP, lanes_of(start, q)] = e.astype(jnp.bfloat16)
                state[q] = peak, total + e
        return state

    def finish(start, state):
        for q, (peak, total) in enumerate(state):
            top_ref[...] = jnp.maximum(top_ref[...], total)
            o_ref[:, lanes_of(start, q)] = peak + jnp.log2(jnp.sum(total, axis=0, keepdims=True))
            if e_ref is not None:
                shift_ref[:, lanes_of(start, q)] = peak

    pipelined(places, chunk, width, a_ref, b_ref, d_ref, tile, finish)

    @pl.when(jnp.logical_not(jnp.max(top_ref[...]) < 2.0 ** 60))
    def _():
        running_max(places, chunk, min(width, 256), a_ref, b_ref, sb_ref, o_ref, e_ref, shift_ref)


def pair_copies(o_ref, at, mass_ref, axis, sem):
    share = (o_ref.shape[1] - at) // 2
    place = lax.axis_index(axis)
    copies = []
    for k in range(2):
        start = pl.multiple_of((place ^ k) * share, share)
        there = o_ref.at[:, at + k * share:at + (k + 1) * share]
        copies.append(pltpu.make_async_copy(mass_ref.at[:, pl.ds(start, share)], there, sem.at[k]))
    return copies


def fill(out_ref, own_ref, others, sem):
    share = own_ref.shape[0]
    copy = pltpu.make_async_copy(own_ref, out_ref.at[pl.ds(0, share), :], sem)
    copy.start()
    for k, shard in enumerate(others):
        out_ref[(k + 1) * share:(k + 2) * share, :] = shard[...]
    return copy


def put_norms(places, share, y_ref, sb_ref):
    for at in places:
        y = y_ref[at:at + share, :].astype(jnp.float32)
        total = jnp.sum(y * y, axis=1, keepdims=True) * (-LOG2E / EPSILON)
        sb_ref[at:at + share, :] = jnp.broadcast_to(total, (share, 128))


def row_lse_early_kernel(width, nx, x_own, y_own, *refs):
    xs, y_other, refs = refs[:nx], refs[nx], refs[nx + 1:]
    x_ref, xt_ref, o_ref, y_ref, sb_ref, d_ref, top_ref, sem = refs
    share = y_own.shape[0]
    copies = [fill(x_ref, x_own, xs, sem.at[0]), fill(y_ref, y_own, [y_other], sem.at[1])]
    for copy in copies:
        copy.wait()
    for k in range(x_ref.shape[0] // 128):
        at = k * 128
        xt_ref[:, at:at + 128] = jnp.transpose(x_ref[at:at + 128, :].astype(jnp.float32)).astype(jnp.bfloat16)
    places = [0, share]
    put_norms(places, share, y_ref, sb_ref)
    lse_pass(places, share, width, y_ref, x_ref, sb_ref, d_ref, top_ref, o_ref)


def row_lse_late_kernel(width, ny, y_own, mass_ref, x_ref, first_ref, *refs):
    ys, (y_ref, o_ref, sb_ref, d_ref, top_ref, sum_ref, sem) = refs[:ny], refs[ny:]
    share, rows = y_own.shape[0], x_ref.shape[0]
    copies = [fill(y_ref, y_own, ys, sem.at[2])]
    masses = pair_copies(o_ref, rows, mass_ref, "col", sem)
    for copy in masses:
        copy.start()
    places = [k * share for k in range(ny + 1) if k % ((ny + 1) // 2)]
    put_norms(places, share, y_ref, sb_ref)
    lse_pass(places, share, width, y_ref, x_ref, sb_ref, d_ref, top_ref, sum_ref)
    o_ref[:, :rows] = lse2([first_ref[...], sum_ref[...]])
    for copy in copies + masses:
        copy.wait()


def column_lse_kernel(width, chunk, na, x_ref, y_ref, mass_ref, *refs):
    got, (o_ref, e_ref, shift_ref, a_ref, s_ref, sb_ref, d_ref, top_ref, sem) = refs[:na], refs[na:]
    rows, cols = x_ref.shape[0], y_ref.shape[0]
    masses = pair_copies(o_ref, cols, mass_ref, "row", sem)
    for copy in masses:
        copy.start()
    share = rows // na
    for k in range(na):
        at = rows + (k % 2) * share
        a_ref[:, k * share:(k + 1) * share] = got[k - k % 2][:, at:at + share]
    u = jnp.log2(a_ref[...]) - lse2(ordered([part[:, :rows] for part in got], range(na), na))
    spread(u, s_ref, sb_ref)
    places = list(range(0, rows, chunk))
    lse_pass(places, chunk, width, x_ref, y_ref, sb_ref, d_ref, top_ref, o_ref, e_ref, shift_ref)
    for copy in masses:
        copy.wait()


def pair_kernel(size, shift, parts, combine, one_ref, two_ref, o_ref):
    two, = ordered([two_ref[:, :size]], [shift], parts)
    o_ref[:, :size] = combine([one_ref[:, :size], two])
    if o_ref.shape[1] > size:
        o_ref[:, size:] = one_ref[:, size:]


def split3(value):
    high = value.astype(jnp.bfloat16)
    rest = value - high.astype(jnp.float32)
    mid = rest.astype(jnp.bfloat16)
    return high, mid, (rest - mid.astype(jnp.float32)).astype(jnp.bfloat16)


def stacked(value):
    high, mid, low = [part.astype(jnp.float32) for part in split3(value)]
    dims = (16, value.shape[1])
    place = lax.broadcasted_iota(jnp.int32, dims, 0)
    parts = jnp.where(place == 0, high, jnp.where(place == 1, mid, jnp.where(place == 2, low, 0.0)))
    return parts.astype(jnp.bfloat16)


def row_sums(width, e_ref, w16_ref, o_ref):
    for at in range(0, e_ref.shape[0], width):
        got = lax.dot_general(w16_ref[...], e_ref[at:at + width, :], NT, preferred_element_type=jnp.float32)
        got = jnp.sum(got, axis=0, keepdims=True)
        if len(o_ref.shape) == 2:
            o_ref[:, at:at + width] = got
        else:
            for k in range(o_ref.shape[0]):
                o_ref[k, :, at:at + width] = got


def received(refs):
    if len(refs) == 1 and len(refs[0].shape) == 3:
        place = ((lax.axis_index("row") >> 1) << 1) | (lax.axis_index("col") & 1)
        return [refs[0][place ^ s] for s in range(refs[0].shape[0])]
    return [ref[...] for ref in refs]


def first_row_kernel(width, shifts, parts, e_ref, shift_ref, *refs):
    nz = len(shifts)
    got, (o_ref, beta_ref, b_ref, w16_ref) = refs[:nz], refs[nz:]
    cols = e_ref.shape[1]
    share = cols // parts
    for k in range(parts):
        at = cols + (k // nz) * share
        b_ref[:, k * share:(k + 1) * share] = got[k % nz][:, at:at + share]
    lse = lse2(ordered([part[:, :cols] for part in got], shifts, parts))
    beta_ref[...] = jnp.exp2(jnp.log2(b_ref[...]) - lse + shift_ref[...])
    w16_ref[...] = stacked(beta_ref[...])
    row_sums(width, e_ref, w16_ref, o_ref)


def new_beta(first_ref, b_ref, got, shifts, parts):
    return first_ref[...] * (b_ref[...] / sum(ordered(received(got), shifts, parts)))


def row_kernel(width, shifts, parts, e_ref, first_ref, b_ref, *refs):
    got, (o_ref, w16_ref) = refs[:-2], refs[-2:]
    w16_ref[...] = stacked(new_beta(first_ref, b_ref, got, shifts, parts))
    row_sums(width, e_ref, w16_ref, o_ref)


def column_kernel(width, shifts, parts, e_ref, a_ref, first_ref, *refs):
    got, (o_ref, alpha_ref, w16_ref) = refs[:-3], refs[-3:]
    alpha_ref[...] = a_ref[...] / sum(ordered(received(got), shifts, parts))
    w16_ref[...] = stacked(alpha_ref[...])
    for at in range(0, e_ref.shape[1], width):
        sums = jnp.dot(w16_ref[...], e_ref[:, at:at + width], preferred_element_type=jnp.float32)
        o_ref[:, at:at + width] = first_ref[:, at:at + width] * jnp.sum(sums, axis=0, keepdims=True)


def flat(value):
    return value.reshape(1, -1) if value.ndim == 1 else value


def weighted(kernel, outs, e, rows, got, parts, width=512):
    got, shifts = got
    size = e.shape[0] if kernel is column_kernel else e.shape[1]
    return pl.pallas_call(
        functools.partial(kernel, width, tuple(shifts), parts),
        out_shape=[shape(*dims) for dims in outs],
        in_specs=[VMEM] * (1 + len(rows) + len(got)),
        out_specs=[VMEM] * len(outs),
        scratch_shapes=[pltpu.VMEM((16, size), jnp.bfloat16)],
        compiler_params=pltpu.CompilerParams(vmem_limit_bytes=16 << 20),
        cost_estimate=pl.CostEstimate(flops=2 * e.size, bytes_accessed=2 * e.size, transcendentals=0),
        name="weighted_sum",
    )(e, *rows, *[flat(part) for part in got])


def pass_cost(depth, lanes):
    return pl.CostEstimate(flops=2 * depth * lanes * D, bytes_accessed=2 * D * (depth + lanes), transcendentals=depth * lanes)


def shape(*dims, dtype=jnp.float32):
    return jax.ShapeDtypeStruct(dims, dtype)


def lse_scratch(depth, chunk, width):
    return [
        pltpu.VMEM((depth, 128), jnp.float32),
        pltpu.VMEM((2, chunk, width), jnp.float32),
        pltpu.VMEM((GROUP, 128), jnp.float32),
    ]


def row_lse_early(xs, ys, width=512):
    share_x, share = xs[0].shape[0], ys[0].shape[0]
    rows, depth = len(xs) * share_x, 2 * share
    return pl.pallas_call(
        functools.partial(row_lse_early_kernel, width, len(xs) - 1),
        out_shape=(shape(rows, D, dtype=jnp.bfloat16), shape(D, rows, dtype=jnp.bfloat16), shape(1, rows)),
        in_specs=[HBM] * 2 + [VMEM] * len(xs),
        out_specs=(VMEM,) * 3,
        scratch_shapes=[
            pltpu.VMEM((depth, D), jnp.bfloat16),
            *lse_scratch(depth, share, width),
            pltpu.SemaphoreType.DMA((2,)),
        ],
        compiler_params=pltpu.CompilerParams(vmem_limit_bytes=16 << 20),
        cost_estimate=pass_cost(depth, rows),
        name="row_lse_early",
    )(xs[0], ys[0], *xs[1:], ys[1])


def row_lse_late(x, ys, first, mass, width=512):
    rows, share = x.shape[0], ys[0].shape[0]
    depth = len(ys) * share
    tail = mass.shape[0] // lax.axis_size("col")
    return pl.pallas_call(
        functools.partial(row_lse_late_kernel, width, len(ys) - 1),
        out_shape=(shape(depth, D, dtype=jnp.bfloat16), shape(1, rows + 2 * tail)),
        in_specs=[HBM] * 2 + [VMEM] * (len(ys) + 1),
        out_specs=(VMEM,) * 2,
        scratch_shapes=[
            *lse_scratch(depth, share, width),
            pltpu.VMEM((1, rows), jnp.float32),
            pltpu.SemaphoreType.DMA((3,)),
        ],
        compiler_params=pltpu.CompilerParams(vmem_limit_bytes=16 << 20),
        cost_estimate=pass_cost(depth - 2 * share, rows),
        name="row_lse_late",
    )(ys[0], mass.reshape(1, -1), x, first, *ys[1:])


def column_lse(x, y, mass, got, width=512, chunk=512):
    rows, cols = x.shape[0], y.shape[0]
    tail = mass.shape[0] // lax.axis_size("row")
    return pl.pallas_call(
        functools.partial(column_lse_kernel, width, chunk, len(got)),
        out_shape=(shape(1, cols + 2 * tail), shape(rows, cols, dtype=jnp.bfloat16), shape(1, cols), shape(1, rows)),
        in_specs=[VMEM] * 2 + [HBM] + [VMEM] * len(got),
        out_specs=(VMEM,) * 4,
        scratch_shapes=[
            pltpu.VMEM((rows // 128, 128), jnp.float32),
            *lse_scratch(rows, chunk, width),
            pltpu.SemaphoreType.DMA((2,)),
        ],
        compiler_params=pltpu.CompilerParams(vmem_limit_bytes=16 << 20),
        cost_estimate=pass_cost(rows, cols),
        name="column_lse",
    )(x, y, mass.reshape(1, -1), *[part.reshape(1, -1) for part in got])


def pair_of(combine, one, two, size, shift, parts):
    whole = one.shape[-1]
    return pl.pallas_call(
        functools.partial(pair_kernel, size, shift, parts, combine),
        out_shape=shape(1, whole),
        in_specs=[VMEM] * 2,
        out_specs=VMEM,
        compiler_params=pltpu.CompilerParams(vmem_limit_bytes=16 << 20),
        name="pair",
    )(one.reshape(1, whole), two.reshape(1, whole))


def high_low(value):
    high = value.astype(jnp.bfloat16)
    return high, (value - high.astype(jnp.float32)).astype(jnp.bfloat16)


def column_grad_kernel(width, own, shifts, parts, xt_ref, y_ref, e_ref, alpha_ref, first_ref, b_ref, *refs):
    got, (gc_ref, gcs_ref, beta_ref, bb_ref, cb_ref, xa_ref, s_ref, count_ref, acc_ref) = refs[:-9], refs[-9:]
    rows, cols = xt_ref.shape[1], y_ref.shape[0]
    beta_ref[...] = new_beta(first_ref, b_ref, got, shifts, parts)
    spread(beta_ref[...], s_ref, bb_ref)
    place = lax.broadcasted_iota(jnp.int32, (128, 512), 0)
    for k in range(rows // 512):
        at = k * 512
        alpha = alpha_ref[:, at:at + 512]
        high, low = high_low(xt_ref[:, at:at + 512].astype(jnp.float32) * alpha)
        first, second = high_low(alpha)
        low = jnp.where(place == 126, first.astype(jnp.float32), low.astype(jnp.float32))
        low = jnp.where(place == 127, second.astype(jnp.float32), low)
        xa_ref[:128, at:at + 512] = high
        xa_ref[128:, at:at + 512] = low.astype(jnp.bfloat16)

    lower = lax.broadcasted_iota(jnp.int32, (128, width), 0) < 126
    for k in range(cols // width):
        at = k * width
        got = jnp.dot(xa_ref[...], e_ref[:, at:at + width], preferred_element_type=jnp.float32)
        acc_ref[:, at:at + width] = got[:128] + jnp.where(lower, got[128:], 0.0)
        count_ref[:, at:at + width] = got[254:255] + got[255:256]
    spread(count_ref[...], s_ref, cb_ref)
    for k in range(cols // 128):
        at = k * 128
        pulled = jnp.transpose(acc_ref[:, at:at + 128])
        whole = cb_ref[at:at + 128, :] * y_ref[at:at + 128, :].astype(jnp.float32)
        grad = 2.0 * bb_ref[at:at + 128, :] * (whole - pulled)
        if at < own:
            gc_ref[at:at + 128, :] = grad
        else:
            gcs_ref[at - own:at - own + 128, :] = grad.astype(jnp.bfloat16)


def column_grad(xt, y, e, alpha, first, mass, got, parts, own, width=512):
    rows, cols = xt.shape[1], y.shape[0]
    got, shifts = got
    return pl.pallas_call(
        functools.partial(column_grad_kernel, width, own, tuple(shifts), parts),
        out_shape=(shape(own, D), shape(cols - own, D, dtype=jnp.bfloat16), shape(1, cols)),
        in_specs=[VMEM] * (6 + len(got)),
        out_specs=(VMEM,) * 3,
        scratch_shapes=[
            pltpu.VMEM((cols, 128), jnp.float32),
            pltpu.VMEM((cols, 128), jnp.float32),
            pltpu.VMEM((256, rows), jnp.bfloat16),
            pltpu.VMEM((cols // 128, 128), jnp.float32),
            pltpu.VMEM((1, cols), jnp.float32),
            pltpu.VMEM((128, cols), jnp.float32),
        ],
        compiler_params=pltpu.CompilerParams(vmem_limit_bytes=16 << 20),
        cost_estimate=pl.CostEstimate(flops=4 * e.size * D, bytes_accessed=2 * e.size, transcendentals=0),
        name="column_grad",
    )(xt, y, e, alpha, first, mass, *[flat(part) for part in got])


def row_block(at, chunk, x_ref, e_ref, yb_ref, scale):
    got = jnp.dot(e_ref[pl.ds(at, chunk), :], yb_ref[...], preferred_element_type=jnp.float32)
    lower = lax.broadcasted_iota(jnp.int32, (chunk, 128), 1) < 126
    total = got[:, 254:255] + got[:, 255:256]
    pulled = got[:, :128] + jnp.where(lower, got[:, 128:], 0.0)
    x = x_ref[pl.ds(at, chunk), :].astype(jnp.float32)
    return 2.0 * scale * (total * x - pulled)


def put_yb(y_ref, beta_ref, yb_ref, s_ref, bb_ref):
    spread(beta_ref[...], s_ref, bb_ref)
    place = lax.broadcasted_iota(jnp.int32, (256, 128), 1)
    for at in range(0, y_ref.shape[0], 256):
        beta = bb_ref[at:at + 256, :]
        high, low = high_low(y_ref[at:at + 256, :].astype(jnp.float32) * beta)
        first, second = high_low(beta)
        low = jnp.where(place == 126, first.astype(jnp.float32), low.astype(jnp.float32))
        low = jnp.where(place == 127, second.astype(jnp.float32), low)
        yb_ref[at:at + 256, :128] = high
        yb_ref[at:at + 256, 128:] = low.astype(jnp.bfloat16)


def row_parts(parts, x_ref, e_ref, alpha_ref, yb_ref, outs, sa_ref, ab_ref):
    share = outs[0].shape[0]
    chunk = math.gcd(share, 512)
    for part, out_ref in zip(parts, outs):
        spread(alpha_ref[:, part * share:(part + 1) * share], sa_ref, ab_ref)
        for k in range(0, share, chunk):
            grad = row_block(part * share + k, chunk, x_ref, e_ref, yb_ref, ab_ref[k:k + chunk, :])
            out_ref[k:k + chunk, :] = grad.astype(out_ref.dtype)


def first_rows_kernel(parts, x_ref, y_ref, e_ref, alpha_ref, beta_ref, *refs):
    yb_ref, outs, (s_ref, bb_ref, sa_ref, ab_ref) = refs[0], refs[1:-4], refs[-4:]
    put_yb(y_ref, beta_ref, yb_ref, s_ref, bb_ref)
    row_parts(parts, x_ref, e_ref, alpha_ref, yb_ref, outs, sa_ref, ab_ref)


def rows_kernel(parts, x_ref, yb_ref, e_ref, alpha_ref, *refs):
    row_parts(parts, x_ref, e_ref, alpha_ref, yb_ref, refs[:-2], *refs[-2:])


def rows_scratch(share):
    return [pltpu.VMEM((share // 128, 128), jnp.float32), pltpu.VMEM((share, 128), jnp.float32)]


def rows_cost(share, parts, cols):
    size = share * len(parts) * cols
    return pl.CostEstimate(flops=4 * size * D, bytes_accessed=2 * size, transcendentals=0)


def first_rows(parts, share, x, y, e, alpha, beta):
    cols = y.shape[0]
    return pl.pallas_call(
        functools.partial(first_rows_kernel, parts),
        out_shape=[shape(cols, 256, dtype=jnp.bfloat16)] + [shape(share, D, dtype=jnp.bfloat16)] * len(parts),
        in_specs=[VMEM] * 5,
        out_specs=[VMEM] * (1 + len(parts)),
        scratch_shapes=[
            pltpu.VMEM((cols // 128, 128), jnp.float32),
            pltpu.VMEM((cols, 128), jnp.float32),
            *rows_scratch(share),
        ],
        compiler_params=pltpu.CompilerParams(vmem_limit_bytes=16 << 20),
        cost_estimate=rows_cost(share, parts, cols),
        name="first_rows",
    )(x, y, e, alpha, beta)


def other_rows(parts, share, x, yb, e, alpha, dtype):
    return pl.pallas_call(
        functools.partial(rows_kernel, parts),
        out_shape=[shape(share, D, dtype=dtype)] * len(parts),
        in_specs=[VMEM] * 4,
        out_specs=[VMEM] * len(parts),
        scratch_shapes=rows_scratch(share),
        compiler_params=pltpu.CompilerParams(vmem_limit_bytes=16 << 20),
        cost_estimate=rows_cost(share, parts, yb.shape[0]),
        name="other_rows",
    )(x, yb, e, alpha)


def add_up_kernel(na, *refs):
    ins, outs = refs[:-2], refs[-2:]
    for out_ref, parts in zip(outs, (ins[:na], ins[na:])):
        out_ref[...] = sum(part[...].astype(jnp.float32) for part in parts)


def add_up(rows, columns):
    return pl.pallas_call(
        functools.partial(add_up_kernel, len(rows)),
        out_shape=(shape(*rows[0].shape), shape(*columns[0].shape)),
        in_specs=[VMEM] * (len(rows) + len(columns)),
        out_specs=(VMEM,) * 2,
        compiler_params=pltpu.CompilerParams(vmem_limit_bytes=16 << 20),
        name="add_up",
    )(*rows, *columns)


def shares_kernel(gc_ref, other_ref, own_ref, *outs):
    share = own_ref.shape[0]
    for k in range(len(outs) + 1):
        at = k * share
        total = gc_ref[at:at + share, :] + other_ref[at:at + share, :].astype(jnp.float32)
        if k == 0:
            own_ref[...] = total
        else:
            outs[k - 1][...] = total.astype(jnp.bfloat16)


def shares(gc, other, count):
    share = gc.shape[0] // count
    return pl.pallas_call(
        shares_kernel,
        out_shape=[shape(share, D)] + [shape(share, D, dtype=jnp.bfloat16)] * (count - 1),
        in_specs=[VMEM] * 2,
        out_specs=[VMEM] * count,
        compiler_params=pltpu.CompilerParams(vmem_limit_bytes=16 << 20),
        name="shares",
    )(gc, other)


class Groups:
    def __init__(self, nrow, ncol):
        self.count = nrow * ncol
        self.across = [(a << 1) * ncol + b for a in range(nrow // 2) for b in range(2)]
        self.along = [z << 1 for z in range(ncol // 2)]
        self.core = ncol
        self.squares = [
            [(a * 2 + core) * ncol + z * 2 + b for a in range(nrow // 2) for b in range(2)]
            for core in range(2) for z in range(ncol // 2)
        ]

    def swap(self, value, mask):
        if mask == 0:
            return value
        return lax.ppermute(value, ("row", "col"), [(i, i ^ mask) for i in range(self.count)])


def local(imu, camera, imu_mass, cam_mass):
    nrow, ncol = lax.axis_size("row"), lax.axis_size("col")
    groups = Groups(nrow, ncol)
    swap, across, along, core = groups.swap, groups.across, groups.along, groups.core
    na, nz = len(across), len(along)
    share_x, share_y = imu.shape[0], camera.shape[1]
    rows, cols = na * share_x, 2 * nz * share_y

    def direct(value, masks):
        return [swap(value, mask) for mask in masks], range(len(masks))

    def halved(value, masks, parts):
        size, bit = value.shape[-1], len(masks) // 2
        while bit > 1:
            value = pair_of(sum, value, swap(value.reshape(-1), masks[bit]), size, bit, parts).reshape(-1)
            bit //= 2
        return [value, swap(value, masks[1])], (0, 1)

    near, far = [camera[0]], [swap(camera[0], core)]
    for z in range(1, nz):
        near.append(swap(near[z & (z - 1)], along[z & -z]))
    xs, _ = direct(imu, across)

    x, xt, first = row_lse_early(xs, [near[0], far[0]])
    rest = lax.optimization_barrier((first, *near[1:]))
    far += [swap(part, core) for part in rest[1:]]
    y, sent = row_lse_late(x, [near[0], *rest[1:], *far], rest[0], imu_mass)
    got, _ = direct(sent.reshape(-1), across)

    sent, e, shift, mass_a = column_lse(x, y, cam_mass, got)
    sent = pair_of(lse2, sent, swap(sent.reshape(-1), core), cols, 1, 2)
    got = direct(sent.reshape(-1), along)

    sums, first_beta, mass_b = weighted(
        first_row_kernel, [(na, 1, rows), (1, cols), (1, cols)], e, [shift], got, 2 * nz)
    for step in range(1, ITERS):
        if step == 1:
            got = [lax.all_to_all(sums, ("row", "col"), 0, 0, axis_index_groups=groups.squares)], range(na)
        else:
            sums, = weighted(row_kernel, [(1, rows)], e, [first_beta, mass_b], got, 2 * nz)
            got = halved(sums.reshape(-1), across, na)
        part, alpha = weighted(column_kernel, [(1, cols), (1, rows)], e, [mass_a, first_beta], got, na)
        part = pair_of(sum, part, swap(part.reshape(-1), core), cols, 1, 2).reshape(-1)
        got = halved(part, along, 2 * nz) if step == 1 else direct(part, along)

    gc, gc_send, beta = column_grad(xt, y, e, alpha, first_beta, mass_b, got, 2 * nz, nz * share_y)
    yb, last = first_rows([na - 1], share_x, x, y, e, alpha, beta)
    (grad_cam, *parts), yb = lax.optimization_barrier((shares(gc, swap(gc_send, core), nz), yb))
    parts = [swap(part, along[z + 1]) for z, part in enumerate(parts)]
    sent = [*other_rows(list(range(1, na - 1)), share_x, x, yb, e, alpha, jnp.bfloat16), last]
    sent, parts[0] = lax.optimization_barrier((sent, parts[0]))
    sent = [swap(part, across[s + 1]) for s, part in enumerate(sent)]
    gi, = other_rows([0], share_x, x, yb, e, alpha, jnp.float32)
    grad_imu, grad_cam = add_up([gi, *sent], [grad_cam, *parts])
    return grad_imu, grad_cam[None]


def solution(mesh):
    in_specs = (P(("row", "col"), None), P("col", "row", None), P("row"), P("col"))
    out_specs = (P(("row", "col"), None), P("col", "row", None))
    return jax.shard_map(local, mesh=mesh, in_specs=in_specs, out_specs=out_specs, check_vma=False)
```

```python
import functools
import math

import jax
import jax.numpy as jnp
from jax import lax
from jax.experimental import pallas as pl
from jax.experimental.pallas import tpu as pltpu
from jax.sharding import PartitionSpec as P

D = 128
ITERS = 3
EPSILON = D / 20.0
LOG2E = math.log2(math.e)
CROSS = 2.0 * LOG2E / EPSILON
NT = (((1,), (1,)), ((), ()))
VMEM = pl.BlockSpec(memory_space=pltpu.VMEM)
GROUP = 32
HEAVY = 32


def spread(value, s_ref, sb_ref):
    chunks = value.shape[1] // 128
    for k in range(chunks):
        s_ref[k:k + 1, :] = value[:, k * 128:(k + 1) * 128]
    turned = jnp.transpose(s_ref[...])
    for k in range(chunks):
        sb_ref[k * 128:(k + 1) * 128, :] = jnp.broadcast_to(turned[:, k:k + 1], (128, 128))


def ordered(values, shifts, parts):
    share = values[0].shape[1] // parts
    return [
        jnp.concatenate([value[:, (k ^ s) * share:((k ^ s) + 1) * share] for k in range(parts)], axis=1)
        for value, s in zip(values, shifts)
    ]


def lse2(parts):
    top = functools.reduce(jnp.maximum, parts)
    return top + jnp.log2(sum(jnp.exp2(part - top) for part in parts))


def pipelined(places, chunk, width, a_ref, b_ref, d_ref, tile, finish):
    last = b_ref.shape[0] // width - 1

    def product(n, m):
        b = b_ref[pl.ds(pl.multiple_of(n * width, width), width), :]
        a = a_ref[places[m]:places[m] + chunk, :]
        d_ref[m % 2] = lax.dot_general(a, b, NT, preferred_element_type=jnp.float32)

    product(0, 0)

    def column(n, _):
        start = pl.multiple_of(n * width, width)
        state = None
        for m in range(len(places)):
            if m + 1 < len(places):
                product(n, m + 1)
            else:
                product(jnp.minimum(n + 1, last), 0)
            state = tile(m, start, state)
        finish(start, state)
        return 0

    lax.fori_loop(0, last + 1, column, 0)


def running_max(places, chunk, width, a_ref, b_ref, sb_ref, o_ref, e_ref, shift_ref):
    def column(n, _):
        start = pl.multiple_of(n * width, width)
        b = b_ref[pl.ds(start, width), :]

        def exponents(at):
            d = lax.dot_general(a_ref[at:at + chunk, :], b, NT, preferred_element_type=jnp.float32)
            s = sb_ref[at:at + chunk, :]
            return [d[:, q * 128:(q + 1) * 128] * CROSS + s for q in range(width // 128)]

        peak, total = jnp.full((1, width), -1e30, jnp.float32), jnp.zeros((1, width), jnp.float32)
        for at in places:
            peaks, totals = [], []
            for q, t in enumerate(exponents(at)):
                old = peak[:, q * 128:(q + 1) * 128]
                new = jnp.maximum(old, jnp.max(t, axis=0, keepdims=True))
                part = jnp.sum(jnp.exp2(t - new), axis=0, keepdims=True)
                peaks.append(new)
                totals.append(total[:, q * 128:(q + 1) * 128] * jnp.exp2(old - new) + part)
            peak, total = jnp.concatenate(peaks, axis=1), jnp.concatenate(totals, axis=1)
        o_ref[:, pl.ds(start, width)] = peak + jnp.log2(total)
        if e_ref is not None:
            shift_ref[:, pl.ds(start, width)] = peak
            for at in places:
                for q, t in enumerate(exponents(at)):
                    place = pl.ds(pl.multiple_of(start + q * 128, 128), 128)
                    e_ref[at:at + chunk, place] = jnp.exp2(t - shift_ref[:, place]).astype(jnp.bfloat16)
        return 0

    lax.fori_loop(0, b_ref.shape[0] // width, column, 0)


def lse_pass(places, chunk, width, a_ref, b_ref, sb_ref, d_ref, top_ref, o_ref, e_ref=None, shift_ref=None):
    tiles = width // 128
    top_ref[...] = jnp.zeros_like(top_ref)

    def lanes_of(start, q):
        return pl.ds(pl.multiple_of(start + q * 128, 128), 128)

    def tile(m, start, state):
        def exponents(g, q):
            at = g * GROUP
            s = sb_ref[places[m] + at:places[m] + at + GROUP, :]
            return d_ref[m % 2, at:at + GROUP, q * 128:(q + 1) * 128] * CROSS + s

        if m == 0:
            tops = [exponents(0, q) for q in range(tiles)]
            for g in range(1, 128 // GROUP):
                tops = [jnp.maximum(top, exponents(g, q)) for q, top in enumerate(tops)]
            state = [(jnp.max(top, axis=0, keepdims=True), jnp.zeros((GROUP, 128), jnp.float32)) for top in tops]
        for g in range(chunk // GROUP):
            for q, (peak, total) in enumerate(state):
                e = jnp.exp2(exponents(g, q) - peak)
                if e_ref is not None:
                    at = places[m] + g * GROUP
                    e_ref[at:at + GROUP, lanes_of(start, q)] = e.astype(jnp.bfloat16)
                state[q] = peak, total + e
        return state

    def finish(start, state):
        for q, (peak, total) in enumerate(state):
            top_ref[...] = jnp.maximum(top_ref[...], total)
            o_ref[:, lanes_of(start, q)] = peak + jnp.log2(jnp.sum(total, axis=0, keepdims=True))
            if e_ref is not None:
                shift_ref[:, lanes_of(start, q)] = peak

    pipelined(places, chunk, width, a_ref, b_ref, d_ref, tile, finish)

    @pl.when(jnp.logical_not(jnp.max(top_ref[...]) < 2.0 ** 60))
    def _():
        running_max(places, chunk, min(width, 256), a_ref, b_ref, sb_ref, o_ref, e_ref, shift_ref)


def put_norms(places, share, y_ref, sb_ref):
    for at in places:
        y = y_ref[at:at + share, :].astype(jnp.float32)
        total = jnp.sum(y * y, axis=1, keepdims=True) * (-LOG2E / EPSILON)
        sb_ref[at:at + share, :] = jnp.broadcast_to(total, (share, 128))


def join(out_ref, parts):
    at = 0
    for part in parts:
        out_ref[at:at + part.shape[0], :] = part[...]
        at += part.shape[0]


def row_lse_early_kernel(width, nx, own_ref, *refs):
    xs, y_other, refs = refs[:nx], refs[nx], refs[nx + 1:]
    x_ref, xt_ref, o_ref, y_ref, sb_ref, d_ref, top_ref = refs
    share = y_other.shape[0]
    mine = own_ref.shape[0] - share
    join(x_ref, [own_ref.at[:mine, :], *xs])
    join(y_ref, [own_ref.at[mine:, :], y_other])
    for k in range(x_ref.shape[0] // 128):
        at = k * 128
        xt_ref[:, at:at + 128] = jnp.transpose(x_ref[at:at + 128, :].astype(jnp.float32)).astype(jnp.bfloat16)
    places = [0, share]
    put_norms(places, share, y_ref, sb_ref)
    lse_pass(places, share, width, y_ref, x_ref, sb_ref, d_ref, top_ref, o_ref)


def row_lse_middle_kernel(width, ny, x_ref, first_ref, *refs):
    ys, (o_ref, y_ref, sb_ref, d_ref, top_ref, sum_ref) = refs[:ny], refs[ny:]
    share = ys[0].shape[0]
    join(y_ref, ys)
    places = [k * share for k in range(ny)]
    put_norms(places, share, y_ref, sb_ref)
    lse_pass(places, share, width, y_ref, x_ref, sb_ref, d_ref, top_ref, sum_ref)
    o_ref[...] = lse2([first_ref[...], sum_ref[...]])


def row_lse_late_kernel(width, ny, own_ref, mass_ref, x_ref, first_ref, *refs):
    ys, (y_ref, o_ref, sb_ref, d_ref, top_ref, sum_ref) = refs[:ny], refs[ny:]
    share, rows, half = ys[0].shape[0], x_ref.shape[0], (ny + 1) // 2
    join(y_ref, [own_ref.at[own_ref.shape[0] - share:, :], *ys])
    places = [k * share for k in range(half - 1, 2 * half) if k != half]
    put_norms(places, share, y_ref, sb_ref)
    lse_pass(places, share, width, y_ref, x_ref, sb_ref, d_ref, top_ref, sum_ref)
    o_ref[:, :rows] = lse2([first_ref[...], sum_ref[...]])
    o_ref[:, rows:] = mass_ref[:, :o_ref.shape[1] - rows]


def column_lse_kernel(width, chunk, na, x_ref, y_ref, mass_ref, *refs):
    got, (o_ref, e_ref, shift_ref, a_ref, s_ref, sb_ref, d_ref, top_ref) = refs[:na], refs[na:]
    rows, cols = x_ref.shape[0], y_ref.shape[0]
    o_ref[:, cols:] = mass_ref[:, mass_ref.shape[1] - o_ref.shape[1] + cols:]
    share = rows // na
    for k in range(na):
        at = rows + (k % 2) * share
        a_ref[:, k * share:(k + 1) * share] = got[k - k % 2][:, at:at + share]
    u = jnp.log2(a_ref[...]) - lse2(ordered([part[:, :rows] for part in got], range(na), na))
    spread(u, s_ref, sb_ref)
    places = list(range(0, rows, chunk))
    lse_pass(places, chunk, width, x_ref, y_ref, sb_ref, d_ref, top_ref, o_ref, e_ref, shift_ref)


def pair_kernel(size, shift, parts, combine, one_ref, two_ref, o_ref):
    two, = ordered([two_ref[:, :size]], [shift], parts)
    o_ref[:, :size] = combine([one_ref[:, :size], two])
    if o_ref.shape[1] > size:
        o_ref[:, size:] = one_ref[:, size:]


def split3(value):
    high = value.astype(jnp.bfloat16)
    rest = value - high.astype(jnp.float32)
    mid = rest.astype(jnp.bfloat16)
    return high, mid, (rest - mid.astype(jnp.float32)).astype(jnp.bfloat16)


def stacked(value):
    high, mid, low = [part.astype(jnp.float32) for part in split3(value)]
    dims = (16, value.shape[1])
    place = lax.broadcasted_iota(jnp.int32, dims, 0)
    parts = jnp.where(place == 0, high, jnp.where(place == 1, mid, jnp.where(place == 2, low, 0.0)))
    return parts.astype(jnp.bfloat16)


def row_sums(width, e_ref, w16_ref, o_ref):
    for at in range(0, e_ref.shape[0], width):
        got = lax.dot_general(w16_ref[...], e_ref[at:at + width, :], NT, preferred_element_type=jnp.float32)
        o_ref[:, at:at + width] = jnp.sum(got, axis=0, keepdims=True)


def first_row_kernel(width, shifts, parts, e_ref, shift_ref, *refs):
    nz = len(shifts)
    got, (o_ref, beta_ref, b_ref, w16_ref) = refs[:nz], refs[nz:]
    cols = e_ref.shape[1]
    share = cols // parts
    for k in range(parts):
        at = cols + (k // nz) * share
        b_ref[:, k * share:(k + 1) * share] = got[k % nz][:, at:at + share]
    lse = lse2(ordered([part[:, :cols] for part in got], shifts, parts))
    beta_ref[...] = jnp.exp2(jnp.log2(b_ref[...]) - lse + shift_ref[...])
    w16_ref[...] = stacked(beta_ref[...])
    row_sums(width, e_ref, w16_ref, o_ref)


def new_scale(b_ref, got, shifts, parts):
    return b_ref[...] / sum(ordered([part[...] for part in got], shifts, parts))


def row_kernel(width, shifts, parts, e_ref, first_ref, b_ref, *refs):
    got, (o_ref, w16_ref) = refs[:-2], refs[-2:]
    w16_ref[...] = stacked(first_ref[...] * new_scale(b_ref, got, shifts, parts))
    row_sums(width, e_ref, w16_ref, o_ref)


def column_kernel(width, shifts, parts, e_ref, a_ref, first_ref, *refs):
    got, (o_ref, alpha_ref, w16_ref) = refs[:-3], refs[-3:]
    alpha_ref[...] = a_ref[...] / sum(ordered([part[...] for part in got], shifts, parts))
    w16_ref[...] = stacked(alpha_ref[...])
    for at in range(0, e_ref.shape[1], width):
        sums = jnp.dot(w16_ref[...], e_ref[:, at:at + width], preferred_element_type=jnp.float32)
        o_ref[:, at:at + width] = first_ref[:, at:at + width] * jnp.sum(sums, axis=0, keepdims=True)


def flat(value):
    return value.reshape(1, -1) if value.ndim == 1 else value


def weighted(kernel, outs, e, rows, got, parts, width=512):
    got, shifts = got
    size = e.shape[0] if kernel is column_kernel else e.shape[1]
    return pl.pallas_call(
        functools.partial(kernel, width, tuple(shifts), parts),
        out_shape=[shape(*dims) for dims in outs],
        in_specs=[VMEM] * (1 + len(rows) + len(got)),
        out_specs=[VMEM] * len(outs),
        scratch_shapes=[pltpu.VMEM((16, size), jnp.bfloat16)],
        compiler_params=pltpu.CompilerParams(vmem_limit_bytes=16 << 20),
        cost_estimate=pl.CostEstimate(flops=2 * e.size, bytes_accessed=2 * e.size, transcendentals=0),
        name="weighted_sum",
    )(e, *rows, *[flat(part) for part in got])


def pass_cost(depth, lanes):
    return pl.CostEstimate(flops=2 * depth * lanes * D, bytes_accessed=2 * D * (depth + lanes), transcendentals=depth * lanes)


def shape(*dims, dtype=jnp.float32):
    return jax.ShapeDtypeStruct(dims, dtype)


def lse_scratch(depth, chunk, width):
    return [
        pltpu.VMEM((depth, 128), jnp.float32),
        pltpu.VMEM((2, chunk, width), jnp.float32),
        pltpu.VMEM((GROUP, 128), jnp.float32),
    ]


def row_lse_early(own, xs, y_other, width=512):
    share = y_other.shape[0]
    rows, depth = own.shape[0] - share + sum(part.shape[0] for part in xs), 2 * share
    return pl.pallas_call(
        functools.partial(row_lse_early_kernel, width, len(xs)),
        out_shape=(shape(rows, D, dtype=jnp.bfloat16), shape(D, rows, dtype=jnp.bfloat16), shape(1, rows)),
        in_specs=[VMEM] * (len(xs) + 2),
        out_specs=(VMEM,) * 3,
        scratch_shapes=[pltpu.VMEM((depth, D), jnp.bfloat16), *lse_scratch(depth, share, width)],
        compiler_params=pltpu.CompilerParams(vmem_limit_bytes=16 << 20),
        cost_estimate=pass_cost(depth, rows),
        name="row_lse_early",
    )(own, *xs, y_other)


def row_lse_middle(x, ys, first, width=512):
    rows, share = x.shape[0], ys[0].shape[0]
    depth = len(ys) * share
    return pl.pallas_call(
        functools.partial(row_lse_middle_kernel, width, len(ys)),
        out_shape=shape(1, rows),
        in_specs=[VMEM] * (len(ys) + 2),
        out_specs=VMEM,
        scratch_shapes=[
            pltpu.VMEM((depth, D), jnp.bfloat16),
            *lse_scratch(depth, share, width),
            pltpu.VMEM((1, rows), jnp.float32),
        ],
        compiler_params=pltpu.CompilerParams(vmem_limit_bytes=16 << 20),
        cost_estimate=pass_cost(depth, rows),
        name="row_lse_middle",
    )(x, first, *ys)


def row_lse_late(own, x, ys, first, mass, tail, width=512):
    rows, share = x.shape[0], ys[0].shape[0]
    depth = (len(ys) + 1) * share
    return pl.pallas_call(
        functools.partial(row_lse_late_kernel, width, len(ys)),
        out_shape=(shape(depth, D, dtype=jnp.bfloat16), shape(1, rows + tail)),
        in_specs=[VMEM] * (len(ys) + 4),
        out_specs=(VMEM,) * 2,
        scratch_shapes=[*lse_scratch(depth, share, width), pltpu.VMEM((1, rows), jnp.float32)],
        compiler_params=pltpu.CompilerParams(vmem_limit_bytes=16 << 20),
        cost_estimate=pass_cost(depth // 2, rows),
        name="row_lse_late",
    )(own, mass.reshape(1, -1), x, first, *ys)


def column_lse(x, y, mass, tail, got, width=512, chunk=512):
    rows, cols = x.shape[0], y.shape[0]
    return pl.pallas_call(
        functools.partial(column_lse_kernel, width, chunk, len(got)),
        out_shape=(shape(1, cols + tail), shape(rows, cols, dtype=jnp.bfloat16), shape(1, cols), shape(1, rows)),
        in_specs=[VMEM] * (3 + len(got)),
        out_specs=(VMEM,) * 4,
        scratch_shapes=[pltpu.VMEM((rows // 128, 128), jnp.float32), *lse_scratch(rows, chunk, width)],
        compiler_params=pltpu.CompilerParams(vmem_limit_bytes=16 << 20),
        cost_estimate=pass_cost(rows, cols),
        name="column_lse",
    )(x, y, mass.reshape(1, -1), *[part.reshape(1, -1) for part in got])


def pair_of(combine, one, two, size, shift, parts):
    whole = one.shape[-1]
    return pl.pallas_call(
        functools.partial(pair_kernel, size, shift, parts, combine),
        out_shape=shape(1, whole),
        in_specs=[VMEM] * 2,
        out_specs=VMEM,
        compiler_params=pltpu.CompilerParams(vmem_limit_bytes=16 << 20),
        name="pair",
    )(one.reshape(1, whole), two.reshape(1, whole))


def high_low(value):
    high = value.astype(jnp.bfloat16)
    return high, (value - high.astype(jnp.float32)).astype(jnp.bfloat16)


def column_grad_kernel(width, xt_ref, y_ref, e_ref, alpha_ref, first_ref, own_ref, sent_ref,
                       bb_ref, cb_ref, xa_ref, s_ref, count_ref, acc_ref):
    rows, cols = xt_ref.shape[1], y_ref.shape[0]
    own = own_ref.shape[0]
    spread(first_ref[...], s_ref, bb_ref)
    place = lax.broadcasted_iota(jnp.int32, (128, 512), 0)
    for at in range(0, rows, 512):
        alpha = alpha_ref[:, at:at + 512]
        high, low = high_low(xt_ref[:, at:at + 512].astype(jnp.float32) * alpha)
        first, second = high_low(alpha)
        low = jnp.where(place == 126, first.astype(jnp.float32), low.astype(jnp.float32))
        low = jnp.where(place == 127, second.astype(jnp.float32), low)
        xa_ref[:128, at:at + 512] = high
        xa_ref[128:, at:at + 512] = low.astype(jnp.bfloat16)

    lower = lax.broadcasted_iota(jnp.int32, (128, width), 0) < 126
    for at in range(0, cols, width):
        got = jnp.dot(xa_ref[...], e_ref[:, at:at + width], preferred_element_type=jnp.float32)
        acc_ref[:, at:at + width] = got[:128] + jnp.where(lower, got[128:], 0.0)
        count_ref[:, at:at + width] = got[254:255] + got[255:256]
    spread(count_ref[...], s_ref, cb_ref)
    for at in range(0, cols, 128):
        pulled = jnp.transpose(acc_ref[:, at:at + 128])
        whole = cb_ref[at:at + 128, :] * y_ref[at:at + 128, :].astype(jnp.float32)
        grad = bb_ref[at:at + 128, :] * (whole - pulled)
        if at < own:
            own_ref[at:at + 128, :] = grad
        else:
            sent_ref[at - own:at - own + 128, :] = grad.astype(jnp.bfloat16)


def column_grad(xt, y, e, alpha, first, own, width=512):
    rows, cols = xt.shape[1], y.shape[0]
    return pl.pallas_call(
        functools.partial(column_grad_kernel, width),
        out_shape=(shape(own, D), shape(cols - own, D, dtype=jnp.bfloat16)),
        in_specs=[VMEM] * 5,
        out_specs=(VMEM,) * 2,
        scratch_shapes=[
            pltpu.VMEM((cols, 128), jnp.float32),
            pltpu.VMEM((cols, 128), jnp.float32),
            pltpu.VMEM((256, rows), jnp.bfloat16),
            pltpu.VMEM((cols // 128, 128), jnp.float32),
            pltpu.VMEM((1, cols), jnp.float32),
            pltpu.VMEM((128, cols), jnp.float32),
        ],
        compiler_params=pltpu.CompilerParams(vmem_limit_bytes=16 << 20),
        cost_estimate=pl.CostEstimate(flops=4 * e.size * D, bytes_accessed=2 * e.size, transcendentals=0),
        name="column_grad",
    )(xt, y, e, alpha, first)


def row_block(at, chunk, x_ref, e_ref, yb_ref, scale):
    got = jnp.dot(e_ref[pl.ds(at, chunk), :], yb_ref[...], preferred_element_type=jnp.float32)
    lower = lax.broadcasted_iota(jnp.int32, (chunk, 128), 1) < 126
    total = got[:, 254:255] + got[:, 255:256]
    pulled = got[:, :128] + jnp.where(lower, got[:, 128:], 0.0)
    x = x_ref[pl.ds(at, chunk), :].astype(jnp.float32)
    return 2.0 * scale * (total * x - pulled)


def put_yb(y_ref, beta, yb_ref, s_ref, bb_ref):
    spread(beta, s_ref, bb_ref)
    place = lax.broadcasted_iota(jnp.int32, (256, 128), 1)
    for at in range(0, y_ref.shape[0], 256):
        beta = bb_ref[at:at + 256, :]
        high, low = high_low(y_ref[at:at + 256, :].astype(jnp.float32) * beta)
        first, second = high_low(beta)
        low = jnp.where(place == 126, first.astype(jnp.float32), low.astype(jnp.float32))
        low = jnp.where(place == 127, second.astype(jnp.float32), low)
        yb_ref[at:at + 256, :128] = high
        yb_ref[at:at + 256, 128:] = low.astype(jnp.bfloat16)


def row_parts(parts, x_ref, e_ref, alpha_ref, yb_ref, outs, sa_ref, ab_ref):
    share = outs[0].shape[0]
    chunk = math.gcd(share, 512)
    for part, out_ref in zip(parts, outs):
        spread(alpha_ref[:, part * share:(part + 1) * share], sa_ref, ab_ref)
        for k in range(0, share, chunk):
            grad = row_block(part * share + k, chunk, x_ref, e_ref, yb_ref, ab_ref[k:k + chunk, :])
            out_ref[k:k + chunk, :] = grad.astype(out_ref.dtype)


def first_rows_kernel(parts, shifts, blocks, nz, x_ref, y_ref, e_ref, alpha_ref, first_ref, b_ref, *refs):
    got, (yb_ref, scale_ref, *outs), (s_ref, bb_ref, sa_ref, ab_ref) = refs[:nz], refs[nz:-4], refs[-4:]
    scale = new_scale(b_ref, got, shifts, blocks)
    scale_ref[...] = scale[:, :scale_ref.shape[1]]
    put_yb(y_ref, first_ref[...] * scale, yb_ref, s_ref, bb_ref)
    row_parts(parts, x_ref, e_ref, alpha_ref, yb_ref, outs, sa_ref, ab_ref)


def rows_kernel(parts, x_ref, yb_ref, e_ref, alpha_ref, *refs):
    row_parts(parts, x_ref, e_ref, alpha_ref, yb_ref, refs[:-2], *refs[-2:])


def rows_scratch(share):
    return [pltpu.VMEM((share // 128, 128), jnp.float32), pltpu.VMEM((share, 128), jnp.float32)]


def rows_cost(share, parts, cols):
    size = share * len(parts) * cols
    return pl.CostEstimate(flops=4 * size * D, bytes_accessed=2 * size, transcendentals=0)


def first_rows(parts, share, x, y, e, alpha, first, mass, got, blocks):
    cols = y.shape[0]
    got, shifts = got
    return pl.pallas_call(
        functools.partial(first_rows_kernel, parts, tuple(shifts), blocks, len(got)),
        out_shape=[shape(cols, 256, dtype=jnp.bfloat16), shape(1, cols // blocks)]
        + [shape(share, D, dtype=jnp.bfloat16)] * len(parts),
        in_specs=[VMEM] * (6 + len(got)),
        out_specs=[VMEM] * (2 + len(parts)),
        scratch_shapes=[
            pltpu.VMEM((cols // 128, 128), jnp.float32),
            pltpu.VMEM((cols, 128), jnp.float32),
            *rows_scratch(share),
        ],
        compiler_params=pltpu.CompilerParams(vmem_limit_bytes=16 << 20),
        cost_estimate=rows_cost(share * HEAVY, parts, cols),
        name="first_rows",
    )(x, y, e, alpha, first, mass, *[flat(part) for part in got])


def other_rows(parts, share, x, yb, e, alpha, dtype):
    return pl.pallas_call(
        functools.partial(rows_kernel, parts),
        out_shape=[shape(share, D, dtype=dtype)] * len(parts),
        in_specs=[VMEM] * 4,
        out_specs=[VMEM] * len(parts),
        scratch_shapes=rows_scratch(share),
        compiler_params=pltpu.CompilerParams(vmem_limit_bytes=16 << 20),
        cost_estimate=rows_cost(share, parts, yb.shape[0]),
        name="other_rows",
    )(x, yb, e, alpha)


def add_up_kernel(na, scale_ref, *refs):
    ins, (rows_ref, cols_ref, s_ref, sb_ref) = refs[:-4], refs[-4:]
    rows_ref[...] = sum(part[...].astype(jnp.float32) for part in ins[:na])
    spread(scale_ref[...], s_ref, sb_ref)
    cols_ref[...] = 2.0 * sb_ref[...] * sum(part[...].astype(jnp.float32) for part in ins[na:])


def add_up(rows, columns, scale):
    share = scale.shape[1]
    return pl.pallas_call(
        functools.partial(add_up_kernel, len(rows)),
        out_shape=(shape(*rows[0].shape), shape(*columns[0].shape)),
        in_specs=[VMEM] * (1 + len(rows) + len(columns)),
        out_specs=(VMEM,) * 2,
        scratch_shapes=rows_scratch(share),
        compiler_params=pltpu.CompilerParams(vmem_limit_bytes=16 << 20),
        name="add_up",
    )(scale, *rows, *columns)


def shares_kernel(gc_ref, other_ref, own_ref, *outs):
    share = own_ref.shape[0]
    for k in range(len(outs) + 1):
        at = k * share
        total = gc_ref[at:at + share, :] + other_ref[at:at + share, :].astype(jnp.float32)
        if k == 0:
            own_ref[...] = total
        else:
            outs[k - 1][...] = total.astype(jnp.bfloat16)


def shares(gc, other, count):
    share = gc.shape[0] // count
    return pl.pallas_call(
        shares_kernel,
        out_shape=[shape(share, D)] + [shape(share, D, dtype=jnp.bfloat16)] * (count - 1),
        in_specs=[VMEM] * 2,
        out_specs=[VMEM] * count,
        compiler_params=pltpu.CompilerParams(vmem_limit_bytes=16 << 20),
        name="shares",
    )(gc, other)


class Groups:
    def __init__(self, nrow, ncol):
        self.count = nrow * ncol
        self.across = [(a << 1) * ncol + b for a in range(nrow // 2) for b in range(2)]
        self.along = [z << 1 for z in range(ncol // 2)]
        self.core = ncol

    def swap(self, value, mask):
        if mask == 0:
            return value
        return lax.ppermute(value, ("row", "col"), [(i, i ^ mask) for i in range(self.count)])


def local(imu, camera, imu_mass, cam_mass):
    nrow, ncol = lax.axis_size("row"), lax.axis_size("col")
    groups = Groups(nrow, ncol)
    swap, across, along, core = groups.swap, groups.across, groups.along, groups.core
    na, nz = len(across), len(along)
    share_x, share_y = imu.shape[0], camera.shape[1]
    rows, cols = na * share_x, 2 * nz * share_y

    def direct(value, masks):
        return [swap(value, mask) for mask in masks], range(len(masks))

    near, far = [camera[0]], [swap(camera[0], core)]
    for z in range(1, nz):
        near.append(swap(near[z & (z - 1)], along[z & -z]))
    xs, _ = direct(imu, across)

    def pair(mass, place, share):
        return [lax.dynamic_slice_in_dim(mass, (place ^ k) * share, share, 0) for k in range(2)]

    own = jnp.concatenate([imu, camera[0]])
    row, col = lax.axis_index("row"), lax.axis_index("col")
    mass = jnp.concatenate(pair(imu_mass, col, share_x) + pair(cam_mass, row, share_y))

    x, xt, first = row_lse_early(own, xs[1:], far[0])
    first, *middle = lax.optimization_barrier((first, *near[1:-1]))
    far += [swap(part, core) for part in middle]
    first = row_lse_middle(x, middle, first)
    first, last = lax.optimization_barrier((first, near[-1]))
    far.append(swap(last, core))
    y, sent = row_lse_late(own, x, [*middle, last, *far], first, mass, 2 * share_x)
    got, _ = direct(sent.reshape(-1), across)

    sent, e, shift, mass_a = column_lse(x, y, mass, 2 * share_y, got)
    sent = pair_of(lse2, sent, swap(sent.reshape(-1), core), cols, 1, 2)
    got = direct(sent.reshape(-1), along)

    sums, first_beta, mass_b = weighted(
        first_row_kernel, [(1, rows), (1, cols), (1, cols)], e, [shift], got, 2 * nz)
    for step in range(1, ITERS):
        if step > 1:
            sums, = weighted(row_kernel, [(1, rows)], e, [first_beta, mass_b], got, 2 * nz)
        got = direct(sums.reshape(-1), across)
        part, alpha = weighted(column_kernel, [(1, cols), (1, rows)], e, [mass_a, first_beta], got, na)
        part = pair_of(sum, part, swap(part.reshape(-1), core), cols, 1, 2)
        part, alpha = lax.optimization_barrier((part, alpha))
        got = direct(part.reshape(-1), along)

    gc, gc_send = column_grad(xt, y, e, alpha, first_beta, nz * share_y)
    yb, scale, last = first_rows([na - 1], share_x, x, y, e, alpha, first_beta, mass_b, got, 2 * nz)
    (grad_cam, *parts), yb = lax.optimization_barrier((shares(gc, swap(gc_send, core), nz), yb))
    parts = [swap(part, along[z + 1]) for z, part in enumerate(parts)]
    sent = [*other_rows(list(range(1, na - 1)), share_x, x, yb, e, alpha, jnp.bfloat16), last]
    sent, parts[0] = lax.optimization_barrier((sent, parts[0]))
    sent = [swap(part, across[s + 1]) for s, part in enumerate(sent)]
    gi, = other_rows([0], share_x, x, yb, e, alpha, jnp.float32)
    grad_imu, grad_cam = add_up([gi, *sent], [grad_cam, *parts], scale)
    return grad_imu, grad_cam[None]


def solution(mesh):
    in_specs = (P(("row", "col"), None), P("col", "row", None), P("row"), P("col"))
    out_specs = (P(("row", "col"), None), P("col", "row", None))
    return jax.shard_map(local, mesh=mesh, in_specs=in_specs, out_specs=out_specs, check_vma=False)
```

```python
import functools
import math

import jax
import jax.numpy as jnp
from jax import lax
from jax.experimental import pallas as pl
from jax.experimental.pallas import tpu as pltpu
from jax.sharding import PartitionSpec as P

D = 128
ITERS = 3
EPSILON = D / 20.0
LOG2E = math.log2(math.e)
CROSS = 2.0 * LOG2E / EPSILON
NT = (((1,), (1,)), ((), ()))
VMEM = pl.BlockSpec(memory_space=pltpu.VMEM)
GROUP = 32
HEAVY = 32


def spread(value, s_ref, sb_ref):
    chunks = value.shape[1] // 128
    for k in range(chunks):
        s_ref[k:k + 1, :] = value[:, k * 128:(k + 1) * 128]
    turned = jnp.transpose(s_ref[...])
    for k in range(chunks):
        sb_ref[k * 128:(k + 1) * 128, :] = jnp.broadcast_to(turned[:, k:k + 1], (128, 128))


def ordered(values, shifts, parts):
    share = values[0].shape[1] // parts
    return [
        jnp.concatenate([value[:, (k ^ s) * share:((k ^ s) + 1) * share] for k in range(parts)], axis=1)
        for value, s in zip(values, shifts)
    ]


def lse2(parts):
    top = functools.reduce(jnp.maximum, parts)
    return top + jnp.log2(sum(jnp.exp2(part - top) for part in parts))


def pipelined(places, chunk, width, a_ref, b_ref, d_ref, tile, finish):
    last = b_ref.shape[0] // width - 1

    def product(n, m):
        b = b_ref[pl.ds(pl.multiple_of(n * width, width), width), :]
        a = a_ref[places[m]:places[m] + chunk, :]
        d_ref[m % 2] = lax.dot_general(a, b, NT, preferred_element_type=jnp.float32)

    product(0, 0)

    def column(n, _):
        start = pl.multiple_of(n * width, width)
        state = None
        for m in range(len(places)):
            if m + 1 < len(places):
                product(n, m + 1)
            else:
                product(jnp.minimum(n + 1, last), 0)
            state = tile(m, start, state)
        finish(start, state)
        return 0

    lax.fori_loop(0, last + 1, column, 0)


def running_max(places, chunk, width, a_ref, b_ref, sb_ref, o_ref, e_ref, shift_ref):
    def column(n, _):
        start = pl.multiple_of(n * width, width)
        b = b_ref[pl.ds(start, width), :]

        def exponents(at):
            d = lax.dot_general(a_ref[at:at + chunk, :], b, NT, preferred_element_type=jnp.float32)
            s = sb_ref[at:at + chunk, :]
            return [d[:, q * 128:(q + 1) * 128] * CROSS + s for q in range(width // 128)]

        peak, total = jnp.full((1, width), -1e30, jnp.float32), jnp.zeros((1, width), jnp.float32)
        for at in places:
            peaks, totals = [], []
            for q, t in enumerate(exponents(at)):
                old = peak[:, q * 128:(q + 1) * 128]
                new = jnp.maximum(old, jnp.max(t, axis=0, keepdims=True))
                part = jnp.sum(jnp.exp2(t - new), axis=0, keepdims=True)
                peaks.append(new)
                totals.append(total[:, q * 128:(q + 1) * 128] * jnp.exp2(old - new) + part)
            peak, total = jnp.concatenate(peaks, axis=1), jnp.concatenate(totals, axis=1)
        o_ref[:, pl.ds(start, width)] = peak + jnp.log2(total)
        if e_ref is not None:
            shift_ref[:, pl.ds(start, width)] = peak
            for at in places:
                for q, t in enumerate(exponents(at)):
                    place = pl.ds(pl.multiple_of(start + q * 128, 128), 128)
                    e_ref[at:at + chunk, place] = jnp.exp2(t - shift_ref[:, place]).astype(jnp.bfloat16)
        return 0

    lax.fori_loop(0, b_ref.shape[0] // width, column, 0)


def lse_pass(places, chunk, width, a_ref, b_ref, sb_ref, d_ref, top_ref, o_ref, e_ref=None, shift_ref=None):
    tiles = width // 128
    top_ref[...] = jnp.zeros_like(top_ref)

    def lanes_of(start, q):
        return pl.ds(pl.multiple_of(start + q * 128, 128), 128)

    def tile(m, start, state):
        def exponents(g, q):
            at = g * GROUP
            s = sb_ref[places[m] + at:places[m] + at + GROUP, :]
            return d_ref[m % 2, at:at + GROUP, q * 128:(q + 1) * 128] * CROSS + s

        if m == 0:
            tops = [exponents(0, q) for q in range(tiles)]
            for g in range(1, 128 // GROUP):
                tops = [jnp.maximum(top, exponents(g, q)) for q, top in enumerate(tops)]
            state = [(jnp.max(top, axis=0, keepdims=True), jnp.zeros((GROUP, 128), jnp.float32)) for top in tops]
        for g in range(chunk // GROUP):
            for q, (peak, total) in enumerate(state):
                e = jnp.exp2(exponents(g, q) - peak)
                if e_ref is not None:
                    at = places[m] + g * GROUP
                    e_ref[at:at + GROUP, lanes_of(start, q)] = e.astype(jnp.bfloat16)
                state[q] = peak, total + e
        return state

    def finish(start, state):
        for q, (peak, total) in enumerate(state):
            top_ref[...] = jnp.maximum(top_ref[...], total)
            o_ref[:, lanes_of(start, q)] = peak + jnp.log2(jnp.sum(total, axis=0, keepdims=True))
            if e_ref is not None:
                shift_ref[:, lanes_of(start, q)] = peak

    pipelined(places, chunk, width, a_ref, b_ref, d_ref, tile, finish)

    @pl.when(jnp.logical_not(jnp.max(top_ref[...]) < 2.0 ** 60))
    def _():
        running_max(places, chunk, min(width, 256), a_ref, b_ref, sb_ref, o_ref, e_ref, shift_ref)


def put_norms(places, share, y_ref, sb_ref):
    for at in places:
        y = y_ref[at:at + share, :].astype(jnp.float32)
        total = jnp.sum(y * y, axis=1, keepdims=True) * (-LOG2E / EPSILON)
        sb_ref[at:at + share, :] = jnp.broadcast_to(total, (share, 128))


def join(out_ref, parts):
    at = 0
    for part in parts:
        out_ref[at:at + part.shape[0], :] = part[...]
        at += part.shape[0]


def row_lse_early_kernel(width, nx, own_ref, *refs):
    xs, y_other, refs = refs[:nx], refs[nx], refs[nx + 1:]
    x_ref, xt_ref, o_ref, y_ref, sb_ref, d_ref, top_ref = refs
    share = y_other.shape[0]
    mine = own_ref.shape[0] - share
    join(x_ref, [own_ref.at[:mine, :], *xs])
    join(y_ref, [own_ref.at[mine:, :], y_other])
    for k in range(x_ref.shape[0] // 128):
        at = k * 128
        xt_ref[:, at:at + 128] = jnp.transpose(x_ref[at:at + 128, :].astype(jnp.float32)).astype(jnp.bfloat16)
    places = [0, share]
    put_norms(places, share, y_ref, sb_ref)
    lse_pass(places, share, width, y_ref, x_ref, sb_ref, d_ref, top_ref, o_ref)


def row_lse_middle_kernel(width, ny, x_ref, first_ref, *refs):
    ys, (o_ref, y_ref, sb_ref, d_ref, top_ref, sum_ref) = refs[:ny], refs[ny:]
    share = ys[0].shape[0]
    join(y_ref, ys)
    places = [k * share for k in range(ny)]
    put_norms(places, share, y_ref, sb_ref)
    lse_pass(places, share, width, y_ref, x_ref, sb_ref, d_ref, top_ref, sum_ref)
    o_ref[...] = lse2([first_ref[...], sum_ref[...]])


def row_lse_late_kernel(width, ny, own_ref, mass_ref, x_ref, first_ref, *refs):
    ys, (y_ref, o_ref, sb_ref, d_ref, top_ref, sum_ref) = refs[:ny], refs[ny:]
    share, rows, half = ys[0].shape[0], x_ref.shape[0], (ny + 1) // 2
    join(y_ref, [own_ref.at[own_ref.shape[0] - share:, :], *ys])
    places = [k * share for k in range(half - 1, 2 * half) if k != half]
    put_norms(places, share, y_ref, sb_ref)
    lse_pass(places, share, width, y_ref, x_ref, sb_ref, d_ref, top_ref, sum_ref)
    o_ref[:, :rows] = lse2([first_ref[...], sum_ref[...]])
    o_ref[:, rows:] = mass_ref[:, :o_ref.shape[1] - rows]


def column_lse_kernel(width, chunk, na, x_ref, y_ref, mass_ref, *refs):
    got, (o_ref, e_ref, shift_ref, a_ref, s_ref, sb_ref, d_ref, top_ref) = refs[:na], refs[na:]
    rows, cols = x_ref.shape[0], y_ref.shape[0]
    o_ref[:, cols:] = mass_ref[:, mass_ref.shape[1] - o_ref.shape[1] + cols:]
    share = rows // na
    for k in range(na):
        at = rows + (k % 2) * share
        a_ref[:, k * share:(k + 1) * share] = got[k - k % 2][:, at:at + share]
    u = jnp.log2(a_ref[...]) - lse2(ordered([part[:, :rows] for part in got], range(na), na))
    spread(u, s_ref, sb_ref)
    places = list(range(0, rows, chunk))
    lse_pass(places, chunk, width, x_ref, y_ref, sb_ref, d_ref, top_ref, o_ref, e_ref, shift_ref)


def pair_kernel(size, shift, parts, combine, one_ref, two_ref, o_ref):
    two, = ordered([two_ref[:, :size]], [shift], parts)
    o_ref[:, :size] = combine([one_ref[:, :size], two])
    if o_ref.shape[1] > size:
        o_ref[:, size:] = one_ref[:, size:]


def split3(value):
    high = value.astype(jnp.bfloat16)
    rest = value - high.astype(jnp.float32)
    mid = rest.astype(jnp.bfloat16)
    return high, mid, (rest - mid.astype(jnp.float32)).astype(jnp.bfloat16)


def stacked(value):
    high, mid, low = [part.astype(jnp.float32) for part in split3(value)]
    dims = (16, value.shape[1])
    place = lax.broadcasted_iota(jnp.int32, dims, 0)
    parts = jnp.where(place == 0, high, jnp.where(place == 1, mid, jnp.where(place == 2, low, 0.0)))
    return parts.astype(jnp.bfloat16)


def row_sums(width, e_ref, w16_ref, o_ref):
    for at in range(0, e_ref.shape[0], width):
        got = lax.dot_general(w16_ref[...], e_ref[at:at + width, :], NT, preferred_element_type=jnp.float32)
        o_ref[:, at:at + width] = jnp.sum(got, axis=0, keepdims=True)


def first_row_kernel(width, shifts, parts, e_ref, shift_ref, *refs):
    nz = len(shifts)
    got, (o_ref, beta_ref, b_ref, w16_ref) = refs[:nz], refs[nz:]
    cols = e_ref.shape[1]
    share = cols // parts
    for k in range(parts):
        at = cols + (k // nz) * share
        b_ref[:, k * share:(k + 1) * share] = got[k % nz][:, at:at + share]
    lse = lse2(ordered([part[:, :cols] for part in got], shifts, parts))
    beta_ref[...] = jnp.exp2(jnp.log2(b_ref[...]) - lse + shift_ref[...])
    w16_ref[...] = stacked(beta_ref[...])
    row_sums(width, e_ref, w16_ref, o_ref)


def new_scale(b_ref, got, shifts, parts):
    return b_ref[...] / sum(ordered([part[...] for part in got], shifts, parts))


def row_kernel(width, shifts, parts, e_ref, first_ref, b_ref, *refs):
    got, (o_ref, w16_ref) = refs[:-2], refs[-2:]
    w16_ref[...] = stacked(first_ref[...] * new_scale(b_ref, got, shifts, parts))
    row_sums(width, e_ref, w16_ref, o_ref)


def column_kernel(width, shifts, parts, e_ref, a_ref, first_ref, *refs):
    got, (o_ref, alpha_ref, w16_ref) = refs[:-3], refs[-3:]
    alpha_ref[...] = a_ref[...] / sum(ordered([part[...] for part in got], shifts, parts))
    w16_ref[...] = stacked(alpha_ref[...])
    for at in range(0, e_ref.shape[1], width):
        sums = jnp.dot(w16_ref[...], e_ref[:, at:at + width], preferred_element_type=jnp.float32)
        o_ref[:, at:at + width] = first_ref[:, at:at + width] * jnp.sum(sums, axis=0, keepdims=True)


def flat(value):
    return value.reshape(1, -1) if value.ndim == 1 else value


def weighted(kernel, outs, e, rows, got, parts, width=512):
    got, shifts = got
    size = e.shape[0] if kernel is column_kernel else e.shape[1]
    return pl.pallas_call(
        functools.partial(kernel, width, tuple(shifts), parts),
        out_shape=[shape(*dims) for dims in outs],
        in_specs=[VMEM] * (1 + len(rows) + len(got)),
        out_specs=[VMEM] * len(outs),
        scratch_shapes=[pltpu.VMEM((16, size), jnp.bfloat16)],
        compiler_params=pltpu.CompilerParams(vmem_limit_bytes=16 << 20),
        cost_estimate=pl.CostEstimate(flops=2 * e.size, bytes_accessed=2 * e.size, transcendentals=0),
        name="weighted_sum",
    )(e, *rows, *[flat(part) for part in got])


def pass_cost(depth, lanes):
    return pl.CostEstimate(flops=2 * depth * lanes * D, bytes_accessed=2 * D * (depth + lanes), transcendentals=depth * lanes)


def shape(*dims, dtype=jnp.float32):
    return jax.ShapeDtypeStruct(dims, dtype)


def lse_scratch(depth, chunk, width):
    return [
        pltpu.VMEM((depth, 128), jnp.float32),
        pltpu.VMEM((2, chunk, width), jnp.float32),
        pltpu.VMEM((GROUP, 128), jnp.float32),
    ]


def row_lse_early(own, xs, y_other, width=1024):
    share = y_other.shape[0]
    rows, depth = own.shape[0] - share + sum(part.shape[0] for part in xs), 2 * share
    return pl.pallas_call(
        functools.partial(row_lse_early_kernel, width, len(xs)),
        out_shape=(shape(rows, D, dtype=jnp.bfloat16), shape(D, rows, dtype=jnp.bfloat16), shape(1, rows)),
        in_specs=[VMEM] * (len(xs) + 2),
        out_specs=(VMEM,) * 3,
        scratch_shapes=[pltpu.VMEM((depth, D), jnp.bfloat16), *lse_scratch(depth, share, width)],
        compiler_params=pltpu.CompilerParams(vmem_limit_bytes=16 << 20),
        cost_estimate=pass_cost(depth, rows),
        name="row_lse_early",
    )(own, *xs, y_other)


def row_lse_middle(x, ys, first, width=512):
    rows, share = x.shape[0], ys[0].shape[0]
    depth = len(ys) * share
    return pl.pallas_call(
        functools.partial(row_lse_middle_kernel, width, len(ys)),
        out_shape=shape(1, rows),
        in_specs=[VMEM] * (len(ys) + 2),
        out_specs=VMEM,
        scratch_shapes=[
            pltpu.VMEM((depth, D), jnp.bfloat16),
            *lse_scratch(depth, share, width),
            pltpu.VMEM((1, rows), jnp.float32),
        ],
        compiler_params=pltpu.CompilerParams(vmem_limit_bytes=16 << 20),
        cost_estimate=pass_cost(depth, rows),
        name="row_lse_middle",
    )(x, first, *ys)


def row_lse_late(own, x, ys, first, mass, tail, width=256):
    rows, share = x.shape[0], ys[0].shape[0]
    depth = (len(ys) + 1) * share
    return pl.pallas_call(
        functools.partial(row_lse_late_kernel, width, len(ys)),
        out_shape=(shape(depth, D, dtype=jnp.bfloat16), shape(1, rows + tail)),
        in_specs=[VMEM] * (len(ys) + 4),
        out_specs=(VMEM,) * 2,
        scratch_shapes=[*lse_scratch(depth, share, width), pltpu.VMEM((1, rows), jnp.float32)],
        compiler_params=pltpu.CompilerParams(vmem_limit_bytes=16 << 20),
        cost_estimate=pass_cost(depth // 2, rows),
        name="row_lse_late",
    )(own, mass.reshape(1, -1), x, first, *ys)


def column_lse(x, y, mass, tail, got, width=1024, chunk=256):
    rows, cols = x.shape[0], y.shape[0]
    return pl.pallas_call(
        functools.partial(column_lse_kernel, width, chunk, len(got)),
        out_shape=(shape(1, cols + tail), shape(rows, cols, dtype=jnp.bfloat16), shape(1, cols), shape(1, rows)),
        in_specs=[VMEM] * (3 + len(got)),
        out_specs=(VMEM,) * 4,
        scratch_shapes=[pltpu.VMEM((rows // 128, 128), jnp.float32), *lse_scratch(rows, chunk, width)],
        compiler_params=pltpu.CompilerParams(vmem_limit_bytes=16 << 20),
        cost_estimate=pass_cost(rows, cols),
        name="column_lse",
    )(x, y, mass.reshape(1, -1), *[part.reshape(1, -1) for part in got])


def pair_of(combine, one, two, size, shift, parts):
    whole = one.shape[-1]
    return pl.pallas_call(
        functools.partial(pair_kernel, size, shift, parts, combine),
        out_shape=shape(1, whole),
        in_specs=[VMEM] * 2,
        out_specs=VMEM,
        compiler_params=pltpu.CompilerParams(vmem_limit_bytes=16 << 20),
        name="pair",
    )(one.reshape(1, whole), two.reshape(1, whole))


def high_low(value):
    high = value.astype(jnp.bfloat16)
    return high, (value - high.astype(jnp.float32)).astype(jnp.bfloat16)


def column_grad_kernel(width, xt_ref, y_ref, e_ref, alpha_ref, first_ref, own_ref, sent_ref,
                       bb_ref, cb_ref, xa_ref, s_ref, count_ref, acc_ref):
    rows, cols = xt_ref.shape[1], y_ref.shape[0]
    own = own_ref.shape[0]
    spread(first_ref[...], s_ref, bb_ref)
    place = lax.broadcasted_iota(jnp.int32, (128, 512), 0)
    for at in range(0, rows, 512):
        alpha = alpha_ref[:, at:at + 512]
        high, low = high_low(xt_ref[:, at:at + 512].astype(jnp.float32) * alpha)
        first, second = high_low(alpha)
        low = jnp.where(place == 126, first.astype(jnp.float32), low.astype(jnp.float32))
        low = jnp.where(place == 127, second.astype(jnp.float32), low)
        xa_ref[:128, at:at + 512] = high
        xa_ref[128:, at:at + 512] = low.astype(jnp.bfloat16)

    lower = lax.broadcasted_iota(jnp.int32, (128, width), 0) < 126
    for at in range(0, cols, width):
        got = jnp.dot(xa_ref[...], e_ref[:, at:at + width], preferred_element_type=jnp.float32)
        acc_ref[:, at:at + width] = got[:128] + jnp.where(lower, got[128:], 0.0)
        count_ref[:, at:at + width] = got[254:255] + got[255:256]
    spread(count_ref[...], s_ref, cb_ref)
    for at in range(0, cols, 128):
        pulled = jnp.transpose(acc_ref[:, at:at + 128])
        whole = cb_ref[at:at + 128, :] * y_ref[at:at + 128, :].astype(jnp.float32)
        grad = bb_ref[at:at + 128, :] * (whole - pulled)
        if at < own:
            own_ref[at:at + 128, :] = grad
        else:
            sent_ref[at - own:at - own + 128, :] = grad.astype(jnp.bfloat16)


def column_grad(xt, y, e, alpha, first, own, width=512):
    rows, cols = xt.shape[1], y.shape[0]
    return pl.pallas_call(
        functools.partial(column_grad_kernel, width),
        out_shape=(shape(own, D), shape(cols - own, D, dtype=jnp.bfloat16)),
        in_specs=[VMEM] * 5,
        out_specs=(VMEM,) * 2,
        scratch_shapes=[
            pltpu.VMEM((cols, 128), jnp.float32),
            pltpu.VMEM((cols, 128), jnp.float32),
            pltpu.VMEM((256, rows), jnp.bfloat16),
            pltpu.VMEM((cols // 128, 128), jnp.float32),
            pltpu.VMEM((1, cols), jnp.float32),
            pltpu.VMEM((128, cols), jnp.float32),
        ],
        compiler_params=pltpu.CompilerParams(vmem_limit_bytes=16 << 20),
        cost_estimate=pl.CostEstimate(flops=4 * e.size * D, bytes_accessed=2 * e.size, transcendentals=0),
        name="column_grad",
    )(xt, y, e, alpha, first)


def row_block(at, chunk, x_ref, e_ref, yb_ref, scale):
    got = jnp.dot(e_ref[pl.ds(at, chunk), :], yb_ref[...], preferred_element_type=jnp.float32)
    lower = lax.broadcasted_iota(jnp.int32, (chunk, 128), 1) < 126
    total = got[:, 254:255] + got[:, 255:256]
    pulled = got[:, :128] + jnp.where(lower, got[:, 128:], 0.0)
    x = x_ref[pl.ds(at, chunk), :].astype(jnp.float32)
    return 2.0 * scale * (total * x - pulled)


def put_yb(y_ref, beta, yb_ref, s_ref, bb_ref):
    spread(beta, s_ref, bb_ref)
    place = lax.broadcasted_iota(jnp.int32, (256, 128), 1)
    for at in range(0, y_ref.shape[0], 256):
        beta = bb_ref[at:at + 256, :]
        high, low = high_low(y_ref[at:at + 256, :].astype(jnp.float32) * beta)
        first, second = high_low(beta)
        low = jnp.where(place == 126, first.astype(jnp.float32), low.astype(jnp.float32))
        low = jnp.where(place == 127, second.astype(jnp.float32), low)
        yb_ref[at:at + 256, :128] = high
        yb_ref[at:at + 256, 128:] = low.astype(jnp.bfloat16)


def row_parts(parts, x_ref, e_ref, alpha_ref, yb_ref, outs, sa_ref, ab_ref):
    share = outs[0].shape[0]
    chunk = math.gcd(share, 512)
    for part, out_ref in zip(parts, outs):
        spread(alpha_ref[:, part * share:(part + 1) * share], sa_ref, ab_ref)
        for k in range(0, share, chunk):
            grad = row_block(part * share + k, chunk, x_ref, e_ref, yb_ref, ab_ref[k:k + chunk, :])
            out_ref[k:k + chunk, :] = grad.astype(out_ref.dtype)


def first_rows_kernel(parts, shifts, blocks, nz, x_ref, y_ref, e_ref, alpha_ref, first_ref, b_ref, *refs):
    got, (yb_ref, scale_ref, *outs), (s_ref, bb_ref, sa_ref, ab_ref) = refs[:nz], refs[nz:-4], refs[-4:]
    scale = new_scale(b_ref, got, shifts, blocks)
    scale_ref[...] = scale[:, :scale_ref.shape[1]]
    put_yb(y_ref, first_ref[...] * scale, yb_ref, s_ref, bb_ref)
    row_parts(parts, x_ref, e_ref, alpha_ref, yb_ref, outs, sa_ref, ab_ref)


def rows_kernel(parts, x_ref, yb_ref, e_ref, alpha_ref, *refs):
    row_parts(parts, x_ref, e_ref, alpha_ref, yb_ref, refs[:-2], *refs[-2:])


def rows_scratch(share):
    return [pltpu.VMEM((share // 128, 128), jnp.float32), pltpu.VMEM((share, 128), jnp.float32)]


def rows_cost(share, parts, cols):
    size = share * len(parts) * cols
    return pl.CostEstimate(flops=4 * size * D, bytes_accessed=2 * size, transcendentals=0)


def first_rows(parts, share, x, y, e, alpha, first, mass, got, blocks):
    cols = y.shape[0]
    got, shifts = got
    return pl.pallas_call(
        functools.partial(first_rows_kernel, parts, tuple(shifts), blocks, len(got)),
        out_shape=[shape(cols, 256, dtype=jnp.bfloat16), shape(1, cols // blocks)]
        + [shape(share, D, dtype=jnp.bfloat16)] * len(parts),
        in_specs=[VMEM] * (6 + len(got)),
        out_specs=[VMEM] * (2 + len(parts)),
        scratch_shapes=[
            pltpu.VMEM((cols // 128, 128), jnp.float32),
            pltpu.VMEM((cols, 128), jnp.float32),
            *rows_scratch(share),
        ],
        compiler_params=pltpu.CompilerParams(vmem_limit_bytes=16 << 20),
        cost_estimate=rows_cost(share * HEAVY, parts, cols),
        name="first_rows",
    )(x, y, e, alpha, first, mass, *[flat(part) for part in got])


def other_rows(parts, share, x, yb, e, alpha, dtype):
    return pl.pallas_call(
        functools.partial(rows_kernel, parts),
        out_shape=[shape(share, D, dtype=dtype)] * len(parts),
        in_specs=[VMEM] * 4,
        out_specs=[VMEM] * len(parts),
        scratch_shapes=rows_scratch(share),
        compiler_params=pltpu.CompilerParams(vmem_limit_bytes=16 << 20),
        cost_estimate=rows_cost(share, parts, yb.shape[0]),
        name="other_rows",
    )(x, yb, e, alpha)


def add_up_kernel(na, scale_ref, *refs):
    ins, (rows_ref, cols_ref, s_ref, sb_ref) = refs[:-4], refs[-4:]
    rows_ref[...] = sum(part[...].astype(jnp.float32) for part in ins[:na])
    spread(scale_ref[...], s_ref, sb_ref)
    cols_ref[...] = 2.0 * sb_ref[...] * sum(part[...].astype(jnp.float32) for part in ins[na:])


def add_up(rows, columns, scale):
    share = scale.shape[1]
    return pl.pallas_call(
        functools.partial(add_up_kernel, len(rows)),
        out_shape=(shape(*rows[0].shape), shape(*columns[0].shape)),
        in_specs=[VMEM] * (1 + len(rows) + len(columns)),
        out_specs=(VMEM,) * 2,
        scratch_shapes=rows_scratch(share),
        compiler_params=pltpu.CompilerParams(vmem_limit_bytes=16 << 20),
        name="add_up",
    )(scale, *rows, *columns)


def shares_kernel(gc_ref, other_ref, own_ref, *outs):
    share = own_ref.shape[0]
    for k in range(len(outs) + 1):
        at = k * share
        total = gc_ref[at:at + share, :] + other_ref[at:at + share, :].astype(jnp.float32)
        if k == 0:
            own_ref[...] = total
        else:
            outs[k - 1][...] = total.astype(jnp.bfloat16)


def shares(gc, other, count):
    share = gc.shape[0] // count
    return pl.pallas_call(
        shares_kernel,
        out_shape=[shape(share, D)] + [shape(share, D, dtype=jnp.bfloat16)] * (count - 1),
        in_specs=[VMEM] * 2,
        out_specs=[VMEM] * count,
        compiler_params=pltpu.CompilerParams(vmem_limit_bytes=16 << 20),
        name="shares",
    )(gc, other)


class Groups:
    def __init__(self, nrow, ncol):
        self.count = nrow * ncol
        self.across = [(a << 1) * ncol + b for a in range(nrow // 2) for b in range(2)]
        self.along = [z << 1 for z in range(ncol // 2)]
        self.core = ncol

    def swap(self, value, mask):
        if mask == 0:
            return value
        return lax.ppermute(value, ("row", "col"), [(i, i ^ mask) for i in range(self.count)])


def local(imu, camera, imu_mass, cam_mass):
    nrow, ncol = lax.axis_size("row"), lax.axis_size("col")
    groups = Groups(nrow, ncol)
    swap, across, along, core = groups.swap, groups.across, groups.along, groups.core
    na, nz = len(across), len(along)
    share_x, share_y = imu.shape[0], camera.shape[1]
    rows, cols = na * share_x, 2 * nz * share_y

    def direct(value, masks):
        return [swap(value, mask) for mask in masks], range(len(masks))

    xs, _ = direct(imu, across)
    near, far = [camera[0]], [swap(camera[0], core)]
    for z in range(1, nz):
        part = near[z & (z - 1)]
        if z & (z - 1):
            part, near[z & -z], xs = lax.optimization_barrier((part, near[z & -z], xs))
        near.append(swap(part, along[z & -z]))

    def pair(mass, place, share):
        return [lax.dynamic_slice_in_dim(mass, (place ^ k) * share, share, 0) for k in range(2)]

    own = jnp.concatenate([imu, camera[0]])
    row, col = lax.axis_index("row"), lax.axis_index("col")
    mass = jnp.concatenate(pair(imu_mass, col, share_x) + pair(cam_mass, row, share_y))

    x, xt, first = row_lse_early(own, xs[1:], far[0])
    first, *middle = lax.optimization_barrier((first, *near[1:-1]))
    far += [swap(part, core) for part in middle]
    first = row_lse_middle(x, middle, first)
    first, last = lax.optimization_barrier((first, near[-1]))
    far.append(swap(last, core))
    y, sent = row_lse_late(own, x, [*middle, last, *far], first, mass, 2 * share_x)
    got, _ = direct(sent.reshape(-1), across)

    sent, e, shift, mass_a = column_lse(x, y, mass, 2 * share_y, got)
    sent = pair_of(lse2, sent, swap(sent.reshape(-1), core), cols, 1, 2)
    got = direct(sent.reshape(-1), along)

    sums, first_beta, mass_b = weighted(
        first_row_kernel, [(1, rows), (1, cols), (1, cols)], e, [shift], got, 2 * nz)
    for step in range(1, ITERS):
        if step > 1:
            sums, = weighted(row_kernel, [(1, rows)], e, [first_beta, mass_b], got, 2 * nz)
        got = direct(sums.reshape(-1), across)
        part, alpha = weighted(column_kernel, [(1, cols), (1, rows)], e, [mass_a, first_beta], got, na)
        part = pair_of(sum, part, swap(part.reshape(-1), core), cols, 1, 2)
        part, alpha = lax.optimization_barrier((part, alpha))
        got = direct(part.reshape(-1), along)

    gc, gc_send = column_grad(xt, y, e, alpha, first_beta, nz * share_y)
    yb, scale, last = first_rows([na - 1], share_x, x, y, e, alpha, first_beta, mass_b, got, 2 * nz)
    (grad_cam, *parts), yb = lax.optimization_barrier((shares(gc, swap(gc_send, core), nz), yb))
    parts = [swap(part, along[z + 1]) for z, part in enumerate(parts)]
    last = swap(last, across[na - 1])
    sent = other_rows(list(range(1, na - 1)), share_x, x, yb, e, alpha, jnp.bfloat16)
    sent, parts[0], last = lax.optimization_barrier((sent, parts[0], last))
    sent = [swap(part, across[s + 1]) for s, part in enumerate(sent)] + [last]
    gi, = other_rows([0], share_x, x, yb, e, alpha, jnp.float32)
    grad_imu, grad_cam = add_up([gi, *sent], [grad_cam, *parts], scale)
    return grad_imu, grad_cam[None]


def solution(mesh):
    in_specs = (P(("row", "col"), None), P("col", "row", None), P("row"), P("col"))
    out_specs = (P(("row", "col"), None), P("col", "row", None))
    return jax.shard_map(local, mesh=mesh, in_specs=in_specs, out_specs=out_specs, check_vma=False)
```

```python
import functools
import math

import jax
import jax.numpy as jnp
from jax import lax
from jax.experimental import pallas as pl
from jax.experimental.pallas import tpu as pltpu
from jax.sharding import PartitionSpec as P

D = 128
ITERS = 3
EPSILON = D / 20.0
LOG2E = math.log2(math.e)
CROSS = 2.0 * LOG2E / EPSILON
NT = (((1,), (1,)), ((), ()))
VMEM = pl.BlockSpec(memory_space=pltpu.VMEM)
GROUP = 32
HEAVY = 32


def spread(value, s_ref, sb_ref):
    chunks = value.shape[1] // 128
    for k in range(chunks):
        s_ref[k:k + 1, :] = value[:, k * 128:(k + 1) * 128]
    turned = jnp.transpose(s_ref[...])
    for k in range(chunks):
        sb_ref[k * 128:(k + 1) * 128, :] = jnp.broadcast_to(turned[:, k:k + 1], (128, 128))


def ordered(values, shifts, parts):
    share = values[0].shape[1] // parts
    return [
        jnp.concatenate([value[:, (k ^ s) * share:((k ^ s) + 1) * share] for k in range(parts)], axis=1)
        for value, s in zip(values, shifts)
    ]


def lse2(parts):
    top = functools.reduce(jnp.maximum, parts)
    return top + jnp.log2(sum(jnp.exp2(part - top) for part in parts))


def pipelined(places, chunk, width, a_ref, b_ref, d_ref, tile, finish):
    last = b_ref.shape[0] // width - 1

    def product(n, m):
        b = b_ref[pl.ds(pl.multiple_of(n * width, width), width), :]
        a = a_ref[places[m]:places[m] + chunk, :]
        d_ref[m % 2] = lax.dot_general(a, b, NT, preferred_element_type=jnp.float32)

    product(0, 0)

    def column(n, _):
        start = pl.multiple_of(n * width, width)
        state = None
        for m in range(len(places)):
            if m + 1 < len(places):
                product(n, m + 1)
            else:
                product(jnp.minimum(n + 1, last), 0)
            state = tile(m, start, state)
        finish(start, state)
        return 0

    lax.fori_loop(0, last + 1, column, 0)


def running_max(places, chunk, width, a_ref, b_ref, sb_ref, o_ref, e_ref, shift_ref):
    def column(n, _):
        start = pl.multiple_of(n * width, width)
        b = b_ref[pl.ds(start, width), :]

        def exponents(at):
            d = lax.dot_general(a_ref[at:at + chunk, :], b, NT, preferred_element_type=jnp.float32)
            s = sb_ref[at:at + chunk, :]
            return [d[:, q * 128:(q + 1) * 128] * CROSS + s for q in range(width // 128)]

        peak, total = jnp.full((1, width), -1e30, jnp.float32), jnp.zeros((1, width), jnp.float32)
        for at in places:
            peaks, totals = [], []
            for q, t in enumerate(exponents(at)):
                old = peak[:, q * 128:(q + 1) * 128]
                new = jnp.maximum(old, jnp.max(t, axis=0, keepdims=True))
                part = jnp.sum(jnp.exp2(t - new), axis=0, keepdims=True)
                peaks.append(new)
                totals.append(total[:, q * 128:(q + 1) * 128] * jnp.exp2(old - new) + part)
            peak, total = jnp.concatenate(peaks, axis=1), jnp.concatenate(totals, axis=1)
        o_ref[:, pl.ds(start, width)] = peak + jnp.log2(total)
        if e_ref is not None:
            shift_ref[:, pl.ds(start, width)] = peak
            for at in places:
                for q, t in enumerate(exponents(at)):
                    place = pl.ds(pl.multiple_of(start + q * 128, 128), 128)
                    e_ref[at:at + chunk, place] = jnp.exp2(t - shift_ref[:, place]).astype(jnp.bfloat16)
        return 0

    lax.fori_loop(0, b_ref.shape[0] // width, column, 0)


def lse_pass(places, chunk, width, a_ref, b_ref, sb_ref, d_ref, top_ref, o_ref, e_ref=None, shift_ref=None):
    tiles = width // 128
    top_ref[...] = jnp.zeros_like(top_ref)

    def lanes_of(start, q):
        return pl.ds(pl.multiple_of(start + q * 128, 128), 128)

    def tile(m, start, state):
        def exponents(g, q):
            at = g * GROUP
            s = sb_ref[places[m] + at:places[m] + at + GROUP, :]
            return d_ref[m % 2, at:at + GROUP, q * 128:(q + 1) * 128] * CROSS + s

        if m == 0:
            tops = [exponents(0, q) for q in range(tiles)]
            for g in range(1, 128 // GROUP):
                tops = [jnp.maximum(top, exponents(g, q)) for q, top in enumerate(tops)]
            state = [(jnp.max(top, axis=0, keepdims=True), jnp.zeros((GROUP, 128), jnp.float32)) for top in tops]
        for g in range(chunk // GROUP):
            for q, (peak, total) in enumerate(state):
                e = jnp.exp2(exponents(g, q) - peak)
                if e_ref is not None:
                    at = places[m] + g * GROUP
                    e_ref[at:at + GROUP, lanes_of(start, q)] = e.astype(jnp.bfloat16)
                state[q] = peak, total + e
        return state

    def finish(start, state):
        for q, (peak, total) in enumerate(state):
            top_ref[...] = jnp.maximum(top_ref[...], total)
            o_ref[:, lanes_of(start, q)] = peak + jnp.log2(jnp.sum(total, axis=0, keepdims=True))
            if e_ref is not None:
                shift_ref[:, lanes_of(start, q)] = peak

    pipelined(places, chunk, width, a_ref, b_ref, d_ref, tile, finish)

    @pl.when(jnp.logical_not(jnp.max(top_ref[...]) < 2.0 ** 60))
    def _():
        running_max(places, chunk, min(width, 256), a_ref, b_ref, sb_ref, o_ref, e_ref, shift_ref)


def put_norms(places, share, y_ref, sb_ref):
    for at in places:
        y = y_ref[at:at + share, :].astype(jnp.float32)
        total = jnp.sum(y * y, axis=1, keepdims=True) * (-LOG2E / EPSILON)
        sb_ref[at:at + share, :] = jnp.broadcast_to(total, (share, 128))


def join(out_ref, parts):
    at = 0
    for part in parts:
        out_ref[at:at + part.shape[0], :] = part[...]
        at += part.shape[0]


def row_lse_early_kernel(width, nx, own_ref, *refs):
    xs, y_other, refs = refs[:nx], refs[nx], refs[nx + 1:]
    x_ref, xt_ref, o_ref, y_ref, sb_ref, d_ref, top_ref = refs
    share = y_other.shape[0]
    mine = own_ref.shape[0] - share
    join(x_ref, [own_ref.at[:mine, :], *xs])
    join(y_ref, [own_ref.at[mine:, :], y_other])
    for k in range(x_ref.shape[0] // 128):
        at = k * 128
        xt_ref[:, at:at + 128] = jnp.transpose(x_ref[at:at + 128, :].astype(jnp.float32)).astype(jnp.bfloat16)
    places = [0, share]
    put_norms(places, share, y_ref, sb_ref)
    lse_pass(places, share, width, y_ref, x_ref, sb_ref, d_ref, top_ref, o_ref)


def row_lse_middle_kernel(width, ny, x_ref, first_ref, *refs):
    ys, (o_ref, y_ref, sb_ref, d_ref, top_ref, sum_ref) = refs[:ny], refs[ny:]
    share = ys[0].shape[0]
    join(y_ref, ys)
    places = [k * share for k in range(ny)]
    put_norms(places, share, y_ref, sb_ref)
    lse_pass(places, share, width, y_ref, x_ref, sb_ref, d_ref, top_ref, sum_ref)
    o_ref[...] = lse2([first_ref[...], sum_ref[...]])


def row_lse_late_kernel(width, ny, own_ref, mass_ref, x_ref, first_ref, *refs):
    ys, (y_ref, o_ref, sb_ref, d_ref, top_ref, sum_ref) = refs[:ny], refs[ny:]
    share, rows, half = ys[0].shape[0], x_ref.shape[0], (ny + 1) // 2
    join(y_ref, [own_ref.at[own_ref.shape[0] - share:, :], *ys])
    places = [k * share for k in range(half - 1, 2 * half) if k != half]
    put_norms(places, share, y_ref, sb_ref)
    lse_pass(places, share, width, y_ref, x_ref, sb_ref, d_ref, top_ref, sum_ref)
    o_ref[:, :rows] = lse2([first_ref[...], sum_ref[...]])
    o_ref[:, rows:] = mass_ref[:, :o_ref.shape[1] - rows]


def column_lse_kernel(width, chunk, na, x_ref, y_ref, mass_ref, *refs):
    got, (o_ref, e_ref, shift_ref, a_ref, s_ref, sb_ref, d_ref, top_ref) = refs[:na], refs[na:]
    rows, cols = x_ref.shape[0], y_ref.shape[0]
    o_ref[:, cols:] = mass_ref[:, mass_ref.shape[1] - o_ref.shape[1] + cols:]
    share = rows // na
    for k in range(na):
        at = rows + (k % 2) * share
        a_ref[:, k * share:(k + 1) * share] = got[k - k % 2][:, at:at + share]
    u = jnp.log2(a_ref[...]) - lse2(ordered([part[:, :rows] for part in got], range(na), na))
    spread(u, s_ref, sb_ref)
    places = list(range(0, rows, chunk))
    lse_pass(places, chunk, width, x_ref, y_ref, sb_ref, d_ref, top_ref, o_ref, e_ref, shift_ref)


def pair_kernel(size, shift, parts, combine, one_ref, two_ref, o_ref):
    two, = ordered([two_ref[:, :size]], [shift], parts)
    o_ref[:, :size] = combine([one_ref[:, :size], two])
    if o_ref.shape[1] > size:
        o_ref[:, size:] = one_ref[:, size:]


def split3(value):
    high = value.astype(jnp.bfloat16)
    rest = value - high.astype(jnp.float32)
    mid = rest.astype(jnp.bfloat16)
    return high, mid, (rest - mid.astype(jnp.float32)).astype(jnp.bfloat16)


def stacked(value):
    high, mid, low = [part.astype(jnp.float32) for part in split3(value)]
    dims = (16, value.shape[1])
    place = lax.broadcasted_iota(jnp.int32, dims, 0)
    parts = jnp.where(place == 0, high, jnp.where(place == 1, mid, jnp.where(place == 2, low, 0.0)))
    return parts.astype(jnp.bfloat16)


def row_sums(width, e_ref, w16_ref, o_ref):
    for at in range(0, e_ref.shape[0], width):
        got = lax.dot_general(w16_ref[...], e_ref[at:at + width, :], NT, preferred_element_type=jnp.float32)
        o_ref[:, at:at + width] = jnp.sum(got, axis=0, keepdims=True)


def first_row_kernel(width, shifts, parts, e_ref, shift_ref, *refs):
    nz = len(shifts)
    got, (o_ref, beta_ref, b_ref, w16_ref) = refs[:nz], refs[nz:]
    cols = e_ref.shape[1]
    share = cols // parts
    for k in range(parts):
        at = cols + (k // nz) * share
        b_ref[:, k * share:(k + 1) * share] = got[k % nz][:, at:at + share]
    lse = lse2(ordered([part[:, :cols] for part in got], shifts, parts))
    beta_ref[...] = jnp.exp2(jnp.log2(b_ref[...]) - lse + shift_ref[...])
    w16_ref[...] = stacked(beta_ref[...])
    row_sums(width, e_ref, w16_ref, o_ref)


def new_scale(b_ref, got, shifts, parts):
    return b_ref[...] / sum(ordered([part[...] for part in got], shifts, parts))


def row_kernel(width, shifts, parts, e_ref, first_ref, b_ref, *refs):
    got, (o_ref, w16_ref) = refs[:-2], refs[-2:]
    w16_ref[...] = stacked(first_ref[...] * new_scale(b_ref, got, shifts, parts))
    row_sums(width, e_ref, w16_ref, o_ref)


def column_kernel(width, shifts, parts, e_ref, a_ref, first_ref, *refs):
    got, (o_ref, alpha_ref, w16_ref) = refs[:-3], refs[-3:]
    alpha_ref[...] = a_ref[...] / sum(ordered([part[...] for part in got], shifts, parts))
    w16_ref[...] = stacked(alpha_ref[...])
    for at in range(0, e_ref.shape[1], width):
        sums = jnp.dot(w16_ref[...], e_ref[:, at:at + width], preferred_element_type=jnp.float32)
        o_ref[:, at:at + width] = first_ref[:, at:at + width] * jnp.sum(sums, axis=0, keepdims=True)


def flat(value):
    return value.reshape(1, -1) if value.ndim == 1 else value


def weighted(kernel, outs, e, rows, got, parts, width=512):
    got, shifts = got
    size = e.shape[0] if kernel is column_kernel else e.shape[1]
    return pl.pallas_call(
        functools.partial(kernel, width, tuple(shifts), parts),
        out_shape=[shape(*dims) for dims in outs],
        in_specs=[VMEM] * (1 + len(rows) + len(got)),
        out_specs=[VMEM] * len(outs),
        scratch_shapes=[pltpu.VMEM((16, size), jnp.bfloat16)],
        compiler_params=pltpu.CompilerParams(vmem_limit_bytes=16 << 20),
        cost_estimate=pl.CostEstimate(flops=2 * e.size, bytes_accessed=2 * e.size, transcendentals=0),
        name="weighted_sum",
    )(e, *rows, *[flat(part) for part in got])


def pass_cost(depth, lanes):
    return pl.CostEstimate(flops=2 * depth * lanes * D, bytes_accessed=2 * D * (depth + lanes), transcendentals=depth * lanes)


def shape(*dims, dtype=jnp.float32):
    return jax.ShapeDtypeStruct(dims, dtype)


def lse_scratch(depth, chunk, width):
    return [
        pltpu.VMEM((depth, 128), jnp.float32),
        pltpu.VMEM((2, chunk, width), jnp.float32),
        pltpu.VMEM((GROUP, 128), jnp.float32),
    ]


def row_lse_early(own, xs, y_other, width=1024):
    share = y_other.shape[0]
    rows, depth = own.shape[0] - share + sum(part.shape[0] for part in xs), 2 * share
    return pl.pallas_call(
        functools.partial(row_lse_early_kernel, width, len(xs)),
        out_shape=(shape(rows, D, dtype=jnp.bfloat16), shape(D, rows, dtype=jnp.bfloat16), shape(1, rows)),
        in_specs=[VMEM] * (len(xs) + 2),
        out_specs=(VMEM,) * 3,
        scratch_shapes=[pltpu.VMEM((depth, D), jnp.bfloat16), *lse_scratch(depth, share, width)],
        compiler_params=pltpu.CompilerParams(vmem_limit_bytes=16 << 20),
        cost_estimate=pass_cost(depth, rows),
        name="row_lse_early",
    )(own, *xs, y_other)


def row_lse_middle(x, ys, first, width=1024):
    rows, share = x.shape[0], ys[0].shape[0]
    depth = len(ys) * share
    return pl.pallas_call(
        functools.partial(row_lse_middle_kernel, width, len(ys)),
        out_shape=shape(1, rows),
        in_specs=[VMEM] * (len(ys) + 2),
        out_specs=VMEM,
        scratch_shapes=[
            pltpu.VMEM((depth, D), jnp.bfloat16),
            *lse_scratch(depth, share, width),
            pltpu.VMEM((1, rows), jnp.float32),
        ],
        compiler_params=pltpu.CompilerParams(vmem_limit_bytes=16 << 20),
        cost_estimate=pass_cost(depth, rows),
        name="row_lse_middle",
    )(x, first, *ys)


def row_lse_late(own, x, ys, first, mass, tail, width=1024):
    rows, share = x.shape[0], ys[0].shape[0]
    depth = (len(ys) + 1) * share
    return pl.pallas_call(
        functools.partial(row_lse_late_kernel, width, len(ys)),
        out_shape=(shape(depth, D, dtype=jnp.bfloat16), shape(1, rows + tail)),
        in_specs=[VMEM] * (len(ys) + 4),
        out_specs=(VMEM,) * 2,
        scratch_shapes=[*lse_scratch(depth, share, width), pltpu.VMEM((1, rows), jnp.float32)],
        compiler_params=pltpu.CompilerParams(vmem_limit_bytes=16 << 20),
        cost_estimate=pass_cost(depth // 2, rows),
        name="row_lse_late",
    )(own, mass.reshape(1, -1), x, first, *ys)


def column_lse(x, y, mass, tail, got, width=1024, chunk=512):
    rows, cols = x.shape[0], y.shape[0]
    return pl.pallas_call(
        functools.partial(column_lse_kernel, width, chunk, len(got)),
        out_shape=(shape(1, cols + tail), shape(rows, cols, dtype=jnp.bfloat16), shape(1, cols), shape(1, rows)),
        in_specs=[VMEM] * (3 + len(got)),
        out_specs=(VMEM,) * 4,
        scratch_shapes=[pltpu.VMEM((rows // 128, 128), jnp.float32), *lse_scratch(rows, chunk, width)],
        compiler_params=pltpu.CompilerParams(vmem_limit_bytes=16 << 20),
        cost_estimate=pass_cost(rows, cols),
        name="column_lse",
    )(x, y, mass.reshape(1, -1), *[part.reshape(1, -1) for part in got])


def pair_of(combine, one, two, size, shift, parts):
    whole = one.shape[-1]
    return pl.pallas_call(
        functools.partial(pair_kernel, size, shift, parts, combine),
        out_shape=shape(1, whole),
        in_specs=[VMEM] * 2,
        out_specs=VMEM,
        compiler_params=pltpu.CompilerParams(vmem_limit_bytes=16 << 20),
        name="pair",
    )(one.reshape(1, whole), two.reshape(1, whole))


def high_low(value):
    high = value.astype(jnp.bfloat16)
    return high, (value - high.astype(jnp.float32)).astype(jnp.bfloat16)


def column_grad_kernel(width, xt_ref, y_ref, e_ref, alpha_ref, first_ref, own_ref, sent_ref,
                       bb_ref, cb_ref, xa_ref, s_ref, count_ref, acc_ref):
    rows, cols = xt_ref.shape[1], y_ref.shape[0]
    own = own_ref.shape[0]
    spread(first_ref[...], s_ref, bb_ref)
    place = lax.broadcasted_iota(jnp.int32, (128, 512), 0)
    for at in range(0, rows, 512):
        alpha = alpha_ref[:, at:at + 512]
        high, low = high_low(xt_ref[:, at:at + 512].astype(jnp.float32) * alpha)
        first, second = high_low(alpha)
        low = jnp.where(place == 126, first.astype(jnp.float32), low.astype(jnp.float32))
        low = jnp.where(place == 127, second.astype(jnp.float32), low)
        xa_ref[:128, at:at + 512] = high
        xa_ref[128:, at:at + 512] = low.astype(jnp.bfloat16)

    lower = lax.broadcasted_iota(jnp.int32, (128, width), 0) < 126
    for at in range(0, cols, width):
        got = jnp.dot(xa_ref[...], e_ref[:, at:at + width], preferred_element_type=jnp.float32)
        acc_ref[:, at:at + width] = got[:128] + jnp.where(lower, got[128:], 0.0)
        count_ref[:, at:at + width] = got[254:255] + got[255:256]
    spread(count_ref[...], s_ref, cb_ref)
    for at in range(0, cols, 128):
        pulled = jnp.transpose(acc_ref[:, at:at + 128])
        whole = cb_ref[at:at + 128, :] * y_ref[at:at + 128, :].astype(jnp.float32)
        grad = bb_ref[at:at + 128, :] * (whole - pulled)
        if at < own:
            own_ref[at:at + 128, :] = grad
        else:
            sent_ref[at - own:at - own + 128, :] = grad.astype(jnp.bfloat16)


def column_grad(xt, y, e, alpha, first, own, width=512):
    rows, cols = xt.shape[1], y.shape[0]
    return pl.pallas_call(
        functools.partial(column_grad_kernel, width),
        out_shape=(shape(own, D), shape(cols - own, D, dtype=jnp.bfloat16)),
        in_specs=[VMEM] * 5,
        out_specs=(VMEM,) * 2,
        scratch_shapes=[
            pltpu.VMEM((cols, 128), jnp.float32),
            pltpu.VMEM((cols, 128), jnp.float32),
            pltpu.VMEM((256, rows), jnp.bfloat16),
            pltpu.VMEM((cols // 128, 128), jnp.float32),
            pltpu.VMEM((1, cols), jnp.float32),
            pltpu.VMEM((128, cols), jnp.float32),
        ],
        compiler_params=pltpu.CompilerParams(vmem_limit_bytes=16 << 20),
        cost_estimate=pl.CostEstimate(flops=4 * e.size * D, bytes_accessed=2 * e.size, transcendentals=0),
        name="column_grad",
    )(xt, y, e, alpha, first)


def row_block(at, chunk, x_ref, e_ref, yb_ref, scale):
    got = jnp.dot(e_ref[pl.ds(at, chunk), :], yb_ref[...], preferred_element_type=jnp.float32)
    lower = lax.broadcasted_iota(jnp.int32, (chunk, 128), 1) < 126
    total = got[:, 254:255] + got[:, 255:256]
    pulled = got[:, :128] + jnp.where(lower, got[:, 128:], 0.0)
    x = x_ref[pl.ds(at, chunk), :].astype(jnp.float32)
    return 2.0 * scale * (total * x - pulled)


def put_yb(y_ref, beta, yb_ref, s_ref, bb_ref):
    spread(beta, s_ref, bb_ref)
    place = lax.broadcasted_iota(jnp.int32, (256, 128), 1)
    for at in range(0, y_ref.shape[0], 256):
        beta = bb_ref[at:at + 256, :]
        high, low = high_low(y_ref[at:at + 256, :].astype(jnp.float32) * beta)
        first, second = high_low(beta)
        low = jnp.where(place == 126, first.astype(jnp.float32), low.astype(jnp.float32))
        low = jnp.where(place == 127, second.astype(jnp.float32), low)
        yb_ref[at:at + 256, :128] = high
        yb_ref[at:at + 256, 128:] = low.astype(jnp.bfloat16)


def row_parts(parts, x_ref, e_ref, alpha_ref, yb_ref, outs, sa_ref, ab_ref):
    share = outs[0].shape[0]
    chunk = math.gcd(share, 512)
    for part, out_ref in zip(parts, outs):
        spread(alpha_ref[:, part * share:(part + 1) * share], sa_ref, ab_ref)
        for k in range(0, share, chunk):
            grad = row_block(part * share + k, chunk, x_ref, e_ref, yb_ref, ab_ref[k:k + chunk, :])
            out_ref[k:k + chunk, :] = grad.astype(out_ref.dtype)


def first_rows_kernel(parts, shifts, blocks, nz, x_ref, y_ref, e_ref, alpha_ref, first_ref, b_ref, *refs):
    got, (yb_ref, scale_ref, *outs), (s_ref, bb_ref, sa_ref, ab_ref) = refs[:nz], refs[nz:-4], refs[-4:]
    scale = new_scale(b_ref, got, shifts, blocks)
    scale_ref[...] = scale[:, :scale_ref.shape[1]]
    put_yb(y_ref, first_ref[...] * scale, yb_ref, s_ref, bb_ref)
    row_parts(parts, x_ref, e_ref, alpha_ref, yb_ref, outs, sa_ref, ab_ref)


def rows_kernel(parts, x_ref, yb_ref, e_ref, alpha_ref, *refs):
    row_parts(parts, x_ref, e_ref, alpha_ref, yb_ref, refs[:-2], *refs[-2:])


def rows_scratch(share):
    return [pltpu.VMEM((share // 128, 128), jnp.float32), pltpu.VMEM((share, 128), jnp.float32)]


def rows_cost(share, parts, cols):
    size = share * len(parts) * cols
    return pl.CostEstimate(flops=4 * size * D, bytes_accessed=2 * size, transcendentals=0)


def first_rows(parts, share, x, y, e, alpha, first, mass, got, blocks):
    cols = y.shape[0]
    got, shifts = got
    return pl.pallas_call(
        functools.partial(first_rows_kernel, parts, tuple(shifts), blocks, len(got)),
        out_shape=[shape(cols, 256, dtype=jnp.bfloat16), shape(1, cols // blocks)]
        + [shape(share, D, dtype=jnp.bfloat16)] * len(parts),
        in_specs=[VMEM] * (6 + len(got)),
        out_specs=[VMEM] * (2 + len(parts)),
        scratch_shapes=[
            pltpu.VMEM((cols // 128, 128), jnp.float32),
            pltpu.VMEM((cols, 128), jnp.float32),
            *rows_scratch(share),
        ],
        compiler_params=pltpu.CompilerParams(vmem_limit_bytes=16 << 20),
        cost_estimate=rows_cost(share * HEAVY, parts, cols),
        name="first_rows",
    )(x, y, e, alpha, first, mass, *[flat(part) for part in got])


def other_rows(parts, share, x, yb, e, alpha, dtype):
    return pl.pallas_call(
        functools.partial(rows_kernel, parts),
        out_shape=[shape(share, D, dtype=dtype)] * len(parts),
        in_specs=[VMEM] * 4,
        out_specs=[VMEM] * len(parts),
        scratch_shapes=rows_scratch(share),
        compiler_params=pltpu.CompilerParams(vmem_limit_bytes=16 << 20),
        cost_estimate=rows_cost(share, parts, yb.shape[0]),
        name="other_rows",
    )(x, yb, e, alpha)


def add_up_kernel(na, scale_ref, *refs):
    ins, (rows_ref, cols_ref, s_ref, sb_ref) = refs[:-4], refs[-4:]
    rows_ref[...] = sum(part[...].astype(jnp.float32) for part in ins[:na])
    spread(scale_ref[...], s_ref, sb_ref)
    cols_ref[...] = 2.0 * sb_ref[...] * sum(part[...].astype(jnp.float32) for part in ins[na:])


def add_up(rows, columns, scale):
    share = scale.shape[1]
    return pl.pallas_call(
        functools.partial(add_up_kernel, len(rows)),
        out_shape=(shape(*rows[0].shape), shape(*columns[0].shape)),
        in_specs=[VMEM] * (1 + len(rows) + len(columns)),
        out_specs=(VMEM,) * 2,
        scratch_shapes=rows_scratch(share),
        compiler_params=pltpu.CompilerParams(vmem_limit_bytes=16 << 20),
        name="add_up",
    )(scale, *rows, *columns)


def shares_kernel(gc_ref, other_ref, own_ref, *outs):
    share = own_ref.shape[0]
    for k in range(len(outs) + 1):
        at = k * share
        total = gc_ref[at:at + share, :] + other_ref[at:at + share, :].astype(jnp.float32)
        if k == 0:
            own_ref[...] = total
        else:
            outs[k - 1][...] = total.astype(jnp.bfloat16)


def shares(gc, other, count):
    share = gc.shape[0] // count
    return pl.pallas_call(
        shares_kernel,
        out_shape=[shape(share, D)] + [shape(share, D, dtype=jnp.bfloat16)] * (count - 1),
        in_specs=[VMEM] * 2,
        out_specs=[VMEM] * count,
        compiler_params=pltpu.CompilerParams(vmem_limit_bytes=16 << 20),
        name="shares",
    )(gc, other)


class Groups:
    def __init__(self, nrow, ncol):
        self.count = nrow * ncol
        self.across = [(a << 1) * ncol + b for a in range(nrow // 2) for b in range(2)]
        self.along = [z << 1 for z in range(ncol // 2)]
        self.core = ncol

    def swap(self, value, mask):
        if mask == 0:
            return value
        return lax.ppermute(value, ("row", "col"), [(i, i ^ mask) for i in range(self.count)])


def local(imu, camera, imu_mass, cam_mass):
    nrow, ncol = lax.axis_size("row"), lax.axis_size("col")
    groups = Groups(nrow, ncol)
    swap, across, along, core = groups.swap, groups.across, groups.along, groups.core
    na, nz = len(across), len(along)
    share_x, share_y = imu.shape[0], camera.shape[1]
    rows, cols = na * share_x, 2 * nz * share_y

    def direct(value, masks):
        return [swap(value, mask) for mask in masks], range(len(masks))

    xs, _ = direct(imu, across)
    own, mine = lax.optimization_barrier((jnp.concatenate([imu, camera[0]]), camera[0]))
    far = [swap(mine, core)]
    near = [mine if z == 0 else None if z & (z - 1) else swap(mine, along[z]) for z in range(nz)]

    def pair(mass, place, share):
        return [lax.dynamic_slice_in_dim(mass, (place ^ k) * share, share, 0) for k in range(2)]

    row, col = lax.axis_index("row"), lax.axis_index("col")
    mass = jnp.concatenate(pair(imu_mass, col, share_x) + pair(cam_mass, row, share_y))

    x, xt, first = row_lse_early(own, xs[1:], far[0])
    first, near, mass = lax.optimization_barrier((first, near, mass))
    for z in range(1, nz):
        if z & (z - 1):
            near[z] = swap(near[z & (z - 1)], along[z & -z])
    middle = near[1:-1]
    far += [swap(part, core) for part in middle]
    first = row_lse_middle(x, middle, first)
    first, last = lax.optimization_barrier((first, near[-1]))
    far.append(swap(last, core))
    y, sent = row_lse_late(own, x, [*middle, last, *far], first, mass, 2 * share_x)
    got, _ = direct(sent.reshape(-1), across)

    sent, e, shift, mass_a = column_lse(x, y, mass, 2 * share_y, got)
    sent = pair_of(lse2, sent, swap(sent.reshape(-1), core), cols, 1, 2)
    got = direct(sent.reshape(-1), along)

    sums, first_beta, mass_b = weighted(
        first_row_kernel, [(1, rows), (1, cols), (1, cols)], e, [shift], got, 2 * nz)
    for step in range(1, ITERS):
        if step > 1:
            sums, = weighted(row_kernel, [(1, rows)], e, [first_beta, mass_b], got, 2 * nz)
        got = direct(sums.reshape(-1), across)
        part, alpha = weighted(column_kernel, [(1, cols), (1, rows)], e, [mass_a, first_beta], got, na)
        part = pair_of(sum, part, swap(part.reshape(-1), core), cols, 1, 2)
        part, alpha = lax.optimization_barrier((part, alpha))
        got = direct(part.reshape(-1), along)

    gc, gc_send = column_grad(xt, y, e, alpha, first_beta, nz * share_y)
    yb, scale, last = first_rows([na - 1], share_x, x, y, e, alpha, first_beta, mass_b, got, 2 * nz)
    (grad_cam, *parts), yb = lax.optimization_barrier((shares(gc, swap(gc_send, core), nz), yb))
    parts = [swap(part, along[z + 1]) for z, part in enumerate(parts)]
    last = swap(last, across[na - 1])
    sent = other_rows(list(range(1, na - 1)), share_x, x, yb, e, alpha, jnp.bfloat16)
    sent, parts[0], last = lax.optimization_barrier((sent, parts[0], last))
    sent = [swap(part, across[s + 1]) for s, part in enumerate(sent)] + [last]
    gi, = other_rows([0], share_x, x, yb, e, alpha, jnp.float32)
    grad_imu, grad_cam = add_up([gi, *sent], [grad_cam, *parts], scale)
    return grad_imu, grad_cam[None]


def solution(mesh):
    in_specs = (P(("row", "col"), None), P("col", "row", None), P("row"), P("col"))
    out_specs = (P(("row", "col"), None), P("col", "row", None))
    return jax.shard_map(local, mesh=mesh, in_specs=in_specs, out_specs=out_specs, check_vma=False)
```

```python
import functools
import math

import jax
import jax.numpy as jnp
from jax import lax
from jax.experimental import pallas as pl
from jax.experimental.pallas import tpu as pltpu
from jax.sharding import PartitionSpec as P

D = 128
ITERS = 3
EPSILON = D / 20.0
LOG2E = math.log2(math.e)
CROSS = 2.0 * LOG2E / EPSILON
NT = (((1,), (1,)), ((), ()))
VMEM = pl.BlockSpec(memory_space=pltpu.VMEM)
GROUP = 64
HEAVY = 32


def spread(value, s_ref, sb_ref):
    chunks = value.shape[1] // 128
    for k in range(chunks):
        s_ref[k:k + 1, :] = value[:, k * 128:(k + 1) * 128]
    turned = jnp.transpose(s_ref[...])
    for k in range(chunks):
        sb_ref[k * 128:(k + 1) * 128, :] = jnp.broadcast_to(turned[:, k:k + 1], (128, 128))


def ordered(values, shifts, parts):
    share = values[0].shape[1] // parts
    return [
        jnp.concatenate([value[:, (k ^ s) * share:((k ^ s) + 1) * share] for k in range(parts)], axis=1)
        for value, s in zip(values, shifts)
    ]


def lse2(parts):
    top = functools.reduce(jnp.maximum, parts)
    return top + jnp.log2(sum(jnp.exp2(part - top) for part in parts))


def pipelined(places, chunk, width, a_ref, b_ref, d_ref, tile, finish):
    last = b_ref.shape[0] // width - 1

    def product(n, m):
        b = b_ref[pl.ds(pl.multiple_of(n * width, width), width), :]
        a = a_ref[places[m]:places[m] + chunk, :]
        d_ref[m % 2] = lax.dot_general(a, b, NT, preferred_element_type=jnp.float32)

    product(0, 0)

    def column(n, _):
        start = pl.multiple_of(n * width, width)
        state = None
        for m in range(len(places)):
            if m + 1 < len(places):
                product(n, m + 1)
            else:
                product(jnp.minimum(n + 1, last), 0)
            state = tile(m, start, state)
        finish(start, state)
        return 0

    lax.fori_loop(0, last + 1, column, 0)


def running_max(places, chunk, width, a_ref, b_ref, sb_ref, o_ref, e_ref, shift_ref):
    def column(n, _):
        start = pl.multiple_of(n * width, width)
        b = b_ref[pl.ds(start, width), :]

        def exponents(at):
            d = lax.dot_general(a_ref[at:at + chunk, :], b, NT, preferred_element_type=jnp.float32)
            s = sb_ref[at:at + chunk, :]
            return [d[:, q * 128:(q + 1) * 128] * CROSS + s for q in range(width // 128)]

        peak, total = jnp.full((1, width), -1e30, jnp.float32), jnp.zeros((1, width), jnp.float32)
        for at in places:
            peaks, totals = [], []
            for q, t in enumerate(exponents(at)):
                old = peak[:, q * 128:(q + 1) * 128]
                new = jnp.maximum(old, jnp.max(t, axis=0, keepdims=True))
                part = jnp.sum(jnp.exp2(t - new), axis=0, keepdims=True)
                peaks.append(new)
                totals.append(total[:, q * 128:(q + 1) * 128] * jnp.exp2(old - new) + part)
            peak, total = jnp.concatenate(peaks, axis=1), jnp.concatenate(totals, axis=1)
        o_ref[:, pl.ds(start, width)] = peak + jnp.log2(total)
        if e_ref is not None:
            shift_ref[:, pl.ds(start, width)] = peak
            for at in places:
                for q, t in enumerate(exponents(at)):
                    place = pl.ds(pl.multiple_of(start + q * 128, 128), 128)
                    e_ref[at:at + chunk, place] = jnp.exp2(t - shift_ref[:, place]).astype(jnp.bfloat16)
        return 0

    lax.fori_loop(0, b_ref.shape[0] // width, column, 0)


def lse_pass(places, chunk, width, a_ref, b_ref, sb_ref, d_ref, top_ref, o_ref, e_ref=None, shift_ref=None):
    tiles = width // 128
    top_ref[...] = jnp.zeros_like(top_ref)

    def lanes_of(start, q):
        return pl.ds(pl.multiple_of(start + q * 128, 128), 128)

    def tile(m, start, state):
        def exponents(g, q):
            at = g * GROUP
            s = sb_ref[places[m] + at:places[m] + at + GROUP, :]
            return d_ref[m % 2, at:at + GROUP, q * 128:(q + 1) * 128] * CROSS + s

        if m == 0:
            tops = [exponents(0, q) for q in range(tiles)]
            for g in range(1, 128 // GROUP):
                tops = [jnp.maximum(top, exponents(g, q)) for q, top in enumerate(tops)]
            state = [(jnp.max(top, axis=0, keepdims=True), jnp.zeros((GROUP, 128), jnp.float32)) for top in tops]
        for g in range(chunk // GROUP):
            for q, (peak, total) in enumerate(state):
                e = jnp.exp2(exponents(g, q) - peak)
                if e_ref is not None:
                    at = places[m] + g * GROUP
                    e_ref[at:at + GROUP, lanes_of(start, q)] = e.astype(jnp.bfloat16)
                state[q] = peak, total + e
        return state

    def finish(start, state):
        for q, (peak, total) in enumerate(state):
            top_ref[...] = jnp.maximum(top_ref[...], total)
            o_ref[:, lanes_of(start, q)] = peak + jnp.log2(jnp.sum(total, axis=0, keepdims=True))
            if e_ref is not None:
                shift_ref[:, lanes_of(start, q)] = peak

    pipelined(places, chunk, width, a_ref, b_ref, d_ref, tile, finish)

    @pl.when(jnp.logical_not(jnp.max(top_ref[...]) < 2.0 ** 60))
    def _():
        running_max(places, chunk, min(width, 256), a_ref, b_ref, sb_ref, o_ref, e_ref, shift_ref)


def put_norms(places, share, y_ref, sb_ref):
    for at in places:
        y = y_ref[at:at + share, :].astype(jnp.float32)
        total = jnp.sum(y * y, axis=1, keepdims=True) * (-LOG2E / EPSILON)
        sb_ref[at:at + share, :] = jnp.broadcast_to(total, (share, 128))


def join(out_ref, parts):
    at = 0
    for part in parts:
        out_ref[at:at + part.shape[0], :] = part[...]
        at += part.shape[0]


def row_lse_early_kernel(width, nx, own_ref, *refs):
    xs, y_other, refs = refs[:nx], refs[nx], refs[nx + 1:]
    x_ref, xt_ref, o_ref, y_ref, sb_ref, d_ref, top_ref = refs
    share = y_other.shape[0]
    mine = own_ref.shape[0] - share
    join(x_ref, [own_ref.at[:mine, :], *xs])
    join(y_ref, [own_ref.at[mine:, :], y_other])
    for k in range(x_ref.shape[0] // 128):
        at = k * 128
        xt_ref[:, at:at + 128] = jnp.transpose(x_ref[at:at + 128, :].astype(jnp.float32)).astype(jnp.bfloat16)
    places = [0, share]
    put_norms(places, share, y_ref, sb_ref)
    lse_pass(places, share, width, y_ref, x_ref, sb_ref, d_ref, top_ref, o_ref)


def row_lse_middle_kernel(width, ny, x_ref, first_ref, *refs):
    ys, (o_ref, y_ref, sb_ref, d_ref, top_ref, sum_ref) = refs[:ny], refs[ny:]
    share = ys[0].shape[0]
    join(y_ref, ys)
    places = [k * share for k in range(ny)]
    put_norms(places, share, y_ref, sb_ref)
    lse_pass(places, share, width, y_ref, x_ref, sb_ref, d_ref, top_ref, sum_ref)
    o_ref[...] = lse2([first_ref[...], sum_ref[...]])


def row_lse_late_kernel(width, ny, own_ref, mass_ref, x_ref, first_ref, *refs):
    ys, (y_ref, o_ref, sb_ref, d_ref, top_ref, sum_ref) = refs[:ny], refs[ny:]
    share, rows, half = ys[0].shape[0], x_ref.shape[0], (ny + 1) // 2
    join(y_ref, [own_ref.at[own_ref.shape[0] - share:, :], *ys])
    places = [k * share for k in range(half - 1, 2 * half) if k != half]
    put_norms(places, share, y_ref, sb_ref)
    lse_pass(places, share, width, y_ref, x_ref, sb_ref, d_ref, top_ref, sum_ref)
    o_ref[:, :rows] = lse2([first_ref[...], sum_ref[...]])
    o_ref[:, rows:] = mass_ref[:, :o_ref.shape[1] - rows]


def column_lse_kernel(width, chunk, na, x_ref, y_ref, mass_ref, *refs):
    got, (o_ref, e_ref, shift_ref, a_ref, s_ref, sb_ref, d_ref, top_ref) = refs[:na], refs[na:]
    rows, cols = x_ref.shape[0], y_ref.shape[0]
    o_ref[:, cols:] = mass_ref[:, mass_ref.shape[1] - o_ref.shape[1] + cols:]
    share = rows // na
    for k in range(na):
        at = rows + (k % 2) * share
        a_ref[:, k * share:(k + 1) * share] = got[k - k % 2][:, at:at + share]
    u = jnp.log2(a_ref[...]) - lse2(ordered([part[:, :rows] for part in got], range(na), na))
    spread(u, s_ref, sb_ref)
    places = list(range(0, rows, chunk))
    lse_pass(places, chunk, width, x_ref, y_ref, sb_ref, d_ref, top_ref, o_ref, e_ref, shift_ref)


def pair_kernel(size, shift, parts, combine, one_ref, two_ref, o_ref):
    two, = ordered([two_ref[:, :size]], [shift], parts)
    o_ref[:, :size] = combine([one_ref[:, :size], two])
    if o_ref.shape[1] > size:
        o_ref[:, size:] = one_ref[:, size:]


def split3(value):
    high = value.astype(jnp.bfloat16)
    rest = value - high.astype(jnp.float32)
    mid = rest.astype(jnp.bfloat16)
    return high, mid, (rest - mid.astype(jnp.float32)).astype(jnp.bfloat16)


def stacked(value):
    high, mid, low = [part.astype(jnp.float32) for part in split3(value)]
    dims = (16, value.shape[1])
    place = lax.broadcasted_iota(jnp.int32, dims, 0)
    parts = jnp.where(place == 0, high, jnp.where(place == 1, mid, jnp.where(place == 2, low, 0.0)))
    return parts.astype(jnp.bfloat16)


def row_sums(width, e_ref, w_ref, w16_ref, acc_ref, o_ref):
    rows, cols = e_ref.shape
    half = rows - acc_ref.shape[0]
    for at in range(0, half, width):
        got = lax.dot_general(w16_ref[...], e_ref[at:at + width, :], NT, preferred_element_type=jnp.float32)
        for k in range(at, at + width, 64):
            total = jnp.zeros((64, 128), jnp.float32)
            for q in range(0, cols, 128):
                e = e_ref[half + k:half + k + 64, q:q + 128].astype(jnp.float32)
                total = total + e * w_ref[:, q:q + 128]
            acc_ref[k:k + 64, :] = total
        o_ref[:, at:at + width] = jnp.sum(got, axis=0, keepdims=True)
    for at in range(0, rows - half, 128):
        total = jnp.sum(jnp.transpose(acc_ref[at:at + 128, :]), axis=0, keepdims=True)
        o_ref[:, half + at:half + at + 128] = total


def first_row_kernel(width, shifts, parts, e_ref, shift_ref, *refs):
    nz = len(shifts)
    got, (o_ref, beta_ref, b_ref, w16_ref, acc_ref) = refs[:nz], refs[nz:]
    cols = e_ref.shape[1]
    share = cols // parts
    for k in range(parts):
        at = cols + (k // nz) * share
        b_ref[:, k * share:(k + 1) * share] = got[k % nz][:, at:at + share]
    lse = lse2(ordered([part[:, :cols] for part in got], shifts, parts))
    beta_ref[...] = jnp.exp2(jnp.log2(b_ref[...]) - lse + shift_ref[...])
    w16_ref[...] = stacked(beta_ref[...])
    row_sums(width, e_ref, beta_ref, w16_ref, acc_ref, o_ref)


def new_scale(b_ref, got, shifts, parts):
    return b_ref[...] / sum(ordered([part[...] for part in got], shifts, parts))


def row_kernel(width, shifts, parts, e_ref, first_ref, b_ref, *refs):
    got, (o_ref, w16_ref, acc_ref, w_ref) = refs[:-4], refs[-4:]
    w_ref[...] = first_ref[...] * new_scale(b_ref, got, shifts, parts)
    w16_ref[...] = stacked(w_ref[...])
    row_sums(width, e_ref, w_ref, w16_ref, acc_ref, o_ref)


def column_kernel(width, shifts, parts, e_ref, a_ref, first_ref, *refs):
    got, (o_ref, alpha_ref, w16_ref) = refs[:-3], refs[-3:]
    alpha_ref[...] = a_ref[...] / sum(ordered([part[...] for part in got], shifts, parts))
    w16_ref[...] = stacked(alpha_ref[...])
    for at in range(0, e_ref.shape[1], width):
        sums = jnp.dot(w16_ref[...], e_ref[:, at:at + width], preferred_element_type=jnp.float32)
        o_ref[:, at:at + width] = first_ref[:, at:at + width] * jnp.sum(sums, axis=0, keepdims=True)


def flat(value):
    return value.reshape(1, -1) if value.ndim == 1 else value


def weighted(kernel, outs, e, rows, got, parts):
    got, shifts = got
    size = e.shape[0] if kernel is column_kernel else e.shape[1]
    width = 512 if kernel is column_kernel else 256
    scratch = [pltpu.VMEM((16, size), jnp.bfloat16)]
    if kernel is not column_kernel:
        scratch.append(pltpu.VMEM((e.shape[0] // 2, 128), jnp.float32))
    if kernel is row_kernel:
        scratch.append(pltpu.VMEM((1, size), jnp.float32))
    return pl.pallas_call(
        functools.partial(kernel, width, tuple(shifts), parts),
        out_shape=[shape(*dims) for dims in outs],
        in_specs=[VMEM] * (1 + len(rows) + len(got)),
        out_specs=[VMEM] * len(outs),
        scratch_shapes=scratch,
        compiler_params=pltpu.CompilerParams(vmem_limit_bytes=16 << 20),
        cost_estimate=pl.CostEstimate(flops=2 * e.size, bytes_accessed=2 * e.size, transcendentals=0),
        name="weighted_sum",
    )(e, *rows, *[flat(part) for part in got])


def pass_cost(depth, lanes):
    return pl.CostEstimate(flops=2 * depth * lanes * D, bytes_accessed=2 * D * (depth + lanes), transcendentals=depth * lanes)


def shape(*dims, dtype=jnp.float32):
    return jax.ShapeDtypeStruct(dims, dtype)


def lse_scratch(depth, chunk, width):
    return [
        pltpu.VMEM((depth, 128), jnp.float32),
        pltpu.VMEM((2, chunk, width), jnp.float32),
        pltpu.VMEM((GROUP, 128), jnp.float32),
    ]


def row_lse_early(own, xs, y_other, width=1024):
    share = y_other.shape[0]
    rows, depth = own.shape[0] - share + sum(part.shape[0] for part in xs), 2 * share
    return pl.pallas_call(
        functools.partial(row_lse_early_kernel, width, len(xs)),
        out_shape=(shape(rows, D, dtype=jnp.bfloat16), shape(D, rows, dtype=jnp.bfloat16), shape(1, rows)),
        in_specs=[VMEM] * (len(xs) + 2),
        out_specs=(VMEM,) * 3,
        scratch_shapes=[pltpu.VMEM((depth, D), jnp.bfloat16), *lse_scratch(depth, share, width)],
        compiler_params=pltpu.CompilerParams(vmem_limit_bytes=16 << 20),
        cost_estimate=pass_cost(depth, rows),
        name="row_lse_early",
    )(own, *xs, y_other)


def row_lse_middle(x, ys, first, width=1024):
    rows, share = x.shape[0], ys[0].shape[0]
    depth = len(ys) * share
    return pl.pallas_call(
        functools.partial(row_lse_middle_kernel, width, len(ys)),
        out_shape=shape(1, rows),
        in_specs=[VMEM] * (len(ys) + 2),
        out_specs=VMEM,
        scratch_shapes=[
            pltpu.VMEM((depth, D), jnp.bfloat16),
            *lse_scratch(depth, share, width),
            pltpu.VMEM((1, rows), jnp.float32),
        ],
        compiler_params=pltpu.CompilerParams(vmem_limit_bytes=16 << 20),
        cost_estimate=pass_cost(depth, rows),
        name="row_lse_middle",
    )(x, first, *ys)


def row_lse_late(own, x, ys, first, mass, tail, width=1024):
    rows, share = x.shape[0], ys[0].shape[0]
    depth = (len(ys) + 1) * share
    return pl.pallas_call(
        functools.partial(row_lse_late_kernel, width, len(ys)),
        out_shape=(shape(depth, D, dtype=jnp.bfloat16), shape(1, rows + tail)),
        in_specs=[VMEM] * (len(ys) + 4),
        out_specs=(VMEM,) * 2,
        scratch_shapes=[*lse_scratch(depth, share, width), pltpu.VMEM((1, rows), jnp.float32)],
        compiler_params=pltpu.CompilerParams(vmem_limit_bytes=16 << 20),
        cost_estimate=pass_cost(depth // 2, rows),
        name="row_lse_late",
    )(own, mass.reshape(1, -1), x, first, *ys)


def column_lse(x, y, mass, tail, got, width=512, chunk=512):
    rows, cols = x.shape[0], y.shape[0]
    return pl.pallas_call(
        functools.partial(column_lse_kernel, width, chunk, len(got)),
        out_shape=(shape(1, cols + tail), shape(rows, cols, dtype=jnp.bfloat16), shape(1, cols), shape(1, rows)),
        in_specs=[VMEM] * (3 + len(got)),
        out_specs=(VMEM,) * 4,
        scratch_shapes=[pltpu.VMEM((rows // 128, 128), jnp.float32), *lse_scratch(rows, chunk, width)],
        compiler_params=pltpu.CompilerParams(vmem_limit_bytes=16 << 20),
        cost_estimate=pass_cost(rows, cols),
        name="column_lse",
    )(x, y, mass.reshape(1, -1), *[part.reshape(1, -1) for part in got])


def pair_of(combine, one, two, size, shift, parts):
    whole = one.shape[-1]
    return pl.pallas_call(
        functools.partial(pair_kernel, size, shift, parts, combine),
        out_shape=shape(1, whole),
        in_specs=[VMEM] * 2,
        out_specs=VMEM,
        compiler_params=pltpu.CompilerParams(vmem_limit_bytes=16 << 20),
        name="pair",
    )(one.reshape(1, whole), two.reshape(1, whole))


def high_low(value):
    high = value.astype(jnp.bfloat16)
    return high, (value - high.astype(jnp.float32)).astype(jnp.bfloat16)


def column_grad_kernel(width, xt_ref, y_ref, e_ref, alpha_ref, first_ref, own_ref, sent_ref,
                       bb_ref, cb_ref, xa_ref, s_ref, count_ref, acc_ref):
    rows, cols = xt_ref.shape[1], y_ref.shape[0]
    own = own_ref.shape[0]
    spread(first_ref[...], s_ref, bb_ref)
    place = lax.broadcasted_iota(jnp.int32, (128, 512), 0)
    for at in range(0, rows, 512):
        alpha = alpha_ref[:, at:at + 512]
        high, low = high_low(xt_ref[:, at:at + 512].astype(jnp.float32) * alpha)
        first, second = high_low(alpha)
        low = jnp.where(place == 126, first.astype(jnp.float32), low.astype(jnp.float32))
        low = jnp.where(place == 127, second.astype(jnp.float32), low)
        xa_ref[:128, at:at + 512] = high
        xa_ref[128:, at:at + 512] = low.astype(jnp.bfloat16)

    lower = lax.broadcasted_iota(jnp.int32, (128, width), 0) < 126
    for at in range(0, cols, width):
        got = jnp.dot(xa_ref[...], e_ref[:, at:at + width], preferred_element_type=jnp.float32)
        acc_ref[:, at:at + width] = got[:128] + jnp.where(lower, got[128:], 0.0)
        count_ref[:, at:at + width] = got[254:255] + got[255:256]
    spread(count_ref[...], s_ref, cb_ref)
    for at in range(0, cols, 128):
        pulled = jnp.transpose(acc_ref[:, at:at + 128])
        whole = cb_ref[at:at + 128, :] * y_ref[at:at + 128, :].astype(jnp.float32)
        grad = bb_ref[at:at + 128, :] * (whole - pulled)
        if at < own:
            own_ref[at:at + 128, :] = grad
        else:
            sent_ref[at - own:at - own + 128, :] = grad.astype(jnp.bfloat16)


def column_grad(xt, y, e, alpha, first, own, width=512):
    rows, cols = xt.shape[1], y.shape[0]
    return pl.pallas_call(
        functools.partial(column_grad_kernel, width),
        out_shape=(shape(own, D), shape(cols - own, D, dtype=jnp.bfloat16)),
        in_specs=[VMEM] * 5,
        out_specs=(VMEM,) * 2,
        scratch_shapes=[
            pltpu.VMEM((cols, 128), jnp.float32),
            pltpu.VMEM((cols, 128), jnp.float32),
            pltpu.VMEM((256, rows), jnp.bfloat16),
            pltpu.VMEM((cols // 128, 128), jnp.float32),
            pltpu.VMEM((1, cols), jnp.float32),
            pltpu.VMEM((128, cols), jnp.float32),
        ],
        compiler_params=pltpu.CompilerParams(vmem_limit_bytes=16 << 20),
        cost_estimate=pl.CostEstimate(flops=4 * e.size * D, bytes_accessed=2 * e.size, transcendentals=0),
        name="column_grad",
    )(xt, y, e, alpha, first)


def row_block(at, chunk, x_ref, e_ref, yb_ref, scale):
    got = jnp.dot(e_ref[pl.ds(at, chunk), :], yb_ref[...], preferred_element_type=jnp.float32)
    lower = lax.broadcasted_iota(jnp.int32, (chunk, 128), 1) < 126
    total = got[:, 254:255] + got[:, 255:256]
    pulled = got[:, :128] + jnp.where(lower, got[:, 128:], 0.0)
    x = x_ref[pl.ds(at, chunk), :].astype(jnp.float32)
    return 2.0 * scale * (total * x - pulled)


def put_yb(y_ref, beta, yb_ref, s_ref, bb_ref):
    spread(beta, s_ref, bb_ref)
    place = lax.broadcasted_iota(jnp.int32, (256, 128), 1)
    for at in range(0, y_ref.shape[0], 256):
        beta = bb_ref[at:at + 256, :]
        high, low = high_low(y_ref[at:at + 256, :].astype(jnp.float32) * beta)
        first, second = high_low(beta)
        low = jnp.where(place == 126, first.astype(jnp.float32), low.astype(jnp.float32))
        low = jnp.where(place == 127, second.astype(jnp.float32), low)
        yb_ref[at:at + 256, :128] = high
        yb_ref[at:at + 256, 128:] = low.astype(jnp.bfloat16)


def row_parts(parts, x_ref, e_ref, alpha_ref, yb_ref, outs, sa_ref, ab_ref):
    share = outs[0].shape[0]
    chunk = math.gcd(share, 512)
    for part, out_ref in zip(parts, outs):
        spread(alpha_ref[:, part * share:(part + 1) * share], sa_ref, ab_ref)
        for k in range(0, share, chunk):
            grad = row_block(part * share + k, chunk, x_ref, e_ref, yb_ref, ab_ref[k:k + chunk, :])
            out_ref[k:k + chunk, :] = grad.astype(out_ref.dtype)


def first_rows_kernel(parts, shifts, blocks, nz, x_ref, y_ref, e_ref, alpha_ref, first_ref, b_ref, *refs):
    got, (yb_ref, scale_ref, *outs), (s_ref, bb_ref, sa_ref, ab_ref) = refs[:nz], refs[nz:-4], refs[-4:]
    scale = new_scale(b_ref, got, shifts, blocks)
    scale_ref[...] = scale[:, :scale_ref.shape[1]]
    put_yb(y_ref, first_ref[...] * scale, yb_ref, s_ref, bb_ref)
    row_parts(parts, x_ref, e_ref, alpha_ref, yb_ref, outs, sa_ref, ab_ref)


def rows_kernel(parts, x_ref, yb_ref, e_ref, alpha_ref, *refs):
    row_parts(parts, x_ref, e_ref, alpha_ref, yb_ref, refs[:-2], *refs[-2:])


def rows_scratch(share):
    return [pltpu.VMEM((share // 128, 128), jnp.float32), pltpu.VMEM((share, 128), jnp.float32)]


def rows_cost(share, parts, cols):
    size = share * len(parts) * cols
    return pl.CostEstimate(flops=4 * size * D, bytes_accessed=2 * size, transcendentals=0)


def first_rows(parts, share, x, y, e, alpha, first, mass, got, blocks):
    cols = y.shape[0]
    got, shifts = got
    return pl.pallas_call(
        functools.partial(first_rows_kernel, parts, tuple(shifts), blocks, len(got)),
        out_shape=[shape(cols, 256, dtype=jnp.bfloat16), shape(1, cols // blocks)]
        + [shape(share, D, dtype=jnp.bfloat16)] * len(parts),
        in_specs=[VMEM] * (6 + len(got)),
        out_specs=[VMEM] * (2 + len(parts)),
        scratch_shapes=[
            pltpu.VMEM((cols // 128, 128), jnp.float32),
            pltpu.VMEM((cols, 128), jnp.float32),
            *rows_scratch(share),
        ],
        compiler_params=pltpu.CompilerParams(vmem_limit_bytes=16 << 20),
        cost_estimate=rows_cost(share * HEAVY, parts, cols),
        name="first_rows",
    )(x, y, e, alpha, first, mass, *[flat(part) for part in got])


def other_rows(parts, share, x, yb, e, alpha, dtype):
    return pl.pallas_call(
        functools.partial(rows_kernel, parts),
        out_shape=[shape(share, D, dtype=dtype)] * len(parts),
        in_specs=[VMEM] * 4,
        out_specs=[VMEM] * len(parts),
        scratch_shapes=rows_scratch(share),
        compiler_params=pltpu.CompilerParams(vmem_limit_bytes=16 << 20),
        cost_estimate=rows_cost(share, parts, yb.shape[0]),
        name="other_rows",
    )(x, yb, e, alpha)


def add_up_kernel(na, scale_ref, *refs):
    ins, (rows_ref, cols_ref, s_ref, sb_ref) = refs[:-4], refs[-4:]
    rows_ref[...] = sum(part[...].astype(jnp.float32) for part in ins[:na])
    spread(scale_ref[...], s_ref, sb_ref)
    cols_ref[...] = 2.0 * sb_ref[...] * sum(part[...].astype(jnp.float32) for part in ins[na:])


def add_up(rows, columns, scale):
    share = scale.shape[1]
    return pl.pallas_call(
        functools.partial(add_up_kernel, len(rows)),
        out_shape=(shape(*rows[0].shape), shape(*columns[0].shape)),
        in_specs=[VMEM] * (1 + len(rows) + len(columns)),
        out_specs=(VMEM,) * 2,
        scratch_shapes=rows_scratch(share),
        compiler_params=pltpu.CompilerParams(vmem_limit_bytes=16 << 20),
        name="add_up",
    )(scale, *rows, *columns)


def shares_kernel(gc_ref, other_ref, own_ref, *outs):
    share = own_ref.shape[0]
    for k in range(len(outs) + 1):
        at = k * share
        total = gc_ref[at:at + share, :] + other_ref[at:at + share, :].astype(jnp.float32)
        if k == 0:
            own_ref[...] = total
        else:
            outs[k - 1][...] = total.astype(jnp.bfloat16)


def shares(gc, other, count):
    share = gc.shape[0] // count
    return pl.pallas_call(
        shares_kernel,
        out_shape=[shape(share, D)] + [shape(share, D, dtype=jnp.bfloat16)] * (count - 1),
        in_specs=[VMEM] * 2,
        out_specs=[VMEM] * count,
        compiler_params=pltpu.CompilerParams(vmem_limit_bytes=16 << 20),
        name="shares",
    )(gc, other)


class Groups:
    def __init__(self, nrow, ncol):
        self.count = nrow * ncol
        self.across = [(a << 1) * ncol + b for a in range(nrow // 2) for b in range(2)]
        self.along = [z << 1 for z in range(ncol // 2)]
        self.core = ncol

    def swap(self, value, mask):
        if mask == 0:
            return value
        return lax.ppermute(value, ("row", "col"), [(i, i ^ mask) for i in range(self.count)])


def local(imu, camera, imu_mass, cam_mass):
    nrow, ncol = lax.axis_size("row"), lax.axis_size("col")
    groups = Groups(nrow, ncol)
    swap, across, along, core = groups.swap, groups.across, groups.along, groups.core
    na, nz = len(across), len(along)
    share_x, share_y = imu.shape[0], camera.shape[1]
    rows, cols = na * share_x, 2 * nz * share_y

    def direct(value, masks):
        return [swap(value, mask) for mask in masks], range(len(masks))

    xs, _ = direct(imu, across)
    own, mine = lax.optimization_barrier((jnp.concatenate([imu, camera[0]]), camera[0]))
    near = [mine] + [None] * (nz - 1)
    for z in range(1, nz):
        if not z & (z - 1):
            near[z] = swap(mine if z == 1 else camera[0], along[z])
    far = [swap(mine, core)]

    def pair(mass, place, share):
        return [lax.dynamic_slice_in_dim(mass, (place ^ k) * share, share, 0) for k in range(2)]

    row, col = lax.axis_index("row"), lax.axis_index("col")
    mass = jnp.concatenate(pair(imu_mass, col, share_x) + pair(cam_mass, row, share_y))

    x, xt, first = row_lse_early(own, xs[1:], far[0])
    relays = [z for z in range(2, nz) if not z & (z - 1)]
    first, mass, got = lax.optimization_barrier((first, mass, [near[z] for z in relays]))
    for z, part in zip(relays, got):
        near[z] = part
    for z in range(1, nz):
        if z & (z - 1):
            near[z] = swap(near[z & (z - 1)], along[z & -z])
    middle = near[1:-1]
    far += [swap(part, core) for part in middle]
    first = row_lse_middle(x, middle, first)
    first, last = lax.optimization_barrier((first, near[-1]))
    far.append(swap(last, core))
    y, sent = row_lse_late(own, x, [*middle, last, *far], first, mass, 2 * share_x)
    got, _ = direct(sent.reshape(-1), across)

    sent, e, shift, mass_a = column_lse(x, y, mass, 2 * share_y, got)
    sent = pair_of(lse2, sent, swap(sent.reshape(-1), core), cols, 1, 2)
    got = direct(sent.reshape(-1), along)

    sums, first_beta, mass_b = weighted(
        first_row_kernel, [(1, rows), (1, cols), (1, cols)], e, [shift], got, 2 * nz)
    for step in range(1, ITERS):
        if step > 1:
            sums, = weighted(row_kernel, [(1, rows)], e, [first_beta, mass_b], got, 2 * nz)
        got = direct(sums.reshape(-1), across)
        part, alpha = weighted(column_kernel, [(1, cols), (1, rows)], e, [mass_a, first_beta], got, na)
        part = pair_of(sum, part, swap(part.reshape(-1), core), cols, 1, 2)
        part, alpha = lax.optimization_barrier((part, alpha))
        got = direct(part.reshape(-1), along)

    gc, gc_send = column_grad(xt, y, e, alpha, first_beta, nz * share_y)
    yb, scale, last = first_rows([na - 1], share_x, x, y, e, alpha, first_beta, mass_b, got, 2 * nz)
    (grad_cam, *parts), yb = lax.optimization_barrier((shares(gc, swap(gc_send, core), nz), yb))
    parts = [swap(part, along[z + 1]) for z, part in enumerate(parts)]
    last = swap(last, across[na - 1])
    sent = other_rows(list(range(1, na - 1)), share_x, x, yb, e, alpha, jnp.bfloat16)
    sent, parts[0], last = lax.optimization_barrier((sent, parts[0], last))
    sent = [swap(part, across[s + 1]) for s, part in enumerate(sent)] + [last]
    gi, = other_rows([0], share_x, x, yb, e, alpha, jnp.float32)
    grad_imu, grad_cam = add_up([gi, *sent], [grad_cam, *parts], scale)
    return grad_imu, grad_cam[None]


def solution(mesh):
    in_specs = (P(("row", "col"), None), P("col", "row", None), P("row"), P("col"))
    out_specs = (P(("row", "col"), None), P("col", "row", None))
    return jax.shard_map(local, mesh=mesh, in_specs=in_specs, out_specs=out_specs, check_vma=False)
```

```python
import functools
import math

import jax
import jax.numpy as jnp
from jax import lax
from jax.experimental import pallas as pl
from jax.experimental.pallas import tpu as pltpu
from jax.sharding import PartitionSpec as P

D = 128
ITERS = 3
EPSILON = D / 20.0
LOG2E = math.log2(math.e)
CROSS = 2.0 * LOG2E / EPSILON
NT = (((1,), (1,)), ((), ()))
VMEM = pl.BlockSpec(memory_space=pltpu.VMEM)
GROUP = 16
HEAVY = 32


def spread(value, s_ref, sb_ref):
    chunks = value.shape[1] // 128
    for k in range(chunks):
        s_ref[k:k + 1, :] = value[:, k * 128:(k + 1) * 128]
    turned = jnp.transpose(s_ref[...])
    for k in range(chunks):
        sb_ref[k * 128:(k + 1) * 128, :] = jnp.broadcast_to(turned[:, k:k + 1], (128, 128))


def ordered(values, shifts, parts):
    share = values[0].shape[1] // parts
    return [
        jnp.concatenate([value[:, (k ^ s) * share:((k ^ s) + 1) * share] for k in range(parts)], axis=1)
        for value, s in zip(values, shifts)
    ]


def lse2(parts):
    top = functools.reduce(jnp.maximum, parts)
    return top + jnp.log2(sum(jnp.exp2(part - top) for part in parts))


def pipelined(places, chunk, width, a_ref, b_ref, d_ref, tile, finish):
    last = b_ref.shape[0] // width - 1

    def product(n, m):
        b = b_ref[pl.ds(pl.multiple_of(n * width, width), width), :]
        a = a_ref[places[m]:places[m] + chunk, :]
        d_ref[m % 2] = lax.dot_general(a, b, NT, preferred_element_type=jnp.float32)

    product(0, 0)

    def column(n, _):
        start = pl.multiple_of(n * width, width)
        state = None
        for m in range(len(places)):
            if m + 1 < len(places):
                product(n, m + 1)
            else:
                product(jnp.minimum(n + 1, last), 0)
            state = tile(m, start, state)
        finish(start, state)
        return 0

    lax.fori_loop(0, last + 1, column, 0)


def running_max(places, chunk, width, a_ref, b_ref, sb_ref, o_ref, e_ref, shift_ref):
    def column(n, _):
        start = pl.multiple_of(n * width, width)
        b = b_ref[pl.ds(start, width), :]

        def exponents(at):
            d = lax.dot_general(a_ref[at:at + chunk, :], b, NT, preferred_element_type=jnp.float32)
            s = sb_ref[at:at + chunk, :]
            return [d[:, q * 128:(q + 1) * 128] * CROSS + s for q in range(width // 128)]

        peak, total = jnp.full((1, width), -1e30, jnp.float32), jnp.zeros((1, width), jnp.float32)
        for at in places:
            peaks, totals = [], []
            for q, t in enumerate(exponents(at)):
                old = peak[:, q * 128:(q + 1) * 128]
                new = jnp.maximum(old, jnp.max(t, axis=0, keepdims=True))
                part = jnp.sum(jnp.exp2(t - new), axis=0, keepdims=True)
                peaks.append(new)
                totals.append(total[:, q * 128:(q + 1) * 128] * jnp.exp2(old - new) + part)
            peak, total = jnp.concatenate(peaks, axis=1), jnp.concatenate(totals, axis=1)
        o_ref[:, pl.ds(start, width)] = peak + jnp.log2(total)
        if e_ref is not None:
            shift_ref[:, pl.ds(start, width)] = peak
            for at in places:
                for q, t in enumerate(exponents(at)):
                    place = pl.ds(pl.multiple_of(start + q * 128, 128), 128)
                    e_ref[at:at + chunk, place] = jnp.exp2(t - shift_ref[:, place]).astype(jnp.bfloat16)
        return 0

    lax.fori_loop(0, b_ref.shape[0] // width, column, 0)


def lse_pass(places, chunk, width, a_ref, b_ref, sb_ref, d_ref, top_ref, o_ref, e_ref=None, shift_ref=None):
    tiles = width // 128
    top_ref[...] = jnp.zeros_like(top_ref)

    def lanes_of(start, q):
        return pl.ds(pl.multiple_of(start + q * 128, 128), 128)

    def tile(m, start, state):
        def exponents(g, q):
            at = g * GROUP
            s = sb_ref[places[m] + at:places[m] + at + GROUP, :]
            return d_ref[m % 2, at:at + GROUP, q * 128:(q + 1) * 128] * CROSS + s

        if m == 0:
            tops = [exponents(0, q) for q in range(tiles)]
            for g in range(1, 128 // GROUP):
                tops = [jnp.maximum(top, exponents(g, q)) for q, top in enumerate(tops)]
            state = [(jnp.max(top, axis=0, keepdims=True), jnp.zeros((GROUP, 128), jnp.float32)) for top in tops]
        for g in range(chunk // GROUP):
            for q, (peak, total) in enumerate(state):
                e = jnp.exp2(exponents(g, q) - peak)
                if e_ref is not None:
                    at = places[m] + g * GROUP
                    e_ref[at:at + GROUP, lanes_of(start, q)] = e.astype(jnp.bfloat16)
                state[q] = peak, total + e
        return state

    def finish(start, state):
        for q, (peak, total) in enumerate(state):
            top_ref[...] = jnp.maximum(top_ref[...], total)
            o_ref[:, lanes_of(start, q)] = peak + jnp.log2(jnp.sum(total, axis=0, keepdims=True))
            if e_ref is not None:
                shift_ref[:, lanes_of(start, q)] = peak

    pipelined(places, chunk, width, a_ref, b_ref, d_ref, tile, finish)

    @pl.when(jnp.logical_not(jnp.max(top_ref[...]) < 2.0 ** 60))
    def _():
        running_max(places, chunk, min(width, 256), a_ref, b_ref, sb_ref, o_ref, e_ref, shift_ref)


def put_norms(places, share, y_ref, sb_ref):
    for at in places:
        y = y_ref[at:at + share, :].astype(jnp.float32)
        total = jnp.sum(y * y, axis=1, keepdims=True) * (-LOG2E / EPSILON)
        sb_ref[at:at + share, :] = jnp.broadcast_to(total, (share, 128))


def join(out_ref, parts):
    at = 0
    for part in parts:
        out_ref[at:at + part.shape[0], :] = part[...]
        at += part.shape[0]


def row_lse_early_kernel(width, nx, own_ref, *refs):
    xs, y_other, refs = refs[:nx], refs[nx], refs[nx + 1:]
    x_ref, xt_ref, o_ref, y_ref, sb_ref, d_ref, top_ref = refs
    share = y_other.shape[0]
    mine = own_ref.shape[0] - share
    join(x_ref, [own_ref.at[:mine, :], *xs])
    join(y_ref, [own_ref.at[mine:, :], y_other])
    for k in range(x_ref.shape[0] // 128):
        at = k * 128
        xt_ref[:, at:at + 128] = jnp.transpose(x_ref[at:at + 128, :].astype(jnp.float32)).astype(jnp.bfloat16)
    places = [0, share]
    put_norms(places, share, y_ref, sb_ref)
    lse_pass(places, share, width, y_ref, x_ref, sb_ref, d_ref, top_ref, o_ref)


def row_lse_middle_kernel(width, ny, x_ref, first_ref, *refs):
    ys, (o_ref, y_ref, sb_ref, d_ref, top_ref, sum_ref) = refs[:ny], refs[ny:]
    share = ys[0].shape[0]
    join(y_ref, ys)
    places = [k * share for k in range(ny)]
    put_norms(places, share, y_ref, sb_ref)
    lse_pass(places, share, width, y_ref, x_ref, sb_ref, d_ref, top_ref, sum_ref)
    o_ref[...] = lse2([first_ref[...], sum_ref[...]])


def row_lse_late_kernel(width, ny, own_ref, mass_ref, x_ref, first_ref, *refs):
    ys, (y_ref, o_ref, sb_ref, d_ref, top_ref, sum_ref) = refs[:ny], refs[ny:]
    share, rows, half = ys[0].shape[0], x_ref.shape[0], (ny + 1) // 2
    join(y_ref, [own_ref.at[own_ref.shape[0] - share:, :], *ys])
    places = [k * share for k in range(half - 1, 2 * half) if k != half]
    put_norms(places, share, y_ref, sb_ref)
    lse_pass(places, share, width, y_ref, x_ref, sb_ref, d_ref, top_ref, sum_ref)
    o_ref[:, :rows] = lse2([first_ref[...], sum_ref[...]])
    o_ref[:, rows:] = mass_ref[:, :o_ref.shape[1] - rows]


def column_lse_kernel(width, chunk, na, x_ref, y_ref, mass_ref, *refs):
    got, (o_ref, e_ref, shift_ref, a_ref, s_ref, sb_ref, d_ref, top_ref) = refs[:na], refs[na:]
    rows, cols = x_ref.shape[0], y_ref.shape[0]
    o_ref[:, cols:] = mass_ref[:, mass_ref.shape[1] - o_ref.shape[1] + cols:]
    share = rows // na
    for k in range(na):
        at = rows + (k % 2) * share
        a_ref[:, k * share:(k + 1) * share] = got[k - k % 2][:, at:at + share]
    u = jnp.log2(a_ref[...]) - lse2(ordered([part[:, :rows] for part in got], range(na), na))
    spread(u, s_ref, sb_ref)
    places = list(range(0, rows, chunk))
    lse_pass(places, chunk, width, x_ref, y_ref, sb_ref, d_ref, top_ref, o_ref, e_ref, shift_ref)


def pair_kernel(size, shift, parts, combine, one_ref, two_ref, o_ref):
    two, = ordered([two_ref[:, :size]], [shift], parts)
    o_ref[:, :size] = combine([one_ref[:, :size], two])
    if o_ref.shape[1] > size:
        o_ref[:, size:] = one_ref[:, size:]


def split3(value):
    high = value.astype(jnp.bfloat16)
    rest = value - high.astype(jnp.float32)
    mid = rest.astype(jnp.bfloat16)
    return high, mid, (rest - mid.astype(jnp.float32)).astype(jnp.bfloat16)


def stacked(value):
    high, mid, low = [part.astype(jnp.float32) for part in split3(value)]
    dims = (16, value.shape[1])
    place = lax.broadcasted_iota(jnp.int32, dims, 0)
    parts = jnp.where(place == 0, high, jnp.where(place == 1, mid, jnp.where(place == 2, low, 0.0)))
    return parts.astype(jnp.bfloat16)


def row_sums(width, e_ref, w_ref, w16_ref, acc_ref, o_ref):
    rows, cols = e_ref.shape
    half = rows - acc_ref.shape[0]
    for at in range(0, half, width):
        got = lax.dot_general(w16_ref[...], e_ref[at:at + width, :], NT, preferred_element_type=jnp.float32)
        for k in range(at, at + width, 64):
            total = jnp.zeros((64, 128), jnp.float32)
            for q in range(0, cols, 128):
                e = e_ref[half + k:half + k + 64, q:q + 128].astype(jnp.float32)
                total = total + e * w_ref[:, q:q + 128]
            acc_ref[k:k + 64, :] = total
        o_ref[:, at:at + width] = jnp.sum(got, axis=0, keepdims=True)
    for at in range(0, rows - half, 128):
        total = jnp.sum(jnp.transpose(acc_ref[at:at + 128, :]), axis=0, keepdims=True)
        o_ref[:, half + at:half + at + 128] = total


def first_row_kernel(width, shifts, parts, e_ref, shift_ref, *refs):
    nz = len(shifts)
    got, (o_ref, beta_ref, b_ref, w16_ref, acc_ref) = refs[:nz], refs[nz:]
    cols = e_ref.shape[1]
    share = cols // parts
    for k in range(parts):
        at = cols + (k // nz) * share
        b_ref[:, k * share:(k + 1) * share] = got[k % nz][:, at:at + share]
    lse = lse2(ordered([part[:, :cols] for part in got], shifts, parts))
    beta_ref[...] = jnp.exp2(jnp.log2(b_ref[...]) - lse + shift_ref[...])
    w16_ref[...] = stacked(beta_ref[...])
    row_sums(width, e_ref, beta_ref, w16_ref, acc_ref, o_ref)


def new_scale(b_ref, got, shifts, parts):
    return b_ref[...] / sum(ordered([part[...] for part in got], shifts, parts))


def row_kernel(width, shifts, parts, e_ref, first_ref, b_ref, *refs):
    got, (o_ref, w16_ref, acc_ref, w_ref) = refs[:-4], refs[-4:]
    w_ref[...] = first_ref[...] * new_scale(b_ref, got, shifts, parts)
    w16_ref[...] = stacked(w_ref[...])
    row_sums(width, e_ref, w_ref, w16_ref, acc_ref, o_ref)


def column_kernel(width, shifts, parts, e_ref, a_ref, first_ref, *refs):
    got, (o_ref, alpha_ref, w16_ref) = refs[:-3], refs[-3:]
    alpha_ref[...] = a_ref[...] / sum(ordered([part[...] for part in got], shifts, parts))
    w16_ref[...] = stacked(alpha_ref[...])
    for at in range(0, e_ref.shape[1], width):
        sums = jnp.dot(w16_ref[...], e_ref[:, at:at + width], preferred_element_type=jnp.float32)
        o_ref[:, at:at + width] = first_ref[:, at:at + width] * jnp.sum(sums, axis=0, keepdims=True)


def flat(value):
    return value.reshape(1, -1) if value.ndim == 1 else value


def weighted(kernel, outs, e, rows, got, parts):
    got, shifts = got
    size = e.shape[0] if kernel is column_kernel else e.shape[1]
    width = 512 if kernel is column_kernel else 256
    scratch = [pltpu.VMEM((16, size), jnp.bfloat16)]
    if kernel is not column_kernel:
        scratch.append(pltpu.VMEM((e.shape[0] // 2, 128), jnp.float32))
    if kernel is row_kernel:
        scratch.append(pltpu.VMEM((1, size), jnp.float32))
    return pl.pallas_call(
        functools.partial(kernel, width, tuple(shifts), parts),
        out_shape=[shape(*dims) for dims in outs],
        in_specs=[VMEM] * (1 + len(rows) + len(got)),
        out_specs=[VMEM] * len(outs),
        scratch_shapes=scratch,
        compiler_params=pltpu.CompilerParams(vmem_limit_bytes=16 << 20),
        cost_estimate=pl.CostEstimate(flops=2 * e.size, bytes_accessed=2 * e.size, transcendentals=0),
        name="weighted_sum",
    )(e, *rows, *[flat(part) for part in got])


def pass_cost(depth, lanes):
    return pl.CostEstimate(flops=2 * depth * lanes * D, bytes_accessed=2 * D * (depth + lanes), transcendentals=depth * lanes)


def shape(*dims, dtype=jnp.float32):
    return jax.ShapeDtypeStruct(dims, dtype)


def lse_scratch(depth, chunk, width):
    return [
        pltpu.VMEM((depth, 128), jnp.float32),
        pltpu.VMEM((2, chunk, width), jnp.float32),
        pltpu.VMEM((GROUP, 128), jnp.float32),
    ]


def row_lse_early(own, xs, y_other, width=1024):
    share = y_other.shape[0]
    rows, depth = own.shape[0] - share + sum(part.shape[0] for part in xs), 2 * share
    return pl.pallas_call(
        functools.partial(row_lse_early_kernel, width, len(xs)),
        out_shape=(shape(rows, D, dtype=jnp.bfloat16), shape(D, rows, dtype=jnp.bfloat16), shape(1, rows)),
        in_specs=[VMEM] * (len(xs) + 2),
        out_specs=(VMEM,) * 3,
        scratch_shapes=[pltpu.VMEM((depth, D), jnp.bfloat16), *lse_scratch(depth, share, width)],
        compiler_params=pltpu.CompilerParams(vmem_limit_bytes=16 << 20),
        cost_estimate=pass_cost(depth, rows),
        name="row_lse_early",
    )(own, *xs, y_other)


def row_lse_middle(x, ys, first, width=1024):
    rows, share = x.shape[0], ys[0].shape[0]
    depth = len(ys) * share
    return pl.pallas_call(
        functools.partial(row_lse_middle_kernel, width, len(ys)),
        out_shape=shape(1, rows),
        in_specs=[VMEM] * (len(ys) + 2),
        out_specs=VMEM,
        scratch_shapes=[
            pltpu.VMEM((depth, D), jnp.bfloat16),
            *lse_scratch(depth, share, width),
            pltpu.VMEM((1, rows), jnp.float32),
        ],
        compiler_params=pltpu.CompilerParams(vmem_limit_bytes=16 << 20),
        cost_estimate=pass_cost(depth, rows),
        name="row_lse_middle",
    )(x, first, *ys)


def row_lse_late(own, x, ys, first, mass, tail, width=1024):
    rows, share = x.shape[0], ys[0].shape[0]
    depth = (len(ys) + 1) * share
    return pl.pallas_call(
        functools.partial(row_lse_late_kernel, width, len(ys)),
        out_shape=(shape(depth, D, dtype=jnp.bfloat16), shape(1, rows + tail)),
        in_specs=[VMEM] * (len(ys) + 4),
        out_specs=(VMEM,) * 2,
        scratch_shapes=[*lse_scratch(depth, share, width), pltpu.VMEM((1, rows), jnp.float32)],
        compiler_params=pltpu.CompilerParams(vmem_limit_bytes=16 << 20),
        cost_estimate=pass_cost(depth // 2, rows),
        name="row_lse_late",
    )(own, mass.reshape(1, -1), x, first, *ys)


def column_lse(x, y, mass, tail, got, width=512, chunk=512):
    rows, cols = x.shape[0], y.shape[0]
    return pl.pallas_call(
        functools.partial(column_lse_kernel, width, chunk, len(got)),
        out_shape=(shape(1, cols + tail), shape(rows, cols, dtype=jnp.bfloat16), shape(1, cols), shape(1, rows)),
        in_specs=[VMEM] * (3 + len(got)),
        out_specs=(VMEM,) * 4,
        scratch_shapes=[pltpu.VMEM((rows // 128, 128), jnp.float32), *lse_scratch(rows, chunk, width)],
        compiler_params=pltpu.CompilerParams(vmem_limit_bytes=16 << 20),
        cost_estimate=pass_cost(rows, cols),
        name="column_lse",
    )(x, y, mass.reshape(1, -1), *[part.reshape(1, -1) for part in got])


def pair_of(combine, one, two, size, shift, parts):
    whole = one.shape[-1]
    return pl.pallas_call(
        functools.partial(pair_kernel, size, shift, parts, combine),
        out_shape=shape(1, whole),
        in_specs=[VMEM] * 2,
        out_specs=VMEM,
        compiler_params=pltpu.CompilerParams(vmem_limit_bytes=16 << 20),
        name="pair",
    )(one.reshape(1, whole), two.reshape(1, whole))


def high_low(value):
    high = value.astype(jnp.bfloat16)
    return high, (value - high.astype(jnp.float32)).astype(jnp.bfloat16)


def put_xa(xt_ref, alpha_ref, xa_ref):
    place = lax.broadcasted_iota(jnp.int32, (128, 512), 0)
    for at in range(0, xt_ref.shape[1], 512):
        alpha = alpha_ref[:, at:at + 512]
        high, low = high_low(xt_ref[:, at:at + 512].astype(jnp.float32) * alpha)
        first, second = high_low(alpha)
        low = jnp.where(place == 126, first.astype(jnp.float32), low.astype(jnp.float32))
        low = jnp.where(place == 127, second.astype(jnp.float32), low)
        xa_ref[:128, at:at + 512] = high
        xa_ref[128:, at:at + 512] = low.astype(jnp.bfloat16)


def column_parts(blocks, share, xa_ref, y_ref, e_ref, first_ref, own_ref, sent_ref,
                 bb_ref, cb_ref, s_ref, count_ref, acc_ref):
    spread(jnp.concatenate([first_ref[:, at:at + share] for at in blocks], axis=1), s_ref, bb_ref)
    lower = lax.broadcasted_iota(jnp.int32, (128, share), 0) < 126
    for k, at in enumerate(blocks):
        to = k * share
        got = jnp.dot(xa_ref[...], e_ref[:, at:at + share], preferred_element_type=jnp.float32)
        acc_ref[:, to:to + share] = got[:128] + jnp.where(lower, got[128:], 0.0)
        count_ref[:, to:to + share] = got[254:255] + got[255:256]
    spread(count_ref[...], s_ref, cb_ref)
    own = own_ref.shape[0]
    for k, at in enumerate(blocks):
        for q in range(0, share, 128):
            to = k * share + q
            pulled = jnp.transpose(acc_ref[:, to:to + 128])
            whole = cb_ref[to:to + 128, :] * y_ref[at + q:at + q + 128, :].astype(jnp.float32)
            grad = bb_ref[to:to + 128, :] * (whole - pulled)
            if to < own:
                own_ref[to:to + 128, :] = grad
            else:
                sent_ref[to - own:to - own + 128, :] = grad.astype(jnp.bfloat16)


def first_columns_kernel(blocks, share, xt_ref, y_ref, e_ref, alpha_ref, first_ref, own_ref, sent_ref, xa_ref, *rest):
    put_xa(xt_ref, alpha_ref, xa_ref)
    column_parts(blocks, share, xa_ref, y_ref, e_ref, first_ref, own_ref, sent_ref, *rest)


def columns_kernel(blocks, share, xa_ref, y_ref, e_ref, first_ref, own_ref, sent_ref, *rest):
    column_parts(blocks, share, xa_ref, y_ref, e_ref, first_ref, own_ref, sent_ref, *rest)


def column_grad(zs, nz, share, y, e, first, xt=None, alpha=None, xa=None):
    rows, size = e.shape[0], 2 * len(zs) * share
    blocks = [z * share for z in zs] + [(nz + z) * share for z in zs]
    out_shape = [shape(size // 2, D), shape(size // 2, D, dtype=jnp.bfloat16)]
    if xa is None:
        kernel, args = first_columns_kernel, (xt, y, e, alpha, first)
        out_shape.append(shape(256, rows, dtype=jnp.bfloat16))
    else:
        kernel, args = columns_kernel, (xa, y, e, first)
    return pl.pallas_call(
        functools.partial(kernel, blocks, share),
        out_shape=out_shape,
        in_specs=[VMEM] * len(args),
        out_specs=[VMEM] * len(out_shape),
        scratch_shapes=[
            pltpu.VMEM((size, 128), jnp.float32),
            pltpu.VMEM((size, 128), jnp.float32),
            pltpu.VMEM((size // 128, 128), jnp.float32),
            pltpu.VMEM((1, size), jnp.float32),
            pltpu.VMEM((128, size), jnp.float32),
        ],
        compiler_params=pltpu.CompilerParams(vmem_limit_bytes=16 << 20),
        cost_estimate=pl.CostEstimate(flops=4 * rows * size * D, bytes_accessed=2 * rows * size, transcendentals=0),
        name="column_grad",
    )(*args)


def row_block(at, chunk, x_ref, e_ref, yb_ref, scale):
    got = jnp.dot(e_ref[pl.ds(at, chunk), :], yb_ref[...], preferred_element_type=jnp.float32)
    lower = lax.broadcasted_iota(jnp.int32, (chunk, 128), 1) < 126
    total = got[:, 254:255] + got[:, 255:256]
    pulled = got[:, :128] + jnp.where(lower, got[:, 128:], 0.0)
    x = x_ref[pl.ds(at, chunk), :].astype(jnp.float32)
    return 2.0 * scale * (total * x - pulled)


def put_yb(y_ref, beta, yb_ref, s_ref, bb_ref):
    spread(beta, s_ref, bb_ref)
    place = lax.broadcasted_iota(jnp.int32, (256, 128), 1)
    for at in range(0, y_ref.shape[0], 256):
        beta = bb_ref[at:at + 256, :]
        high, low = high_low(y_ref[at:at + 256, :].astype(jnp.float32) * beta)
        first, second = high_low(beta)
        low = jnp.where(place == 126, first.astype(jnp.float32), low.astype(jnp.float32))
        low = jnp.where(place == 127, second.astype(jnp.float32), low)
        yb_ref[at:at + 256, :128] = high
        yb_ref[at:at + 256, 128:] = low.astype(jnp.bfloat16)


def row_parts(parts, x_ref, e_ref, alpha_ref, yb_ref, outs, sa_ref, ab_ref):
    share = outs[0].shape[0]
    chunk = math.gcd(share, 512)
    for part, out_ref in zip(parts, outs):
        spread(alpha_ref[:, part * share:(part + 1) * share], sa_ref, ab_ref)
        for k in range(0, share, chunk):
            grad = row_block(part * share + k, chunk, x_ref, e_ref, yb_ref, ab_ref[k:k + chunk, :])
            out_ref[k:k + chunk, :] = grad.astype(out_ref.dtype)


def first_rows_kernel(parts, shifts, blocks, nz, x_ref, y_ref, e_ref, alpha_ref, first_ref, b_ref, *refs):
    got, (yb_ref, scale_ref, *outs), (s_ref, bb_ref, sa_ref, ab_ref) = refs[:nz], refs[nz:-4], refs[-4:]
    scale = new_scale(b_ref, got, shifts, blocks)
    scale_ref[...] = scale[:, :scale_ref.shape[1]]
    put_yb(y_ref, first_ref[...] * scale, yb_ref, s_ref, bb_ref)
    row_parts(parts, x_ref, e_ref, alpha_ref, yb_ref, outs, sa_ref, ab_ref)


def rows_kernel(parts, x_ref, yb_ref, e_ref, alpha_ref, *refs):
    row_parts(parts, x_ref, e_ref, alpha_ref, yb_ref, refs[:-2], *refs[-2:])


def rows_scratch(share):
    return [pltpu.VMEM((share // 128, 128), jnp.float32), pltpu.VMEM((share, 128), jnp.float32)]


def rows_cost(share, parts, cols):
    size = share * len(parts) * cols
    return pl.CostEstimate(flops=4 * size * D, bytes_accessed=2 * size, transcendentals=0)


def first_rows(parts, share, x, y, e, alpha, first, mass, got, blocks):
    cols = y.shape[0]
    got, shifts = got
    return pl.pallas_call(
        functools.partial(first_rows_kernel, parts, tuple(shifts), blocks, len(got)),
        out_shape=[shape(cols, 256, dtype=jnp.bfloat16), shape(1, cols // blocks)]
        + [shape(share, D, dtype=jnp.bfloat16)] * len(parts),
        in_specs=[VMEM] * (6 + len(got)),
        out_specs=[VMEM] * (2 + len(parts)),
        scratch_shapes=[
            pltpu.VMEM((cols // 128, 128), jnp.float32),
            pltpu.VMEM((cols, 128), jnp.float32),
            *rows_scratch(share),
        ],
        compiler_params=pltpu.CompilerParams(vmem_limit_bytes=16 << 20),
        cost_estimate=rows_cost(share * HEAVY, parts, cols),
        name="first_rows",
    )(x, y, e, alpha, first, mass, *[flat(part) for part in got])


def other_rows(parts, share, x, yb, e, alpha, dtype):
    return pl.pallas_call(
        functools.partial(rows_kernel, parts),
        out_shape=[shape(share, D, dtype=dtype)] * len(parts),
        in_specs=[VMEM] * 4,
        out_specs=[VMEM] * len(parts),
        scratch_shapes=rows_scratch(share),
        compiler_params=pltpu.CompilerParams(vmem_limit_bytes=16 << 20),
        cost_estimate=rows_cost(share, parts, yb.shape[0]),
        name="other_rows",
    )(x, yb, e, alpha)


def add_up_kernel(na, scale_ref, *refs):
    ins, (rows_ref, cols_ref, s_ref, sb_ref) = refs[:-4], refs[-4:]
    rows_ref[...] = sum(part[...].astype(jnp.float32) for part in ins[:na])
    spread(scale_ref[...], s_ref, sb_ref)
    cols_ref[...] = 2.0 * sb_ref[...] * sum(part[...].astype(jnp.float32) for part in ins[na:])


def add_up(rows, columns, scale):
    share = scale.shape[1]
    return pl.pallas_call(
        functools.partial(add_up_kernel, len(rows)),
        out_shape=(shape(*rows[0].shape), shape(*columns[0].shape)),
        in_specs=[VMEM] * (1 + len(rows) + len(columns)),
        out_specs=(VMEM,) * 2,
        scratch_shapes=rows_scratch(share),
        compiler_params=pltpu.CompilerParams(vmem_limit_bytes=16 << 20),
        name="add_up",
    )(scale, *rows, *columns)


def shares_kernel(gc_ref, other_ref, *outs):
    share = outs[0].shape[0]
    for k, out_ref in enumerate(outs):
        at = k * share
        total = gc_ref[at:at + share, :] + other_ref[at:at + share, :].astype(jnp.float32)
        out_ref[...] = total.astype(out_ref.dtype)


def shares(gc, other, dtypes):
    share = gc.shape[0] // len(dtypes)
    return pl.pallas_call(
        shares_kernel,
        out_shape=[shape(share, D, dtype=dtype) for dtype in dtypes],
        in_specs=[VMEM] * 2,
        out_specs=[VMEM] * len(dtypes),
        compiler_params=pltpu.CompilerParams(vmem_limit_bytes=16 << 20),
        name="shares",
    )(gc, other)


class Groups:
    def __init__(self, nrow, ncol):
        self.count = nrow * ncol
        self.across = [(a << 1) * ncol + b for a in range(nrow // 2) for b in range(2)]
        self.along = [z << 1 for z in range(ncol // 2)]
        self.core = ncol

    def swap(self, value, mask):
        if mask == 0:
            return value
        return lax.ppermute(value, ("row", "col"), [(i, i ^ mask) for i in range(self.count)])


def local(imu, camera, imu_mass, cam_mass):
    nrow, ncol = lax.axis_size("row"), lax.axis_size("col")
    groups = Groups(nrow, ncol)
    swap, across, along, core = groups.swap, groups.across, groups.along, groups.core
    na, nz = len(across), len(along)
    share_x, share_y = imu.shape[0], camera.shape[1]
    rows, cols = na * share_x, 2 * nz * share_y

    def direct(value, masks):
        return [swap(value, mask) for mask in masks], range(len(masks))

    xs, _ = direct(imu, across)
    own, mine = lax.optimization_barrier((jnp.concatenate([imu, camera[0]]), camera[0]))
    near = [mine] + [None] * (nz - 1)
    for z in range(1, nz):
        if not z & (z - 1):
            near[z] = swap(mine if z == 1 else camera[0], along[z])
    far = [swap(mine, core)]

    def pair(mass, place, share):
        return [lax.dynamic_slice_in_dim(mass, (place ^ k) * share, share, 0) for k in range(2)]

    row, col = lax.axis_index("row"), lax.axis_index("col")
    mass = jnp.concatenate(pair(imu_mass, col, share_x) + pair(cam_mass, row, share_y))

    x, xt, first = row_lse_early(own, xs[1:], far[0])
    relays = [z for z in range(2, nz) if not z & (z - 1)]
    first, mass, got = lax.optimization_barrier((first, mass, [near[z] for z in relays]))
    for z, part in zip(relays, got):
        near[z] = part
    for z in range(1, nz):
        if z & (z - 1):
            near[z] = swap(near[z & (z - 1)], along[z & -z])
    middle = near[1:-1]
    far += [swap(part, core) for part in middle]
    first = row_lse_middle(x, middle, first)
    first, last = lax.optimization_barrier((first, near[-1]))
    far.append(swap(last, core))
    y, sent = row_lse_late(own, x, [*middle, last, *far], first, mass, 2 * share_x)
    got, _ = direct(sent.reshape(-1), across)

    sent, e, shift, mass_a = column_lse(x, y, mass, 2 * share_y, got)
    sent = pair_of(lse2, sent, swap(sent.reshape(-1), core), cols, 1, 2)
    got = direct(sent.reshape(-1), along)

    sums, first_beta, mass_b = weighted(
        first_row_kernel, [(1, rows), (1, cols), (1, cols)], e, [shift], got, 2 * nz)
    for step in range(1, ITERS):
        if step > 1:
            sums, = weighted(row_kernel, [(1, rows)], e, [first_beta, mass_b], got, 2 * nz)
        got = direct(sums.reshape(-1), across)
        part, alpha = weighted(column_kernel, [(1, cols), (1, rows)], e, [mass_a, first_beta], got, na)
        part = pair_of(sum, part, swap(part.reshape(-1), core), cols, 1, 2)
        part, alpha = lax.optimization_barrier((part, alpha))
        got = direct(part.reshape(-1), along)

    half = nz // 2
    gc, gc_send, xa = column_grad(range(half, nz), nz, share_y, y, e, first_beta, xt=xt, alpha=alpha)
    far_gc = shares(gc, swap(gc_send, core), [jnp.bfloat16] * (nz - half))
    gc, gc_send = column_grad(range(half), nz, share_y, y, e, first_beta, xa=xa)
    far_gc, alpha = lax.optimization_barrier((far_gc, alpha))
    far_gc = [swap(part, along[half + z]) for z, part in enumerate(far_gc)]
    yb, scale, last = first_rows([na - 1], share_x, x, y, e, alpha, first_beta, mass_b, got, 2 * nz)
    near_gc = shares(gc, swap(gc_send, core), [jnp.float32] + [jnp.bfloat16] * (half - 1))
    (grad_cam, *parts), yb = lax.optimization_barrier((near_gc, yb))
    parts = [swap(part, along[z + 1]) for z, part in enumerate(parts)]
    last = swap(last, across[na - 1])
    sent = other_rows(list(range(1, na - 1)), share_x, x, yb, e, alpha, jnp.bfloat16)
    sent, parts[0], last = lax.optimization_barrier((sent, parts[0], last))
    sent = [swap(part, across[s + 1]) for s, part in enumerate(sent)] + [last]
    gi, = other_rows([0], share_x, x, yb, e, alpha, jnp.float32)
    grad_imu, grad_cam = add_up([gi, *sent], [grad_cam, *parts, *far_gc], scale)
    return grad_imu, grad_cam[None]


def solution(mesh):
    in_specs = (P(("row", "col"), None), P("col", "row", None), P("row"), P("col"))
    out_specs = (P(("row", "col"), None), P("col", "row", None))
    return jax.shard_map(local, mesh=mesh, in_specs=in_specs, out_specs=out_specs, check_vma=False)
```

```python
import functools
import math

import jax
import jax.numpy as jnp
from jax import lax
from jax.experimental import pallas as pl
from jax.experimental.pallas import tpu as pltpu
from jax.sharding import PartitionSpec as P

D = 128
ITERS = 3
EPSILON = D / 20.0
LOG2E = math.log2(math.e)
CROSS = 2.0 * LOG2E / EPSILON
NT = (((1,), (1,)), ((), ()))
VMEM = pl.BlockSpec(memory_space=pltpu.VMEM)
HEAVY = 32


def spread(value, s_ref, sb_ref):
    chunks = value.shape[1] // 128
    for k in range(chunks):
        s_ref[k:k + 1, :] = value[:, k * 128:(k + 1) * 128]
    turned = jnp.transpose(s_ref[...])
    for k in range(chunks):
        sb_ref[k * 128:(k + 1) * 128, :] = jnp.broadcast_to(turned[:, k:k + 1], (128, 128))


def ordered(values, shifts, parts):
    share = values[0].shape[1] // parts
    return [
        jnp.concatenate([value[:, (k ^ s) * share:((k ^ s) + 1) * share] for k in range(parts)], axis=1)
        for value, s in zip(values, shifts)
    ]


def lse2(parts):
    top = functools.reduce(jnp.maximum, parts)
    return top + jnp.log2(sum(jnp.exp2(part - top) for part in parts))


def pipelined(places, chunk, width, a_ref, b_ref, d_ref, tile, finish):
    last = b_ref.shape[0] // width - 1

    def product(n, m):
        b = b_ref[pl.ds(pl.multiple_of(n * width, width), width), :]
        a = a_ref[places[m]:places[m] + chunk, :]
        d_ref[m % 2] = lax.dot_general(a, b, NT, preferred_element_type=jnp.float32)

    product(0, 0)

    def column(n, _):
        start = pl.multiple_of(n * width, width)
        state = None
        for m in range(len(places)):
            if m + 1 < len(places):
                product(n, m + 1)
            else:
                product(jnp.minimum(n + 1, last), 0)
            state = tile(m, start, state)
        finish(start, state)
        return 0

    lax.fori_loop(0, last + 1, column, 0)


def running_max(places, chunk, width, a_ref, b_ref, sb_ref, o_ref, e_ref, shift_ref):
    def column(n, _):
        start = pl.multiple_of(n * width, width)
        b = b_ref[pl.ds(start, width), :]

        def exponents(at):
            d = lax.dot_general(a_ref[at:at + chunk, :], b, NT, preferred_element_type=jnp.float32)
            s = sb_ref[at:at + chunk, :]
            return [d[:, q * 128:(q + 1) * 128] * CROSS + s for q in range(width // 128)]

        peak, total = jnp.full((1, width), -1e30, jnp.float32), jnp.zeros((1, width), jnp.float32)
        for at in places:
            peaks, totals = [], []
            for q, t in enumerate(exponents(at)):
                old = peak[:, q * 128:(q + 1) * 128]
                new = jnp.maximum(old, jnp.max(t, axis=0, keepdims=True))
                part = jnp.sum(jnp.exp2(t - new), axis=0, keepdims=True)
                peaks.append(new)
                totals.append(total[:, q * 128:(q + 1) * 128] * jnp.exp2(old - new) + part)
            peak, total = jnp.concatenate(peaks, axis=1), jnp.concatenate(totals, axis=1)
        o_ref[:, pl.ds(start, width)] = peak + jnp.log2(total)
        if e_ref is not None:
            shift_ref[:, pl.ds(start, width)] = peak
            for at in places:
                for q, t in enumerate(exponents(at)):
                    place = pl.ds(pl.multiple_of(start + q * 128, 128), 128)
                    e_ref[at:at + chunk, place] = jnp.exp2(t - shift_ref[:, place]).astype(jnp.bfloat16)
        return 0

    lax.fori_loop(0, b_ref.shape[0] // width, column, 0)


def lse_pass(places, chunk, width, a_ref, b_ref, sb_ref, d_ref, top_ref, o_ref, e_ref=None, shift_ref=None):
    tiles, group = width // 128, top_ref.shape[0]
    top_ref[...] = jnp.zeros_like(top_ref)

    def lanes_of(start, q):
        return pl.ds(pl.multiple_of(start + q * 128, 128), 128)

    def tile(m, start, state):
        def exponents(g, q):
            at = g * group
            s = sb_ref[places[m] + at:places[m] + at + group, :]
            return d_ref[m % 2, at:at + group, q * 128:(q + 1) * 128] * CROSS + s

        if m == 0:
            tops = [exponents(0, q) for q in range(tiles)]
            for g in range(1, 128 // group):
                tops = [jnp.maximum(top, exponents(g, q)) for q, top in enumerate(tops)]
            state = [(jnp.max(top, axis=0, keepdims=True), jnp.zeros((group, 128), jnp.float32)) for top in tops]
        for g in range(chunk // group):
            for q, (peak, total) in enumerate(state):
                e = jnp.exp2(exponents(g, q) - peak)
                if e_ref is not None:
                    at = places[m] + g * group
                    e_ref[at:at + group, lanes_of(start, q)] = e.astype(jnp.bfloat16)
                state[q] = peak, total + e
        return state

    def finish(start, state):
        for q, (peak, total) in enumerate(state):
            top_ref[...] = jnp.maximum(top_ref[...], total)
            o_ref[:, lanes_of(start, q)] = peak + jnp.log2(jnp.sum(total, axis=0, keepdims=True))
            if e_ref is not None:
                shift_ref[:, lanes_of(start, q)] = peak

    pipelined(places, chunk, width, a_ref, b_ref, d_ref, tile, finish)

    @pl.when(jnp.logical_not(jnp.max(top_ref[...]) < 2.0 ** 60))
    def _():
        running_max(places, chunk, min(width, 256), a_ref, b_ref, sb_ref, o_ref, e_ref, shift_ref)


def put_norms(places, share, y_ref, sb_ref):
    for at in places:
        y = y_ref[at:at + share, :].astype(jnp.float32)
        total = jnp.sum(y * y, axis=1, keepdims=True) * (-LOG2E / EPSILON)
        sb_ref[at:at + share, :] = jnp.broadcast_to(total, (share, 128))


def join(out_ref, parts):
    at = 0
    for part in parts:
        out_ref[at:at + part.shape[0], :] = part[...]
        at += part.shape[0]


def row_lse_early_kernel(width, nx, own_ref, *refs):
    xs, y_other, refs = refs[:nx], refs[nx], refs[nx + 1:]
    x_ref, xt_ref, o_ref, y_ref, sb_ref, d_ref, top_ref = refs
    share = y_other.shape[0]
    mine = own_ref.shape[0] - share
    join(x_ref, [own_ref.at[:mine, :], *xs])
    join(y_ref, [own_ref.at[mine:, :], y_other])
    for k in range(x_ref.shape[0] // 128):
        at = k * 128
        xt_ref[:, at:at + 128] = jnp.transpose(x_ref[at:at + 128, :].astype(jnp.float32)).astype(jnp.bfloat16)
    places = [0, share]
    put_norms(places, share, y_ref, sb_ref)
    lse_pass(places, share, width, y_ref, x_ref, sb_ref, d_ref, top_ref, o_ref)


def row_lse_middle_kernel(width, ny, x_ref, first_ref, *refs):
    ys, (o_ref, y_ref, sb_ref, d_ref, top_ref, sum_ref) = refs[:ny], refs[ny:]
    share = ys[0].shape[0]
    join(y_ref, ys)
    places = [k * share for k in range(ny)]
    put_norms(places, share, y_ref, sb_ref)
    lse_pass(places, share, width, y_ref, x_ref, sb_ref, d_ref, top_ref, sum_ref)
    o_ref[...] = lse2([first_ref[...], sum_ref[...]])


def row_lse_late_kernel(width, ny, own_ref, mass_ref, x_ref, first_ref, *refs):
    ys, (y_ref, o_ref, sb_ref, d_ref, top_ref, sum_ref) = refs[:ny], refs[ny:]
    share, rows, half = ys[0].shape[0], x_ref.shape[0], (ny + 1) // 2
    join(y_ref, [own_ref.at[own_ref.shape[0] - share:, :], *ys])
    places = [k * share for k in range(half - 1, 2 * half) if k != half]
    put_norms(places, share, y_ref, sb_ref)
    lse_pass(places, share, width, y_ref, x_ref, sb_ref, d_ref, top_ref, sum_ref)
    o_ref[:, :rows] = lse2([first_ref[...], sum_ref[...]])
    o_ref[:, rows:] = mass_ref[:, :o_ref.shape[1] - rows]


def column_lse_kernel(width, chunk, na, x_ref, y_ref, mass_ref, *refs):
    got, (o_ref, e_ref, shift_ref, a_ref, s_ref, sb_ref, d_ref, top_ref) = refs[:na], refs[na:]
    rows, cols = x_ref.shape[0], y_ref.shape[0]
    o_ref[:, cols:] = mass_ref[:, mass_ref.shape[1] - o_ref.shape[1] + cols:]
    share = rows // na
    for k in range(na):
        at = rows + (k % 2) * share
        a_ref[:, k * share:(k + 1) * share] = got[k - k % 2][:, at:at + share]
    u = jnp.log2(a_ref[...]) - lse2(ordered([part[:, :rows] for part in got], range(na), na))
    spread(u, s_ref, sb_ref)
    places = list(range(0, rows, chunk))
    lse_pass(places, chunk, width, x_ref, y_ref, sb_ref, d_ref, top_ref, o_ref, e_ref, shift_ref)


def pair_kernel(size, shift, parts, combine, one_ref, two_ref, o_ref):
    two, = ordered([two_ref[:, :size]], [shift], parts)
    o_ref[:, :size] = combine([one_ref[:, :size], two])
    if o_ref.shape[1] > size:
        o_ref[:, size:] = one_ref[:, size:]


def split3(value):
    high = value.astype(jnp.bfloat16)
    rest = value - high.astype(jnp.float32)
    mid = rest.astype(jnp.bfloat16)
    return high, mid, (rest - mid.astype(jnp.float32)).astype(jnp.bfloat16)


def stacked(value):
    high, mid, low = [part.astype(jnp.float32) for part in split3(value)]
    dims = (16, value.shape[1])
    place = lax.broadcasted_iota(jnp.int32, dims, 0)
    parts = jnp.where(place == 0, high, jnp.where(place == 1, mid, jnp.where(place == 2, low, 0.0)))
    return parts.astype(jnp.bfloat16)


def row_sums(width, e_ref, w_ref, w16_ref, acc_ref, o_ref):
    rows, cols = e_ref.shape
    half = rows - acc_ref.shape[0]
    for at in range(0, half, width):
        got = lax.dot_general(w16_ref[...], e_ref[at:at + width, :], NT, preferred_element_type=jnp.float32)
        for k in range(at, at + width, 64):
            total = jnp.zeros((64, 128), jnp.float32)
            for q in range(0, cols, 128):
                e = e_ref[half + k:half + k + 64, q:q + 128].astype(jnp.float32)
                total = total + e * w_ref[:, q:q + 128]
            acc_ref[k:k + 64, :] = total
        o_ref[:, at:at + width] = jnp.sum(got, axis=0, keepdims=True)
    for at in range(0, rows - half, 128):
        total = jnp.sum(jnp.transpose(acc_ref[at:at + 128, :]), axis=0, keepdims=True)
        o_ref[:, half + at:half + at + 128] = total


def first_row_kernel(width, shifts, parts, e_ref, shift_ref, *refs):
    nz = len(shifts)
    got, (o_ref, beta_ref, b_ref, w16_ref, acc_ref) = refs[:nz], refs[nz:]
    cols = e_ref.shape[1]
    share = cols // parts
    for k in range(parts):
        at = cols + (k // nz) * share
        b_ref[:, k * share:(k + 1) * share] = got[k % nz][:, at:at + share]
    lse = lse2(ordered([part[:, :cols] for part in got], shifts, parts))
    beta_ref[...] = jnp.exp2(jnp.log2(b_ref[...]) - lse + shift_ref[...])
    w16_ref[...] = stacked(beta_ref[...])
    row_sums(width, e_ref, beta_ref, w16_ref, acc_ref, o_ref)


def new_scale(b_ref, got, shifts, parts):
    return b_ref[...] / sum(ordered([part[...] for part in got], shifts, parts))


def row_kernel(width, shifts, parts, e_ref, first_ref, b_ref, *refs):
    got, (o_ref, w16_ref, acc_ref, w_ref) = refs[:-4], refs[-4:]
    w_ref[...] = first_ref[...] * new_scale(b_ref, got, shifts, parts)
    w16_ref[...] = stacked(w_ref[...])
    row_sums(width, e_ref, w_ref, w16_ref, acc_ref, o_ref)


def column_kernel(width, shifts, parts, e_ref, a_ref, first_ref, *refs):
    got, (o_ref, alpha_ref, w16_ref) = refs[:-3], refs[-3:]
    alpha_ref[...] = a_ref[...] / sum(ordered([part[...] for part in got], shifts, parts))
    w16_ref[...] = stacked(alpha_ref[...])
    for at in range(0, e_ref.shape[1], width):
        sums = jnp.dot(w16_ref[...], e_ref[:, at:at + width], preferred_element_type=jnp.float32)
        o_ref[:, at:at + width] = first_ref[:, at:at + width] * jnp.sum(sums, axis=0, keepdims=True)


def flat(value):
    return value.reshape(1, -1) if value.ndim == 1 else value


def weighted(kernel, outs, e, rows, got, parts):
    got, shifts = got
    size = e.shape[0] if kernel is column_kernel else e.shape[1]
    width = 512 if kernel is column_kernel else 256
    scratch = [pltpu.VMEM((16, size), jnp.bfloat16)]
    if kernel is not column_kernel:
        scratch.append(pltpu.VMEM((e.shape[0] // 2, 128), jnp.float32))
    if kernel is row_kernel:
        scratch.append(pltpu.VMEM((1, size), jnp.float32))
    return pl.pallas_call(
        functools.partial(kernel, width, tuple(shifts), parts),
        out_shape=[shape(*dims) for dims in outs],
        in_specs=[VMEM] * (1 + len(rows) + len(got)),
        out_specs=[VMEM] * len(outs),
        scratch_shapes=scratch,
        compiler_params=pltpu.CompilerParams(vmem_limit_bytes=16 << 20),
        cost_estimate=pl.CostEstimate(flops=2 * e.size, bytes_accessed=2 * e.size, transcendentals=0),
        name="weighted_sum",
    )(e, *rows, *[flat(part) for part in got])


def pass_cost(depth, lanes):
    return pl.CostEstimate(flops=2 * depth * lanes * D, bytes_accessed=2 * D * (depth + lanes), transcendentals=depth * lanes)


def shape(*dims, dtype=jnp.float32):
    return jax.ShapeDtypeStruct(dims, dtype)


def lse_scratch(depth, chunk, width, group=32):
    return [
        pltpu.VMEM((depth, 128), jnp.float32),
        pltpu.VMEM((2, chunk, width), jnp.float32),
        pltpu.VMEM((group, 128), jnp.float32),
    ]


def row_lse_early(own, xs, y_other, width=1024):
    share = y_other.shape[0]
    rows, depth = own.shape[0] - share + sum(part.shape[0] for part in xs), 2 * share
    return pl.pallas_call(
        functools.partial(row_lse_early_kernel, width, len(xs)),
        out_shape=(shape(rows, D, dtype=jnp.bfloat16), shape(D, rows, dtype=jnp.bfloat16), shape(1, rows)),
        in_specs=[VMEM] * (len(xs) + 2),
        out_specs=(VMEM,) * 3,
        scratch_shapes=[pltpu.VMEM((depth, D), jnp.bfloat16), *lse_scratch(depth, share, width)],
        compiler_params=pltpu.CompilerParams(vmem_limit_bytes=16 << 20),
        cost_estimate=pass_cost(depth, rows),
        name="row_lse_early",
    )(own, *xs, y_other)


def row_lse_middle(x, ys, first, width=1024):
    rows, share = x.shape[0], ys[0].shape[0]
    depth = len(ys) * share
    return pl.pallas_call(
        functools.partial(row_lse_middle_kernel, width, len(ys)),
        out_shape=shape(1, rows),
        in_specs=[VMEM] * (len(ys) + 2),
        out_specs=VMEM,
        scratch_shapes=[
            pltpu.VMEM((depth, D), jnp.bfloat16),
            *lse_scratch(depth, share, width),
            pltpu.VMEM((1, rows), jnp.float32),
        ],
        compiler_params=pltpu.CompilerParams(vmem_limit_bytes=16 << 20),
        cost_estimate=pass_cost(depth, rows),
        name="row_lse_middle",
    )(x, first, *ys)


def row_lse_late(own, x, ys, first, mass, tail, width=1024):
    rows, share = x.shape[0], ys[0].shape[0]
    depth = (len(ys) + 1) * share
    return pl.pallas_call(
        functools.partial(row_lse_late_kernel, width, len(ys)),
        out_shape=(shape(depth, D, dtype=jnp.bfloat16), shape(1, rows + tail)),
        in_specs=[VMEM] * (len(ys) + 4),
        out_specs=(VMEM,) * 2,
        scratch_shapes=[*lse_scratch(depth, share, width), pltpu.VMEM((1, rows), jnp.float32)],
        compiler_params=pltpu.CompilerParams(vmem_limit_bytes=16 << 20),
        cost_estimate=pass_cost(depth // 2, rows),
        name="row_lse_late",
    )(own, mass.reshape(1, -1), x, first, *ys)


def column_lse(x, y, mass, tail, got, width=512, chunk=512):
    rows, cols = x.shape[0], y.shape[0]
    return pl.pallas_call(
        functools.partial(column_lse_kernel, width, chunk, len(got)),
        out_shape=(shape(1, cols + tail), shape(rows, cols, dtype=jnp.bfloat16), shape(1, cols), shape(1, rows)),
        in_specs=[VMEM] * (3 + len(got)),
        out_specs=(VMEM,) * 4,
        scratch_shapes=[pltpu.VMEM((rows // 128, 128), jnp.float32), *lse_scratch(rows, chunk, width, 16)],
        compiler_params=pltpu.CompilerParams(vmem_limit_bytes=16 << 20),
        cost_estimate=pass_cost(rows, cols),
        name="column_lse",
    )(x, y, mass.reshape(1, -1), *[part.reshape(1, -1) for part in got])


def pair_of(combine, one, two, size, shift, parts):
    whole = one.shape[-1]
    return pl.pallas_call(
        functools.partial(pair_kernel, size, shift, parts, combine),
        out_shape=shape(1, whole),
        in_specs=[VMEM] * 2,
        out_specs=VMEM,
        compiler_params=pltpu.CompilerParams(vmem_limit_bytes=16 << 20),
        name="pair",
    )(one.reshape(1, whole), two.reshape(1, whole))


def high_low(value):
    high = value.astype(jnp.bfloat16)
    return high, (value - high.astype(jnp.float32)).astype(jnp.bfloat16)


def put_xa(xt_ref, alpha_ref, xa_ref):
    place = lax.broadcasted_iota(jnp.int32, (128, 512), 0)
    for at in range(0, xt_ref.shape[1], 512):
        alpha = alpha_ref[:, at:at + 512]
        high, low = high_low(xt_ref[:, at:at + 512].astype(jnp.float32) * alpha)
        first, second = high_low(alpha)
        low = jnp.where(place == 126, first.astype(jnp.float32), low.astype(jnp.float32))
        low = jnp.where(place == 127, second.astype(jnp.float32), low)
        xa_ref[:128, at:at + 512] = high
        xa_ref[128:, at:at + 512] = low.astype(jnp.bfloat16)


def column_parts(blocks, share, xa_ref, y_ref, e_ref, first_ref, own_ref, sent_ref,
                 bb_ref, cb_ref, s_ref, count_ref, acc_ref):
    spread(jnp.concatenate([first_ref[:, at:at + share] for at in blocks], axis=1), s_ref, bb_ref)
    lower = lax.broadcasted_iota(jnp.int32, (128, share), 0) < 126
    for k, at in enumerate(blocks):
        to = k * share
        got = jnp.dot(xa_ref[...], e_ref[:, at:at + share], preferred_element_type=jnp.float32)
        acc_ref[:, to:to + share] = got[:128] + jnp.where(lower, got[128:], 0.0)
        count_ref[:, to:to + share] = got[254:255] + got[255:256]
    spread(count_ref[...], s_ref, cb_ref)
    own = own_ref.shape[0]
    for k, at in enumerate(blocks):
        for q in range(0, share, 128):
            to = k * share + q
            pulled = jnp.transpose(acc_ref[:, to:to + 128])
            whole = cb_ref[to:to + 128, :] * y_ref[at + q:at + q + 128, :].astype(jnp.float32)
            grad = bb_ref[to:to + 128, :] * (whole - pulled)
            if to < own:
                own_ref[to:to + 128, :] = grad
            else:
                sent_ref[to - own:to - own + 128, :] = grad.astype(jnp.bfloat16)


def first_columns_kernel(blocks, share, xt_ref, y_ref, e_ref, alpha_ref, first_ref, own_ref, sent_ref, xa_ref, *rest):
    put_xa(xt_ref, alpha_ref, xa_ref)
    column_parts(blocks, share, xa_ref, y_ref, e_ref, first_ref, own_ref, sent_ref, *rest)


def columns_kernel(blocks, share, xa_ref, y_ref, e_ref, first_ref, own_ref, sent_ref, *rest):
    column_parts(blocks, share, xa_ref, y_ref, e_ref, first_ref, own_ref, sent_ref, *rest)


def column_grad(zs, nz, share, y, e, first, xt=None, alpha=None, xa=None):
    rows, size = e.shape[0], 2 * len(zs) * share
    blocks = [z * share for z in zs] + [(nz + z) * share for z in zs]
    out_shape = [shape(size // 2, D), shape(size // 2, D, dtype=jnp.bfloat16)]
    if xa is None:
        kernel, args = first_columns_kernel, (xt, y, e, alpha, first)
        out_shape.append(shape(256, rows, dtype=jnp.bfloat16))
    else:
        kernel, args = columns_kernel, (xa, y, e, first)
    return pl.pallas_call(
        functools.partial(kernel, blocks, share),
        out_shape=out_shape,
        in_specs=[VMEM] * len(args),
        out_specs=[VMEM] * len(out_shape),
        scratch_shapes=[
            pltpu.VMEM((size, 128), jnp.float32),
            pltpu.VMEM((size, 128), jnp.float32),
            pltpu.VMEM((size // 128, 128), jnp.float32),
            pltpu.VMEM((1, size), jnp.float32),
            pltpu.VMEM((128, size), jnp.float32),
        ],
        compiler_params=pltpu.CompilerParams(vmem_limit_bytes=16 << 20),
        cost_estimate=pl.CostEstimate(flops=4 * rows * size * D, bytes_accessed=2 * rows * size, transcendentals=0),
        name="column_grad",
    )(*args)


def row_block(at, chunk, x_ref, e_ref, yb_ref, scale):
    got = jnp.dot(e_ref[pl.ds(at, chunk), :], yb_ref[...], preferred_element_type=jnp.float32)
    lower = lax.broadcasted_iota(jnp.int32, (chunk, 128), 1) < 126
    total = got[:, 254:255] + got[:, 255:256]
    pulled = got[:, :128] + jnp.where(lower, got[:, 128:], 0.0)
    x = x_ref[pl.ds(at, chunk), :].astype(jnp.float32)
    return 2.0 * scale * (total * x - pulled)


def put_yb(y_ref, beta, yb_ref, s_ref, bb_ref):
    spread(beta, s_ref, bb_ref)
    place = lax.broadcasted_iota(jnp.int32, (256, 128), 1)
    for at in range(0, y_ref.shape[0], 256):
        beta = bb_ref[at:at + 256, :]
        high, low = high_low(y_ref[at:at + 256, :].astype(jnp.float32) * beta)
        first, second = high_low(beta)
        low = jnp.where(place == 126, first.astype(jnp.float32), low.astype(jnp.float32))
        low = jnp.where(place == 127, second.astype(jnp.float32), low)
        yb_ref[at:at + 256, :128] = high
        yb_ref[at:at + 256, 128:] = low.astype(jnp.bfloat16)


def row_parts(parts, x_ref, e_ref, alpha_ref, yb_ref, outs, sa_ref, ab_ref):
    share = outs[0].shape[0]
    chunk = math.gcd(share, 512)
    for part, out_ref in zip(parts, outs):
        spread(alpha_ref[:, part * share:(part + 1) * share], sa_ref, ab_ref)
        for k in range(0, share, chunk):
            grad = row_block(part * share + k, chunk, x_ref, e_ref, yb_ref, ab_ref[k:k + chunk, :])
            out_ref[k:k + chunk, :] = grad.astype(out_ref.dtype)


def first_rows_kernel(parts, shifts, blocks, nz, x_ref, y_ref, e_ref, alpha_ref, first_ref, b_ref, *refs):
    got, (yb_ref, scale_ref, *outs), (s_ref, bb_ref, sa_ref, ab_ref) = refs[:nz], refs[nz:-4], refs[-4:]
    scale = new_scale(b_ref, got, shifts, blocks)
    scale_ref[...] = scale[:, :scale_ref.shape[1]]
    put_yb(y_ref, first_ref[...] * scale, yb_ref, s_ref, bb_ref)
    row_parts(parts, x_ref, e_ref, alpha_ref, yb_ref, outs, sa_ref, ab_ref)


def rows_kernel(parts, x_ref, yb_ref, e_ref, alpha_ref, *refs):
    row_parts(parts, x_ref, e_ref, alpha_ref, yb_ref, refs[:-2], *refs[-2:])


def rows_scratch(share):
    return [pltpu.VMEM((share // 128, 128), jnp.float32), pltpu.VMEM((share, 128), jnp.float32)]


def rows_cost(share, parts, cols):
    size = share * len(parts) * cols
    return pl.CostEstimate(flops=4 * size * D, bytes_accessed=2 * size, transcendentals=0)


def first_rows(parts, share, x, y, e, alpha, first, mass, got, blocks):
    cols = y.shape[0]
    got, shifts = got
    return pl.pallas_call(
        functools.partial(first_rows_kernel, parts, tuple(shifts), blocks, len(got)),
        out_shape=[shape(cols, 256, dtype=jnp.bfloat16), shape(1, cols // blocks)]
        + [shape(share, D, dtype=jnp.bfloat16)] * len(parts),
        in_specs=[VMEM] * (6 + len(got)),
        out_specs=[VMEM] * (2 + len(parts)),
        scratch_shapes=[
            pltpu.VMEM((cols // 128, 128), jnp.float32),
            pltpu.VMEM((cols, 128), jnp.float32),
            *rows_scratch(share),
        ],
        compiler_params=pltpu.CompilerParams(vmem_limit_bytes=16 << 20),
        cost_estimate=rows_cost(share * HEAVY, parts, cols),
        name="first_rows",
    )(x, y, e, alpha, first, mass, *[flat(part) for part in got])


def other_rows(parts, share, x, yb, e, alpha, dtype):
    return pl.pallas_call(
        functools.partial(rows_kernel, parts),
        out_shape=[shape(share, D, dtype=dtype)] * len(parts),
        in_specs=[VMEM] * 4,
        out_specs=[VMEM] * len(parts),
        scratch_shapes=rows_scratch(share),
        compiler_params=pltpu.CompilerParams(vmem_limit_bytes=16 << 20),
        cost_estimate=rows_cost(share, parts, yb.shape[0]),
        name="other_rows",
    )(x, yb, e, alpha)


def add_up_kernel(na, scale_ref, *refs):
    ins, (rows_ref, cols_ref, s_ref, sb_ref) = refs[:-4], refs[-4:]
    rows_ref[...] = sum(part[...].astype(jnp.float32) for part in ins[:na])
    spread(scale_ref[...], s_ref, sb_ref)
    cols_ref[...] = 2.0 * sb_ref[...] * sum(part[...].astype(jnp.float32) for part in ins[na:])


def add_up(rows, columns, scale):
    share = scale.shape[1]
    return pl.pallas_call(
        functools.partial(add_up_kernel, len(rows)),
        out_shape=(shape(*rows[0].shape), shape(*columns[0].shape)),
        in_specs=[VMEM] * (1 + len(rows) + len(columns)),
        out_specs=(VMEM,) * 2,
        scratch_shapes=rows_scratch(share),
        compiler_params=pltpu.CompilerParams(vmem_limit_bytes=16 << 20),
        name="add_up",
    )(scale, *rows, *columns)


def shares_kernel(gc_ref, other_ref, *outs):
    share = outs[0].shape[0]
    for k, out_ref in enumerate(outs):
        at = k * share
        total = gc_ref[at:at + share, :] + other_ref[at:at + share, :].astype(jnp.float32)
        out_ref[...] = total.astype(out_ref.dtype)


def shares(gc, other, dtypes):
    share = gc.shape[0] // len(dtypes)
    return pl.pallas_call(
        shares_kernel,
        out_shape=[shape(share, D, dtype=dtype) for dtype in dtypes],
        in_specs=[VMEM] * 2,
        out_specs=[VMEM] * len(dtypes),
        compiler_params=pltpu.CompilerParams(vmem_limit_bytes=16 << 20),
        name="shares",
    )(gc, other)


class Groups:
    def __init__(self, nrow, ncol):
        self.count = nrow * ncol
        self.across = [(a << 1) * ncol + b for a in range(nrow // 2) for b in range(2)]
        self.along = [z << 1 for z in range(ncol // 2)]
        self.core = ncol

    def swap(self, value, mask):
        if mask == 0:
            return value
        return lax.ppermute(value, ("row", "col"), [(i, i ^ mask) for i in range(self.count)])


def local(imu, camera, imu_mass, cam_mass):
    nrow, ncol = lax.axis_size("row"), lax.axis_size("col")
    groups = Groups(nrow, ncol)
    swap, across, along, core = groups.swap, groups.across, groups.along, groups.core
    na, nz = len(across), len(along)
    share_x, share_y = imu.shape[0], camera.shape[1]
    rows, cols = na * share_x, 2 * nz * share_y

    def direct(value, masks):
        return [swap(value, mask) for mask in masks], range(len(masks))

    xs, _ = direct(imu, across)
    own, mine = lax.optimization_barrier((jnp.concatenate([imu, camera[0]]), camera[0]))
    near = [mine] + [None] * (nz - 1)
    for z in range(1, nz):
        if not z & (z - 1):
            near[z] = swap(mine if z == 1 else camera[0], along[z])
    far = [swap(mine, core)]

    def pair(mass, place, share):
        return [lax.dynamic_slice_in_dim(mass, (place ^ k) * share, share, 0) for k in range(2)]

    row, col = lax.axis_index("row"), lax.axis_index("col")
    mass = jnp.concatenate(pair(imu_mass, col, share_x) + pair(cam_mass, row, share_y))

    x, xt, first = row_lse_early(own, xs[1:], far[0])
    relays = [z for z in range(2, nz) if not z & (z - 1)]
    first, mass, got = lax.optimization_barrier((first, mass, [near[z] for z in relays]))
    for z, part in zip(relays, got):
        near[z] = part
    for z in range(1, nz):
        if z & (z - 1):
            near[z] = swap(near[z & (z - 1)], along[z & -z])
    middle = near[1:-1]
    far += [swap(part, core) for part in middle]
    first = row_lse_middle(x, middle, first)
    first, last = lax.optimization_barrier((first, near[-1]))
    far.append(swap(last, core))
    y, sent = row_lse_late(own, x, [*middle, last, *far], first, mass, 2 * share_x)
    got, _ = direct(sent.reshape(-1), across)

    sent, e, shift, mass_a = column_lse(x, y, mass, 2 * share_y, got)
    sent = pair_of(lse2, sent, swap(sent.reshape(-1), core), cols, 1, 2)
    got = direct(sent.reshape(-1), along)

    sums, first_beta, mass_b = weighted(
        first_row_kernel, [(1, rows), (1, cols), (1, cols)], e, [shift], got, 2 * nz)
    for step in range(1, ITERS):
        if step > 1:
            sums, = weighted(row_kernel, [(1, rows)], e, [first_beta, mass_b], got, 2 * nz)
        got = direct(sums.reshape(-1), across)
        part, alpha = weighted(column_kernel, [(1, cols), (1, rows)], e, [mass_a, first_beta], got, na)
        part = pair_of(sum, part, swap(part.reshape(-1), core), cols, 1, 2)
        part, alpha = lax.optimization_barrier((part, alpha))
        got = direct(part.reshape(-1), along)

    half = nz // 2
    gc, gc_send, xa = column_grad(range(half, nz), nz, share_y, y, e, first_beta, xt=xt, alpha=alpha)
    far_gc = shares(gc, swap(gc_send, core), [jnp.bfloat16] * (nz - half))
    gc, gc_send = column_grad(range(half), nz, share_y, y, e, first_beta, xa=xa)
    far_gc, alpha = lax.optimization_barrier((far_gc, alpha))
    far_gc = [swap(part, along[half + z]) for z, part in enumerate(far_gc)]
    yb, scale, last = first_rows([na - 1], share_x, x, y, e, alpha, first_beta, mass_b, got, 2 * nz)
    near_gc = shares(gc, swap(gc_send, core), [jnp.float32] + [jnp.bfloat16] * (half - 1))
    (grad_cam, *parts), yb = lax.optimization_barrier((near_gc, yb))
    parts = [swap(part, along[z + 1]) for z, part in enumerate(parts)]
    last = swap(last, across[na - 1])
    sent = other_rows(list(range(1, na - 1)), share_x, x, yb, e, alpha, jnp.bfloat16)
    sent, last = lax.optimization_barrier((sent, last))
    sent = [swap(part, across[s + 1]) for s, part in enumerate(sent)] + [last]
    gi, = other_rows([0], share_x, x, yb, e, alpha, jnp.float32)
    grad_imu, grad_cam = add_up([gi, *sent], [grad_cam, *parts, *far_gc], scale)
    return grad_imu, grad_cam[None]


def solution(mesh):
    in_specs = (P(("row", "col"), None), P("col", "row", None), P("row"), P("col"))
    out_specs = (P(("row", "col"), None), P("col", "row", None))
    return jax.shard_map(local, mesh=mesh, in_specs=in_specs, out_specs=out_specs, check_vma=False)
```

```python
import functools
import math

import jax
import jax.numpy as jnp
from jax import lax
from jax.experimental import pallas as pl
from jax.experimental.pallas import tpu as pltpu
from jax.sharding import PartitionSpec as P

D = 128
ITERS = 3
EPSILON = D / 20.0
LOG2E = math.log2(math.e)
CROSS = 2.0 * LOG2E / EPSILON
NT = (((1,), (1,)), ((), ()))
VMEM = pl.BlockSpec(memory_space=pltpu.VMEM)
HEAVY = 32


def spread(value, s_ref, sb_ref):
    chunks = value.shape[1] // 128
    for k in range(chunks):
        s_ref[k:k + 1, :] = value[:, k * 128:(k + 1) * 128]
    turned = jnp.transpose(s_ref[...])
    for k in range(chunks):
        sb_ref[k * 128:(k + 1) * 128, :] = jnp.broadcast_to(turned[:, k:k + 1], (128, 128))


def ordered(values, shifts, parts):
    share = values[0].shape[1] // parts
    return [
        jnp.concatenate([value[:, (k ^ s) * share:((k ^ s) + 1) * share] for k in range(parts)], axis=1)
        for value, s in zip(values, shifts)
    ]


def lse2(parts):
    top = functools.reduce(jnp.maximum, parts)
    return top + jnp.log2(sum(jnp.exp2(part - top) for part in parts))


def pipelined(places, chunk, width, a_ref, b_ref, d_ref, tile, finish):
    last = b_ref.shape[0] // width - 1

    def product(n, m):
        b = b_ref[pl.ds(pl.multiple_of(n * width, width), width), :]
        a = a_ref[places[m]:places[m] + chunk, :]
        d_ref[m % 2] = lax.dot_general(a, b, NT, preferred_element_type=jnp.float32)

    product(0, 0)

    def column(n, _):
        start = pl.multiple_of(n * width, width)
        state = None
        for m in range(len(places)):
            if m + 1 < len(places):
                product(n, m + 1)
            else:
                product(jnp.minimum(n + 1, last), 0)
            state = tile(m, start, state)
        finish(start, state)
        return 0

    lax.fori_loop(0, last + 1, column, 0)


def running_max(places, chunk, width, a_ref, b_ref, sb_ref, o_ref, e_ref, shift_ref):
    def column(n, _):
        start = pl.multiple_of(n * width, width)
        b = b_ref[pl.ds(start, width), :]

        def exponents(at):
            d = lax.dot_general(a_ref[at:at + chunk, :], b, NT, preferred_element_type=jnp.float32)
            s = sb_ref[at:at + chunk, :]
            return [d[:, q * 128:(q + 1) * 128] * CROSS + s for q in range(width // 128)]

        peak, total = jnp.full((1, width), -1e30, jnp.float32), jnp.zeros((1, width), jnp.float32)
        for at in places:
            peaks, totals = [], []
            for q, t in enumerate(exponents(at)):
                old = peak[:, q * 128:(q + 1) * 128]
                new = jnp.maximum(old, jnp.max(t, axis=0, keepdims=True))
                part = jnp.sum(jnp.exp2(t - new), axis=0, keepdims=True)
                peaks.append(new)
                totals.append(total[:, q * 128:(q + 1) * 128] * jnp.exp2(old - new) + part)
            peak, total = jnp.concatenate(peaks, axis=1), jnp.concatenate(totals, axis=1)
        o_ref[:, pl.ds(start, width)] = peak + jnp.log2(total)
        if e_ref is not None:
            shift_ref[:, pl.ds(start, width)] = peak
            for at in places:
                for q, t in enumerate(exponents(at)):
                    place = pl.ds(pl.multiple_of(start + q * 128, 128), 128)
                    e_ref[at:at + chunk, place] = jnp.exp2(t - shift_ref[:, place]).astype(jnp.bfloat16)
        return 0

    lax.fori_loop(0, b_ref.shape[0] // width, column, 0)


def lse_pass(places, chunk, width, a_ref, b_ref, sb_ref, d_ref, top_ref, o_ref, e_ref=None, shift_ref=None):
    tiles, group = width // 128, top_ref.shape[0]
    top_ref[...] = jnp.zeros_like(top_ref)

    def lanes_of(start, q):
        return pl.ds(pl.multiple_of(start + q * 128, 128), 128)

    def tile(m, start, state):
        def exponents(g, q):
            at = g * group
            s = sb_ref[places[m] + at:places[m] + at + group, :]
            return d_ref[m % 2, at:at + group, q * 128:(q + 1) * 128] * CROSS + s

        if m == 0:
            tops = [exponents(0, q) for q in range(tiles)]
            for g in range(1, 32 // group):
                tops = [jnp.maximum(top, exponents(g, q)) for q, top in enumerate(tops)]
            state = [(jnp.max(top, axis=0, keepdims=True), jnp.zeros((group, 128), jnp.float32)) for top in tops]
        for g in range(chunk // group):
            for q, (peak, total) in enumerate(state):
                e = jnp.exp2(exponents(g, q) - peak)
                if e_ref is not None:
                    at = places[m] + g * group
                    e_ref[at:at + group, lanes_of(start, q)] = e.astype(jnp.bfloat16)
                state[q] = peak, total + e
        return state

    def finish(start, state):
        for q, (peak, total) in enumerate(state):
            top_ref[...] = jnp.maximum(top_ref[...], total)
            o_ref[:, lanes_of(start, q)] = peak + jnp.log2(jnp.sum(total, axis=0, keepdims=True))
            if e_ref is not None:
                shift_ref[:, lanes_of(start, q)] = peak

    pipelined(places, chunk, width, a_ref, b_ref, d_ref, tile, finish)

    @pl.when(jnp.logical_not(jnp.max(top_ref[...]) < 2.0 ** 60))
    def _():
        running_max(places, chunk, min(width, 256), a_ref, b_ref, sb_ref, o_ref, e_ref, shift_ref)


def put_norms(places, share, y_ref, sb_ref):
    for at in places:
        y = y_ref[at:at + share, :].astype(jnp.float32)
        total = jnp.sum(y * y, axis=1, keepdims=True) * (-LOG2E / EPSILON)
        sb_ref[at:at + share, :] = jnp.broadcast_to(total, (share, 128))


def join(out_ref, parts):
    at = 0
    for part in parts:
        out_ref[at:at + part.shape[0], :] = part[...]
        at += part.shape[0]


def row_lse_early_kernel(width, nx, own_ref, *refs):
    xs, y_other, refs = refs[:nx], refs[nx], refs[nx + 1:]
    x_ref, xt_ref, o_ref, y_ref, sb_ref, d_ref, top_ref = refs
    share = y_other.shape[0]
    mine = own_ref.shape[0] - share
    join(x_ref, [own_ref.at[:mine, :], *xs])
    join(y_ref, [own_ref.at[mine:, :], y_other])
    for k in range(x_ref.shape[0] // 128):
        at = k * 128
        xt_ref[:, at:at + 128] = jnp.transpose(x_ref[at:at + 128, :].astype(jnp.float32)).astype(jnp.bfloat16)
    places = [0, share]
    put_norms(places, share, y_ref, sb_ref)
    lse_pass(places, share, width, y_ref, x_ref, sb_ref, d_ref, top_ref, o_ref)


def row_lse_middle_kernel(width, ny, x_ref, first_ref, *refs):
    ys, (o_ref, y_ref, sb_ref, d_ref, top_ref, sum_ref) = refs[:ny], refs[ny:]
    share = ys[0].shape[0]
    join(y_ref, ys)
    places = [k * share for k in range(ny)]
    put_norms(places, share, y_ref, sb_ref)
    lse_pass(places, share, width, y_ref, x_ref, sb_ref, d_ref, top_ref, sum_ref)
    o_ref[...] = lse2([first_ref[...], sum_ref[...]])


def row_lse_late_kernel(width, ny, own_ref, mass_ref, x_ref, first_ref, *refs):
    ys, (y_ref, o_ref, sb_ref, d_ref, top_ref, sum_ref) = refs[:ny], refs[ny:]
    share, rows, half = ys[0].shape[0], x_ref.shape[0], (ny + 1) // 2
    join(y_ref, [own_ref.at[own_ref.shape[0] - share:, :], *ys])
    places = [k * share for k in range(half - 1, 2 * half) if k != half]
    put_norms(places, share, y_ref, sb_ref)
    lse_pass(places, share, width, y_ref, x_ref, sb_ref, d_ref, top_ref, sum_ref)
    o_ref[:, :rows] = lse2([first_ref[...], sum_ref[...]])
    o_ref[:, rows:] = mass_ref[:, :o_ref.shape[1] - rows]


def column_lse_kernel(width, chunk, na, x_ref, y_ref, mass_ref, *refs):
    got, (o_ref, e_ref, shift_ref, a_ref, s_ref, sb_ref, d_ref, top_ref) = refs[:na], refs[na:]
    rows, cols = x_ref.shape[0], y_ref.shape[0]
    o_ref[:, cols:] = mass_ref[:, mass_ref.shape[1] - o_ref.shape[1] + cols:]
    share = rows // na
    for k in range(na):
        at = rows + (k % 2) * share
        a_ref[:, k * share:(k + 1) * share] = got[k - k % 2][:, at:at + share]
    u = jnp.log2(a_ref[...]) - lse2(ordered([part[:, :rows] for part in got], range(na), na))
    spread(u, s_ref, sb_ref)
    places = list(range(0, rows, chunk))
    lse_pass(places, chunk, width, x_ref, y_ref, sb_ref, d_ref, top_ref, o_ref, e_ref, shift_ref)


def pair_kernel(size, shift, parts, combine, one_ref, two_ref, o_ref):
    two, = ordered([two_ref[:, :size]], [shift], parts)
    o_ref[:, :size] = combine([one_ref[:, :size], two])
    if o_ref.shape[1] > size:
        o_ref[:, size:] = one_ref[:, size:]


def split3(value):
    high = value.astype(jnp.bfloat16)
    rest = value - high.astype(jnp.float32)
    mid = rest.astype(jnp.bfloat16)
    return high, mid, (rest - mid.astype(jnp.float32)).astype(jnp.bfloat16)


def stacked(value):
    high, mid, low = [part.astype(jnp.float32) for part in split3(value)]
    dims = (16, value.shape[1])
    place = lax.broadcasted_iota(jnp.int32, dims, 0)
    parts = jnp.where(place == 0, high, jnp.where(place == 1, mid, jnp.where(place == 2, low, 0.0)))
    return parts.astype(jnp.bfloat16)


def row_sums(width, e_ref, w_ref, w16_ref, acc_ref, o_ref):
    rows, cols = e_ref.shape
    split = rows - acc_ref.shape[0]
    blocks = list(range(0, rows - split, 64))
    dots = list(range(0, split, width))
    for n, at in enumerate(dots):
        got = lax.dot_general(w16_ref[...], e_ref[at:at + width, :], NT, preferred_element_type=jnp.float32)
        for k in blocks[n * len(blocks) // len(dots):(n + 1) * len(blocks) // len(dots)]:
            total = jnp.zeros((64, 128), jnp.float32)
            for q in range(0, cols, 128):
                e = e_ref[split + k:split + k + 64, q:q + 128].astype(jnp.float32)
                total = total + e * w_ref[:, q:q + 128]
            acc_ref[k:k + 64, :] = total
        o_ref[:, at:at + width] = jnp.sum(got, axis=0, keepdims=True)
    for at in range(0, rows - split, 128):
        total = jnp.sum(jnp.transpose(acc_ref[at:at + 128, :]), axis=0, keepdims=True)
        o_ref[:, split + at:split + at + 128] = total


def first_row_kernel(width, shifts, parts, e_ref, shift_ref, *refs):
    nz = len(shifts)
    got, (o_ref, beta_ref, b_ref, w16_ref, acc_ref) = refs[:nz], refs[nz:]
    cols = e_ref.shape[1]
    share = cols // parts
    for k in range(parts):
        at = cols + (k // nz) * share
        b_ref[:, k * share:(k + 1) * share] = got[k % nz][:, at:at + share]
    lse = lse2(ordered([part[:, :cols] for part in got], shifts, parts))
    beta_ref[...] = jnp.exp2(jnp.log2(b_ref[...]) - lse + shift_ref[...])
    w16_ref[...] = stacked(beta_ref[...])
    row_sums(width, e_ref, beta_ref, w16_ref, acc_ref, o_ref)


def new_scale(b_ref, got, shifts, parts):
    return b_ref[...] / sum(ordered([part[...] for part in got], shifts, parts))


def row_kernel(width, shifts, parts, e_ref, first_ref, b_ref, *refs):
    got, (o_ref, w16_ref, acc_ref, w_ref) = refs[:-4], refs[-4:]
    w_ref[...] = first_ref[...] * new_scale(b_ref, got, shifts, parts)
    w16_ref[...] = stacked(w_ref[...])
    row_sums(width, e_ref, w_ref, w16_ref, acc_ref, o_ref)


def column_kernel(width, shifts, parts, e_ref, a_ref, first_ref, *refs):
    got, (o_ref, alpha_ref, w16_ref) = refs[:-3], refs[-3:]
    alpha_ref[...] = a_ref[...] / sum(ordered([part[...] for part in got], shifts, parts))
    w16_ref[...] = stacked(alpha_ref[...])
    for at in range(0, e_ref.shape[1], width):
        sums = jnp.dot(w16_ref[...], e_ref[:, at:at + width], preferred_element_type=jnp.float32)
        o_ref[:, at:at + width] = first_ref[:, at:at + width] * jnp.sum(sums, axis=0, keepdims=True)


def flat(value):
    return value.reshape(1, -1) if value.ndim == 1 else value


def weighted(kernel, outs, e, rows, got, parts):
    got, shifts = got
    size = e.shape[0] if kernel is column_kernel else e.shape[1]
    width = 512 if kernel is column_kernel else 256
    scratch = [pltpu.VMEM((16, size), jnp.bfloat16)]
    if kernel is not column_kernel:
        part = 3 if kernel is row_kernel else 1
        scratch.append(pltpu.VMEM((e.shape[0] * part // 4, 128), jnp.float32))
    if kernel is row_kernel:
        scratch.append(pltpu.VMEM((1, size), jnp.float32))
    return pl.pallas_call(
        functools.partial(kernel, width, tuple(shifts), parts),
        out_shape=[shape(*dims) for dims in outs],
        in_specs=[VMEM] * (1 + len(rows) + len(got)),
        out_specs=[VMEM] * len(outs),
        scratch_shapes=scratch,
        compiler_params=pltpu.CompilerParams(vmem_limit_bytes=16 << 20),
        cost_estimate=pl.CostEstimate(flops=2 * e.size, bytes_accessed=2 * e.size, transcendentals=0),
        name="weighted_sum",
    )(e, *rows, *[flat(part) for part in got])


def pass_cost(depth, lanes):
    return pl.CostEstimate(flops=2 * depth * lanes * D, bytes_accessed=2 * D * (depth + lanes), transcendentals=depth * lanes)


def shape(*dims, dtype=jnp.float32):
    return jax.ShapeDtypeStruct(dims, dtype)


def lse_scratch(depth, chunk, width, group=32):
    return [
        pltpu.VMEM((depth, 128), jnp.float32),
        pltpu.VMEM((2, chunk, width), jnp.float32),
        pltpu.VMEM((group, 128), jnp.float32),
    ]


def row_lse_early(own, xs, y_other, width=1024):
    share = y_other.shape[0]
    rows, depth = own.shape[0] - share + sum(part.shape[0] for part in xs), 2 * share
    return pl.pallas_call(
        functools.partial(row_lse_early_kernel, width, len(xs)),
        out_shape=(shape(rows, D, dtype=jnp.bfloat16), shape(D, rows, dtype=jnp.bfloat16), shape(1, rows)),
        in_specs=[VMEM] * (len(xs) + 2),
        out_specs=(VMEM,) * 3,
        scratch_shapes=[pltpu.VMEM((depth, D), jnp.bfloat16), *lse_scratch(depth, share, width)],
        compiler_params=pltpu.CompilerParams(vmem_limit_bytes=16 << 20),
        cost_estimate=pass_cost(depth, rows),
        name="row_lse_early",
    )(own, *xs, y_other)


def row_lse_middle(x, ys, first, width=1024):
    rows, share = x.shape[0], ys[0].shape[0]
    depth = len(ys) * share
    return pl.pallas_call(
        functools.partial(row_lse_middle_kernel, width, len(ys)),
        out_shape=shape(1, rows),
        in_specs=[VMEM] * (len(ys) + 2),
        out_specs=VMEM,
        scratch_shapes=[
            pltpu.VMEM((depth, D), jnp.bfloat16),
            *lse_scratch(depth, share, width),
            pltpu.VMEM((1, rows), jnp.float32),
        ],
        compiler_params=pltpu.CompilerParams(vmem_limit_bytes=16 << 20),
        cost_estimate=pass_cost(depth, rows),
        name="row_lse_middle",
    )(x, first, *ys)


def row_lse_late(own, x, ys, first, mass, tail, width=1024):
    rows, share = x.shape[0], ys[0].shape[0]
    depth = (len(ys) + 1) * share
    return pl.pallas_call(
        functools.partial(row_lse_late_kernel, width, len(ys)),
        out_shape=(shape(depth, D, dtype=jnp.bfloat16), shape(1, rows + tail)),
        in_specs=[VMEM] * (len(ys) + 4),
        out_specs=(VMEM,) * 2,
        scratch_shapes=[*lse_scratch(depth, share, width), pltpu.VMEM((1, rows), jnp.float32)],
        compiler_params=pltpu.CompilerParams(vmem_limit_bytes=16 << 20),
        cost_estimate=pass_cost(depth // 2, rows),
        name="row_lse_late",
    )(own, mass.reshape(1, -1), x, first, *ys)


def column_lse(x, y, mass, tail, got, width=512, chunk=512):
    rows, cols = x.shape[0], y.shape[0]
    return pl.pallas_call(
        functools.partial(column_lse_kernel, width, chunk, len(got)),
        out_shape=(shape(1, cols + tail), shape(rows, cols, dtype=jnp.bfloat16), shape(1, cols), shape(1, rows)),
        in_specs=[VMEM] * (3 + len(got)),
        out_specs=(VMEM,) * 4,
        scratch_shapes=[pltpu.VMEM((rows // 128, 128), jnp.float32), *lse_scratch(rows, chunk, width, 16)],
        compiler_params=pltpu.CompilerParams(vmem_limit_bytes=16 << 20),
        cost_estimate=pass_cost(rows, cols),
        name="column_lse",
    )(x, y, mass.reshape(1, -1), *[part.reshape(1, -1) for part in got])


def pair_of(combine, one, two, size, shift, parts):
    whole = one.shape[-1]
    return pl.pallas_call(
        functools.partial(pair_kernel, size, shift, parts, combine),
        out_shape=shape(1, whole),
        in_specs=[VMEM] * 2,
        out_specs=VMEM,
        compiler_params=pltpu.CompilerParams(vmem_limit_bytes=16 << 20),
        name="pair",
    )(one.reshape(1, whole), two.reshape(1, whole))


def high_low(value):
    high = value.astype(jnp.bfloat16)
    return high, (value - high.astype(jnp.float32)).astype(jnp.bfloat16)


def put_xa(xt_ref, alpha_ref, xa_ref):
    place = lax.broadcasted_iota(jnp.int32, (128, 512), 0)
    for at in range(0, xt_ref.shape[1], 512):
        alpha = alpha_ref[:, at:at + 512]
        high, low = high_low(xt_ref[:, at:at + 512].astype(jnp.float32) * alpha)
        first, second = high_low(alpha)
        low = jnp.where(place == 126, first.astype(jnp.float32), low.astype(jnp.float32))
        low = jnp.where(place == 127, second.astype(jnp.float32), low)
        xa_ref[:128, at:at + 512] = high
        xa_ref[128:, at:at + 512] = low.astype(jnp.bfloat16)


def column_parts(blocks, share, xa_ref, y_ref, e_ref, first_ref, own_ref, sent_ref,
                 bb_ref, cb_ref, s_ref, count_ref, acc_ref):
    spread(jnp.concatenate([first_ref[:, at:at + share] for at in blocks], axis=1), s_ref, bb_ref)
    lower = lax.broadcasted_iota(jnp.int32, (128, share), 0) < 126
    for k, at in enumerate(blocks):
        to = k * share
        got = jnp.dot(xa_ref[...], e_ref[:, at:at + share], preferred_element_type=jnp.float32)
        acc_ref[:, to:to + share] = got[:128] + jnp.where(lower, got[128:], 0.0)
        count_ref[:, to:to + share] = got[254:255] + got[255:256]
    spread(count_ref[...], s_ref, cb_ref)
    own = own_ref.shape[0]
    for k, at in enumerate(blocks):
        for q in range(0, share, 128):
            to = k * share + q
            pulled = jnp.transpose(acc_ref[:, to:to + 128])
            whole = cb_ref[to:to + 128, :] * y_ref[at + q:at + q + 128, :].astype(jnp.float32)
            grad = bb_ref[to:to + 128, :] * (whole - pulled)
            if to < own:
                own_ref[to:to + 128, :] = grad
            else:
                sent_ref[to - own:to - own + 128, :] = grad.astype(jnp.bfloat16)


def first_columns_kernel(blocks, share, xt_ref, y_ref, e_ref, alpha_ref, first_ref, own_ref, sent_ref, xa_ref, *rest):
    put_xa(xt_ref, alpha_ref, xa_ref)
    column_parts(blocks, share, xa_ref, y_ref, e_ref, first_ref, own_ref, sent_ref, *rest)


def columns_kernel(blocks, share, xa_ref, y_ref, e_ref, first_ref, own_ref, sent_ref, *rest):
    column_parts(blocks, share, xa_ref, y_ref, e_ref, first_ref, own_ref, sent_ref, *rest)


def column_grad(zs, nz, share, y, e, first, xt=None, alpha=None, xa=None):
    rows, size = e.shape[0], 2 * len(zs) * share
    blocks = [z * share for z in zs] + [(nz + z) * share for z in zs]
    out_shape = [shape(size // 2, D), shape(size // 2, D, dtype=jnp.bfloat16)]
    if xa is None:
        kernel, args = first_columns_kernel, (xt, y, e, alpha, first)
        out_shape.append(shape(256, rows, dtype=jnp.bfloat16))
    else:
        kernel, args = columns_kernel, (xa, y, e, first)
    return pl.pallas_call(
        functools.partial(kernel, blocks, share),
        out_shape=out_shape,
        in_specs=[VMEM] * len(args),
        out_specs=[VMEM] * len(out_shape),
        scratch_shapes=[
            pltpu.VMEM((size, 128), jnp.float32),
            pltpu.VMEM((size, 128), jnp.float32),
            pltpu.VMEM((size // 128, 128), jnp.float32),
            pltpu.VMEM((1, size), jnp.float32),
            pltpu.VMEM((128, size), jnp.float32),
        ],
        compiler_params=pltpu.CompilerParams(vmem_limit_bytes=16 << 20),
        cost_estimate=pl.CostEstimate(flops=4 * rows * size * D, bytes_accessed=2 * rows * size, transcendentals=0),
        name="column_grad",
    )(*args)


def row_block(at, chunk, x_ref, e_ref, yb_ref, scale):
    got = jnp.dot(e_ref[pl.ds(at, chunk), :], yb_ref[...], preferred_element_type=jnp.float32)
    lower = lax.broadcasted_iota(jnp.int32, (chunk, 128), 1) < 126
    total = got[:, 254:255] + got[:, 255:256]
    pulled = got[:, :128] + jnp.where(lower, got[:, 128:], 0.0)
    x = x_ref[pl.ds(at, chunk), :].astype(jnp.float32)
    return 2.0 * scale * (total * x - pulled)


def put_yb(y_ref, beta, yb_ref, s_ref, bb_ref):
    spread(beta, s_ref, bb_ref)
    place = lax.broadcasted_iota(jnp.int32, (256, 128), 1)
    for at in range(0, y_ref.shape[0], 256):
        beta = bb_ref[at:at + 256, :]
        high, low = high_low(y_ref[at:at + 256, :].astype(jnp.float32) * beta)
        first, second = high_low(beta)
        low = jnp.where(place == 126, first.astype(jnp.float32), low.astype(jnp.float32))
        low = jnp.where(place == 127, second.astype(jnp.float32), low)
        yb_ref[at:at + 256, :128] = high
        yb_ref[at:at + 256, 128:] = low.astype(jnp.bfloat16)


def row_parts(parts, x_ref, e_ref, alpha_ref, yb_ref, outs, sa_ref, ab_ref):
    share = outs[0].shape[0]
    chunk = math.gcd(share, 512)
    for part, out_ref in zip(parts, outs):
        spread(alpha_ref[:, part * share:(part + 1) * share], sa_ref, ab_ref)
        for k in range(0, share, chunk):
            grad = row_block(part * share + k, chunk, x_ref, e_ref, yb_ref, ab_ref[k:k + chunk, :])
            out_ref[k:k + chunk, :] = grad.astype(out_ref.dtype)


def first_rows_kernel(parts, shifts, blocks, nz, x_ref, y_ref, e_ref, alpha_ref, first_ref, b_ref, *refs):
    got, (yb_ref, scale_ref, *outs), (s_ref, bb_ref, sa_ref, ab_ref) = refs[:nz], refs[nz:-4], refs[-4:]
    scale = new_scale(b_ref, got, shifts, blocks)
    scale_ref[...] = scale[:, :scale_ref.shape[1]]
    put_yb(y_ref, first_ref[...] * scale, yb_ref, s_ref, bb_ref)
    row_parts(parts, x_ref, e_ref, alpha_ref, yb_ref, outs, sa_ref, ab_ref)


def rows_kernel(parts, x_ref, yb_ref, e_ref, alpha_ref, *refs):
    row_parts(parts, x_ref, e_ref, alpha_ref, yb_ref, refs[:-2], *refs[-2:])


def rows_scratch(share):
    return [pltpu.VMEM((share // 128, 128), jnp.float32), pltpu.VMEM((share, 128), jnp.float32)]


def rows_cost(share, parts, cols):
    size = share * len(parts) * cols
    return pl.CostEstimate(flops=4 * size * D, bytes_accessed=2 * size, transcendentals=0)


def first_rows(parts, share, x, y, e, alpha, first, mass, got, blocks):
    cols = y.shape[0]
    got, shifts = got
    return pl.pallas_call(
        functools.partial(first_rows_kernel, parts, tuple(shifts), blocks, len(got)),
        out_shape=[shape(cols, 256, dtype=jnp.bfloat16), shape(1, cols // blocks)]
        + [shape(share, D, dtype=jnp.bfloat16)] * len(parts),
        in_specs=[VMEM] * (6 + len(got)),
        out_specs=[VMEM] * (2 + len(parts)),
        scratch_shapes=[
            pltpu.VMEM((cols // 128, 128), jnp.float32),
            pltpu.VMEM((cols, 128), jnp.float32),
            *rows_scratch(share),
        ],
        compiler_params=pltpu.CompilerParams(vmem_limit_bytes=16 << 20),
        cost_estimate=rows_cost(share * HEAVY, parts, cols),
        name="first_rows",
    )(x, y, e, alpha, first, mass, *[flat(part) for part in got])


def other_rows(parts, share, x, yb, e, alpha, dtype):
    return pl.pallas_call(
        functools.partial(rows_kernel, parts),
        out_shape=[shape(share, D, dtype=dtype)] * len(parts),
        in_specs=[VMEM] * 4,
        out_specs=[VMEM] * len(parts),
        scratch_shapes=rows_scratch(share),
        compiler_params=pltpu.CompilerParams(vmem_limit_bytes=16 << 20),
        cost_estimate=rows_cost(share, parts, yb.shape[0]),
        name="other_rows",
    )(x, yb, e, alpha)


def add_up_kernel(na, scale_ref, *refs):
    ins, (rows_ref, cols_ref, s_ref, sb_ref) = refs[:-4], refs[-4:]
    rows_ref[...] = sum(part[...].astype(jnp.float32) for part in ins[:na])
    spread(scale_ref[...], s_ref, sb_ref)
    cols_ref[...] = 2.0 * sb_ref[...] * sum(part[...].astype(jnp.float32) for part in ins[na:])


def add_up(rows, columns, scale):
    share = scale.shape[1]
    return pl.pallas_call(
        functools.partial(add_up_kernel, len(rows)),
        out_shape=(shape(*rows[0].shape), shape(*columns[0].shape)),
        in_specs=[VMEM] * (1 + len(rows) + len(columns)),
        out_specs=(VMEM,) * 2,
        scratch_shapes=rows_scratch(share),
        compiler_params=pltpu.CompilerParams(vmem_limit_bytes=16 << 20),
        name="add_up",
    )(scale, *rows, *columns)


def shares_kernel(gc_ref, other_ref, *outs):
    share = outs[0].shape[0]
    for k, out_ref in enumerate(outs):
        at = k * share
        total = gc_ref[at:at + share, :] + other_ref[at:at + share, :].astype(jnp.float32)
        out_ref[...] = total.astype(out_ref.dtype)


def shares(gc, other, dtypes):
    share = gc.shape[0] // len(dtypes)
    return pl.pallas_call(
        shares_kernel,
        out_shape=[shape(share, D, dtype=dtype) for dtype in dtypes],
        in_specs=[VMEM] * 2,
        out_specs=[VMEM] * len(dtypes),
        compiler_params=pltpu.CompilerParams(vmem_limit_bytes=16 << 20),
        name="shares",
    )(gc, other)


class Groups:
    def __init__(self, nrow, ncol):
        self.count = nrow * ncol
        self.across = [(a << 1) * ncol + b for a in range(nrow // 2) for b in range(2)]
        self.along = [z << 1 for z in range(ncol // 2)]
        self.core = ncol

    def swap(self, value, mask):
        if mask == 0:
            return value
        return lax.ppermute(value, ("row", "col"), [(i, i ^ mask) for i in range(self.count)])


def local(imu, camera, imu_mass, cam_mass):
    nrow, ncol = lax.axis_size("row"), lax.axis_size("col")
    groups = Groups(nrow, ncol)
    swap, across, along, core = groups.swap, groups.across, groups.along, groups.core
    na, nz = len(across), len(along)
    share_x, share_y = imu.shape[0], camera.shape[1]
    rows, cols = na * share_x, 2 * nz * share_y

    def direct(value, masks):
        return [swap(value, mask) for mask in masks], range(len(masks))

    xs, _ = direct(imu, across)
    own, mine = lax.optimization_barrier((jnp.concatenate([imu, camera[0]]), camera[0]))
    near = [mine] + [None] * (nz - 1)
    for z in range(1, nz):
        if not z & (z - 1):
            near[z] = swap(mine if z == 1 else camera[0], along[z])
    far = [swap(mine, core)]

    def pair(mass, place, share):
        return [lax.dynamic_slice_in_dim(mass, (place ^ k) * share, share, 0) for k in range(2)]

    row, col = lax.axis_index("row"), lax.axis_index("col")
    mass = jnp.concatenate(pair(imu_mass, col, share_x) + pair(cam_mass, row, share_y))

    x, xt, first = row_lse_early(own, xs[1:], far[0])
    relays = [z for z in range(2, nz) if not z & (z - 1)]
    first, mass, got = lax.optimization_barrier((first, mass, [near[z] for z in relays]))
    for z, part in zip(relays, got):
        near[z] = part
    for z in range(1, nz):
        if z & (z - 1):
            near[z] = swap(near[z & (z - 1)], along[z & -z])
    middle = near[1:-1]
    far += [swap(part, core) for part in middle]
    first = row_lse_middle(x, middle, first)
    first, last = lax.optimization_barrier((first, near[-1]))
    far.append(swap(last, core))
    y, sent = row_lse_late(own, x, [*middle, last, *far], first, mass, 2 * share_x)
    got, _ = direct(sent.reshape(-1), across)

    sent, e, shift, mass_a = column_lse(x, y, mass, 2 * share_y, got)
    sent = pair_of(lse2, sent, swap(sent.reshape(-1), core), cols, 1, 2)
    got = direct(sent.reshape(-1), along)

    sums, first_beta, mass_b = weighted(
        first_row_kernel, [(1, rows), (1, cols), (1, cols)], e, [shift], got, 2 * nz)
    for step in range(1, ITERS):
        if step > 1:
            sums, = weighted(row_kernel, [(1, rows)], e, [first_beta, mass_b], got, 2 * nz)
        got = direct(sums.reshape(-1), across)
        part, alpha = weighted(column_kernel, [(1, cols), (1, rows)], e, [mass_a, first_beta], got, na)
        part = pair_of(sum, part, swap(part.reshape(-1), core), cols, 1, 2)
        part, alpha = lax.optimization_barrier((part, alpha))
        got = direct(part.reshape(-1), along)

    half = nz // 2
    gc, gc_send, xa = column_grad(range(half, nz), nz, share_y, y, e, first_beta, xt=xt, alpha=alpha)
    far_gc = shares(gc, swap(gc_send, core), [jnp.bfloat16] * (nz - half))
    gc, gc_send = column_grad(range(half), nz, share_y, y, e, first_beta, xa=xa)
    far_gc, alpha = lax.optimization_barrier((far_gc, alpha))
    far_gc = [swap(part, along[half + z]) for z, part in enumerate(far_gc)]
    yb, scale, last = first_rows([na - 1], share_x, x, y, e, alpha, first_beta, mass_b, got, 2 * nz)
    near_gc = shares(gc, swap(gc_send, core), [jnp.float32] + [jnp.bfloat16] * (half - 1))
    (grad_cam, *parts), yb = lax.optimization_barrier((near_gc, yb))
    parts = [swap(part, along[z + 1]) for z, part in enumerate(parts)]
    last = swap(last, across[na - 1])
    sent = other_rows(list(range(1, na - 1)), share_x, x, yb, e, alpha, jnp.bfloat16)
    sent = [swap(part, across[s + 1]) for s, part in enumerate(sent)] + [last]
    gi, = other_rows([0], share_x, x, yb, e, alpha, jnp.float32)
    grad_imu, grad_cam = add_up([gi, *sent], [grad_cam, *parts, *far_gc], scale)
    return grad_imu, grad_cam[None]


def solution(mesh):
    in_specs = (P(("row", "col"), None), P("col", "row", None), P("row"), P("col"))
    out_specs = (P(("row", "col"), None), P("col", "row", None))
    return jax.shard_map(local, mesh=mesh, in_specs=in_specs, out_specs=out_specs, check_vma=False)
```

```python
import functools
import math

import jax
import jax.numpy as jnp
from jax import lax
from jax.experimental import pallas as pl
from jax.experimental.pallas import tpu as pltpu
from jax.sharding import PartitionSpec as P

D = 128
ITERS = 3
EPSILON = D / 20.0
LOG2E = math.log2(math.e)
CROSS = 2.0 * LOG2E / EPSILON
NT = (((1,), (1,)), ((), ()))
VMEM = pl.BlockSpec(memory_space=pltpu.VMEM)
HEAVY = 32


def spread(value, s_ref, sb_ref):
    chunks = value.shape[1] // 128
    for k in range(chunks):
        s_ref[k:k + 1, :] = value[:, k * 128:(k + 1) * 128]
    turned = jnp.transpose(s_ref[...])
    for k in range(chunks):
        sb_ref[k * 128:(k + 1) * 128, :] = jnp.broadcast_to(turned[:, k:k + 1], (128, 128))


def ordered(values, shifts, parts):
    share = values[0].shape[1] // parts
    return [
        jnp.concatenate([value[:, (k ^ s) * share:((k ^ s) + 1) * share] for k in range(parts)], axis=1)
        for value, s in zip(values, shifts)
    ]


def lse2(parts):
    top = functools.reduce(jnp.maximum, parts)
    return top + jnp.log2(sum(jnp.exp2(part - top) for part in parts))


def pipelined(places, chunk, width, a_ref, b_ref, d_ref, tile, finish):
    last = b_ref.shape[0] // width - 1

    def product(n, m):
        b = b_ref[pl.ds(pl.multiple_of(n * width, width), width), :]
        a = a_ref[places[m]:places[m] + chunk, :]
        d_ref[m % 2] = lax.dot_general(a, b, NT, preferred_element_type=jnp.float32)

    product(0, 0)

    def column(n, _):
        start = pl.multiple_of(n * width, width)
        state = None
        for m in range(len(places)):
            if m + 1 < len(places):
                product(n, m + 1)
            else:
                product(jnp.minimum(n + 1, last), 0)
            state = tile(m, start, state)
        finish(start, state)
        return 0

    lax.fori_loop(0, last + 1, column, 0)


def running_max(places, chunk, width, a_ref, b_ref, sb_ref, o_ref, e_ref, shift_ref):
    def column(n, _):
        start = pl.multiple_of(n * width, width)
        b = b_ref[pl.ds(start, width), :]

        def exponents(at):
            d = lax.dot_general(a_ref[at:at + chunk, :], b, NT, preferred_element_type=jnp.float32)
            s = sb_ref[at:at + chunk, :]
            return [d[:, q * 128:(q + 1) * 128] * CROSS + s for q in range(width // 128)]

        peak, total = jnp.full((1, width), -1e30, jnp.float32), jnp.zeros((1, width), jnp.float32)
        for at in places:
            peaks, totals = [], []
            for q, t in enumerate(exponents(at)):
                old = peak[:, q * 128:(q + 1) * 128]
                new = jnp.maximum(old, jnp.max(t, axis=0, keepdims=True))
                part = jnp.sum(jnp.exp2(t - new), axis=0, keepdims=True)
                peaks.append(new)
                totals.append(total[:, q * 128:(q + 1) * 128] * jnp.exp2(old - new) + part)
            peak, total = jnp.concatenate(peaks, axis=1), jnp.concatenate(totals, axis=1)
        o_ref[:, pl.ds(start, width)] = peak + jnp.log2(total)
        if e_ref is not None:
            shift_ref[:, pl.ds(start, width)] = peak
            for at in places:
                for q, t in enumerate(exponents(at)):
                    place = pl.ds(pl.multiple_of(start + q * 128, 128), 128)
                    e_ref[at:at + chunk, place] = jnp.exp2(t - shift_ref[:, place]).astype(jnp.bfloat16)
        return 0

    lax.fori_loop(0, b_ref.shape[0] // width, column, 0)


def lse_pass(places, chunk, width, a_ref, b_ref, sb_ref, d_ref, top_ref, o_ref, e_ref=None, shift_ref=None):
    tiles, group = width // 128, top_ref.shape[0]
    top_ref[...] = jnp.zeros_like(top_ref)

    def lanes_of(start, q):
        return pl.ds(pl.multiple_of(start + q * 128, 128), 128)

    def tile(m, start, state):
        def exponents(g, q):
            at = g * group
            s = sb_ref[places[m] + at:places[m] + at + group, :]
            return d_ref[m % 2, at:at + group, q * 128:(q + 1) * 128] * CROSS + s

        if m == 0:
            tops = [exponents(0, q) for q in range(tiles)]
            for g in range(1, 32 // group):
                tops = [jnp.maximum(top, exponents(g, q)) for q, top in enumerate(tops)]
            state = [(jnp.max(top, axis=0, keepdims=True), jnp.zeros((group, 128), jnp.float32)) for top in tops]
        for g in range(chunk // group):
            for q, (peak, total) in enumerate(state):
                e = jnp.exp2(exponents(g, q) - peak)
                if e_ref is not None:
                    at = places[m] + g * group
                    e_ref[at:at + group, lanes_of(start, q)] = e.astype(jnp.bfloat16)
                state[q] = peak, total + e
        return state

    def finish(start, state):
        for q, (peak, total) in enumerate(state):
            top_ref[...] = jnp.maximum(top_ref[...], total)
            o_ref[:, lanes_of(start, q)] = peak + jnp.log2(jnp.sum(total, axis=0, keepdims=True))
            if e_ref is not None:
                shift_ref[:, lanes_of(start, q)] = peak

    pipelined(places, chunk, width, a_ref, b_ref, d_ref, tile, finish)

    @pl.when(jnp.logical_not(jnp.max(top_ref[...]) < 2.0 ** 60))
    def _():
        running_max(places, chunk, min(width, 256), a_ref, b_ref, sb_ref, o_ref, e_ref, shift_ref)


def put_norms(places, share, y_ref, sb_ref):
    for at in places:
        y = y_ref[at:at + share, :].astype(jnp.float32)
        total = jnp.sum(y * y, axis=1, keepdims=True) * (-LOG2E / EPSILON)
        sb_ref[at:at + share, :] = jnp.broadcast_to(total, (share, 128))


def join(out_ref, parts):
    at = 0
    for part in parts:
        out_ref[at:at + part.shape[0], :] = part[...]
        at += part.shape[0]


def row_lse_early_kernel(width, nx, own_ref, *refs):
    xs, y_other, refs = refs[:nx], refs[nx], refs[nx + 1:]
    x_ref, xt_ref, o_ref, y_ref, sb_ref, d_ref, top_ref = refs
    share = y_other.shape[0]
    mine = own_ref.shape[0] - share
    join(x_ref, [own_ref.at[:mine, :], *xs])
    join(y_ref, [own_ref.at[mine:, :], y_other])
    for k in range(x_ref.shape[0] // 128):
        at = k * 128
        xt_ref[:, at:at + 128] = jnp.transpose(x_ref[at:at + 128, :].astype(jnp.float32)).astype(jnp.bfloat16)
    places = [0, share]
    put_norms(places, share, y_ref, sb_ref)
    lse_pass(places, share, width, y_ref, x_ref, sb_ref, d_ref, top_ref, o_ref)


def row_lse_middle_kernel(width, ny, x_ref, first_ref, *refs):
    ys, (o_ref, y_ref, sb_ref, d_ref, top_ref, sum_ref) = refs[:ny], refs[ny:]
    share = ys[0].shape[0]
    join(y_ref, ys)
    places = [k * share for k in range(ny)]
    put_norms(places, share, y_ref, sb_ref)
    lse_pass(places, share, width, y_ref, x_ref, sb_ref, d_ref, top_ref, sum_ref)
    o_ref[...] = lse2([first_ref[...], sum_ref[...]])


def row_lse_late_kernel(width, ny, own_ref, mass_ref, x_ref, first_ref, *refs):
    ys, (y_ref, o_ref, sb_ref, d_ref, top_ref, sum_ref) = refs[:ny], refs[ny:]
    share, rows, half = ys[0].shape[0], x_ref.shape[0], (ny + 1) // 2
    join(y_ref, [own_ref.at[own_ref.shape[0] - share:, :], *ys])
    places = [k * share for k in range(half - 1, 2 * half) if k != half]
    put_norms(places, share, y_ref, sb_ref)
    lse_pass(places, share, width, y_ref, x_ref, sb_ref, d_ref, top_ref, sum_ref)
    o_ref[:, :rows] = lse2([first_ref[...], sum_ref[...]])
    o_ref[:, rows:] = mass_ref[:, :o_ref.shape[1] - rows]


def column_lse_kernel(width, chunk, na, x_ref, y_ref, mass_ref, *refs):
    got, (o_ref, e_ref, shift_ref, a_ref, s_ref, sb_ref, d_ref, top_ref) = refs[:na], refs[na:]
    rows, cols = x_ref.shape[0], y_ref.shape[0]
    o_ref[:, cols:] = mass_ref[:, mass_ref.shape[1] - o_ref.shape[1] + cols:]
    share = rows // na
    for k in range(na):
        at = rows + (k % 2) * share
        a_ref[:, k * share:(k + 1) * share] = got[k - k % 2][:, at:at + share]
    u = jnp.log2(a_ref[...]) - lse2(ordered([part[:, :rows] for part in got], range(na), na))
    spread(u, s_ref, sb_ref)
    places = list(range(0, rows, chunk))
    lse_pass(places, chunk, width, x_ref, y_ref, sb_ref, d_ref, top_ref, o_ref, e_ref, shift_ref)


def pair_kernel(size, shift, parts, combine, one_ref, two_ref, o_ref):
    two, = ordered([two_ref[:, :size]], [shift], parts)
    o_ref[:, :size] = combine([one_ref[:, :size], two])
    if o_ref.shape[1] > size:
        o_ref[:, size:] = one_ref[:, size:]


def split3(value):
    high = value.astype(jnp.bfloat16)
    rest = value - high.astype(jnp.float32)
    mid = rest.astype(jnp.bfloat16)
    return high, mid, (rest - mid.astype(jnp.float32)).astype(jnp.bfloat16)


def stacked(value):
    high, mid, low = [part.astype(jnp.float32) for part in split3(value)]
    dims = (16, value.shape[1])
    place = lax.broadcasted_iota(jnp.int32, dims, 0)
    parts = jnp.where(place == 0, high, jnp.where(place == 1, mid, jnp.where(place == 2, low, 0.0)))
    return parts.astype(jnp.bfloat16)


def row_sums(e_ref, w_ref, o_ref):
    rows, cols = e_ref.shape

    def block(n, _):
        totals = []
        for k in range(0, 128, 64):
            at = pl.multiple_of(n * 128 + k, 64)
            total = jnp.zeros((64, 128), jnp.float32)
            for q in range(0, cols, 128):
                total = total + e_ref[pl.ds(at, 64), q:q + 128].astype(jnp.float32) * w_ref[:, q:q + 128]
            totals.append(total)
        whole = jnp.transpose(jnp.concatenate(totals, axis=0))
        o_ref[:, pl.ds(pl.multiple_of(n * 128, 128), 128)] = jnp.sum(whole, axis=0, keepdims=True)
        return 0

    lax.fori_loop(0, rows // 128, block, 0)


def first_row_kernel(shifts, parts, e_ref, shift_ref, *refs):
    nz = len(shifts)
    got, (o_ref, beta_ref, b_ref) = refs[:nz], refs[nz:]
    cols = e_ref.shape[1]
    share = cols // parts
    for k in range(parts):
        at = cols + (k // nz) * share
        b_ref[:, k * share:(k + 1) * share] = got[k % nz][:, at:at + share]
    lse = lse2(ordered([part[:, :cols] for part in got], shifts, parts))
    beta_ref[...] = jnp.exp2(jnp.log2(b_ref[...]) - lse + shift_ref[...])
    row_sums(e_ref, beta_ref, o_ref)


def new_scale(b_ref, got, shifts, parts):
    return b_ref[...] / sum(ordered([part[...] for part in got], shifts, parts))


def row_kernel(shifts, parts, e_ref, first_ref, b_ref, *refs):
    got, (o_ref, w_ref) = refs[:-2], refs[-2:]
    w_ref[...] = first_ref[...] * new_scale(b_ref, got, shifts, parts)
    row_sums(e_ref, w_ref, o_ref)


def column_kernel(shifts, parts, e_ref, a_ref, first_ref, *refs):
    got, (o_ref, alpha_ref, w16_ref) = refs[:-3], refs[-3:]
    alpha_ref[...] = a_ref[...] / sum(ordered([part[...] for part in got], shifts, parts))
    w16_ref[...] = stacked(alpha_ref[...])
    width = 512
    for at in range(0, e_ref.shape[1], width):
        sums = jnp.dot(w16_ref[...], e_ref[:, at:at + width], preferred_element_type=jnp.float32)
        o_ref[:, at:at + width] = first_ref[:, at:at + width] * jnp.sum(sums, axis=0, keepdims=True)


def flat(value):
    return value.reshape(1, -1) if value.ndim == 1 else value


def weighted(kernel, outs, e, rows, got, parts):
    got, shifts = got
    scratch = []
    if kernel is column_kernel:
        scratch = [pltpu.VMEM((16, e.shape[0]), jnp.bfloat16)]
    if kernel is row_kernel:
        scratch = [pltpu.VMEM((1, e.shape[1]), jnp.float32)]
    return pl.pallas_call(
        functools.partial(kernel, tuple(shifts), parts),
        out_shape=[shape(*dims) for dims in outs],
        in_specs=[VMEM] * (1 + len(rows) + len(got)),
        out_specs=[VMEM] * len(outs),
        scratch_shapes=scratch,
        compiler_params=pltpu.CompilerParams(vmem_limit_bytes=16 << 20),
        cost_estimate=pl.CostEstimate(flops=2 * e.size, bytes_accessed=2 * e.size, transcendentals=0),
        name="weighted_sum",
    )(e, *rows, *[flat(part) for part in got])


def pass_cost(depth, lanes):
    return pl.CostEstimate(flops=2 * depth * lanes * D, bytes_accessed=2 * D * (depth + lanes), transcendentals=depth * lanes)


def shape(*dims, dtype=jnp.float32):
    return jax.ShapeDtypeStruct(dims, dtype)


def lse_scratch(depth, chunk, width, group=32):
    return [
        pltpu.VMEM((depth, 128), jnp.float32),
        pltpu.VMEM((2, chunk, width), jnp.float32),
        pltpu.VMEM((group, 128), jnp.float32),
    ]


def row_lse_early(own, xs, y_other, width=1024):
    share = y_other.shape[0]
    rows, depth = own.shape[0] - share + sum(part.shape[0] for part in xs), 2 * share
    return pl.pallas_call(
        functools.partial(row_lse_early_kernel, width, len(xs)),
        out_shape=(shape(rows, D, dtype=jnp.bfloat16), shape(D, rows, dtype=jnp.bfloat16), shape(1, rows)),
        in_specs=[VMEM] * (len(xs) + 2),
        out_specs=(VMEM,) * 3,
        scratch_shapes=[pltpu.VMEM((depth, D), jnp.bfloat16), *lse_scratch(depth, share, width)],
        compiler_params=pltpu.CompilerParams(vmem_limit_bytes=16 << 20),
        cost_estimate=pass_cost(depth, rows),
        name="row_lse_early",
    )(own, *xs, y_other)


def row_lse_middle(x, ys, first, width=1024):
    rows, share = x.shape[0], ys[0].shape[0]
    depth = len(ys) * share
    return pl.pallas_call(
        functools.partial(row_lse_middle_kernel, width, len(ys)),
        out_shape=shape(1, rows),
        in_specs=[VMEM] * (len(ys) + 2),
        out_specs=VMEM,
        scratch_shapes=[
            pltpu.VMEM((depth, D), jnp.bfloat16),
            *lse_scratch(depth, share, width),
            pltpu.VMEM((1, rows), jnp.float32),
        ],
        compiler_params=pltpu.CompilerParams(vmem_limit_bytes=16 << 20),
        cost_estimate=pass_cost(depth, rows),
        name="row_lse_middle",
    )(x, first, *ys)


def row_lse_late(own, x, ys, first, mass, tail, width=1024):
    rows, share = x.shape[0], ys[0].shape[0]
    depth = (len(ys) + 1) * share
    return pl.pallas_call(
        functools.partial(row_lse_late_kernel, width, len(ys)),
        out_shape=(shape(depth, D, dtype=jnp.bfloat16), shape(1, rows + tail)),
        in_specs=[VMEM] * (len(ys) + 4),
        out_specs=(VMEM,) * 2,
        scratch_shapes=[*lse_scratch(depth, share, width), pltpu.VMEM((1, rows), jnp.float32)],
        compiler_params=pltpu.CompilerParams(vmem_limit_bytes=16 << 20),
        cost_estimate=pass_cost(depth // 2, rows),
        name="row_lse_late",
    )(own, mass.reshape(1, -1), x, first, *ys)


def column_lse(x, y, mass, tail, got, width=1024, chunk=512):
    rows, cols = x.shape[0], y.shape[0]
    return pl.pallas_call(
        functools.partial(column_lse_kernel, width, chunk, len(got)),
        out_shape=(shape(1, cols + tail), shape(rows, cols, dtype=jnp.bfloat16), shape(1, cols), shape(1, rows)),
        in_specs=[VMEM] * (3 + len(got)),
        out_specs=(VMEM,) * 4,
        scratch_shapes=[pltpu.VMEM((rows // 128, 128), jnp.float32), *lse_scratch(rows, chunk, width, 16)],
        compiler_params=pltpu.CompilerParams(vmem_limit_bytes=16 << 20),
        cost_estimate=pass_cost(rows, cols),
        name="column_lse",
    )(x, y, mass.reshape(1, -1), *[part.reshape(1, -1) for part in got])


def pair_of(combine, one, two, size, shift, parts):
    whole = one.shape[-1]
    return pl.pallas_call(
        functools.partial(pair_kernel, size, shift, parts, combine),
        out_shape=shape(1, whole),
        in_specs=[VMEM] * 2,
        out_specs=VMEM,
        compiler_params=pltpu.CompilerParams(vmem_limit_bytes=16 << 20),
        name="pair",
    )(one.reshape(1, whole), two.reshape(1, whole))


def high_low(value):
    high = value.astype(jnp.bfloat16)
    return high, (value - high.astype(jnp.float32)).astype(jnp.bfloat16)


def put_xa(xt_ref, alpha_ref, xa_ref):
    place = lax.broadcasted_iota(jnp.int32, (128, 512), 0)
    for at in range(0, xt_ref.shape[1], 512):
        alpha = alpha_ref[:, at:at + 512]
        high, low = high_low(xt_ref[:, at:at + 512].astype(jnp.float32) * alpha)
        first, second = high_low(alpha)
        low = jnp.where(place == 126, first.astype(jnp.float32), low.astype(jnp.float32))
        low = jnp.where(place == 127, second.astype(jnp.float32), low)
        xa_ref[:128, at:at + 512] = high
        xa_ref[128:, at:at + 512] = low.astype(jnp.bfloat16)


def column_parts(blocks, share, xa_ref, y_ref, e_ref, first_ref, own_ref, sent_ref,
                 bb_ref, cb_ref, s_ref, count_ref, acc_ref):
    spread(jnp.concatenate([first_ref[:, at:at + share] for at in blocks], axis=1), s_ref, bb_ref)
    lower = lax.broadcasted_iota(jnp.int32, (128, share), 0) < 126
    for k, at in enumerate(blocks):
        to = k * share
        got = jnp.dot(xa_ref[...], e_ref[:, at:at + share], preferred_element_type=jnp.float32)
        acc_ref[:, to:to + share] = got[:128] + jnp.where(lower, got[128:], 0.0)
        count_ref[:, to:to + share] = got[254:255] + got[255:256]
    spread(count_ref[...], s_ref, cb_ref)
    own = own_ref.shape[0]
    for k, at in enumerate(blocks):
        for q in range(0, share, 128):
            to = k * share + q
            pulled = jnp.transpose(acc_ref[:, to:to + 128])
            whole = cb_ref[to:to + 128, :] * y_ref[at + q:at + q + 128, :].astype(jnp.float32)
            grad = bb_ref[to:to + 128, :] * (whole - pulled)
            if to < own:
                own_ref[to:to + 128, :] = grad
            else:
                sent_ref[to - own:to - own + 128, :] = grad.astype(jnp.bfloat16)


def first_columns_kernel(blocks, share, xt_ref, y_ref, e_ref, alpha_ref, first_ref, own_ref, sent_ref, xa_ref, *rest):
    put_xa(xt_ref, alpha_ref, xa_ref)
    column_parts(blocks, share, xa_ref, y_ref, e_ref, first_ref, own_ref, sent_ref, *rest)


def columns_kernel(blocks, share, xa_ref, y_ref, e_ref, first_ref, own_ref, sent_ref, *rest):
    column_parts(blocks, share, xa_ref, y_ref, e_ref, first_ref, own_ref, sent_ref, *rest)


def column_grad(zs, nz, share, y, e, first, xt=None, alpha=None, xa=None):
    rows, size = e.shape[0], 2 * len(zs) * share
    blocks = [z * share for z in zs] + [(nz + z) * share for z in zs]
    out_shape = [shape(size // 2, D), shape(size // 2, D, dtype=jnp.bfloat16)]
    if xa is None:
        kernel, args = first_columns_kernel, (xt, y, e, alpha, first)
        out_shape.append(shape(256, rows, dtype=jnp.bfloat16))
    else:
        kernel, args = columns_kernel, (xa, y, e, first)
    return pl.pallas_call(
        functools.partial(kernel, blocks, share),
        out_shape=out_shape,
        in_specs=[VMEM] * len(args),
        out_specs=[VMEM] * len(out_shape),
        scratch_shapes=[
            pltpu.VMEM((size, 128), jnp.float32),
            pltpu.VMEM((size, 128), jnp.float32),
            pltpu.VMEM((size // 128, 128), jnp.float32),
            pltpu.VMEM((1, size), jnp.float32),
            pltpu.VMEM((128, size), jnp.float32),
        ],
        compiler_params=pltpu.CompilerParams(vmem_limit_bytes=16 << 20),
        cost_estimate=pl.CostEstimate(flops=4 * rows * size * D, bytes_accessed=2 * rows * size, transcendentals=0),
        name="column_grad",
    )(*args)


def row_block(at, chunk, x_ref, e_ref, yb_ref, scale):
    got = jnp.dot(e_ref[pl.ds(at, chunk), :], yb_ref[...], preferred_element_type=jnp.float32)
    lower = lax.broadcasted_iota(jnp.int32, (chunk, 128), 1) < 126
    total = got[:, 254:255] + got[:, 255:256]
    pulled = got[:, :128] + jnp.where(lower, got[:, 128:], 0.0)
    x = x_ref[pl.ds(at, chunk), :].astype(jnp.float32)
    return 2.0 * scale * (total * x - pulled)


def put_yb(y_ref, beta, yb_ref, s_ref, bb_ref):
    spread(beta, s_ref, bb_ref)
    place = lax.broadcasted_iota(jnp.int32, (256, 128), 1)
    for at in range(0, y_ref.shape[0], 256):
        beta = bb_ref[at:at + 256, :]
        high, low = high_low(y_ref[at:at + 256, :].astype(jnp.float32) * beta)
        first, second = high_low(beta)
        low = jnp.where(place == 126, first.astype(jnp.float32), low.astype(jnp.float32))
        low = jnp.where(place == 127, second.astype(jnp.float32), low)
        yb_ref[at:at + 256, :128] = high
        yb_ref[at:at + 256, 128:] = low.astype(jnp.bfloat16)


def row_parts(parts, x_ref, e_ref, alpha_ref, yb_ref, outs, sa_ref, ab_ref):
    share = outs[0].shape[0]
    chunk = math.gcd(share, 512)
    for part, out_ref in zip(parts, outs):
        spread(alpha_ref[:, part * share:(part + 1) * share], sa_ref, ab_ref)
        for k in range(0, share, chunk):
            grad = row_block(part * share + k, chunk, x_ref, e_ref, yb_ref, ab_ref[k:k + chunk, :])
            out_ref[k:k + chunk, :] = grad.astype(out_ref.dtype)


def first_rows_kernel(parts, shifts, blocks, nz, x_ref, y_ref, e_ref, alpha_ref, first_ref, b_ref, *refs):
    got, (yb_ref, scale_ref, *outs), (s_ref, bb_ref, sa_ref, ab_ref) = refs[:nz], refs[nz:-4], refs[-4:]
    scale = new_scale(b_ref, got, shifts, blocks)
    scale_ref[...] = scale[:, :scale_ref.shape[1]]
    put_yb(y_ref, first_ref[...] * scale, yb_ref, s_ref, bb_ref)
    row_parts(parts, x_ref, e_ref, alpha_ref, yb_ref, outs, sa_ref, ab_ref)


def rows_kernel(parts, x_ref, yb_ref, e_ref, alpha_ref, *refs):
    row_parts(parts, x_ref, e_ref, alpha_ref, yb_ref, refs[:-2], *refs[-2:])


def rows_scratch(share):
    return [pltpu.VMEM((share // 128, 128), jnp.float32), pltpu.VMEM((share, 128), jnp.float32)]


def rows_cost(share, parts, cols):
    size = share * len(parts) * cols
    return pl.CostEstimate(flops=4 * size * D, bytes_accessed=2 * size, transcendentals=0)


def first_rows(parts, share, x, y, e, alpha, first, mass, got, blocks):
    cols = y.shape[0]
    got, shifts = got
    return pl.pallas_call(
        functools.partial(first_rows_kernel, parts, tuple(shifts), blocks, len(got)),
        out_shape=[shape(cols, 256, dtype=jnp.bfloat16), shape(1, cols // blocks)]
        + [shape(share, D, dtype=jnp.bfloat16)] * len(parts),
        in_specs=[VMEM] * (6 + len(got)),
        out_specs=[VMEM] * (2 + len(parts)),
        scratch_shapes=[
            pltpu.VMEM((cols // 128, 128), jnp.float32),
            pltpu.VMEM((cols, 128), jnp.float32),
            *rows_scratch(share),
        ],
        compiler_params=pltpu.CompilerParams(vmem_limit_bytes=16 << 20),
        cost_estimate=rows_cost(share * HEAVY, parts, cols),
        name="first_rows",
    )(x, y, e, alpha, first, mass, *[flat(part) for part in got])


def other_rows(parts, share, x, yb, e, alpha, dtype):
    return pl.pallas_call(
        functools.partial(rows_kernel, parts),
        out_shape=[shape(share, D, dtype=dtype)] * len(parts),
        in_specs=[VMEM] * 4,
        out_specs=[VMEM] * len(parts),
        scratch_shapes=rows_scratch(share),
        compiler_params=pltpu.CompilerParams(vmem_limit_bytes=16 << 20),
        cost_estimate=rows_cost(share, parts, yb.shape[0]),
        name="other_rows",
    )(x, yb, e, alpha)


def add_up_kernel(na, scale_ref, *refs):
    ins, (rows_ref, cols_ref, s_ref, sb_ref) = refs[:-4], refs[-4:]
    rows_ref[...] = sum(part[...].astype(jnp.float32) for part in ins[:na])
    spread(scale_ref[...], s_ref, sb_ref)
    cols_ref[...] = 2.0 * sb_ref[...] * sum(part[...].astype(jnp.float32) for part in ins[na:])


def add_up(rows, columns, scale):
    share = scale.shape[1]
    return pl.pallas_call(
        functools.partial(add_up_kernel, len(rows)),
        out_shape=(shape(*rows[0].shape), shape(*columns[0].shape)),
        in_specs=[VMEM] * (1 + len(rows) + len(columns)),
        out_specs=(VMEM,) * 2,
        scratch_shapes=rows_scratch(share),
        compiler_params=pltpu.CompilerParams(vmem_limit_bytes=16 << 20),
        name="add_up",
    )(scale, *rows, *columns)


def shares_kernel(gc_ref, other_ref, *outs):
    share = outs[0].shape[0]
    for k, out_ref in enumerate(outs):
        at = k * share
        total = gc_ref[at:at + share, :] + other_ref[at:at + share, :].astype(jnp.float32)
        out_ref[...] = total.astype(out_ref.dtype)


def shares(gc, other, dtypes):
    share = gc.shape[0] // len(dtypes)
    return pl.pallas_call(
        shares_kernel,
        out_shape=[shape(share, D, dtype=dtype) for dtype in dtypes],
        in_specs=[VMEM] * 2,
        out_specs=[VMEM] * len(dtypes),
        compiler_params=pltpu.CompilerParams(vmem_limit_bytes=16 << 20),
        name="shares",
    )(gc, other)


class Groups:
    def __init__(self, nrow, ncol):
        self.count = nrow * ncol
        self.across = [(a << 1) * ncol + b for a in range(nrow // 2) for b in range(2)]
        self.along = [z << 1 for z in range(ncol // 2)]
        self.core = ncol

    def swap(self, value, mask):
        if mask == 0:
            return value
        return lax.ppermute(value, ("row", "col"), [(i, i ^ mask) for i in range(self.count)])


def local(imu, camera, imu_mass, cam_mass):
    nrow, ncol = lax.axis_size("row"), lax.axis_size("col")
    groups = Groups(nrow, ncol)
    swap, across, along, core = groups.swap, groups.across, groups.along, groups.core
    na, nz = len(across), len(along)
    share_x, share_y = imu.shape[0], camera.shape[1]
    rows, cols = na * share_x, 2 * nz * share_y

    def direct(value, masks):
        return [swap(value, mask) for mask in masks], range(len(masks))

    xs, _ = direct(imu, across)
    own, mine = lax.optimization_barrier((jnp.concatenate([imu, camera[0]]), camera[0]))
    near = [mine] + [None] * (nz - 1)
    for z in range(1, nz):
        if not z & (z - 1):
            near[z] = swap(mine if z == 1 else camera[0], along[z])
    far = [swap(mine, core)]

    def pair(mass, place, share):
        return [lax.dynamic_slice_in_dim(mass, (place ^ k) * share, share, 0) for k in range(2)]

    row, col = lax.axis_index("row"), lax.axis_index("col")
    mass = jnp.concatenate(pair(imu_mass, col, share_x) + pair(cam_mass, row, share_y))

    x, xt, first = row_lse_early(own, xs[1:], far[0])
    relays = [z for z in range(2, nz) if not z & (z - 1)]
    first, mass, got = lax.optimization_barrier((first, mass, [near[z] for z in relays]))
    for z, part in zip(relays, got):
        near[z] = part
    for z in range(1, nz):
        if z & (z - 1):
            near[z] = swap(near[z & (z - 1)], along[z & -z])
    middle = near[1:-1]
    far += [swap(part, core) for part in middle]
    first = row_lse_middle(x, middle, first)
    first, last = lax.optimization_barrier((first, near[-1]))
    far.append(swap(last, core))
    y, sent = row_lse_late(own, x, [*middle, last, *far], first, mass, 2 * share_x)
    got, _ = direct(sent.reshape(-1), across)

    sent, e, shift, mass_a = column_lse(x, y, mass, 2 * share_y, got)
    sent = pair_of(lse2, sent, swap(sent.reshape(-1), core), cols, 1, 2)
    got = direct(sent.reshape(-1), along)

    sums, first_beta, mass_b = weighted(
        first_row_kernel, [(1, rows), (1, cols), (1, cols)], e, [shift], got, 2 * nz)
    for step in range(1, ITERS):
        if step > 1:
            sums, = weighted(row_kernel, [(1, rows)], e, [first_beta, mass_b], got, 2 * nz)
        got = direct(sums.reshape(-1), across)
        part, alpha = weighted(column_kernel, [(1, cols), (1, rows)], e, [mass_a, first_beta], got, na)
        part = pair_of(sum, part, swap(part.reshape(-1), core), cols, 1, 2)
        part, alpha = lax.optimization_barrier((part, alpha))
        got = direct(part.reshape(-1), along)

    half = nz // 2
    gc, gc_send, xa = column_grad(range(half, nz), nz, share_y, y, e, first_beta, xt=xt, alpha=alpha)
    far_gc = shares(gc, swap(gc_send, core), [jnp.bfloat16] * (nz - half))
    gc, gc_send = column_grad(range(half), nz, share_y, y, e, first_beta, xa=xa)
    far_gc, alpha = lax.optimization_barrier((far_gc, alpha))
    far_gc = [swap(part, along[half + z]) for z, part in enumerate(far_gc)]
    yb, scale, last = first_rows([na - 1], share_x, x, y, e, alpha, first_beta, mass_b, got, 2 * nz)
    near_gc = shares(gc, swap(gc_send, core), [jnp.float32] + [jnp.bfloat16] * (half - 1))
    (grad_cam, *parts), yb = lax.optimization_barrier((near_gc, yb))
    parts = [swap(part, along[z + 1]) for z, part in enumerate(parts)]
    last = swap(last, across[na - 1])
    sent = other_rows(list(range(1, na - 1)), share_x, x, yb, e, alpha, jnp.bfloat16)
    sent = [swap(part, across[s + 1]) for s, part in enumerate(sent)] + [last]
    gi, = other_rows([0], share_x, x, yb, e, alpha, jnp.float32)
    grad_imu, grad_cam = add_up([gi, *sent], [grad_cam, *parts, *far_gc], scale)
    return grad_imu, grad_cam[None]


def solution(mesh):
    in_specs = (P(("row", "col"), None), P("col", "row", None), P("row"), P("col"))
    out_specs = (P(("row", "col"), None), P("col", "row", None))
    return jax.shard_map(local, mesh=mesh, in_specs=in_specs, out_specs=out_specs, check_vma=False)
```

```python
import functools
import math

import jax
import jax.numpy as jnp
from jax import lax
from jax.experimental import pallas as pl
from jax.experimental.pallas import tpu as pltpu
from jax.sharding import PartitionSpec as P

D = 128
ITERS = 3
EPSILON = D / 20.0
LOG2E = math.log2(math.e)
CROSS = 2.0 * LOG2E / EPSILON
NT = (((1,), (1,)), ((), ()))
VMEM = pl.BlockSpec(memory_space=pltpu.VMEM)
HEAVY = 32


def spread(value, s_ref, sb_ref):
    chunks = value.shape[1] // 128
    for k in range(chunks):
        s_ref[k:k + 1, :] = value[:, k * 128:(k + 1) * 128]
    turned = jnp.transpose(s_ref[...])
    for k in range(chunks):
        sb_ref[k * 128:(k + 1) * 128, :] = jnp.broadcast_to(turned[:, k:k + 1], (128, 128))


def ordered(values, shifts, parts):
    share = values[0].shape[1] // parts
    return [
        jnp.concatenate([value[:, (k ^ s) * share:((k ^ s) + 1) * share] for k in range(parts)], axis=1)
        for value, s in zip(values, shifts)
    ]


def lse2(parts):
    top = functools.reduce(jnp.maximum, parts)
    return top + jnp.log2(sum(jnp.exp2(part - top) for part in parts))


def pipelined(places, chunk, width, a_ref, b_ref, d_ref, tile, finish):
    last = b_ref.shape[0] // width - 1

    def product(n, m):
        b = b_ref[pl.ds(pl.multiple_of(n * width, width), width), :]
        a = a_ref[places[m]:places[m] + chunk, :]
        d_ref[m % 2] = lax.dot_general(a, b, NT, preferred_element_type=jnp.float32)

    product(0, 0)

    def column(n, _):
        start = pl.multiple_of(n * width, width)
        state = None
        for m in range(len(places)):
            if m + 1 < len(places):
                product(n, m + 1)
            else:
                product(jnp.minimum(n + 1, last), 0)
            state = tile(m, start, state)
        finish(start, state)
        return 0

    lax.fori_loop(0, last + 1, column, 0)


def running_max(places, chunk, width, a_ref, b_ref, sb_ref, o_ref, e_ref, shift_ref):
    def column(n, _):
        start = pl.multiple_of(n * width, width)
        b = b_ref[pl.ds(start, width), :]

        def exponents(at):
            d = lax.dot_general(a_ref[at:at + chunk, :], b, NT, preferred_element_type=jnp.float32)
            s = sb_ref[at:at + chunk, :]
            return [d[:, q * 128:(q + 1) * 128] * CROSS + s for q in range(width // 128)]

        peak, total = jnp.full((1, width), -1e30, jnp.float32), jnp.zeros((1, width), jnp.float32)
        for at in places:
            peaks, totals = [], []
            for q, t in enumerate(exponents(at)):
                old = peak[:, q * 128:(q + 1) * 128]
                new = jnp.maximum(old, jnp.max(t, axis=0, keepdims=True))
                part = jnp.sum(jnp.exp2(t - new), axis=0, keepdims=True)
                peaks.append(new)
                totals.append(total[:, q * 128:(q + 1) * 128] * jnp.exp2(old - new) + part)
            peak, total = jnp.concatenate(peaks, axis=1), jnp.concatenate(totals, axis=1)
        o_ref[:, pl.ds(start, width)] = peak + jnp.log2(total)
        if e_ref is not None:
            shift_ref[:, pl.ds(start, width)] = peak
            for at in places:
                for q, t in enumerate(exponents(at)):
                    place = pl.ds(pl.multiple_of(start + q * 128, 128), 128)
                    e_ref[at:at + chunk, place] = jnp.exp2(t - shift_ref[:, place]).astype(jnp.bfloat16)
        return 0

    lax.fori_loop(0, b_ref.shape[0] // width, column, 0)


def lse_pass(places, chunk, width, a_ref, b_ref, sb_ref, d_ref, top_ref, o_ref, e_ref=None, shift_ref=None):
    tiles, group = width // 128, top_ref.shape[0]
    top_ref[...] = jnp.zeros_like(top_ref)

    def lanes_of(start, q):
        return pl.ds(pl.multiple_of(start + q * 128, 128), 128)

    def tile(m, start, state):
        def exponents(g, q):
            at = g * group
            s = sb_ref[places[m] + at:places[m] + at + group, :]
            return d_ref[m % 2, at:at + group, q * 128:(q + 1) * 128] * CROSS + s

        if m == 0:
            tops = [exponents(0, q) for q in range(tiles)]
            for g in range(1, 32 // group):
                tops = [jnp.maximum(top, exponents(g, q)) for q, top in enumerate(tops)]
            state = [(jnp.max(top, axis=0, keepdims=True), jnp.zeros((group, 128), jnp.float32)) for top in tops]
        for g in range(chunk // group):
            for q, (peak, total) in enumerate(state):
                e = jnp.exp2(exponents(g, q) - peak)
                if e_ref is not None:
                    at = places[m] + g * group
                    e_ref[at:at + group, lanes_of(start, q)] = e.astype(jnp.bfloat16)
                state[q] = peak, total + e
        return state

    def finish(start, state):
        for q, (peak, total) in enumerate(state):
            top_ref[...] = jnp.maximum(top_ref[...], total)
            o_ref[:, lanes_of(start, q)] = peak + jnp.log2(jnp.sum(total, axis=0, keepdims=True))
            if e_ref is not None:
                shift_ref[:, lanes_of(start, q)] = peak

    pipelined(places, chunk, width, a_ref, b_ref, d_ref, tile, finish)

    @pl.when(jnp.logical_not(jnp.max(top_ref[...]) < 2.0 ** 60))
    def _():
        running_max(places, chunk, min(width, 256), a_ref, b_ref, sb_ref, o_ref, e_ref, shift_ref)


def put_norms(places, share, y_ref, sb_ref):
    for at in places:
        y = y_ref[at:at + share, :].astype(jnp.float32)
        total = jnp.sum(y * y, axis=1, keepdims=True) * (-LOG2E / EPSILON)
        sb_ref[at:at + share, :] = jnp.broadcast_to(total, (share, 128))


def join(out_ref, parts):
    at = 0
    for part in parts:
        out_ref[at:at + part.shape[0], :] = part[...]
        at += part.shape[0]


def row_lse_early_kernel(width, nx, own_ref, *refs):
    xs, y_other, refs = refs[:nx], refs[nx], refs[nx + 1:]
    x_ref, xt_ref, o_ref, y_ref, sb_ref, d_ref, top_ref = refs
    share = y_other.shape[0]
    mine = own_ref.shape[0] - share
    join(x_ref, [own_ref.at[:mine, :], *xs])
    join(y_ref, [own_ref.at[mine:, :], y_other])
    for k in range(x_ref.shape[0] // 128):
        at = k * 128
        xt_ref[:, at:at + 128] = jnp.transpose(x_ref[at:at + 128, :].astype(jnp.float32)).astype(jnp.bfloat16)
    places = [0, share]
    put_norms(places, share, y_ref, sb_ref)
    lse_pass(places, share, width, y_ref, x_ref, sb_ref, d_ref, top_ref, o_ref)


def row_lse_middle_kernel(width, ny, x_ref, first_ref, *refs):
    ys, (o_ref, y_ref, sb_ref, d_ref, top_ref, sum_ref) = refs[:ny], refs[ny:]
    share = ys[0].shape[0]
    join(y_ref, ys)
    places = [k * share for k in range(ny)]
    put_norms(places, share, y_ref, sb_ref)
    lse_pass(places, share, width, y_ref, x_ref, sb_ref, d_ref, top_ref, sum_ref)
    o_ref[...] = lse2([first_ref[...], sum_ref[...]])


def row_lse_late_kernel(width, ny, own_ref, mass_ref, x_ref, first_ref, *refs):
    ys, (y_ref, o_ref, sb_ref, d_ref, top_ref, sum_ref) = refs[:ny], refs[ny:]
    share, rows, half = ys[0].shape[0], x_ref.shape[0], (ny + 1) // 2
    join(y_ref, [own_ref.at[own_ref.shape[0] - share:, :], *ys])
    places = [k * share for k in range(half - 1, 2 * half) if k != half]
    put_norms(places, share, y_ref, sb_ref)
    lse_pass(places, share, width, y_ref, x_ref, sb_ref, d_ref, top_ref, sum_ref)
    o_ref[:, :rows] = lse2([first_ref[...], sum_ref[...]])
    o_ref[:, rows:] = mass_ref[:, :o_ref.shape[1] - rows]


def column_lse_kernel(width, chunk, na, x_ref, y_ref, mass_ref, *refs):
    got, (o_ref, e_ref, shift_ref, a_ref, s_ref, sb_ref, d_ref, top_ref) = refs[:na], refs[na:]
    rows, cols = x_ref.shape[0], y_ref.shape[0]
    o_ref[:, cols:] = mass_ref[:, mass_ref.shape[1] - o_ref.shape[1] + cols:]
    share = rows // na
    for k in range(na):
        at = rows + (k % 2) * share
        a_ref[:, k * share:(k + 1) * share] = got[k - k % 2][:, at:at + share]
    u = jnp.log2(a_ref[...]) - lse2(ordered([part[:, :rows] for part in got], range(na), na))
    spread(u, s_ref, sb_ref)
    places = list(range(0, rows, chunk))
    lse_pass(places, chunk, width, x_ref, y_ref, sb_ref, d_ref, top_ref, o_ref, e_ref, shift_ref)


def pair_kernel(size, shift, parts, combine, one_ref, two_ref, o_ref):
    two, = ordered([two_ref[:, :size]], [shift], parts)
    o_ref[:, :size] = combine([one_ref[:, :size], two])
    if o_ref.shape[1] > size:
        o_ref[:, size:] = one_ref[:, size:]


def split3(value):
    high = value.astype(jnp.bfloat16)
    rest = value - high.astype(jnp.float32)
    mid = rest.astype(jnp.bfloat16)
    return high, mid, (rest - mid.astype(jnp.float32)).astype(jnp.bfloat16)


def stacked(value):
    high, mid, low = [part.astype(jnp.float32) for part in split3(value)]
    dims = (16, value.shape[1])
    place = lax.broadcasted_iota(jnp.int32, dims, 0)
    parts = jnp.where(place == 0, high, jnp.where(place == 1, mid, jnp.where(place == 2, low, 0.0)))
    return parts.astype(jnp.bfloat16)


def row_sums(width, e_ref, w_ref, w16_ref, acc_ref, o_ref):
    rows, cols = e_ref.shape
    split = rows - acc_ref.shape[0]
    blocks = list(range(0, rows - split, 64))
    dots = list(range(0, split, width))
    for n, at in enumerate(dots):
        got = lax.dot_general(w16_ref[...], e_ref[at:at + width, :], NT, preferred_element_type=jnp.float32)
        for k in blocks[n * len(blocks) // len(dots):(n + 1) * len(blocks) // len(dots)]:
            total = jnp.zeros((64, 128), jnp.float32)
            for q in range(0, cols, 128):
                e = e_ref[split + k:split + k + 64, q:q + 128].astype(jnp.float32)
                total = total + e * w_ref[:, q:q + 128]
            acc_ref[k:k + 64, :] = total
        o_ref[:, at:at + width] = jnp.sum(got, axis=0, keepdims=True)
    for at in range(0, rows - split, 128):
        total = jnp.sum(jnp.transpose(acc_ref[at:at + 128, :]), axis=0, keepdims=True)
        o_ref[:, split + at:split + at + 128] = total


def first_row_kernel(width, shifts, parts, e_ref, shift_ref, *refs):
    nz = len(shifts)
    got, (o_ref, beta_ref, b_ref, w16_ref, acc_ref) = refs[:nz], refs[nz:]
    cols = e_ref.shape[1]
    share = cols // parts
    for k in range(parts):
        at = cols + (k // nz) * share
        b_ref[:, k * share:(k + 1) * share] = got[k % nz][:, at:at + share]
    lse = lse2(ordered([part[:, :cols] for part in got], shifts, parts))
    beta_ref[...] = jnp.exp2(jnp.log2(b_ref[...]) - lse + shift_ref[...])
    w16_ref[...] = stacked(beta_ref[...])
    row_sums(width, e_ref, beta_ref, w16_ref, acc_ref, o_ref)


def new_scale(b_ref, got, shifts, parts):
    return b_ref[...] / sum(ordered([part[...] for part in got], shifts, parts))


def row_kernel(width, shifts, parts, e_ref, first_ref, b_ref, *refs):
    got, (o_ref, w16_ref, acc_ref, w_ref) = refs[:-4], refs[-4:]
    w_ref[...] = first_ref[...] * new_scale(b_ref, got, shifts, parts)
    w16_ref[...] = stacked(w_ref[...])
    row_sums(width, e_ref, w_ref, w16_ref, acc_ref, o_ref)


def column_kernel(width, shifts, parts, e_ref, a_ref, first_ref, *refs):
    got, (o_ref, alpha_ref, w16_ref) = refs[:-3], refs[-3:]
    alpha_ref[...] = a_ref[...] / sum(ordered([part[...] for part in got], shifts, parts))
    w16_ref[...] = stacked(alpha_ref[...])
    for at in range(0, e_ref.shape[1], width):
        sums = jnp.dot(w16_ref[...], e_ref[:, at:at + width], preferred_element_type=jnp.float32)
        o_ref[:, at:at + width] = first_ref[:, at:at + width] * jnp.sum(sums, axis=0, keepdims=True)


def flat(value):
    return value.reshape(1, -1) if value.ndim == 1 else value


def weighted(kernel, outs, e, rows, got, parts):
    got, shifts = got
    size = e.shape[0] if kernel is column_kernel else e.shape[1]
    width = 512 if kernel is column_kernel else 256
    scratch = [pltpu.VMEM((16, size), jnp.bfloat16)]
    if kernel is not column_kernel:
        part = 7 if kernel is row_kernel else 6
        scratch.append(pltpu.VMEM((e.shape[0] * part // 8, 128), jnp.float32))
    if kernel is row_kernel:
        scratch.append(pltpu.VMEM((1, size), jnp.float32))
    return pl.pallas_call(
        functools.partial(kernel, width, tuple(shifts), parts),
        out_shape=[shape(*dims) for dims in outs],
        in_specs=[VMEM] * (1 + len(rows) + len(got)),
        out_specs=[VMEM] * len(outs),
        scratch_shapes=scratch,
        compiler_params=pltpu.CompilerParams(vmem_limit_bytes=16 << 20),
        cost_estimate=pl.CostEstimate(flops=2 * e.size, bytes_accessed=2 * e.size, transcendentals=0),
        name="weighted_sum",
    )(e, *rows, *[flat(part) for part in got])


def pass_cost(depth, lanes):
    return pl.CostEstimate(flops=2 * depth * lanes * D, bytes_accessed=2 * D * (depth + lanes), transcendentals=depth * lanes)


def shape(*dims, dtype=jnp.float32):
    return jax.ShapeDtypeStruct(dims, dtype)


def lse_scratch(depth, chunk, width, group=32):
    return [
        pltpu.VMEM((depth, 128), jnp.float32),
        pltpu.VMEM((2, chunk, width), jnp.float32),
        pltpu.VMEM((group, 128), jnp.float32),
    ]


def row_lse_early(own, xs, y_other, width=1024):
    share = y_other.shape[0]
    rows, depth = own.shape[0] - share + sum(part.shape[0] for part in xs), 2 * share
    return pl.pallas_call(
        functools.partial(row_lse_early_kernel, width, len(xs)),
        out_shape=(shape(rows, D, dtype=jnp.bfloat16), shape(D, rows, dtype=jnp.bfloat16), shape(1, rows)),
        in_specs=[VMEM] * (len(xs) + 2),
        out_specs=(VMEM,) * 3,
        scratch_shapes=[pltpu.VMEM((depth, D), jnp.bfloat16), *lse_scratch(depth, share, width)],
        compiler_params=pltpu.CompilerParams(vmem_limit_bytes=16 << 20),
        cost_estimate=pass_cost(depth, rows),
        name="row_lse_early",
    )(own, *xs, y_other)


def row_lse_middle(x, ys, first, width=1024):
    rows, share = x.shape[0], ys[0].shape[0]
    depth = len(ys) * share
    return pl.pallas_call(
        functools.partial(row_lse_middle_kernel, width, len(ys)),
        out_shape=shape(1, rows),
        in_specs=[VMEM] * (len(ys) + 2),
        out_specs=VMEM,
        scratch_shapes=[
            pltpu.VMEM((depth, D), jnp.bfloat16),
            *lse_scratch(depth, share, width),
            pltpu.VMEM((1, rows), jnp.float32),
        ],
        compiler_params=pltpu.CompilerParams(vmem_limit_bytes=16 << 20),
        cost_estimate=pass_cost(depth, rows),
        name="row_lse_middle",
    )(x, first, *ys)


def row_lse_late(own, x, ys, first, mass, tail, width=1024):
    rows, share = x.shape[0], ys[0].shape[0]
    depth = (len(ys) + 1) * share
    return pl.pallas_call(
        functools.partial(row_lse_late_kernel, width, len(ys)),
        out_shape=(shape(depth, D, dtype=jnp.bfloat16), shape(1, rows + tail)),
        in_specs=[VMEM] * (len(ys) + 4),
        out_specs=(VMEM,) * 2,
        scratch_shapes=[*lse_scratch(depth, share, width), pltpu.VMEM((1, rows), jnp.float32)],
        compiler_params=pltpu.CompilerParams(vmem_limit_bytes=16 << 20),
        cost_estimate=pass_cost(depth // 2, rows),
        name="row_lse_late",
    )(own, mass.reshape(1, -1), x, first, *ys)


def column_lse(x, y, mass, tail, got, width=512, chunk=512):
    rows, cols = x.shape[0], y.shape[0]
    return pl.pallas_call(
        functools.partial(column_lse_kernel, width, chunk, len(got)),
        out_shape=(shape(1, cols + tail), shape(rows, cols, dtype=jnp.bfloat16), shape(1, cols), shape(1, rows)),
        in_specs=[VMEM] * (3 + len(got)),
        out_specs=(VMEM,) * 4,
        scratch_shapes=[pltpu.VMEM((rows // 128, 128), jnp.float32), *lse_scratch(rows, chunk, width, 16)],
        compiler_params=pltpu.CompilerParams(vmem_limit_bytes=16 << 20),
        cost_estimate=pass_cost(rows, cols),
        name="column_lse",
    )(x, y, mass.reshape(1, -1), *[part.reshape(1, -1) for part in got])


def pair_of(combine, one, two, size, shift, parts):
    whole = one.shape[-1]
    return pl.pallas_call(
        functools.partial(pair_kernel, size, shift, parts, combine),
        out_shape=shape(1, whole),
        in_specs=[VMEM] * 2,
        out_specs=VMEM,
        compiler_params=pltpu.CompilerParams(vmem_limit_bytes=16 << 20),
        name="pair",
    )(one.reshape(1, whole), two.reshape(1, whole))


def high_low(value):
    high = value.astype(jnp.bfloat16)
    return high, (value - high.astype(jnp.float32)).astype(jnp.bfloat16)


def put_xa(xt_ref, alpha_ref, xa_ref):
    place = lax.broadcasted_iota(jnp.int32, (128, 512), 0)
    for at in range(0, xt_ref.shape[1], 512):
        alpha = alpha_ref[:, at:at + 512]
        high, low = high_low(xt_ref[:, at:at + 512].astype(jnp.float32) * alpha)
        first, second = high_low(alpha)
        low = jnp.where(place == 126, first.astype(jnp.float32), low.astype(jnp.float32))
        low = jnp.where(place == 127, second.astype(jnp.float32), low)
        xa_ref[:128, at:at + 512] = high
        xa_ref[128:, at:at + 512] = low.astype(jnp.bfloat16)


def column_parts(blocks, share, xa_ref, y_ref, e_ref, first_ref, own_ref, sent_ref,
                 bb_ref, cb_ref, s_ref, count_ref, acc_ref):
    spread(jnp.concatenate([first_ref[:, at:at + share] for at in blocks], axis=1), s_ref, bb_ref)
    lower = lax.broadcasted_iota(jnp.int32, (128, share), 0) < 126
    for k, at in enumerate(blocks):
        to = k * share
        got = jnp.dot(xa_ref[...], e_ref[:, at:at + share], preferred_element_type=jnp.float32)
        acc_ref[:, to:to + share] = got[:128] + jnp.where(lower, got[128:], 0.0)
        count_ref[:, to:to + share] = got[254:255] + got[255:256]
    spread(count_ref[...], s_ref, cb_ref)
    own = own_ref.shape[0]
    for k, at in enumerate(blocks):
        for q in range(0, share, 128):
            to = k * share + q
            pulled = jnp.transpose(acc_ref[:, to:to + 128])
            whole = cb_ref[to:to + 128, :] * y_ref[at + q:at + q + 128, :].astype(jnp.float32)
            grad = bb_ref[to:to + 128, :] * (whole - pulled)
            if to < own:
                own_ref[to:to + 128, :] = grad
            else:
                sent_ref[to - own:to - own + 128, :] = grad.astype(jnp.bfloat16)


def first_columns_kernel(blocks, share, xt_ref, y_ref, e_ref, alpha_ref, first_ref, own_ref, sent_ref, xa_ref, *rest):
    put_xa(xt_ref, alpha_ref, xa_ref)
    column_parts(blocks, share, xa_ref, y_ref, e_ref, first_ref, own_ref, sent_ref, *rest)


def columns_kernel(blocks, share, xa_ref, y_ref, e_ref, first_ref, own_ref, sent_ref, *rest):
    column_parts(blocks, share, xa_ref, y_ref, e_ref, first_ref, own_ref, sent_ref, *rest)


def column_grad(zs, nz, share, y, e, first, xt=None, alpha=None, xa=None):
    rows, size = e.shape[0], 2 * len(zs) * share
    blocks = [z * share for z in zs] + [(nz + z) * share for z in zs]
    out_shape = [shape(size // 2, D), shape(size // 2, D, dtype=jnp.bfloat16)]
    if xa is None:
        kernel, args = first_columns_kernel, (xt, y, e, alpha, first)
        out_shape.append(shape(256, rows, dtype=jnp.bfloat16))
    else:
        kernel, args = columns_kernel, (xa, y, e, first)
    return pl.pallas_call(
        functools.partial(kernel, blocks, share),
        out_shape=out_shape,
        in_specs=[VMEM] * len(args),
        out_specs=[VMEM] * len(out_shape),
        scratch_shapes=[
            pltpu.VMEM((size, 128), jnp.float32),
            pltpu.VMEM((size, 128), jnp.float32),
            pltpu.VMEM((size // 128, 128), jnp.float32),
            pltpu.VMEM((1, size), jnp.float32),
            pltpu.VMEM((128, size), jnp.float32),
        ],
        compiler_params=pltpu.CompilerParams(vmem_limit_bytes=16 << 20),
        cost_estimate=pl.CostEstimate(flops=4 * rows * size * D, bytes_accessed=2 * rows * size, transcendentals=0),
        name="column_grad",
    )(*args)


def row_block(at, chunk, x_ref, e_ref, yb_ref, scale):
    got = jnp.dot(e_ref[pl.ds(at, chunk), :], yb_ref[...], preferred_element_type=jnp.float32)
    lower = lax.broadcasted_iota(jnp.int32, (chunk, 128), 1) < 126
    total = got[:, 254:255] + got[:, 255:256]
    pulled = got[:, :128] + jnp.where(lower, got[:, 128:], 0.0)
    x = x_ref[pl.ds(at, chunk), :].astype(jnp.float32)
    return 2.0 * scale * (total * x - pulled)


def put_yb(y_ref, beta, yb_ref, s_ref, bb_ref):
    spread(beta, s_ref, bb_ref)
    place = lax.broadcasted_iota(jnp.int32, (256, 128), 1)
    for at in range(0, y_ref.shape[0], 256):
        beta = bb_ref[at:at + 256, :]
        high, low = high_low(y_ref[at:at + 256, :].astype(jnp.float32) * beta)
        first, second = high_low(beta)
        low = jnp.where(place == 126, first.astype(jnp.float32), low.astype(jnp.float32))
        low = jnp.where(place == 127, second.astype(jnp.float32), low)
        yb_ref[at:at + 256, :128] = high
        yb_ref[at:at + 256, 128:] = low.astype(jnp.bfloat16)


def row_parts(parts, x_ref, e_ref, alpha_ref, yb_ref, outs, sa_ref, ab_ref):
    share = outs[0].shape[0]
    chunk = math.gcd(share, 512)
    for part, out_ref in zip(parts, outs):
        spread(alpha_ref[:, part * share:(part + 1) * share], sa_ref, ab_ref)
        for k in range(0, share, chunk):
            grad = row_block(part * share + k, chunk, x_ref, e_ref, yb_ref, ab_ref[k:k + chunk, :])
            out_ref[k:k + chunk, :] = grad.astype(out_ref.dtype)


def first_rows_kernel(parts, shifts, blocks, nz, x_ref, y_ref, e_ref, alpha_ref, first_ref, b_ref, *refs):
    got, (yb_ref, scale_ref, *outs), (s_ref, bb_ref, sa_ref, ab_ref) = refs[:nz], refs[nz:-4], refs[-4:]
    scale = new_scale(b_ref, got, shifts, blocks)
    scale_ref[...] = scale[:, :scale_ref.shape[1]]
    put_yb(y_ref, first_ref[...] * scale, yb_ref, s_ref, bb_ref)
    row_parts(parts, x_ref, e_ref, alpha_ref, yb_ref, outs, sa_ref, ab_ref)


def rows_kernel(parts, x_ref, yb_ref, e_ref, alpha_ref, *refs):
    row_parts(parts, x_ref, e_ref, alpha_ref, yb_ref, refs[:-2], *refs[-2:])


def rows_scratch(share):
    return [pltpu.VMEM((share // 128, 128), jnp.float32), pltpu.VMEM((share, 128), jnp.float32)]


def rows_cost(share, parts, cols):
    size = share * len(parts) * cols
    return pl.CostEstimate(flops=4 * size * D, bytes_accessed=2 * size, transcendentals=0)


def first_rows(parts, share, x, y, e, alpha, first, mass, got, blocks):
    cols = y.shape[0]
    got, shifts = got
    return pl.pallas_call(
        functools.partial(first_rows_kernel, parts, tuple(shifts), blocks, len(got)),
        out_shape=[shape(cols, 256, dtype=jnp.bfloat16), shape(1, cols // blocks)]
        + [shape(share, D, dtype=jnp.bfloat16)] * len(parts),
        in_specs=[VMEM] * (6 + len(got)),
        out_specs=[VMEM] * (2 + len(parts)),
        scratch_shapes=[
            pltpu.VMEM((cols // 128, 128), jnp.float32),
            pltpu.VMEM((cols, 128), jnp.float32),
            *rows_scratch(share),
        ],
        compiler_params=pltpu.CompilerParams(vmem_limit_bytes=16 << 20),
        cost_estimate=rows_cost(share * HEAVY, parts, cols),
        name="first_rows",
    )(x, y, e, alpha, first, mass, *[flat(part) for part in got])


def other_rows(parts, share, x, yb, e, alpha, dtype):
    return pl.pallas_call(
        functools.partial(rows_kernel, parts),
        out_shape=[shape(share, D, dtype=dtype)] * len(parts),
        in_specs=[VMEM] * 4,
        out_specs=[VMEM] * len(parts),
        scratch_shapes=rows_scratch(share),
        compiler_params=pltpu.CompilerParams(vmem_limit_bytes=16 << 20),
        cost_estimate=rows_cost(share, parts, yb.shape[0]),
        name="other_rows",
    )(x, yb, e, alpha)


def add_up_kernel(na, scale_ref, *refs):
    ins, (rows_ref, cols_ref, s_ref, sb_ref) = refs[:-4], refs[-4:]
    rows_ref[...] = sum(part[...].astype(jnp.float32) for part in ins[:na])
    spread(scale_ref[...], s_ref, sb_ref)
    cols_ref[...] = 2.0 * sb_ref[...] * sum(part[...].astype(jnp.float32) for part in ins[na:])


def add_up(rows, columns, scale):
    share = scale.shape[1]
    return pl.pallas_call(
        functools.partial(add_up_kernel, len(rows)),
        out_shape=(shape(*rows[0].shape), shape(*columns[0].shape)),
        in_specs=[VMEM] * (1 + len(rows) + len(columns)),
        out_specs=(VMEM,) * 2,
        scratch_shapes=rows_scratch(share),
        compiler_params=pltpu.CompilerParams(vmem_limit_bytes=16 << 20),
        name="add_up",
    )(scale, *rows, *columns)


def shares_kernel(gc_ref, other_ref, *outs):
    share = outs[0].shape[0]
    for k, out_ref in enumerate(outs):
        at = k * share
        total = gc_ref[at:at + share, :] + other_ref[at:at + share, :].astype(jnp.float32)
        out_ref[...] = total.astype(out_ref.dtype)


def shares(gc, other, dtypes):
    share = gc.shape[0] // len(dtypes)
    return pl.pallas_call(
        shares_kernel,
        out_shape=[shape(share, D, dtype=dtype) for dtype in dtypes],
        in_specs=[VMEM] * 2,
        out_specs=[VMEM] * len(dtypes),
        compiler_params=pltpu.CompilerParams(vmem_limit_bytes=16 << 20),
        name="shares",
    )(gc, other)


class Groups:
    def __init__(self, nrow, ncol):
        self.count = nrow * ncol
        self.across = [(a << 1) * ncol + b for a in range(nrow // 2) for b in range(2)]
        self.along = [z << 1 for z in range(ncol // 2)]
        self.core = ncol

    def swap(self, value, mask):
        if mask == 0:
            return value
        return lax.ppermute(value, ("row", "col"), [(i, i ^ mask) for i in range(self.count)])


def local(imu, camera, imu_mass, cam_mass):
    nrow, ncol = lax.axis_size("row"), lax.axis_size("col")
    groups = Groups(nrow, ncol)
    swap, across, along, core = groups.swap, groups.across, groups.along, groups.core
    na, nz = len(across), len(along)
    share_x, share_y = imu.shape[0], camera.shape[1]
    rows, cols = na * share_x, 2 * nz * share_y

    def direct(value, masks):
        return [swap(value, mask) for mask in masks], range(len(masks))

    xs, _ = direct(imu, across)
    own, mine = lax.optimization_barrier((jnp.concatenate([imu, camera[0]]), camera[0]))
    near = [mine] + [None] * (nz - 1)
    for z in range(1, nz):
        if not z & (z - 1):
            near[z] = swap(mine if z == 1 else camera[0], along[z])
    far = [swap(mine, core)]

    def pair(mass, place, share):
        return [lax.dynamic_slice_in_dim(mass, (place ^ k) * share, share, 0) for k in range(2)]

    row, col = lax.axis_index("row"), lax.axis_index("col")
    mass = jnp.concatenate(pair(imu_mass, col, share_x) + pair(cam_mass, row, share_y))

    x, xt, first = row_lse_early(own, xs[1:], far[0])
    relays = [z for z in range(2, nz) if not z & (z - 1)]
    first, mass, got = lax.optimization_barrier((first, mass, [near[z] for z in relays]))
    for z, part in zip(relays, got):
        near[z] = part
    for z in range(1, nz):
        if z & (z - 1):
            near[z] = swap(near[z & (z - 1)], along[z & -z])
    middle = near[1:-1]
    far += [swap(part, core) for part in middle]
    first = row_lse_middle(x, middle, first)
    first, last = lax.optimization_barrier((first, near[-1]))
    far.append(swap(last, core))
    y, sent = row_lse_late(own, x, [*middle, last, *far], first, mass, 2 * share_x)
    got, _ = direct(sent.reshape(-1), across)

    sent, e, shift, mass_a = column_lse(x, y, mass, 2 * share_y, got)
    sent = pair_of(lse2, sent, swap(sent.reshape(-1), core), cols, 1, 2)
    got = direct(sent.reshape(-1), along)

    sums, first_beta, mass_b = weighted(
        first_row_kernel, [(1, rows), (1, cols), (1, cols)], e, [shift], got, 2 * nz)
    for step in range(1, ITERS):
        if step > 1:
            sums, = weighted(row_kernel, [(1, rows)], e, [first_beta, mass_b], got, 2 * nz)
        got = direct(sums.reshape(-1), across)
        part, alpha = weighted(column_kernel, [(1, cols), (1, rows)], e, [mass_a, first_beta], got, na)
        part = pair_of(sum, part, swap(part.reshape(-1), core), cols, 1, 2)
        part, alpha = lax.optimization_barrier((part, alpha))
        got = direct(part.reshape(-1), along)

    half = nz // 2
    gc, gc_send, xa = column_grad(range(half, nz), nz, share_y, y, e, first_beta, xt=xt, alpha=alpha)
    far_gc = shares(gc, swap(gc_send, core), [jnp.bfloat16] * (nz - half))
    gc, gc_send = column_grad(range(half), nz, share_y, y, e, first_beta, xa=xa)
    far_gc, alpha = lax.optimization_barrier((far_gc, alpha))
    far_gc = [swap(part, along[half + z]) for z, part in enumerate(far_gc)]
    yb, scale, last = first_rows([na - 1], share_x, x, y, e, alpha, first_beta, mass_b, got, 2 * nz)
    near_gc = shares(gc, swap(gc_send, core), [jnp.float32] + [jnp.bfloat16] * (half - 1))
    (grad_cam, *parts), yb = lax.optimization_barrier((near_gc, yb))
    parts = [swap(part, along[z + 1]) for z, part in enumerate(parts)]
    last = swap(last, across[na - 1])
    sent = other_rows(list(range(1, na - 1)), share_x, x, yb, e, alpha, jnp.bfloat16)
    sent = [swap(part, across[s + 1]) for s, part in enumerate(sent)]
    last, yb = lax.optimization_barrier((last, yb))
    gi, = other_rows([0], share_x, x, yb, e, alpha, jnp.float32)
    grad_imu, grad_cam = add_up([gi, *sent, last], [grad_cam, *parts, *far_gc], scale)
    return grad_imu, grad_cam[None]


def solution(mesh):
    in_specs = (P(("row", "col"), None), P("col", "row", None), P("row"), P("col"))
    out_specs = (P(("row", "col"), None), P("col", "row", None))
    return jax.shard_map(local, mesh=mesh, in_specs=in_specs, out_specs=out_specs, check_vma=False)
```

```python
import functools
import math

import jax
import jax.numpy as jnp
from jax import lax
from jax.experimental import pallas as pl
from jax.experimental.pallas import tpu as pltpu
from jax.sharding import PartitionSpec as P

D = 128
ITERS = 3
EPSILON = D / 20.0
LOG2E = math.log2(math.e)
CROSS = 2.0 * LOG2E / EPSILON
NT = (((1,), (1,)), ((), ()))
VMEM = pl.BlockSpec(memory_space=pltpu.VMEM)
HEAVY = 32


def spread(value, s_ref, sb_ref):
    chunks = value.shape[1] // 128
    for k in range(chunks):
        s_ref[k:k + 1, :] = value[:, k * 128:(k + 1) * 128]
    turned = jnp.transpose(s_ref[...])
    for k in range(chunks):
        sb_ref[k * 128:(k + 1) * 128, :] = jnp.broadcast_to(turned[:, k:k + 1], (128, 128))


def ordered(values, shifts, parts):
    share = values[0].shape[1] // parts
    return [
        jnp.concatenate([value[:, (k ^ s) * share:((k ^ s) + 1) * share] for k in range(parts)], axis=1)
        for value, s in zip(values, shifts)
    ]


def lse2(parts):
    top = functools.reduce(jnp.maximum, parts)
    return top + jnp.log2(sum(jnp.exp2(part - top) for part in parts))


def pipelined(places, chunk, width, a_ref, b_ref, d_ref, tile, finish):
    last = b_ref.shape[0] // width - 1

    def product(n, m):
        b = b_ref[pl.ds(pl.multiple_of(n * width, width), width), :]
        a = a_ref[places[m]:places[m] + chunk, :]
        d_ref[m % 2] = lax.dot_general(a, b, NT, preferred_element_type=jnp.float32)

    product(0, 0)

    def column(n, _):
        start = pl.multiple_of(n * width, width)
        state = None
        for m in range(len(places)):
            if m + 1 < len(places):
                product(n, m + 1)
            else:
                product(jnp.minimum(n + 1, last), 0)
            state = tile(m, start, state)
        finish(start, state)
        return 0

    lax.fori_loop(0, last + 1, column, 0)


def running_max(places, chunk, width, a_ref, b_ref, sb_ref, o_ref, e_ref, shift_ref):
    def column(n, _):
        start = pl.multiple_of(n * width, width)
        b = b_ref[pl.ds(start, width), :]

        def exponents(at):
            d = lax.dot_general(a_ref[at:at + chunk, :], b, NT, preferred_element_type=jnp.float32)
            s = sb_ref[at:at + chunk, :]
            return [d[:, q * 128:(q + 1) * 128] * CROSS + s for q in range(width // 128)]

        peak, total = jnp.full((1, width), -1e30, jnp.float32), jnp.zeros((1, width), jnp.float32)
        for at in places:
            peaks, totals = [], []
            for q, t in enumerate(exponents(at)):
                old = peak[:, q * 128:(q + 1) * 128]
                new = jnp.maximum(old, jnp.max(t, axis=0, keepdims=True))
                part = jnp.sum(jnp.exp2(t - new), axis=0, keepdims=True)
                peaks.append(new)
                totals.append(total[:, q * 128:(q + 1) * 128] * jnp.exp2(old - new) + part)
            peak, total = jnp.concatenate(peaks, axis=1), jnp.concatenate(totals, axis=1)
        o_ref[:, pl.ds(start, width)] = peak + jnp.log2(total)
        if e_ref is not None:
            shift_ref[:, pl.ds(start, width)] = peak
            for at in places:
                for q, t in enumerate(exponents(at)):
                    place = pl.ds(pl.multiple_of(start + q * 128, 128), 128)
                    e_ref[at:at + chunk, place] = jnp.exp2(t - shift_ref[:, place]).astype(jnp.bfloat16)
        return 0

    lax.fori_loop(0, b_ref.shape[0] // width, column, 0)


def lse_pass(places, chunk, width, a_ref, b_ref, sb_ref, d_ref, top_ref, o_ref, e_ref=None, shift_ref=None):
    tiles, group = width // 128, top_ref.shape[0]
    top_ref[...] = jnp.zeros_like(top_ref)

    def lanes_of(start, q):
        return pl.ds(pl.multiple_of(start + q * 128, 128), 128)

    def tile(m, start, state):
        def exponents(g, q):
            at = g * group
            s = sb_ref[places[m] + at:places[m] + at + group, :]
            return d_ref[m % 2, at:at + group, q * 128:(q + 1) * 128] * CROSS + s

        if m == 0:
            tops = [exponents(0, q) for q in range(tiles)]
            for g in range(1, 32 // group):
                tops = [jnp.maximum(top, exponents(g, q)) for q, top in enumerate(tops)]
            state = [(jnp.max(top, axis=0, keepdims=True), jnp.zeros((group, 128), jnp.float32)) for top in tops]
        for g in range(chunk // group):
            for q, (peak, total) in enumerate(state):
                e = jnp.exp2(exponents(g, q) - peak)
                if e_ref is not None:
                    at = places[m] + g * group
                    e_ref[at:at + group, lanes_of(start, q)] = e.astype(jnp.bfloat16)
                state[q] = peak, total + e
        return state

    def finish(start, state):
        for q, (peak, total) in enumerate(state):
            top_ref[...] = jnp.maximum(top_ref[...], total)
            o_ref[:, lanes_of(start, q)] = peak + jnp.log2(jnp.sum(total, axis=0, keepdims=True))
            if e_ref is not None:
                shift_ref[:, lanes_of(start, q)] = peak

    pipelined(places, chunk, width, a_ref, b_ref, d_ref, tile, finish)

    @pl.when(jnp.logical_not(jnp.max(top_ref[...]) < 2.0 ** 60))
    def _():
        running_max(places, chunk, min(width, 256), a_ref, b_ref, sb_ref, o_ref, e_ref, shift_ref)


def put_norms(places, share, y_ref, sb_ref):
    for at in places:
        y = y_ref[at:at + share, :].astype(jnp.float32)
        total = jnp.sum(y * y, axis=1, keepdims=True) * (-LOG2E / EPSILON)
        sb_ref[at:at + share, :] = jnp.broadcast_to(total, (share, 128))


def join(out_ref, parts):
    at = 0
    for part in parts:
        out_ref[at:at + part.shape[0], :] = part[...]
        at += part.shape[0]


def row_lse_early_kernel(width, nx, own_ref, *refs):
    xs, y_other, refs = refs[:nx], refs[nx], refs[nx + 1:]
    x_ref, xt_ref, o_ref, y_ref, sb_ref, d_ref, top_ref = refs
    share = y_other.shape[0]
    mine = own_ref.shape[0] - share
    join(x_ref, [own_ref.at[:mine, :], *xs])
    join(y_ref, [own_ref.at[mine:, :], y_other])
    for k in range(x_ref.shape[0] // 128):
        at = k * 128
        xt_ref[:, at:at + 128] = jnp.transpose(x_ref[at:at + 128, :].astype(jnp.float32)).astype(jnp.bfloat16)
    places = [0, share]
    put_norms(places, share, y_ref, sb_ref)
    lse_pass(places, share, width, y_ref, x_ref, sb_ref, d_ref, top_ref, o_ref)


def row_lse_middle_kernel(width, ny, x_ref, first_ref, *refs):
    ys, (o_ref, y_ref, sb_ref, d_ref, top_ref, sum_ref) = refs[:ny], refs[ny:]
    share = ys[0].shape[0]
    join(y_ref, ys)
    places = [k * share for k in range(ny)]
    put_norms(places, share, y_ref, sb_ref)
    lse_pass(places, share, width, y_ref, x_ref, sb_ref, d_ref, top_ref, sum_ref)
    o_ref[...] = lse2([first_ref[...], sum_ref[...]])


def row_lse_late_kernel(width, ny, own_ref, mass_ref, x_ref, first_ref, *refs):
    ys, (y_ref, o_ref, sb_ref, d_ref, top_ref, sum_ref) = refs[:ny], refs[ny:]
    share, rows, half = ys[0].shape[0], x_ref.shape[0], (ny + 1) // 2
    join(y_ref, [own_ref.at[own_ref.shape[0] - share:, :], *ys])
    places = [(half - 1) * share, (2 * half - 1) * share]
    put_norms(places, share, y_ref, sb_ref)
    lse_pass(places, share, width, y_ref, x_ref, sb_ref, d_ref, top_ref, sum_ref)
    o_ref[:, :rows] = lse2([first_ref[...], sum_ref[...]])
    o_ref[:, rows:] = mass_ref[:, :o_ref.shape[1] - rows]


def column_lse_kernel(width, chunk, na, x_ref, y_ref, mass_ref, *refs):
    got, (o_ref, e_ref, shift_ref, a_ref, s_ref, sb_ref, d_ref, top_ref) = refs[:na], refs[na:]
    rows, cols = x_ref.shape[0], y_ref.shape[0]
    o_ref[:, cols:] = mass_ref[:, mass_ref.shape[1] - o_ref.shape[1] + cols:]
    share = rows // na
    for k in range(na):
        at = rows + (k % 2) * share
        a_ref[:, k * share:(k + 1) * share] = got[k - k % 2][:, at:at + share]
    u = jnp.log2(a_ref[...]) - lse2(ordered([part[:, :rows] for part in got], range(na), na))
    spread(u, s_ref, sb_ref)
    places = list(range(0, rows, chunk))
    lse_pass(places, chunk, width, x_ref, y_ref, sb_ref, d_ref, top_ref, o_ref, e_ref, shift_ref)


def pair_kernel(size, shift, parts, combine, one_ref, two_ref, o_ref):
    two, = ordered([two_ref[:, :size]], [shift], parts)
    o_ref[:, :size] = combine([one_ref[:, :size], two])
    if o_ref.shape[1] > size:
        o_ref[:, size:] = one_ref[:, size:]


def split3(value):
    high = value.astype(jnp.bfloat16)
    rest = value - high.astype(jnp.float32)
    mid = rest.astype(jnp.bfloat16)
    return high, mid, (rest - mid.astype(jnp.float32)).astype(jnp.bfloat16)


def stacked(value):
    high, mid, low = [part.astype(jnp.float32) for part in split3(value)]
    dims = (16, value.shape[1])
    place = lax.broadcasted_iota(jnp.int32, dims, 0)
    parts = jnp.where(place == 0, high, jnp.where(place == 1, mid, jnp.where(place == 2, low, 0.0)))
    return parts.astype(jnp.bfloat16)


def row_sums(width, e_ref, w_ref, w16_ref, acc_ref, o_ref):
    rows, cols = e_ref.shape
    split = rows - acc_ref.shape[0]
    blocks = list(range(0, rows - split, 64))
    dots = list(range(0, split, width))
    for n, at in enumerate(dots):
        got = lax.dot_general(w16_ref[...], e_ref[at:at + width, :], NT, preferred_element_type=jnp.float32)
        for k in blocks[n * len(blocks) // len(dots):(n + 1) * len(blocks) // len(dots)]:
            total = jnp.zeros((64, 128), jnp.float32)
            for q in range(0, cols, 128):
                e = e_ref[split + k:split + k + 64, q:q + 128].astype(jnp.float32)
                total = total + e * w_ref[:, q:q + 128]
            acc_ref[k:k + 64, :] = total
        o_ref[:, at:at + width] = jnp.sum(got, axis=0, keepdims=True)
    for at in range(0, rows - split, 128):
        total = jnp.sum(jnp.transpose(acc_ref[at:at + 128, :]), axis=0, keepdims=True)
        o_ref[:, split + at:split + at + 128] = total


def first_row_kernel(width, shifts, parts, e_ref, shift_ref, *refs):
    nz = len(shifts)
    got, (o_ref, beta_ref, b_ref, w16_ref, acc_ref) = refs[:nz], refs[nz:]
    cols = e_ref.shape[1]
    share = cols // parts
    for k in range(parts):
        at = cols + (k // nz) * share
        b_ref[:, k * share:(k + 1) * share] = got[k % nz][:, at:at + share]
    lse = lse2(ordered([part[:, :cols] for part in got], shifts, parts))
    beta_ref[...] = jnp.exp2(jnp.log2(b_ref[...]) - lse + shift_ref[...])
    w16_ref[...] = stacked(beta_ref[...])
    row_sums(width, e_ref, beta_ref, w16_ref, acc_ref, o_ref)


def new_scale(b_ref, got, shifts, parts):
    return b_ref[...] / sum(ordered([part[...] for part in got], shifts, parts))


def row_kernel(width, shifts, parts, e_ref, first_ref, b_ref, *refs):
    got, (o_ref, w16_ref, acc_ref, w_ref) = refs[:-4], refs[-4:]
    w_ref[...] = first_ref[...] * new_scale(b_ref, got, shifts, parts)
    w16_ref[...] = stacked(w_ref[...])
    row_sums(width, e_ref, w_ref, w16_ref, acc_ref, o_ref)


def column_kernel(width, shifts, parts, e_ref, a_ref, first_ref, *refs):
    got, (o_ref, alpha_ref, w16_ref) = refs[:-3], refs[-3:]
    alpha_ref[...] = a_ref[...] / sum(ordered([part[...] for part in got], shifts, parts))
    w16_ref[...] = stacked(alpha_ref[...])
    for at in range(0, e_ref.shape[1], width):
        sums = jnp.dot(w16_ref[...], e_ref[:, at:at + width], preferred_element_type=jnp.float32)
        o_ref[:, at:at + width] = first_ref[:, at:at + width] * jnp.sum(sums, axis=0, keepdims=True)


def flat(value):
    return value.reshape(1, -1) if value.ndim == 1 else value


def weighted(kernel, outs, e, rows, got, parts):
    got, shifts = got
    size = e.shape[0] if kernel is column_kernel else e.shape[1]
    width = 512 if kernel is column_kernel else 256
    scratch = [pltpu.VMEM((16, size), jnp.bfloat16)]
    if kernel is not column_kernel:
        part = 7 if kernel is row_kernel else 6
        scratch.append(pltpu.VMEM((e.shape[0] * part // 8, 128), jnp.float32))
    if kernel is row_kernel:
        scratch.append(pltpu.VMEM((1, size), jnp.float32))
    return pl.pallas_call(
        functools.partial(kernel, width, tuple(shifts), parts),
        out_shape=[shape(*dims) for dims in outs],
        in_specs=[VMEM] * (1 + len(rows) + len(got)),
        out_specs=[VMEM] * len(outs),
        scratch_shapes=scratch,
        compiler_params=pltpu.CompilerParams(vmem_limit_bytes=16 << 20),
        cost_estimate=pl.CostEstimate(flops=2 * e.size, bytes_accessed=2 * e.size, transcendentals=0),
        name="weighted_sum",
    )(e, *rows, *[flat(part) for part in got])


def pass_cost(depth, lanes):
    return pl.CostEstimate(flops=2 * depth * lanes * D, bytes_accessed=2 * D * (depth + lanes), transcendentals=depth * lanes)


def shape(*dims, dtype=jnp.float32):
    return jax.ShapeDtypeStruct(dims, dtype)


def lse_scratch(depth, chunk, width, group=32):
    return [
        pltpu.VMEM((depth, 128), jnp.float32),
        pltpu.VMEM((2, chunk, width), jnp.float32),
        pltpu.VMEM((group, 128), jnp.float32),
    ]


def row_lse_early(own, xs, y_other, width=1024):
    share = y_other.shape[0]
    rows, depth = own.shape[0] - share + sum(part.shape[0] for part in xs), 2 * share
    return pl.pallas_call(
        functools.partial(row_lse_early_kernel, width, len(xs)),
        out_shape=(shape(rows, D, dtype=jnp.bfloat16), shape(D, rows, dtype=jnp.bfloat16), shape(1, rows)),
        in_specs=[VMEM] * (len(xs) + 2),
        out_specs=(VMEM,) * 3,
        scratch_shapes=[pltpu.VMEM((depth, D), jnp.bfloat16), *lse_scratch(depth, share, width)],
        compiler_params=pltpu.CompilerParams(vmem_limit_bytes=16 << 20),
        cost_estimate=pass_cost(depth, rows),
        name="row_lse_early",
    )(own, *xs, y_other)


def row_lse_middle(x, ys, first, width=1024):
    rows, share = x.shape[0], ys[0].shape[0]
    depth = len(ys) * share
    return pl.pallas_call(
        functools.partial(row_lse_middle_kernel, width, len(ys)),
        out_shape=shape(1, rows),
        in_specs=[VMEM] * (len(ys) + 2),
        out_specs=VMEM,
        scratch_shapes=[
            pltpu.VMEM((depth, D), jnp.bfloat16),
            *lse_scratch(depth, share, width),
            pltpu.VMEM((1, rows), jnp.float32),
        ],
        compiler_params=pltpu.CompilerParams(vmem_limit_bytes=16 << 20),
        cost_estimate=pass_cost(depth, rows),
        name="row_lse_middle",
    )(x, first, *ys)


def row_lse_late(own, x, ys, first, mass, tail, width=1024):
    rows, share = x.shape[0], ys[0].shape[0]
    depth = (len(ys) + 1) * share
    return pl.pallas_call(
        functools.partial(row_lse_late_kernel, width, len(ys)),
        out_shape=(shape(depth, D, dtype=jnp.bfloat16), shape(1, rows + tail)),
        in_specs=[VMEM] * (len(ys) + 4),
        out_specs=(VMEM,) * 2,
        scratch_shapes=[*lse_scratch(depth, share, width), pltpu.VMEM((1, rows), jnp.float32)],
        compiler_params=pltpu.CompilerParams(vmem_limit_bytes=16 << 20),
        cost_estimate=pass_cost(2 * share, rows),
        name="row_lse_late",
    )(own, mass.reshape(1, -1), x, first, *ys)


def column_lse(x, y, mass, tail, got, width=512, chunk=512):
    rows, cols = x.shape[0], y.shape[0]
    return pl.pallas_call(
        functools.partial(column_lse_kernel, width, chunk, len(got)),
        out_shape=(shape(1, cols + tail), shape(rows, cols, dtype=jnp.bfloat16), shape(1, cols), shape(1, rows)),
        in_specs=[VMEM] * (3 + len(got)),
        out_specs=(VMEM,) * 4,
        scratch_shapes=[pltpu.VMEM((rows // 128, 128), jnp.float32), *lse_scratch(rows, chunk, width, 16)],
        compiler_params=pltpu.CompilerParams(vmem_limit_bytes=16 << 20),
        cost_estimate=pass_cost(rows, cols),
        name="column_lse",
    )(x, y, mass.reshape(1, -1), *[part.reshape(1, -1) for part in got])


def pair_of(combine, one, two, size, shift, parts):
    whole = one.shape[-1]
    return pl.pallas_call(
        functools.partial(pair_kernel, size, shift, parts, combine),
        out_shape=shape(1, whole),
        in_specs=[VMEM] * 2,
        out_specs=VMEM,
        compiler_params=pltpu.CompilerParams(vmem_limit_bytes=16 << 20),
        name="pair",
    )(one.reshape(1, whole), two.reshape(1, whole))


def high_low(value):
    high = value.astype(jnp.bfloat16)
    return high, (value - high.astype(jnp.float32)).astype(jnp.bfloat16)


def put_xa(xt_ref, alpha_ref, xa_ref):
    place = lax.broadcasted_iota(jnp.int32, (128, 512), 0)
    for at in range(0, xt_ref.shape[1], 512):
        alpha = alpha_ref[:, at:at + 512]
        high, low = high_low(xt_ref[:, at:at + 512].astype(jnp.float32) * alpha)
        first, second = high_low(alpha)
        low = jnp.where(place == 126, first.astype(jnp.float32), low.astype(jnp.float32))
        low = jnp.where(place == 127, second.astype(jnp.float32), low)
        xa_ref[:128, at:at + 512] = high
        xa_ref[128:, at:at + 512] = low.astype(jnp.bfloat16)


def column_parts(blocks, share, xa_ref, y_ref, e_ref, first_ref, own_ref, sent_ref,
                 bb_ref, cb_ref, s_ref, count_ref, acc_ref):
    spread(jnp.concatenate([first_ref[:, at:at + share] for at in blocks], axis=1), s_ref, bb_ref)
    lower = lax.broadcasted_iota(jnp.int32, (128, share), 0) < 126
    for k, at in enumerate(blocks):
        to = k * share
        got = jnp.dot(xa_ref[...], e_ref[:, at:at + share], preferred_element_type=jnp.float32)
        acc_ref[:, to:to + share] = got[:128] + jnp.where(lower, got[128:], 0.0)
        count_ref[:, to:to + share] = got[254:255] + got[255:256]
    spread(count_ref[...], s_ref, cb_ref)
    own = own_ref.shape[0]
    for k, at in enumerate(blocks):
        for q in range(0, share, 128):
            to = k * share + q
            pulled = jnp.transpose(acc_ref[:, to:to + 128])
            whole = cb_ref[to:to + 128, :] * y_ref[at + q:at + q + 128, :].astype(jnp.float32)
            grad = bb_ref[to:to + 128, :] * (whole - pulled)
            if to < own:
                own_ref[to:to + 128, :] = grad
            else:
                sent_ref[to - own:to - own + 128, :] = grad.astype(jnp.bfloat16)


def first_columns_kernel(blocks, share, xt_ref, y_ref, e_ref, alpha_ref, first_ref, own_ref, sent_ref, xa_ref, *rest):
    put_xa(xt_ref, alpha_ref, xa_ref)
    column_parts(blocks, share, xa_ref, y_ref, e_ref, first_ref, own_ref, sent_ref, *rest)


def columns_kernel(blocks, share, xa_ref, y_ref, e_ref, first_ref, own_ref, sent_ref, *rest):
    column_parts(blocks, share, xa_ref, y_ref, e_ref, first_ref, own_ref, sent_ref, *rest)


def column_grad(zs, nz, share, y, e, first, xt=None, alpha=None, xa=None):
    rows, size = e.shape[0], 2 * len(zs) * share
    blocks = [z * share for z in zs] + [(nz + z) * share for z in zs]
    out_shape = [shape(size // 2, D), shape(size // 2, D, dtype=jnp.bfloat16)]
    if xa is None:
        kernel, args = first_columns_kernel, (xt, y, e, alpha, first)
        out_shape.append(shape(256, rows, dtype=jnp.bfloat16))
    else:
        kernel, args = columns_kernel, (xa, y, e, first)
    return pl.pallas_call(
        functools.partial(kernel, blocks, share),
        out_shape=out_shape,
        in_specs=[VMEM] * len(args),
        out_specs=[VMEM] * len(out_shape),
        scratch_shapes=[
            pltpu.VMEM((size, 128), jnp.float32),
            pltpu.VMEM((size, 128), jnp.float32),
            pltpu.VMEM((size // 128, 128), jnp.float32),
            pltpu.VMEM((1, size), jnp.float32),
            pltpu.VMEM((128, size), jnp.float32),
        ],
        compiler_params=pltpu.CompilerParams(vmem_limit_bytes=16 << 20),
        cost_estimate=pl.CostEstimate(flops=4 * rows * size * D, bytes_accessed=2 * rows * size, transcendentals=0),
        name="column_grad",
    )(*args)


def row_block(at, chunk, x_ref, e_ref, yb_ref, scale):
    got = jnp.dot(e_ref[pl.ds(at, chunk), :], yb_ref[...], preferred_element_type=jnp.float32)
    lower = lax.broadcasted_iota(jnp.int32, (chunk, 128), 1) < 126
    total = got[:, 254:255] + got[:, 255:256]
    pulled = got[:, :128] + jnp.where(lower, got[:, 128:], 0.0)
    x = x_ref[pl.ds(at, chunk), :].astype(jnp.float32)
    return 2.0 * scale * (total * x - pulled)


def put_yb(y_ref, beta, yb_ref, s_ref, bb_ref):
    spread(beta, s_ref, bb_ref)
    place = lax.broadcasted_iota(jnp.int32, (256, 128), 1)
    for at in range(0, y_ref.shape[0], 256):
        beta = bb_ref[at:at + 256, :]
        high, low = high_low(y_ref[at:at + 256, :].astype(jnp.float32) * beta)
        first, second = high_low(beta)
        low = jnp.where(place == 126, first.astype(jnp.float32), low.astype(jnp.float32))
        low = jnp.where(place == 127, second.astype(jnp.float32), low)
        yb_ref[at:at + 256, :128] = high
        yb_ref[at:at + 256, 128:] = low.astype(jnp.bfloat16)


def row_parts(parts, x_ref, e_ref, alpha_ref, yb_ref, outs, sa_ref, ab_ref):
    share = outs[0].shape[0]
    chunk = math.gcd(share, 512)
    for part, out_ref in zip(parts, outs):
        spread(alpha_ref[:, part * share:(part + 1) * share], sa_ref, ab_ref)
        for k in range(0, share, chunk):
            grad = row_block(part * share + k, chunk, x_ref, e_ref, yb_ref, ab_ref[k:k + chunk, :])
            out_ref[k:k + chunk, :] = grad.astype(out_ref.dtype)


def first_rows_kernel(parts, shifts, blocks, nz, x_ref, y_ref, e_ref, alpha_ref, first_ref, b_ref, *refs):
    got, (yb_ref, scale_ref, *outs), (s_ref, bb_ref, sa_ref, ab_ref) = refs[:nz], refs[nz:-4], refs[-4:]
    scale = new_scale(b_ref, got, shifts, blocks)
    scale_ref[...] = scale[:, :scale_ref.shape[1]]
    put_yb(y_ref, first_ref[...] * scale, yb_ref, s_ref, bb_ref)
    row_parts(parts, x_ref, e_ref, alpha_ref, yb_ref, outs, sa_ref, ab_ref)


def rows_kernel(parts, x_ref, yb_ref, e_ref, alpha_ref, *refs):
    row_parts(parts, x_ref, e_ref, alpha_ref, yb_ref, refs[:-2], *refs[-2:])


def rows_scratch(share):
    return [pltpu.VMEM((share // 128, 128), jnp.float32), pltpu.VMEM((share, 128), jnp.float32)]


def rows_cost(share, parts, cols):
    size = share * len(parts) * cols
    return pl.CostEstimate(flops=4 * size * D, bytes_accessed=2 * size, transcendentals=0)


def first_rows(parts, share, x, y, e, alpha, first, mass, got, blocks):
    cols = y.shape[0]
    got, shifts = got
    return pl.pallas_call(
        functools.partial(first_rows_kernel, parts, tuple(shifts), blocks, len(got)),
        out_shape=[shape(cols, 256, dtype=jnp.bfloat16), shape(1, cols // blocks)]
        + [shape(share, D, dtype=jnp.bfloat16)] * len(parts),
        in_specs=[VMEM] * (6 + len(got)),
        out_specs=[VMEM] * (2 + len(parts)),
        scratch_shapes=[
            pltpu.VMEM((cols // 128, 128), jnp.float32),
            pltpu.VMEM((cols, 128), jnp.float32),
            *rows_scratch(share),
        ],
        compiler_params=pltpu.CompilerParams(vmem_limit_bytes=16 << 20),
        cost_estimate=rows_cost(share * HEAVY, parts, cols),
        name="first_rows",
    )(x, y, e, alpha, first, mass, *[flat(part) for part in got])


def other_rows(parts, share, x, yb, e, alpha, dtype):
    return pl.pallas_call(
        functools.partial(rows_kernel, parts),
        out_shape=[shape(share, D, dtype=dtype)] * len(parts),
        in_specs=[VMEM] * 4,
        out_specs=[VMEM] * len(parts),
        scratch_shapes=rows_scratch(share),
        compiler_params=pltpu.CompilerParams(vmem_limit_bytes=16 << 20),
        cost_estimate=rows_cost(share, parts, yb.shape[0]),
        name="other_rows",
    )(x, yb, e, alpha)


def add_up_kernel(na, scale_ref, *refs):
    ins, (rows_ref, cols_ref, s_ref, sb_ref) = refs[:-4], refs[-4:]
    rows_ref[...] = sum(part[...].astype(jnp.float32) for part in ins[:na])
    spread(scale_ref[...], s_ref, sb_ref)
    cols_ref[...] = 2.0 * sb_ref[...] * sum(part[...].astype(jnp.float32) for part in ins[na:])


def add_up(rows, columns, scale):
    share = scale.shape[1]
    return pl.pallas_call(
        functools.partial(add_up_kernel, len(rows)),
        out_shape=(shape(*rows[0].shape), shape(*columns[0].shape)),
        in_specs=[VMEM] * (1 + len(rows) + len(columns)),
        out_specs=(VMEM,) * 2,
        scratch_shapes=rows_scratch(share),
        compiler_params=pltpu.CompilerParams(vmem_limit_bytes=16 << 20),
        name="add_up",
    )(scale, *rows, *columns)


def shares_kernel(gc_ref, other_ref, *outs):
    share = outs[0].shape[0]
    for k, out_ref in enumerate(outs):
        at = k * share
        total = gc_ref[at:at + share, :] + other_ref[at:at + share, :].astype(jnp.float32)
        out_ref[...] = total.astype(out_ref.dtype)


def shares(gc, other, dtypes):
    share = gc.shape[0] // len(dtypes)
    return pl.pallas_call(
        shares_kernel,
        out_shape=[shape(share, D, dtype=dtype) for dtype in dtypes],
        in_specs=[VMEM] * 2,
        out_specs=[VMEM] * len(dtypes),
        compiler_params=pltpu.CompilerParams(vmem_limit_bytes=16 << 20),
        name="shares",
    )(gc, other)


class Groups:
    def __init__(self, nrow, ncol):
        self.count = nrow * ncol
        self.across = [(a << 1) * ncol + b for a in range(nrow // 2) for b in range(2)]
        self.along = [z << 1 for z in range(ncol // 2)]
        self.core = ncol

    def swap(self, value, mask):
        if mask == 0:
            return value
        return lax.ppermute(value, ("row", "col"), [(i, i ^ mask) for i in range(self.count)])


def local(imu, camera, imu_mass, cam_mass):
    nrow, ncol = lax.axis_size("row"), lax.axis_size("col")
    groups = Groups(nrow, ncol)
    swap, across, along, core = groups.swap, groups.across, groups.along, groups.core
    na, nz = len(across), len(along)
    share_x, share_y = imu.shape[0], camera.shape[1]
    rows, cols = na * share_x, 2 * nz * share_y

    def direct(value, masks):
        return [swap(value, mask) for mask in masks], range(len(masks))

    xs, _ = direct(imu, across)
    own, mine = lax.optimization_barrier((jnp.concatenate([imu, camera[0]]), camera[0]))
    near = [mine] + [None] * (nz - 1)
    for z in range(1, nz):
        if not z & (z - 1):
            near[z] = swap(mine if z == 1 else camera[0], along[z])
    far = [swap(mine, core)]

    def pair(mass, place, share):
        return [lax.dynamic_slice_in_dim(mass, (place ^ k) * share, share, 0) for k in range(2)]

    row, col = lax.axis_index("row"), lax.axis_index("col")
    mass = jnp.concatenate(pair(imu_mass, col, share_x) + pair(cam_mass, row, share_y))

    x, xt, first = row_lse_early(own, xs[1:], far[0])
    relays = [z for z in range(2, nz) if not z & (z - 1)]
    first, mass, got = lax.optimization_barrier((first, mass, [near[z] for z in relays]))
    for z, part in zip(relays, got):
        near[z] = part
    for z in range(1, nz):
        if z & (z - 1):
            near[z] = swap(near[z & (z - 1)], along[z & -z])
    middle = near[1:-1]
    far += [swap(part, core) for part in middle]
    first = row_lse_middle(x, middle, first)
    first, last = lax.optimization_barrier((first, near[-1]))
    first = row_lse_middle(x, far[1:], first)
    far.append(swap(last, core))
    y, sent = row_lse_late(own, x, [*middle, last, *far], first, mass, 2 * share_x)
    got, _ = direct(sent.reshape(-1), across)

    sent, e, shift, mass_a = column_lse(x, y, mass, 2 * share_y, got)
    sent = pair_of(lse2, sent, swap(sent.reshape(-1), core), cols, 1, 2)
    got = direct(sent.reshape(-1), along)

    sums, first_beta, mass_b = weighted(
        first_row_kernel, [(1, rows), (1, cols), (1, cols)], e, [shift], got, 2 * nz)
    for step in range(1, ITERS):
        if step > 1:
            sums, = weighted(row_kernel, [(1, rows)], e, [first_beta, mass_b], got, 2 * nz)
        got = direct(sums.reshape(-1), across)
        part, alpha = weighted(column_kernel, [(1, cols), (1, rows)], e, [mass_a, first_beta], got, na)
        part = pair_of(sum, part, swap(part.reshape(-1), core), cols, 1, 2)
        part, alpha = lax.optimization_barrier((part, alpha))
        got = direct(part.reshape(-1), along)

    half = nz // 2
    gc, gc_send, xa = column_grad(range(half, nz), nz, share_y, y, e, first_beta, xt=xt, alpha=alpha)
    far_gc = shares(gc, swap(gc_send, core), [jnp.bfloat16] * (nz - half))
    gc, gc_send = column_grad(range(half), nz, share_y, y, e, first_beta, xa=xa)
    far_gc, alpha = lax.optimization_barrier((far_gc, alpha))
    far_gc = [swap(part, along[half + z]) for z, part in enumerate(far_gc)]
    yb, scale, last = first_rows([na - 1], share_x, x, y, e, alpha, first_beta, mass_b, got, 2 * nz)
    near_gc = shares(gc, swap(gc_send, core), [jnp.float32] + [jnp.bfloat16] * (half - 1))
    (grad_cam, *parts), yb = lax.optimization_barrier((near_gc, yb))
    parts = [swap(part, along[z + 1]) for z, part in enumerate(parts)]
    last = swap(last, across[na - 1])
    sent = other_rows(list(range(1, na - 1)), share_x, x, yb, e, alpha, jnp.bfloat16)
    sent = [swap(part, across[s + 1]) for s, part in enumerate(sent)]
    last, yb = lax.optimization_barrier((last, yb))
    gi, = other_rows([0], share_x, x, yb, e, alpha, jnp.float32)
    grad_imu, grad_cam = add_up([gi, *sent, last], [grad_cam, *parts, *far_gc], scale)
    return grad_imu, grad_cam[None]


def solution(mesh):
    in_specs = (P(("row", "col"), None), P("col", "row", None), P("row"), P("col"))
    out_specs = (P(("row", "col"), None), P("col", "row", None))
    return jax.shard_map(local, mesh=mesh, in_specs=in_specs, out_specs=out_specs, check_vma=False)
```

```python
import functools
import math

import jax
import jax.numpy as jnp
from jax import lax
from jax.experimental import pallas as pl
from jax.experimental.pallas import tpu as pltpu
from jax.sharding import PartitionSpec as P

D = 128
ITERS = 3
EPSILON = D / 20.0
LOG2E = math.log2(math.e)
CROSS = 2.0 * LOG2E / EPSILON
NT = (((1,), (1,)), ((), ()))
VMEM = pl.BlockSpec(memory_space=pltpu.VMEM)
HEAVY = 32


def spread(value, s_ref, sb_ref):
    chunks = value.shape[1] // 128
    for k in range(chunks):
        s_ref[k:k + 1, :] = value[:, k * 128:(k + 1) * 128]
    turned = jnp.transpose(s_ref[...])
    for k in range(chunks):
        sb_ref[k * 128:(k + 1) * 128, :] = jnp.broadcast_to(turned[:, k:k + 1], (128, 128))


def ordered(values, shifts, parts):
    share = values[0].shape[1] // parts
    return [
        jnp.concatenate([value[:, (k ^ s) * share:((k ^ s) + 1) * share] for k in range(parts)], axis=1)
        for value, s in zip(values, shifts)
    ]


def lse2(parts):
    top = functools.reduce(jnp.maximum, parts)
    return top + jnp.log2(sum(jnp.exp2(part - top) for part in parts))


def pipelined(places, chunk, width, a_ref, b_ref, d_ref, tile, finish):
    last = b_ref.shape[0] // width - 1

    def product(n, m):
        b = b_ref[pl.ds(pl.multiple_of(n * width, width), width), :]
        a = a_ref[places[m]:places[m] + chunk, :]
        d_ref[m % 2] = lax.dot_general(a, b, NT, preferred_element_type=jnp.float32)

    product(0, 0)

    def column(n, _):
        start = pl.multiple_of(n * width, width)
        state = None
        for m in range(len(places)):
            if m + 1 < len(places):
                product(n, m + 1)
            else:
                product(jnp.minimum(n + 1, last), 0)
            state = tile(m, start, state)
        finish(start, state)
        return 0

    lax.fori_loop(0, last + 1, column, 0)


def running_max(places, chunk, width, a_ref, b_ref, sb_ref, o_ref, e_ref, shift_ref):
    def column(n, _):
        start = pl.multiple_of(n * width, width)
        b = b_ref[pl.ds(start, width), :]

        def exponents(at):
            d = lax.dot_general(a_ref[at:at + chunk, :], b, NT, preferred_element_type=jnp.float32)
            s = sb_ref[at:at + chunk, :]
            return [d[:, q * 128:(q + 1) * 128] * CROSS + s for q in range(width // 128)]

        peak, total = jnp.full((1, width), -1e30, jnp.float32), jnp.zeros((1, width), jnp.float32)
        for at in places:
            peaks, totals = [], []
            for q, t in enumerate(exponents(at)):
                old = peak[:, q * 128:(q + 1) * 128]
                new = jnp.maximum(old, jnp.max(t, axis=0, keepdims=True))
                part = jnp.sum(jnp.exp2(t - new), axis=0, keepdims=True)
                peaks.append(new)
                totals.append(total[:, q * 128:(q + 1) * 128] * jnp.exp2(old - new) + part)
            peak, total = jnp.concatenate(peaks, axis=1), jnp.concatenate(totals, axis=1)
        o_ref[:, pl.ds(start, width)] = peak + jnp.log2(total)
        if e_ref is not None:
            shift_ref[:, pl.ds(start, width)] = peak
            for at in places:
                for q, t in enumerate(exponents(at)):
                    place = pl.ds(pl.multiple_of(start + q * 128, 128), 128)
                    e_ref[at:at + chunk, place] = jnp.exp2(t - shift_ref[:, place]).astype(jnp.bfloat16)
        return 0

    lax.fori_loop(0, b_ref.shape[0] // width, column, 0)


def lse_pass(places, chunk, width, a_ref, b_ref, sb_ref, d_ref, top_ref, o_ref, e_ref=None, shift_ref=None):
    tiles, group = width // 128, top_ref.shape[0]
    top_ref[...] = jnp.zeros_like(top_ref)

    def lanes_of(start, q):
        return pl.ds(pl.multiple_of(start + q * 128, 128), 128)

    def tile(m, start, state):
        def exponents(g, q):
            at = g * group
            s = sb_ref[places[m] + at:places[m] + at + group, :]
            return d_ref[m % 2, at:at + group, q * 128:(q + 1) * 128] * CROSS + s

        if m == 0:
            tops = [exponents(0, q) for q in range(tiles)]
            for g in range(1, 32 // group):
                tops = [jnp.maximum(top, exponents(g, q)) for q, top in enumerate(tops)]
            state = [(jnp.max(top, axis=0, keepdims=True), jnp.zeros((group, 128), jnp.float32)) for top in tops]
        for g in range(chunk // group):
            for q, (peak, total) in enumerate(state):
                e = jnp.exp2(exponents(g, q) - peak)
                if e_ref is not None:
                    at = places[m] + g * group
                    e_ref[at:at + group, lanes_of(start, q)] = e.astype(jnp.bfloat16)
                state[q] = peak, total + e
        return state

    def finish(start, state):
        for q, (peak, total) in enumerate(state):
            top_ref[...] = jnp.maximum(top_ref[...], total)
            o_ref[:, lanes_of(start, q)] = peak + jnp.log2(jnp.sum(total, axis=0, keepdims=True))
            if e_ref is not None:
                shift_ref[:, lanes_of(start, q)] = peak

    pipelined(places, chunk, width, a_ref, b_ref, d_ref, tile, finish)

    @pl.when(jnp.logical_not(jnp.max(top_ref[...]) < 2.0 ** 60))
    def _():
        running_max(places, chunk, min(width, 256), a_ref, b_ref, sb_ref, o_ref, e_ref, shift_ref)


def put_norms(places, share, y_ref, sb_ref):
    for at in places:
        y = y_ref[at:at + share, :].astype(jnp.float32)
        total = jnp.sum(y * y, axis=1, keepdims=True) * (-LOG2E / EPSILON)
        sb_ref[at:at + share, :] = jnp.broadcast_to(total, (share, 128))


def join(out_ref, parts):
    at = 0
    for part in parts:
        out_ref[at:at + part.shape[0], :] = part[...]
        at += part.shape[0]


def row_lse_early_kernel(width, nx, own_ref, *refs):
    xs, y_other, refs = refs[:nx], refs[nx], refs[nx + 1:]
    x_ref, xt_ref, o_ref, y_ref, sb_ref, d_ref, top_ref = refs
    share = y_other.shape[0]
    mine = own_ref.shape[0] - share
    join(x_ref, [own_ref.at[:mine, :], *xs])
    join(y_ref, [own_ref.at[mine:, :], y_other])
    for k in range(x_ref.shape[0] // 128):
        at = k * 128
        xt_ref[:, at:at + 128] = jnp.transpose(x_ref[at:at + 128, :].astype(jnp.float32)).astype(jnp.bfloat16)
    places = [0, share]
    put_norms(places, share, y_ref, sb_ref)
    lse_pass(places, share, width, y_ref, x_ref, sb_ref, d_ref, top_ref, o_ref)


def row_lse_middle_kernel(width, ny, x_ref, first_ref, *refs):
    ys, (o_ref, y_ref, sb_ref, d_ref, top_ref, sum_ref) = refs[:ny], refs[ny:]
    share = ys[0].shape[0]
    join(y_ref, ys)
    places = [k * share for k in range(ny)]
    put_norms(places, share, y_ref, sb_ref)
    lse_pass(places, share, width, y_ref, x_ref, sb_ref, d_ref, top_ref, sum_ref)
    o_ref[...] = lse2([first_ref[...], sum_ref[...]])


def row_lse_late_kernel(width, ny, own_ref, mass_ref, x_ref, first_ref, *refs):
    ys, (y_ref, o_ref, sb_ref, d_ref, top_ref, sum_ref) = refs[:ny], refs[ny:]
    share, rows, half = ys[0].shape[0], x_ref.shape[0], (ny + 1) // 2
    join(y_ref, [own_ref.at[own_ref.shape[0] - share:, :], *ys])
    places = [k * share for k in range(half - 1, 2 * half) if k != half]
    put_norms(places, share, y_ref, sb_ref)
    lse_pass(places, share, width, y_ref, x_ref, sb_ref, d_ref, top_ref, sum_ref)
    o_ref[:, :rows] = lse2([first_ref[...], sum_ref[...]])
    o_ref[:, rows:] = mass_ref[:, :o_ref.shape[1] - rows]


def column_lse_kernel(width, chunk, na, x_ref, y_ref, mass_ref, *refs):
    got, (o_ref, e_ref, shift_ref, a_ref, s_ref, sb_ref, d_ref, top_ref) = refs[:na], refs[na:]
    rows, cols = x_ref.shape[0], y_ref.shape[0]
    o_ref[:, cols:] = mass_ref[:, mass_ref.shape[1] - o_ref.shape[1] + cols:]
    share = rows // na
    for k in range(na):
        at = rows + (k % 2) * share
        a_ref[:, k * share:(k + 1) * share] = got[k - k % 2][:, at:at + share]
    u = jnp.log2(a_ref[...]) - lse2(ordered([part[:, :rows] for part in got], range(na), na))
    spread(u, s_ref, sb_ref)
    places = list(range(0, rows, chunk))
    lse_pass(places, chunk, width, x_ref, y_ref, sb_ref, d_ref, top_ref, o_ref, e_ref, shift_ref)


def pair_kernel(size, shift, parts, combine, one_ref, two_ref, o_ref):
    two, = ordered([two_ref[:, :size]], [shift], parts)
    o_ref[:, :size] = combine([one_ref[:, :size], two])
    if o_ref.shape[1] > size:
        o_ref[:, size:] = one_ref[:, size:]


def split3(value):
    high = value.astype(jnp.bfloat16)
    rest = value - high.astype(jnp.float32)
    mid = rest.astype(jnp.bfloat16)
    return high, mid, (rest - mid.astype(jnp.float32)).astype(jnp.bfloat16)


def stacked(value):
    high, mid, low = [part.astype(jnp.float32) for part in split3(value)]
    dims = (16, value.shape[1])
    place = lax.broadcasted_iota(jnp.int32, dims, 0)
    parts = jnp.where(place == 0, high, jnp.where(place == 1, mid, jnp.where(place == 2, low, 0.0)))
    return parts.astype(jnp.bfloat16)


def row_sums(width, e_ref, w_ref, w16_ref, acc_ref, o_ref):
    rows, cols = e_ref.shape
    split = rows - acc_ref.shape[0]
    blocks = list(range(0, rows - split, 64))
    dots = list(range(0, split, width))
    for n, at in enumerate(dots):
        got = lax.dot_general(w16_ref[...], e_ref[at:at + width, :], NT, preferred_element_type=jnp.float32)
        for k in blocks[n * len(blocks) // len(dots):(n + 1) * len(blocks) // len(dots)]:
            total = jnp.zeros((64, 128), jnp.float32)
            for q in range(0, cols, 128):
                e = e_ref[split + k:split + k + 64, q:q + 128].astype(jnp.float32)
                total = total + e * w_ref[:, q:q + 128]
            acc_ref[k:k + 64, :] = total
        o_ref[:, at:at + width] = jnp.sum(got, axis=0, keepdims=True)
    for at in range(0, rows - split, 128):
        total = jnp.sum(jnp.transpose(acc_ref[at:at + 128, :]), axis=0, keepdims=True)
        o_ref[:, split + at:split + at + 128] = total


def first_row_kernel(width, shifts, parts, e_ref, shift_ref, *refs):
    nz = len(shifts)
    got, (o_ref, beta_ref, b_ref, w16_ref, acc_ref) = refs[:nz], refs[nz:]
    cols = e_ref.shape[1]
    share = cols // parts
    for k in range(parts):
        at = cols + (k // nz) * share
        b_ref[:, k * share:(k + 1) * share] = got[k % nz][:, at:at + share]
    lse = lse2(ordered([part[:, :cols] for part in got], shifts, parts))
    beta_ref[...] = jnp.exp2(jnp.log2(b_ref[...]) - lse + shift_ref[...])
    w16_ref[...] = stacked(beta_ref[...])
    row_sums(width, e_ref, beta_ref, w16_ref, acc_ref, o_ref)


def new_scale(b_ref, got, shifts, parts):
    return b_ref[...] / sum(ordered([part[...] for part in got], shifts, parts))


def row_kernel(width, shifts, parts, e_ref, first_ref, b_ref, *refs):
    got, (o_ref, w16_ref, acc_ref, w_ref) = refs[:-4], refs[-4:]
    w_ref[...] = first_ref[...] * new_scale(b_ref, got, shifts, parts)
    w16_ref[...] = stacked(w_ref[...])
    row_sums(width, e_ref, w_ref, w16_ref, acc_ref, o_ref)


def column_kernel(width, shifts, parts, e_ref, a_ref, first_ref, *refs):
    got, (o_ref, alpha_ref, w16_ref) = refs[:-3], refs[-3:]
    alpha_ref[...] = a_ref[...] / sum(ordered([part[...] for part in got], shifts, parts))
    w16_ref[...] = stacked(alpha_ref[...])
    for at in range(0, e_ref.shape[1], width):
        sums = jnp.dot(w16_ref[...], e_ref[:, at:at + width], preferred_element_type=jnp.float32)
        o_ref[:, at:at + width] = first_ref[:, at:at + width] * jnp.sum(sums, axis=0, keepdims=True)


def flat(value):
    return value.reshape(1, -1) if value.ndim == 1 else value


def weighted(kernel, outs, e, rows, got, parts):
    got, shifts = got
    size = e.shape[0] if kernel is column_kernel else e.shape[1]
    width = 512 if kernel is column_kernel else 256
    scratch = [pltpu.VMEM((16, size), jnp.bfloat16)]
    if kernel is not column_kernel:
        part = 7 if kernel is row_kernel else 6
        scratch.append(pltpu.VMEM((e.shape[0] * part // 8, 128), jnp.float32))
    if kernel is row_kernel:
        scratch.append(pltpu.VMEM((1, size), jnp.float32))
    return pl.pallas_call(
        functools.partial(kernel, width, tuple(shifts), parts),
        out_shape=[shape(*dims) for dims in outs],
        in_specs=[VMEM] * (1 + len(rows) + len(got)),
        out_specs=[VMEM] * len(outs),
        scratch_shapes=scratch,
        compiler_params=pltpu.CompilerParams(vmem_limit_bytes=16 << 20),
        cost_estimate=pl.CostEstimate(flops=2 * e.size, bytes_accessed=2 * e.size, transcendentals=0),
        name="weighted_sum",
    )(e, *rows, *[flat(part) for part in got])


def pass_cost(depth, lanes):
    return pl.CostEstimate(flops=2 * depth * lanes * D, bytes_accessed=2 * D * (depth + lanes), transcendentals=depth * lanes)


def shape(*dims, dtype=jnp.float32):
    return jax.ShapeDtypeStruct(dims, dtype)


def lse_scratch(depth, chunk, width, group=32):
    return [
        pltpu.VMEM((depth, 128), jnp.float32),
        pltpu.VMEM((2, chunk, width), jnp.float32),
        pltpu.VMEM((group, 128), jnp.float32),
    ]


def row_lse_early(own, xs, y_other, width=1024):
    share = y_other.shape[0]
    rows, depth = own.shape[0] - share + sum(part.shape[0] for part in xs), 2 * share
    return pl.pallas_call(
        functools.partial(row_lse_early_kernel, width, len(xs)),
        out_shape=(shape(rows, D, dtype=jnp.bfloat16), shape(D, rows, dtype=jnp.bfloat16), shape(1, rows)),
        in_specs=[VMEM] * (len(xs) + 2),
        out_specs=(VMEM,) * 3,
        scratch_shapes=[pltpu.VMEM((depth, D), jnp.bfloat16), *lse_scratch(depth, share, width)],
        compiler_params=pltpu.CompilerParams(vmem_limit_bytes=16 << 20),
        cost_estimate=pass_cost(depth, rows),
        name="row_lse_early",
    )(own, *xs, y_other)


def row_lse_middle(x, ys, first, width=1024):
    rows, share = x.shape[0], ys[0].shape[0]
    depth = len(ys) * share
    return pl.pallas_call(
        functools.partial(row_lse_middle_kernel, width, len(ys)),
        out_shape=shape(1, rows),
        in_specs=[VMEM] * (len(ys) + 2),
        out_specs=VMEM,
        scratch_shapes=[
            pltpu.VMEM((depth, D), jnp.bfloat16),
            *lse_scratch(depth, share, width),
            pltpu.VMEM((1, rows), jnp.float32),
        ],
        compiler_params=pltpu.CompilerParams(vmem_limit_bytes=16 << 20),
        cost_estimate=pass_cost(depth, rows),
        name="row_lse_middle",
    )(x, first, *ys)


def row_lse_late(own, x, ys, first, mass, tail, width=1024):
    rows, share = x.shape[0], ys[0].shape[0]
    depth = (len(ys) + 1) * share
    return pl.pallas_call(
        functools.partial(row_lse_late_kernel, width, len(ys)),
        out_shape=(shape(depth, D, dtype=jnp.bfloat16), shape(1, rows + tail)),
        in_specs=[VMEM] * (len(ys) + 4),
        out_specs=(VMEM,) * 2,
        scratch_shapes=[*lse_scratch(depth, share, width), pltpu.VMEM((1, rows), jnp.float32)],
        compiler_params=pltpu.CompilerParams(vmem_limit_bytes=16 << 20),
        cost_estimate=pass_cost(depth // 2, rows),
        name="row_lse_late",
    )(own, mass.reshape(1, -1), x, first, *ys)


def column_lse(x, y, mass, tail, got, width=512, chunk=512):
    rows, cols = x.shape[0], y.shape[0]
    return pl.pallas_call(
        functools.partial(column_lse_kernel, width, chunk, len(got)),
        out_shape=(shape(1, cols + tail), shape(rows, cols, dtype=jnp.bfloat16), shape(1, cols), shape(1, rows)),
        in_specs=[VMEM] * (3 + len(got)),
        out_specs=(VMEM,) * 4,
        scratch_shapes=[pltpu.VMEM((rows // 128, 128), jnp.float32), *lse_scratch(rows, chunk, width, 16)],
        compiler_params=pltpu.CompilerParams(vmem_limit_bytes=16 << 20),
        cost_estimate=pass_cost(rows, cols),
        name="column_lse",
    )(x, y, mass.reshape(1, -1), *[part.reshape(1, -1) for part in got])


def pair_of(combine, one, two, size, shift, parts):
    whole = one.shape[-1]
    return pl.pallas_call(
        functools.partial(pair_kernel, size, shift, parts, combine),
        out_shape=shape(1, whole),
        in_specs=[VMEM] * 2,
        out_specs=VMEM,
        compiler_params=pltpu.CompilerParams(vmem_limit_bytes=16 << 20),
        name="pair",
    )(one.reshape(1, whole), two.reshape(1, whole))


def high_low(value):
    high = value.astype(jnp.bfloat16)
    return high, (value - high.astype(jnp.float32)).astype(jnp.bfloat16)


def put_xa(xt_ref, alpha_ref, xa_ref):
    place = lax.broadcasted_iota(jnp.int32, (128, 512), 0)
    for at in range(0, xt_ref.shape[1], 512):
        alpha = alpha_ref[:, at:at + 512]
        high, low = high_low(xt_ref[:, at:at + 512].astype(jnp.float32) * alpha)
        first, second = high_low(alpha)
        low = jnp.where(place == 126, first.astype(jnp.float32), low.astype(jnp.float32))
        low = jnp.where(place == 127, second.astype(jnp.float32), low)
        xa_ref[:128, at:at + 512] = high
        xa_ref[128:, at:at + 512] = low.astype(jnp.bfloat16)


def column_parts(blocks, share, xa_ref, y_ref, e_ref, first_ref, own_ref, sent_ref,
                 bb_ref, cb_ref, s_ref, count_ref, acc_ref):
    spread(jnp.concatenate([first_ref[:, at:at + share] for at in blocks], axis=1), s_ref, bb_ref)
    lower = lax.broadcasted_iota(jnp.int32, (128, share), 0) < 126
    for k, at in enumerate(blocks):
        to = k * share
        got = jnp.dot(xa_ref[...], e_ref[:, at:at + share], preferred_element_type=jnp.float32)
        acc_ref[:, to:to + share] = got[:128] + jnp.where(lower, got[128:], 0.0)
        count_ref[:, to:to + share] = got[254:255] + got[255:256]
    spread(count_ref[...], s_ref, cb_ref)
    own = own_ref.shape[0]
    for k, at in enumerate(blocks):
        for q in range(0, share, 128):
            to = k * share + q
            pulled = jnp.transpose(acc_ref[:, to:to + 128])
            whole = cb_ref[to:to + 128, :] * y_ref[at + q:at + q + 128, :].astype(jnp.float32)
            grad = bb_ref[to:to + 128, :] * (whole - pulled)
            if to < own:
                own_ref[to:to + 128, :] = grad
            else:
                sent_ref[to - own:to - own + 128, :] = grad.astype(jnp.bfloat16)


def first_columns_kernel(blocks, share, xt_ref, y_ref, e_ref, alpha_ref, first_ref, own_ref, sent_ref, xa_ref, *rest):
    put_xa(xt_ref, alpha_ref, xa_ref)
    column_parts(blocks, share, xa_ref, y_ref, e_ref, first_ref, own_ref, sent_ref, *rest)


def columns_kernel(blocks, share, xa_ref, y_ref, e_ref, first_ref, own_ref, sent_ref, *rest):
    column_parts(blocks, share, xa_ref, y_ref, e_ref, first_ref, own_ref, sent_ref, *rest)


def column_grad(zs, nz, share, y, e, first, xt=None, alpha=None, xa=None):
    rows, size = e.shape[0], 2 * len(zs) * share
    blocks = [z * share for z in zs] + [(nz + z) * share for z in zs]
    out_shape = [shape(size // 2, D), shape(size // 2, D, dtype=jnp.bfloat16)]
    if xa is None:
        kernel, args = first_columns_kernel, (xt, y, e, alpha, first)
        out_shape.append(shape(256, rows, dtype=jnp.bfloat16))
    else:
        kernel, args = columns_kernel, (xa, y, e, first)
    return pl.pallas_call(
        functools.partial(kernel, blocks, share),
        out_shape=out_shape,
        in_specs=[VMEM] * len(args),
        out_specs=[VMEM] * len(out_shape),
        scratch_shapes=[
            pltpu.VMEM((size, 128), jnp.float32),
            pltpu.VMEM((size, 128), jnp.float32),
            pltpu.VMEM((size // 128, 128), jnp.float32),
            pltpu.VMEM((1, size), jnp.float32),
            pltpu.VMEM((128, size), jnp.float32),
        ],
        compiler_params=pltpu.CompilerParams(vmem_limit_bytes=16 << 20),
        cost_estimate=pl.CostEstimate(flops=4 * rows * size * D, bytes_accessed=2 * rows * size, transcendentals=0),
        name="column_grad",
    )(*args)


def row_block(at, chunk, x_ref, e_ref, yb_ref, scale):
    got = jnp.dot(e_ref[pl.ds(at, chunk), :], yb_ref[...], preferred_element_type=jnp.float32)
    lower = lax.broadcasted_iota(jnp.int32, (chunk, 128), 1) < 126
    total = got[:, 254:255] + got[:, 255:256]
    pulled = got[:, :128] + jnp.where(lower, got[:, 128:], 0.0)
    x = x_ref[pl.ds(at, chunk), :].astype(jnp.float32)
    return 2.0 * scale * (total * x - pulled)


def put_yb(y_ref, beta, yb_ref, s_ref, bb_ref):
    spread(beta, s_ref, bb_ref)
    place = lax.broadcasted_iota(jnp.int32, (256, 128), 1)
    for at in range(0, y_ref.shape[0], 256):
        beta = bb_ref[at:at + 256, :]
        high, low = high_low(y_ref[at:at + 256, :].astype(jnp.float32) * beta)
        first, second = high_low(beta)
        low = jnp.where(place == 126, first.astype(jnp.float32), low.astype(jnp.float32))
        low = jnp.where(place == 127, second.astype(jnp.float32), low)
        yb_ref[at:at + 256, :128] = high
        yb_ref[at:at + 256, 128:] = low.astype(jnp.bfloat16)


def row_parts(parts, x_ref, e_ref, alpha_ref, yb_ref, outs, sa_ref, ab_ref):
    share = outs[0].shape[0]
    chunk = math.gcd(share, 512)
    for part, out_ref in zip(parts, outs):
        spread(alpha_ref[:, part * share:(part + 1) * share], sa_ref, ab_ref)
        for k in range(0, share, chunk):
            grad = row_block(part * share + k, chunk, x_ref, e_ref, yb_ref, ab_ref[k:k + chunk, :])
            out_ref[k:k + chunk, :] = grad.astype(out_ref.dtype)


def first_rows_kernel(parts, shifts, blocks, nz, x_ref, y_ref, e_ref, alpha_ref, first_ref, b_ref, *refs):
    got, (yb_ref, scale_ref, *outs), (s_ref, bb_ref, sa_ref, ab_ref) = refs[:nz], refs[nz:-4], refs[-4:]
    scale = new_scale(b_ref, got, shifts, blocks)
    scale_ref[...] = scale[:, :scale_ref.shape[1]]
    put_yb(y_ref, first_ref[...] * scale, yb_ref, s_ref, bb_ref)
    row_parts(parts, x_ref, e_ref, alpha_ref, yb_ref, outs, sa_ref, ab_ref)


def rows_kernel(parts, x_ref, yb_ref, e_ref, alpha_ref, *refs):
    row_parts(parts, x_ref, e_ref, alpha_ref, yb_ref, refs[:-2], *refs[-2:])


def rows_scratch(share):
    return [pltpu.VMEM((share // 128, 128), jnp.float32), pltpu.VMEM((share, 128), jnp.float32)]


def rows_cost(share, parts, cols):
    size = share * len(parts) * cols
    return pl.CostEstimate(flops=4 * size * D, bytes_accessed=2 * size, transcendentals=0)


def first_rows(parts, share, x, y, e, alpha, first, mass, got, blocks):
    cols = y.shape[0]
    got, shifts = got
    return pl.pallas_call(
        functools.partial(first_rows_kernel, parts, tuple(shifts), blocks, len(got)),
        out_shape=[shape(cols, 256, dtype=jnp.bfloat16), shape(1, cols // blocks)]
        + [shape(share, D, dtype=jnp.bfloat16)] * len(parts),
        in_specs=[VMEM] * (6 + len(got)),
        out_specs=[VMEM] * (2 + len(parts)),
        scratch_shapes=[
            pltpu.VMEM((cols // 128, 128), jnp.float32),
            pltpu.VMEM((cols, 128), jnp.float32),
            *rows_scratch(share),
        ],
        compiler_params=pltpu.CompilerParams(vmem_limit_bytes=16 << 20),
        cost_estimate=rows_cost(share * HEAVY, parts, cols),
        name="first_rows",
    )(x, y, e, alpha, first, mass, *[flat(part) for part in got])


def other_rows(parts, share, x, yb, e, alpha, dtype):
    return pl.pallas_call(
        functools.partial(rows_kernel, parts),
        out_shape=[shape(share, D, dtype=dtype)] * len(parts),
        in_specs=[VMEM] * 4,
        out_specs=[VMEM] * len(parts),
        scratch_shapes=rows_scratch(share),
        compiler_params=pltpu.CompilerParams(vmem_limit_bytes=16 << 20),
        cost_estimate=rows_cost(share, parts, yb.shape[0]),
        name="other_rows",
    )(x, yb, e, alpha)


def add_up_kernel(na, scale_ref, *refs):
    ins, (rows_ref, cols_ref, s_ref, sb_ref) = refs[:-4], refs[-4:]
    rows_ref[...] = sum(part[...].astype(jnp.float32) for part in ins[:na])
    spread(scale_ref[...], s_ref, sb_ref)
    cols_ref[...] = 2.0 * sb_ref[...] * sum(part[...].astype(jnp.float32) for part in ins[na:])


def add_up(rows, columns, scale):
    share = scale.shape[1]
    return pl.pallas_call(
        functools.partial(add_up_kernel, len(rows)),
        out_shape=(shape(*rows[0].shape), shape(*columns[0].shape)),
        in_specs=[VMEM] * (1 + len(rows) + len(columns)),
        out_specs=(VMEM,) * 2,
        scratch_shapes=rows_scratch(share),
        compiler_params=pltpu.CompilerParams(vmem_limit_bytes=16 << 20),
        name="add_up",
    )(scale, *rows, *columns)


def shares_kernel(gc_ref, other_ref, *outs):
    share = outs[0].shape[0]
    for k, out_ref in enumerate(outs):
        at = k * share
        total = gc_ref[at:at + share, :] + other_ref[at:at + share, :].astype(jnp.float32)
        out_ref[...] = total.astype(out_ref.dtype)


def shares(gc, other, dtypes):
    share = gc.shape[0] // len(dtypes)
    return pl.pallas_call(
        shares_kernel,
        out_shape=[shape(share, D, dtype=dtype) for dtype in dtypes],
        in_specs=[VMEM] * 2,
        out_specs=[VMEM] * len(dtypes),
        compiler_params=pltpu.CompilerParams(vmem_limit_bytes=16 << 20),
        name="shares",
    )(gc, other)


class Groups:
    def __init__(self, nrow, ncol):
        self.count = nrow * ncol
        self.across = [(a << 1) * ncol + b for a in range(nrow // 2) for b in range(2)]
        self.along = [z << 1 for z in range(ncol // 2)]
        self.core = ncol

    def swap(self, value, mask):
        if mask == 0:
            return value
        return lax.ppermute(value, ("row", "col"), [(i, i ^ mask) for i in range(self.count)])


def local(imu, camera, imu_mass, cam_mass):
    nrow, ncol = lax.axis_size("row"), lax.axis_size("col")
    groups = Groups(nrow, ncol)
    swap, across, along, core = groups.swap, groups.across, groups.along, groups.core
    na, nz = len(across), len(along)
    share_x, share_y = imu.shape[0], camera.shape[1]
    rows, cols = na * share_x, 2 * nz * share_y

    def direct(value, masks):
        return [swap(value, mask) for mask in masks], range(len(masks))

    xs, _ = direct(imu, across)
    own, mine = lax.optimization_barrier((jnp.concatenate([imu, camera[0]]), camera[0]))
    near = [mine] + [None] * (nz - 1)
    for z in range(1, nz):
        if not z & (z - 1):
            near[z] = swap(mine if z == 1 else camera[0], along[z])
    far = [swap(mine, core)]

    def pair(mass, place, share):
        return [lax.dynamic_slice_in_dim(mass, (place ^ k) * share, share, 0) for k in range(2)]

    row, col = lax.axis_index("row"), lax.axis_index("col")
    mass = jnp.concatenate(pair(imu_mass, col, share_x) + pair(cam_mass, row, share_y))

    x, xt, first = row_lse_early(own, xs[1:], far[0])
    relays = [z for z in range(2, nz) if not z & (z - 1)]
    first, got = lax.optimization_barrier((first, [near[z] for z in relays]))
    for z, part in zip(relays, got):
        near[z] = part
    for z in range(1, nz):
        if z & (z - 1):
            near[z] = swap(near[z & (z - 1)], along[z & -z])
    middle = near[1:-1]
    far += [swap(part, core) for part in middle]
    first = row_lse_middle(x, middle, first)
    first, last, mass = lax.optimization_barrier((first, near[-1], mass))
    far.append(swap(last, core))
    y, sent = row_lse_late(own, x, [*middle, last, *far], first, mass, 2 * share_x)
    got, _ = direct(sent.reshape(-1), across)

    sent, e, shift, mass_a = column_lse(x, y, mass, 2 * share_y, got)
    sent = pair_of(lse2, sent, swap(sent.reshape(-1), core), cols, 1, 2)
    got = direct(sent.reshape(-1), along)

    sums, first_beta, mass_b = weighted(
        first_row_kernel, [(1, rows), (1, cols), (1, cols)], e, [shift], got, 2 * nz)
    for step in range(1, ITERS):
        if step > 1:
            sums, = weighted(row_kernel, [(1, rows)], e, [first_beta, mass_b], got, 2 * nz)
        got = direct(sums.reshape(-1), across)
        part, alpha = weighted(column_kernel, [(1, cols), (1, rows)], e, [mass_a, first_beta], got, na)
        part = pair_of(sum, part, swap(part.reshape(-1), core), cols, 1, 2)
        part, alpha = lax.optimization_barrier((part, alpha))
        got = direct(part.reshape(-1), along)

    half = nz // 2
    gc, gc_send, xa = column_grad(range(half, nz), nz, share_y, y, e, first_beta, xt=xt, alpha=alpha)
    far_gc = shares(gc, swap(gc_send, core), [jnp.bfloat16] * (nz - half))
    gc, gc_send = column_grad(range(half), nz, share_y, y, e, first_beta, xa=xa)
    far_gc, alpha = lax.optimization_barrier((far_gc, alpha))
    far_gc = [swap(part, along[half + z]) for z, part in enumerate(far_gc)]
    yb, scale, last = first_rows([na - 1], share_x, x, y, e, alpha, first_beta, mass_b, got, 2 * nz)
    near_gc = shares(gc, swap(gc_send, core), [jnp.float32] + [jnp.bfloat16] * (half - 1))
    (grad_cam, *parts), yb = lax.optimization_barrier((near_gc, yb))
    parts = [swap(part, along[z + 1]) for z, part in enumerate(parts)]
    last = swap(last, across[na - 1])
    sent = other_rows(list(range(1, na - 1)), share_x, x, yb, e, alpha, jnp.bfloat16)
    sent = [swap(part, across[s + 1]) for s, part in enumerate(sent)]
    last, yb = lax.optimization_barrier((last, yb))
    gi, = other_rows([0], share_x, x, yb, e, alpha, jnp.float32)
    grad_imu, grad_cam = add_up([gi, *sent, last], [grad_cam, *parts, *far_gc], scale)
    return grad_imu, grad_cam[None]


def solution(mesh):
    in_specs = (P(("row", "col"), None), P("col", "row", None), P("row"), P("col"))
    out_specs = (P(("row", "col"), None), P("col", "row", None))
    return jax.shard_map(local, mesh=mesh, in_specs=in_specs, out_specs=out_specs, check_vma=False)
```
